128 devices in a mesh: ctx: 16 (over x, y), fsdp: 8 (over z, core).
Axes of the slice: x: 4, y: 4, z: 4, core: 2. Of those that a mesh axis runs over, the one named last changes fastest.
Arguments:
- tokens: bfloat16 [8, 32, 64, 2048], P('fsdp', 'ctx'), may hold values from -6 to 6
- norm_gain: float32 [2048], replicated, may hold values from 0.5 to 1.5
- w_in: bfloat16 [2048, 6704], P('fsdp'), may hold values from -0.125 to 0.125
- w_qkv: bfloat16 [2048, 1536], P('fsdp'), may hold values from -0.125 to 0.125
- conv_weight: float32 [4, 3584], replicated, may hold values from -3 to 3
- conv_bias: float32 [3584], replicated, may hold values from -3 to 3
- dt_bias: float32 [48], replicated, may hold values from -1 to 1
- a_log: float32 [48], replicated, may hold values from -7 to -3
- d_skip: float32 [48], replicated, may hold values from 0.5 to 1.5
- mamba_gain: float32 [3072], replicated, may hold values from 0.5 to 1.5
- w_mout: bfloat16 [3072, 2048], P('fsdp'), may hold values from -0.109375 to 0.109375
- w_aout: bfloat16 [1024, 2048], P('fsdp'), may hold values from -0.5 to 0.5
- mlp_gain: float32 [2048], replicated, may hold values from 0.5 to 1.5
- w_gate_up: bfloat16 [2048, 8192], P('fsdp'), may hold values from -0.125 to 0.125
- w_down: bfloat16 [4096, 2048], P('fsdp'), may hold values from -0.09375 to 0.09375
- cotangent: bfloat16 [8, 32, 64, 2048], P('fsdp', 'ctx'), may hold values from -6 to 6
Outputs:
- output: bfloat16 [8, 32, 64, 2048], P('fsdp', 'ctx')
- d_tokens: bfloat16 [8, 32, 64, 2048], P('fsdp', 'ctx')
- g_norm_gain: float32 [2048], replicated
- g_w_in: float32 [2048, 6704], P('fsdp')
- g_w_qkv: float32 [2048, 1536], P('fsdp')
- g_conv_weight: float32 [4, 3584], replicated
- g_conv_bias: float32 [3584], replicated
- g_dt_bias: float32 [48], replicated
- g_a_log: float32 [48], replicated
- g_d_skip: float32 [48], replicated
- g_mamba_gain: float32 [3072], replicated
- g_w_mout: float32 [3072, 2048], P('fsdp')
- g_w_aout: float32 [1024, 2048], P('fsdp')
- g_mlp_gain: float32 [2048], replicated
- g_w_gate_up: float32 [2048, 8192], P('fsdp')
- g_w_down: float32 [4096, 2048], P('fsdp')
The draws below stay inside these ranges and needn't reach their ends.
All inputs are finite; a program needn't handle non-finite values.
Results may differ from the reference program's by a relative error of at most 0.024.
Values may be sent and summed in bfloat16 or wider, within the bound.
No kernel may reach another device: no remote copies, remote signals or barrier semaphores. Data moves between devices by JAX's collectives and lax.ppermute only.
A program may use at most 576 MiB of HBM per device.

```python
import math
import jax
import jax.numpy as jnp
from jax import lax

D = 2048
MHEADS = 48
MDIM = 64
STATE = 256
CONV_K = 4
QHEADS = 8
KVHEADS = 2
HDIM = 128
FF = 4096
HALF = 64
INNER = 3072
BLOCKS = 32
LENGTH = 2048
SEQS = 8
N_CTX = 16


def steps_of(key, extent, split, least, high):
    def one(dim, parts):
        heights = jax.random.uniform(jax.random.fold_in(jax.random.fold_in(key, 6), dim), (parts,), jnp.float32, least / len(split), high / len(split))
        return jnp.repeat(jnp.exp(heights), extent[dim] // parts).reshape((-1,) + (1,) * (len(extent) - dim - 1))

    loudness = one(*split[0])
    for cut in split[1:]:
        loudness = loudness * one(*cut)
    return loudness


def gaussian(stream_key, shape, width, most, cuts=(), kind=jnp.bfloat16):
    entries = width * jax.random.normal(stream_key, shape, jnp.float32)
    if cuts:
        entries = entries * steps_of(stream_key, shape, cuts, -0.22, 0.18)
    return jnp.clip(entries, -most, most).astype(kind)


def setup_inputs(seed: int = 0) -> dict:
    streams_of = jax.random.split(jax.random.key(seed), 17)
    tokens = gaussian(streams_of[0], (SEQS, BLOCKS, HALF, D), 1.0, 6.0, ((0, 8), (1, 16)))
    norm_gain = jnp.clip(1.0 + 0.1 * jax.random.normal(streams_of[1], (D,), jnp.float32), 0.5, 1.5)
    w_in = gaussian(streams_of[2], (D, 2 * INNER + 2 * STATE + MHEADS), D ** -0.5, 0.125, ((0, 8),))
    w_qkv = gaussian(streams_of[3], (D, (QHEADS + 2 * KVHEADS) * HDIM), D ** -0.5, 0.125, ((0, 8),))
    conv_weight = gaussian(streams_of[4], (CONV_K, INNER + 2 * STATE), CONV_K ** -0.5, 3.0, (), jnp.float32)
    conv_bias = gaussian(streams_of[5], (INNER + 2 * STATE,), 0.5, 3.0, (), jnp.float32)
    dt_bias = jnp.clip(jax.random.uniform(streams_of[6], (MHEADS,), jnp.float32, -1.0, 1.0), -1.0, 1.0)
    a_log = jnp.clip(jax.random.uniform(streams_of[7], (MHEADS,), jnp.float32, -7.0, -3.0), -7.0, -3.0)
    d_skip = jnp.clip(jax.random.uniform(streams_of[8], (MHEADS,), jnp.float32, 0.5, 1.5), 0.5, 1.5)
    mamba_gain = jnp.clip(1.0 + 0.1 * jax.random.normal(streams_of[9], (INNER,), jnp.float32), 0.5, 1.5)
    w_mout = gaussian(streams_of[10], (INNER, D), INNER ** -0.5, 0.109375, ((0, 8),))
    w_aout = gaussian(streams_of[11], (QHEADS * HDIM, D), HDIM ** -0.5, 0.5, ((0, 8),))
    mlp_gain = jnp.clip(1.0 + 0.1 * jax.random.normal(streams_of[12], (D,), jnp.float32), 0.5, 1.5)
    w_gate_up = gaussian(streams_of[13], (D, 2 * FF), D ** -0.5, 0.125, ((0, 8),))
    w_down = gaussian(streams_of[14], (FF, D), FF ** -0.5, 0.09375, ((0, 8),))
    cotangent = gaussian(streams_of[15], (SEQS, BLOCKS, HALF, D), 1.0, 6.0, ((0, 8), (1, 16)))
    return dict(tokens=tokens, norm_gain=norm_gain, w_in=w_in, w_qkv=w_qkv, conv_weight=conv_weight, conv_bias=conv_bias, dt_bias=dt_bias, a_log=a_log, d_skip=d_skip, mamba_gain=mamba_gain, w_mout=w_mout, w_aout=w_aout, mlp_gain=mlp_gain, w_gate_up=w_gate_up, w_down=w_down, cotangent=cotangent)


@jax.custom_vjp
def low(v):
    return lax.optimization_barrier(v.astype(jnp.bfloat16)).astype(jnp.float32)

@jax.custom_vjp
def low_back(v):
    return v

def low_keep(v):
    return (low(v), None)

def low_pass(kept, grad):
    return (grad,)

def back_keep(v):
    return (v, None)

def back_low(kept, grad):
    return (low(grad),)
low.defvjp(low_keep, low_pass)
low_back.defvjp(back_keep, back_low)
EPS = 1e-06
ROPE_BASE = 100000000000.0
HIGH = lax.Precision.HIGHEST
MASKED = -1e+30

def matmul(left, right):
    return jnp.dot(left, right, precision=HIGH, preferred_element_type=jnp.float32)

def norm_rows(values, gain):
    return values * lax.rsqrt(lax.optimization_barrier(jnp.mean(values * values, axis=-1, keepdims=True)) + EPS) * gain

def rotate(values, positions):
    half_dim = values.shape[-1] // 2
    freqs = ROPE_BASE ** (-jnp.arange(half_dim, dtype=jnp.float32) / half_dim)
    angles = positions.astype(jnp.float32)[:, None] * freqs[None, :]
    cosine = jnp.cos(angles)[:, None, :]
    sine = 1.0 * jnp.sin(angles)[:, None, :]
    first = values[..., :half_dim]
    second = values[..., half_dim:]
    return jnp.concatenate([first * cosine - second * sine, second * cosine + first * sine], axis=-1)

def span_step(state, block):
    xs, bmat, cmat, steps_dt, cumul = block
    rows = xs.shape[0]
    lower = jnp.arange(rows)[:, None] >= jnp.arange(rows)[None, :]
    gaps = cumul[:, None, :] - cumul[None, :, :]
    decays = jnp.where(lower[:, :, None], jnp.exp(jnp.where(lower[:, :, None], gaps, 0.0)), 0.0)
    intersection = jnp.einsum('tn,sn->ts', cmat, bmat, precision=HIGH)
    mixing = intersection[..., None] * decays * steps_dt[None, :, :]
    within = jnp.einsum('tsh,shp->thp', mixing, xs, precision=HIGH)
    carried = jnp.exp(cumul)[..., None] * jnp.einsum('tn,hpn->thp', cmat, state, precision=HIGH)
    weights = jnp.exp(cumul[-1:, :] - cumul) * steps_dt
    local = jnp.einsum('sh,shp,sn->hpn', weights, xs, bmat, precision=HIGH)
    leaving = jnp.exp(cumul[-1, :])[:, None, None] * state + local
    return (leaving, within + carried)

def mamba_mix(proj, conv_weight, conv_bias, dt_bias, a_log, d_skip, mamba_gain):
    gate_z = proj[:, :INNER]
    xbc = proj[:, INNER:2 * INNER + 2 * STATE]
    dt_raw = proj[:, 2 * INNER + 2 * STATE:]
    padded = jnp.pad(xbc, ((CONV_K - 1, 0), (0, 0)))
    mixed = sum((conv_weight[tap] * padded[tap:tap + LENGTH] for tap in range(CONV_K))) + conv_bias
    active = jax.nn.silu(mixed)
    xs = active[:, :INNER].reshape(BLOCKS, HALF, MHEADS, MDIM)
    bmat = active[:, INNER:INNER + STATE].reshape(BLOCKS, HALF, STATE)
    cmat = active[:, INNER + STATE:].reshape(BLOCKS, HALF, STATE)
    steps_dt = jax.nn.softplus(dt_raw + dt_bias).reshape(BLOCKS, HALF, MHEADS)
    cumul = jnp.cumsum(steps_dt * -jnp.exp(a_log), axis=1)
    start = jnp.zeros((MHEADS, MDIM, STATE), jnp.float32)
    final, ssd = lax.scan(jax.checkpoint(span_step), start, (xs, bmat, cmat, steps_dt, cumul))
    ssd = ssd + d_skip[:, None] * xs
    gated = ssd.reshape(LENGTH, INNER) * jax.nn.silu(gate_z)
    return norm_rows(gated, mamba_gain)

def attention(qkv, positions):
    width_q = QHEADS * HDIM
    width_k = KVHEADS * HDIM
    groups = QHEADS // KVHEADS
    query = low(rotate(qkv[:, :width_q].reshape(LENGTH, QHEADS, HDIM), positions))
    query = query.reshape(LENGTH, KVHEADS, groups, HDIM)
    keys = low(rotate(qkv[:, width_q:width_q + width_k].reshape(LENGTH, KVHEADS, HDIM), positions))
    values = low(qkv[:, width_q + width_k:].reshape(LENGTH, KVHEADS, HDIM))
    rows = math.gcd(512, LENGTH)
    scale = HDIM ** (-0.5)

    def one_block(start):
        query_part = lax.dynamic_slice_in_dim(query, start, rows, 0)
        raw = jnp.einsum('tkgd,skd->kgts', query_part, keys, precision=HIGH) * scale
        scores = low_back(raw)
        query_pos = start + jnp.arange(rows, dtype=jnp.int32)
        visible = positions[None, :] <= query_pos[:, None]
        scores = jnp.where(visible[None, None], scores, MASKED)
        total = jax.nn.logsumexp(scores, axis=-1, keepdims=True)
        probs = low(jnp.exp(scores - total))
        mixed = jnp.einsum('kgts,skd->tkgd', probs, values, precision=HIGH)
        return mixed.reshape(rows, width_q)
    starts = jnp.arange(0, LENGTH, rows, dtype=jnp.int32)
    blocks = lax.map(jax.checkpoint(one_block), starts)
    return blocks.reshape(LENGTH, width_q)

def layer(x_seq, weights):
    norm_gain, w_in, w_qkv, conv_weight, conv_bias, dt_bias, a_log, d_skip, mamba_gain, w_mout, w_aout, mlp_gain, w_gate_up, w_down = weights
    normed = low(norm_rows(x_seq, norm_gain))
    proj = low_back(matmul(normed, w_in))
    qkv = low_back(matmul(normed, w_qkv))
    positions = jnp.arange(LENGTH, dtype=jnp.int32)
    gated = low(mamba_mix(proj, conv_weight, conv_bias, dt_bias, a_log, d_skip, mamba_gain))
    mamba_out = low_back(matmul(gated, w_mout))
    heads = low(low_back(attention(qkv, positions)))
    attn_out = low_back(matmul(heads, w_aout))
    mixed = x_seq + mamba_out + attn_out
    normed_two = low(norm_rows(mixed, mlp_gain))
    gate_up = low_back(matmul(normed_two, w_gate_up))
    act = low(jax.nn.silu(gate_up[:, :FF]) * gate_up[:, FF:])
    return mixed + low_back(matmul(act, w_down))

def natural_order():
    blocks = jnp.arange(BLOCKS, dtype=jnp.int32)
    return jnp.where(blocks < N_CTX, 2 * blocks, 2 * (BLOCKS - 1 - blocks) + 1).astype(jnp.int32)

def dealt_order():
    slots = jnp.arange(BLOCKS, dtype=jnp.int32)
    return jnp.where(slots % 2 == 0, slots // 2, BLOCKS - 1 - slots // 2).astype(jnp.int32)

def reference(tokens, norm_gain, w_in, w_qkv, conv_weight, conv_bias, dt_bias, a_log, d_skip, mamba_gain, w_mout, w_aout, mlp_gain, w_gate_up, w_down, cotangent):
    order = natural_order()
    x_nat = jnp.take(tokens.astype(jnp.float32), order, axis=1).reshape(SEQS, LENGTH, D)
    cot_nat = jnp.take(cotangent.astype(jnp.float32), order, axis=1).reshape(SEQS, LENGTH, D)
    params = (norm_gain.astype(jnp.float32), w_in.astype(jnp.float32), w_qkv.astype(jnp.float32), conv_weight.astype(jnp.float32), conv_bias.astype(jnp.float32), dt_bias.astype(jnp.float32), a_log.astype(jnp.float32), d_skip.astype(jnp.float32), mamba_gain.astype(jnp.float32), w_mout.astype(jnp.float32), w_aout.astype(jnp.float32), mlp_gain.astype(jnp.float32), w_gate_up.astype(jnp.float32), w_down.astype(jnp.float32))

    def forward(x_all, p0, p1, p2, p3, p4, p5, p6, p7, p8, p9, p10, p11, p12, p13):
        weights = (p0, p1, p2, p3, p4, p5, p6, p7, p8, p9, p10, p11, p12, p13)
        return lax.map(lambda one: layer(one, weights), x_all)
    out, back = jax.vjp(forward, x_nat, params[0], params[1], params[2], params[3], params[4], params[5], params[6], params[7], params[8], params[9], params[10], params[11], params[12], params[13])
    grads = back(cot_nat)
    back_order = dealt_order()

    def dealt(values):
        return jnp.take(values.reshape(SEQS, BLOCKS, HALF, D), back_order, axis=1)
    return (dealt(out).astype(jnp.bfloat16), dealt(grads[0]).astype(jnp.bfloat16), grads[1], grads[2], grads[3], grads[4], grads[5], grads[6], grads[7], grads[8], grads[9], grads[10], grads[11], grads[12], grads[13], grads[14])
```

```python
import jax
import jax.numpy as jnp
from jax import lax
from jax.experimental import pallas as pl
from jax.experimental.pallas import tpu as pltpu
from jax.sharding import PartitionSpec as P

D = 2048
MHEADS = 48
MDIM = 64
STATE = 256
CONV_K = 4
QHEADS = 8
KVHEADS = 2
HDIM = 128
FF = 4096
HALF = 64
INNER = 3072
LENGTH = 2048
SEQS = 8
NC = 16
NF = 8
NZ = 4
LANES = 128
ROWS = 2 * HALF
GROUP = SEQS * ROWS
INNER_F = INNER // NF
HEADS_L = 3
XW = HEADS_L * MDIM
BC_F = 2 * STATE // NF
DT_F = MHEADS // NF
FF_F = FF // NF
CHUNK = 256
CHUNKS = LENGTH // CHUNK
PAIRS = LENGTH // LANES
QROWS = LENGTH // 2
QBLOCK = 128
SHARD = D // NF
SLICE = SHARD // NC
MIX = INNER_F + LANES
QKV = 3 * HDIM
WM_COLS = MIX + QKV
W1_COLS = WM_COLS + INNER_F
MLP_COLS = 2 * FF_F
OUT_ROWS = INNER_F + HDIM
K_AT, V_AT, Q_AT, ATTN = 0, 128, 256, 320
XB = XW + BC_F
B_AT, T_AT, PACK = XW, XB, XB + 16
BOTH = XW + HALF
GATE_SEQS = 4
PART = 16
EPS = 1e-06
ROPE_BASE = 100000000000.0
MASKED = -1e30
SCALE = HDIM ** (-0.5)
BF = jnp.bfloat16
F32 = jnp.float32
PARAMS = pltpu.CompilerParams(vmem_limit_bytes=56 * 1024 * 1024)
SMEM = pl.BlockSpec(memory_space=pltpu.SMEM)


def dot(left, right, left_dim, right_dim):
    return lax.dot_general(
        left, right, (((left_dim,), (right_dim,)), ((), ())), preferred_element_type=F32
    )


def whole(*shape):
    return pl.BlockSpec(shape, lambda *i: (0,) * len(shape))


def cost(flops, moved, transcendentals=0):
    return pl.CostEstimate(
        flops=int(flops), bytes_accessed=int(moved), transcendentals=int(transcendentals)
    )


def shape_of(shape, dtype):
    return jax.ShapeDtypeStruct(shape, dtype)


OTHER_CORE = [(i, i ^ 1) for i in range(NF)]
TO_NEXT = [(i, (i + 2) % NF) for i in range(NF)]
TO_PREV = [(i, (i - 2) % NF) for i in range(NF)]


def send(value, route):
    return lax.ppermute(value, "fsdp", route)


def gather_fsdp(value):
    return lax.all_gather(value, "fsdp", axis=0, tiled=True)


def scatter_fsdp(parts):
    return lax.psum_scatter(parts, "fsdp", scatter_dimension=0, tiled=True).astype(F32)


def ring_pieces(value):
    half = value.shape[0] // 2
    after = send(value, TO_PREV)
    before = send(value, TO_NEXT)
    near = send(value, OTHER_CORE)
    far = jnp.concatenate(
        [send(after[:half], TO_PREV), send(before[half:], TO_NEXT)], axis=0
    )
    near_after = send(after, OTHER_CORE)
    near_before = send(before, OTHER_CORE)
    near_far = send(far, OTHER_CORE)
    return [value, after, far, before, near, near_after, near_far, near_before]


def ring_gather(value, order):
    whole_value = jnp.zeros((NF * value.shape[0],) + value.shape[1:], value.dtype)
    for index, piece in enumerate(ring_pieces(value)):
        whole_value = lax.dynamic_update_slice(
            whole_value, piece, (order[index] * value.shape[0], 0)
        )
    return whole_value


def plus(*terms):
    return sum(term.astype(F32) for term in terms)


def ring_join(mine, other):
    return plus(mine, send(other, OTHER_CORE)).astype(BF)


def ring_scatter(joined):
    size = joined.shape[0] // NZ
    half = size // 2
    own, after, far, before = [joined[i * size : (i + 1) * size] for i in range(NZ)]
    far_next = send(far[:half], TO_NEXT)
    far_prev = send(far[half:], TO_PREV)
    after_two = send(after[half:], TO_NEXT)
    before_one = send(before[:half], TO_PREV)
    after_one = send(plus(after[:half], far_next).astype(BF), TO_NEXT)
    before_two = send(plus(before[half:], far_prev).astype(BF), TO_PREV)
    return plus(
        own,
        jnp.concatenate([after_one, after_two], axis=0),
        jnp.concatenate([before_one, before_two], axis=0),
    )


def after(value, *others):
    return lax.optimization_barrier((value,) + others)[0]


def swap_ctx(value):
    return lax.all_to_all(value, "ctx", 0, 0, tiled=True)


def swap_fsdp(value):
    return lax.all_to_all(value, "fsdp", 0, 0, tiled=True)


def butterfly(value, axis, size):
    bit = 1
    while bit < size:
        value = value + lax.ppermute(value, axis, [(i, i ^ bit) for i in range(size)])
        bit *= 2
    return value


def rotate(values, cosine, sine):
    half = values.shape[-1] // 2
    first = values[:, :half]
    second = values[:, half:]
    return jnp.concatenate(
        [first * cosine - second * sine, second * cosine + first * sine], axis=1
    )


def proj_kernel(n_ref, w_ref, cos_ref, sin_ref, mix_ref, attn_ref):
    acc = jnp.zeros((2 * ROWS, WM_COLS), F32)
    for f in range(NF):
        acc = acc + dot(
            n_ref[:, f * SHARD : (f + 1) * SHARD],
            w_ref[:, f, :, :WM_COLS].reshape(SHARD, WM_COLS),
            1,
            0,
        )
    for j in range(2):
        rows = acc[j * ROWS : (j + 1) * ROWS]
        x_rows = rows[:, :INNER_F].T.astype(BF)
        tail = rows[:, INNER_F:MIX].T
        query = rotate(rows[:, MIX : MIX + HDIM], cos_ref[...], sin_ref[...]).astype(BF)
        key = rotate(
            rows[:, MIX + HDIM : MIX + 2 * HDIM], cos_ref[...], sin_ref[...]
        ).astype(BF)
        value = rows[:, MIX + 2 * HDIM :].astype(BF)
        for p in range(2):
            to = 2 * j + p
            attn_ref[to, K_AT:V_AT] = key
            attn_ref[to, V_AT:Q_AT] = value
            attn_ref[to, Q_AT:] = query[p * HALF : (p + 1) * HALF]
            mix_ref[to, :B_AT] = x_rows[p * XW : (p + 1) * XW]
            mix_ref[to, B_AT:T_AT] = tail[:BC_F].astype(BF)
            steps = tail[BC_F + p * HEADS_L : BC_F + (p + 1) * HEADS_L]
            high = steps.astype(BF).astype(F32)
            mix_ref[to, T_AT:] = jnp.concatenate(
                [high, steps - high, jnp.zeros((16 - 2 * HEADS_L, ROWS), F32)], axis=0
            ).astype(BF)


def packets(rows):
    return pl.BlockSpec((4, rows, LANES), lambda i: (i, 0, 0))


def token_rows(width):
    return pl.BlockSpec((2 * ROWS, width), lambda i: (i, 0))


def project(normed, w_one, cosine, sine):
    return pl.pallas_call(
        proj_kernel,
        grid=(SEQS // 2,),
        in_specs=[
            token_rows(D),
            whole(NC, NF, SLICE, W1_COLS),
            whole(ROWS, HALF),
            whole(ROWS, HALF),
        ],
        out_specs=[packets(PACK), packets(ATTN)],
        out_shape=[shape_of((NC, PACK, LANES), BF), shape_of((NC, ATTN, LANES), BF)],
        compiler_params=PARAMS,
        cost_estimate=cost(2 * GROUP * D * WM_COLS, 10e6),
        name="project",
    )(normed, w_one, cosine, sine)


def proj_z_kernel(n_ref, w_ref, z_ref):
    acc = jnp.zeros((2 * ROWS, INNER_F), F32)
    for f in range(NF):
        acc = acc + dot(
            n_ref[:, f * SHARD : (f + 1) * SHARD],
            w_ref[:, f, :, WM_COLS:].reshape(SHARD, INNER_F),
            1,
            0,
        )
    for j in range(2):
        z_ref[j] = acc[j * ROWS : (j + 1) * ROWS].T


def project_z(normed, w_z):
    return pl.pallas_call(
        proj_z_kernel,
        grid=(SEQS // 2,),
        in_specs=[token_rows(D), whole(NC, NF, SLICE, W1_COLS)],
        out_specs=pl.BlockSpec((2, INNER_F, ROWS), lambda i: (i, 0, 0)),
        out_shape=shape_of((SEQS, INNER_F, ROWS), F32),
        compiler_params=PARAMS,
        cost_estimate=cost(2 * GROUP * D * INNER_F, 8e6),
        name="project_z",
    )(normed, w_z)


def attn_grads_kernel(got_ref, cos_ref, sin_ref, out_ref):
    for j in range(2):
        one = got_ref[2 * j].astype(F32)
        two = got_ref[2 * j + 1].astype(F32)
        both = one + two
        query = jnp.concatenate([one[Q_AT:], two[Q_AT:]], axis=0)
        query = rotate(query, cos_ref[...], -sin_ref[...])
        key = rotate(both[K_AT:V_AT], cos_ref[...], -sin_ref[...])
        out_ref[j * ROWS : (j + 1) * ROWS] = jnp.concatenate(
            [query, key, both[V_AT:Q_AT]], axis=1
        ).astype(BF)


def attn_grads(got, cosine, sine):
    return pl.pallas_call(
        attn_grads_kernel,
        grid=(SEQS // 2,),
        in_specs=[packets(ATTN), whole(ROWS, HALF), whole(ROWS, HALF)],
        out_specs=token_rows(QKV),
        out_shape=shape_of((GROUP, QKV), BF),
        compiler_params=PARAMS,
        cost_estimate=cost(10 * GROUP * QKV, 2e6),
        name="attn_grads",
    )(got, cosine, sine)


def mix_grads_kernel(got_ref, out_ref):
    for j in range(2):
        one = got_ref[2 * j].astype(F32)
        two = got_ref[2 * j + 1].astype(F32)
        x_rows = jnp.concatenate([one[:B_AT], two[:B_AT]], axis=0).T
        tail = jnp.concatenate(
            [
                one[B_AT:T_AT] + two[B_AT:T_AT],
                one[T_AT : T_AT + HEADS_L],
                two[T_AT : T_AT + HEADS_L],
                jnp.zeros((LANES - BC_F - DT_F, ROWS), F32),
            ],
            axis=0,
        ).T
        out_ref[j * ROWS : (j + 1) * ROWS] = jnp.concatenate([x_rows, tail], axis=1).astype(BF)


def mix_grads(got):
    return pl.pallas_call(
        mix_grads_kernel,
        grid=(SEQS // 2,),
        in_specs=[packets(PACK)],
        out_specs=token_rows(MIX),
        out_shape=shape_of((GROUP, MIX), BF),
        compiler_params=PARAMS,
        cost_estimate=cost(4 * GROUP * MIX, 2.2e6),
        name="mix_grads",
    )(got)


def back_kernel(
    spot_ref, mix_ref, dqkv_ref, dz_ref, n_ref, w_ref, mine_ref, other_ref, gain_ref
):
    @pl.when(pl.program_id(0) == 0)
    def _():
        gain_ref[...] = jnp.zeros_like(gain_ref)

    first = spot_ref[NZ] == 0
    grad = jnp.concatenate([mix_ref[...], dqkv_ref[...], dz_ref[...]], axis=1)
    for f in range(NF):
        part = slice(f * SHARD, (f + 1) * SHARD)
        dn = dot(grad, w_ref[:, f].reshape(SHARD, W1_COLS), 1, 1)
        gain_ref[:, part] += jnp.sum(dn * n_ref[:, part].astype(F32), axis=0, keepdims=True)
        dn = dn.astype(BF)
        mine_ref[0, :, part] = jnp.where(first, dn[:ROWS], dn[ROWS:])
        other_ref[0, :, part] = jnp.where(first, dn[ROWS:], dn[:ROWS])


def back_project(spot, mix, dqkv, dz, normed, w_one):
    def rows(width):
        return pl.BlockSpec((2 * ROWS, width), lambda i, spot: (i, 0))

    specs, shapes = ring_specs(D)
    return pl.pallas_call(
        back_kernel,
        grid_spec=pltpu.PrefetchScalarGridSpec(
            num_scalar_prefetch=1,
            grid=(SEQS // 2,),
            in_specs=[
                rows(MIX),
                rows(QKV),
                rows(INNER_F),
                rows(D),
                pl.BlockSpec((NC, NF, SLICE, W1_COLS), lambda i, spot: (0, 0, 0, 0)),
            ],
            out_specs=specs + [pl.BlockSpec((1, D), lambda i, spot: (0, 0))],
        ),
        out_shape=shapes + [shape_of((1, D), F32)],
        compiler_params=PARAMS,
        cost_estimate=cost(2 * GROUP * D * W1_COLS, 18e6),
        name="back_project",
    )(spot, mix, dqkv, dz, normed, w_one)


def column_grad_kernel(left_ref, *refs):
    out_ref = refs[-1]
    first = 0
    for right_ref in refs[:-1]:
        term = dot(left_ref[...], right_ref[...], 0, 0).astype(BF)
        for block in range(out_ref.shape[1]):
            for tile in range(right_ref.shape[1] // LANES):
                out_ref[:, block, first + tile] = term[
                    block * SHARD : (block + 1) * SHARD, tile * LANES : (tile + 1) * LANES
                ].reshape(NC, SLICE, LANES)
        first += right_ref.shape[1] // LANES


def column_grad(left, *rights):
    count, width = left.shape[1] // SHARD, sum(right.shape[1] for right in rights)
    tiles = width // LANES
    many = 2
    return pl.pallas_call(
        column_grad_kernel,
        grid=(count // many,),
        in_specs=[pl.BlockSpec((GROUP, many * SHARD), lambda i: (0, i))]
        + [whole(GROUP, right.shape[1]) for right in rights],
        out_specs=pl.BlockSpec((NC, many, tiles, SLICE, LANES), lambda i: (0, i, 0, 0, 0)),
        out_shape=shape_of((NC, count, tiles, SLICE, LANES), BF),
        compiler_params=PARAMS,
        cost_estimate=cost(
            2 * GROUP * left.shape[1] * width,
            2 * GROUP * (left.shape[1] + width) + 2 * left.shape[1] * width,
        ),
        name="column_grad",
    )(left, *rights)


def channels(count):
    return pl.BlockSpec((count, INNER_F, ROWS), lambda i: (i, 0, 0))


def gate_packets(rows):
    return pl.BlockSpec((2 * GATE_SEQS, rows, LANES), lambda i: (i, 0, 0))


def gate_kernel(got_ref, z_ref, g_ref, sq_ref):
    for j in range(GATE_SEQS):
        ssd = got_ref[2 * j : 2 * j + 2, :XW].reshape(INNER_F, ROWS).astype(F32)
        z = z_ref[j]
        g = ssd * (z * jax.nn.sigmoid(z))
        g_ref[j] = g
        seq = pl.program_id(0) * GATE_SEQS + j
        sq_ref[pl.ds(seq, 1)] = jnp.sum(g * g, axis=0, keepdims=True)


def gate(got, z):
    return pl.pallas_call(
        gate_kernel,
        grid=(SEQS // GATE_SEQS,),
        in_specs=[gate_packets(XW), channels(GATE_SEQS)],
        out_specs=[channels(GATE_SEQS), whole(SEQS, ROWS)],
        out_shape=[shape_of((SEQS, INNER_F, ROWS), F32), shape_of((SEQS, ROWS), F32)],
        compiler_params=PARAMS,
        cost_estimate=cost(8 * GROUP * INNER_F, 4.2e6, GROUP * INNER_F),
        name="gate",
    )(got, z)


def branch_kernel(heads_ref, g_ref, sq_ref, gain_ref, w_ref, gh_ref, out_ref):
    step = pl.program_id(0)
    for j in range(2):
        scale = lax.rsqrt(sq_ref[pl.ds(2 * step + j, 1)] / INNER + EPS)
        gated = (g_ref[j] * scale * gain_ref[...]).T.astype(BF)
        heads = heads_ref[2 * j : 2 * j + 2].reshape(ROWS, HDIM)
        gh_ref[j * ROWS : (j + 1) * ROWS] = jnp.concatenate([gated, heads], axis=1)
    out_ref[...] = dot(gh_ref[...], w_ref[...], 1, 0).astype(BF)


def branch_out(heads, g, squares, gain, w_out):
    return pl.pallas_call(
        branch_kernel,
        grid=(SEQS // 2,),
        in_specs=[
            packets(HALF),
            channels(2),
            whole(SEQS, ROWS),
            whole(INNER_F, 1),
            whole(OUT_ROWS, D),
        ],
        out_specs=[token_rows(OUT_ROWS), token_rows(D)],
        out_shape=[shape_of((GROUP, OUT_ROWS), BF), shape_of((GROUP, D), BF)],
        compiler_params=PARAMS,
        cost_estimate=cost(2 * GROUP * OUT_ROWS * D, 10e6),
        name="branch_out",
    )(heads, g, squares, gain, w_out)


def branch_back_kernel(d_ref, w_ref, g_ref, gain_ref, dg_ref, inner_ref, dh_ref):
    step = pl.program_id(0)
    both = dot(d_ref[...], w_ref[...], 1, 1)
    for j in range(2):
        rows = both[j * ROWS : (j + 1) * ROWS]
        d_gated = rows[:, :INNER_F].T
        dg_ref[j] = d_gated
        inner_ref[pl.ds(2 * step + j, 1)] = jnp.sum(
            d_gated * gain_ref[...] * g_ref[j], axis=0, keepdims=True
        )
        heads = rows[:, INNER_F:].astype(BF)
        dh_ref[2 * j : 2 * j + 2] = heads.reshape(2, HALF, HDIM)


def branch_back(branch, w_out, g, gain):
    return pl.pallas_call(
        branch_back_kernel,
        grid=(SEQS // 2,),
        in_specs=[token_rows(D), whole(OUT_ROWS, D), channels(2), whole(INNER_F, 1)],
        out_specs=[channels(2), whole(SEQS, ROWS), packets(HALF)],
        out_shape=[
            shape_of((SEQS, INNER_F, ROWS), F32),
            shape_of((SEQS, ROWS), F32),
            shape_of((NC, HALF, HDIM), BF),
        ],
        compiler_params=PARAMS,
        cost_estimate=cost(2 * GROUP * OUT_ROWS * D, 10e6),
        name="branch_back",
    )(branch, w_out, g, gain)


def gate_back_kernel(
    got_ref, z_ref, g_ref, dg_ref, dh_ref, sq_ref, inner_ref, gain_ref,
    pack_ref, dz_ref, gain_grad_ref,
):
    index = pl.program_id(0)

    @pl.when(index == 0)
    def _():
        gain_grad_ref[...] = jnp.zeros_like(gain_grad_ref)

    pack_ref[:, XW:] = dh_ref[...]
    for j in range(GATE_SEQS):
        ssd = got_ref[2 * j : 2 * j + 2, :XW].reshape(INNER_F, ROWS).astype(F32)
        z = z_ref[j]
        g = g_ref[j]
        sig = jax.nn.sigmoid(z)
        silu = z * sig
        seq = index * GATE_SEQS + j
        scale = lax.rsqrt(sq_ref[pl.ds(seq, 1)] / INNER + EPS)
        inner = inner_ref[pl.ds(seq, 1)] / INNER
        scaled = dg_ref[j] * scale
        d_g = scaled * gain_ref[...] - g * (scale * scale * scale * inner)
        gain_grad_ref[...] += jnp.sum(scaled * g, axis=1, keepdims=True)
        pack_ref[2 * j : 2 * j + 2, :XW] = (d_g * silu).astype(BF).reshape(2, XW, LANES)
        dz_ref[j * ROWS : (j + 1) * ROWS] = (
            (d_g * ssd * (sig + silu * (1.0 - sig))).T.astype(BF)
        )


def gate_back(got, z, g, dg, dh, squares, inner, gain):
    return pl.pallas_call(
        gate_back_kernel,
        grid=(SEQS // GATE_SEQS,),
        in_specs=[
            gate_packets(XW),
            channels(GATE_SEQS),
            channels(GATE_SEQS),
            channels(GATE_SEQS),
            gate_packets(HALF),
            whole(SEQS, ROWS),
            whole(SEQS, ROWS),
            whole(INNER_F, 1),
        ],
        out_specs=[
            gate_packets(BOTH),
            pl.BlockSpec((GATE_SEQS * ROWS, INNER_F), lambda i: (i, 0)),
            whole(INNER_F, 1),
        ],
        out_shape=[
            shape_of((NC, BOTH, LANES), BF),
            shape_of((GROUP, INNER_F), BF),
            shape_of((INNER_F, 1), F32),
        ],
        compiler_params=PARAMS,
        cost_estimate=cost(20 * GROUP * INNER_F, 8e6, GROUP * INNER_F),
        name="gate_back",
    )(got, z, g, dg, dh, squares, inner, gain)


def act_back_kernel(cot_ref, down_ref, out_ref):
    out_ref[...] = dot(cot_ref[...], down_ref[...], 1, 1)


def act_back(cot, w_down):
    return pl.pallas_call(
        act_back_kernel,
        grid=(SEQS // 2,),
        in_specs=[token_rows(D), whole(FF_F, D)],
        out_specs=token_rows(FF_F),
        out_shape=shape_of((GROUP, FF_F), F32),
        compiler_params=PARAMS,
        cost_estimate=cost(2 * GROUP * D * FF_F, 9e6),
        name="act_back",
    )(cot, w_down)


def mlp_kernel(n_ref, d_act_ref, w_ref, act_ref, dgu_ref, dn_ref):
    acc = jnp.zeros((2 * ROWS, MLP_COLS), F32)
    for f in range(NF):
        acc = acc + dot(
            n_ref[:, f * SHARD : (f + 1) * SHARD], w_ref[:, f].reshape(SHARD, MLP_COLS), 1, 0
        )
    gate_part, upper = acc[:, :FF_F], acc[:, FF_F:]
    sig = jax.nn.sigmoid(gate_part)
    silu = gate_part * sig
    act_ref[...] = (silu * upper).astype(BF)
    d_act = d_act_ref[...]
    d_gu = jnp.concatenate(
        [d_act * upper * (sig + silu * (1.0 - sig)), d_act * silu], axis=1
    ).astype(BF)
    dgu_ref[...] = d_gu
    for f in range(NF):
        dn_ref[:, f * SHARD : (f + 1) * SHARD] = dot(
            d_gu, w_ref[:, f].reshape(SHARD, MLP_COLS), 1, 1
        ).astype(BF)


def mlp(normed, d_act, w_gu):
    return pl.pallas_call(
        mlp_kernel,
        grid=(SEQS // 2,),
        in_specs=[token_rows(D), token_rows(FF_F), whole(NC, NF, SLICE, MLP_COLS)],
        out_specs=[token_rows(FF_F), token_rows(MLP_COLS), token_rows(D)],
        out_shape=[
            shape_of((GROUP, FF_F), BF),
            shape_of((GROUP, MLP_COLS), BF),
            shape_of((GROUP, D), BF),
        ],
        compiler_params=PARAMS,
        cost_estimate=cost(8 * GROUP * D * FF_F, 20e6, GROUP * FF_F),
        name="mlp",
    )(normed, d_act, w_gu)


def ring_specs(width):
    def spec(*_):
        return pl.BlockSpec((1, ROWS, width), lambda i, spot: (spot[i], 0, 0))

    return [spec(), spec()], [shape_of((NZ, ROWS, width), BF)] * 2


def down_kernel(spot_ref, act_ref, down_ref, mine_ref, other_ref):
    rows = dot(act_ref[...], down_ref[...], 1, 0).astype(BF)
    first = spot_ref[NZ] == 0
    mine_ref[0] = jnp.where(first, rows[:ROWS], rows[ROWS:])
    other_ref[0] = jnp.where(first, rows[ROWS:], rows[:ROWS])


def down_out(spot, act, w_down):
    specs, shapes = ring_specs(D)
    return pl.pallas_call(
        down_kernel,
        grid_spec=pltpu.PrefetchScalarGridSpec(
            num_scalar_prefetch=1,
            grid=(SEQS // 2,),
            in_specs=[
                pl.BlockSpec((2 * ROWS, FF_F), lambda i, spot: (i, 0)),
                pl.BlockSpec((FF_F, D), lambda i, spot: (0, 0)),
            ],
            out_specs=specs,
        ),
        out_shape=shapes,
        compiler_params=PARAMS,
        cost_estimate=cost(2 * GROUP * D * FF_F, 8e6),
        name="down_out",
    )(spot, act, w_down)


def lane_of(shape):
    return lax.broadcasted_iota(jnp.int32, shape, 1)


def sources(pair, first):
    if first:
        return 2 * pair, 2 * pair + 1
    return NC - 1 - 2 * pair, NC - 2 - 2 * pair


def assemble(ref, low, high, pair, first):
    one, two = sources(pair, first)
    left = lane_of((high - low, LANES)) < HALF
    return jnp.where(left, ref[one, low:high].astype(F32), ref[two, low:high].astype(F32))


def deal(ref, low, high, pair, first, values):
    one, two = sources(pair, first)
    values = values.astype(BF)
    ref[one, low:high, :HALF] = values[:, :HALF]
    ref[two, low:high, HALF:] = values[:, HALF:]


def taps_of(padded, taps):
    current = padded[:, LANES:]
    total = current * taps[:, CONV_K - 1 : CONV_K] + taps[:, CONV_K : CONV_K + 1]
    inputs = [current]
    for back in range(1, CONV_K):
        moved = pltpu.roll(padded, back, 1)[:, LANES:]
        inputs.append(moved)
        total = total + moved * taps[:, CONV_K - 1 - back : CONV_K - back]
    return inputs[::-1], total


def softplus(values):
    return jnp.maximum(values, 0.0) + jnp.log1p(jnp.exp(-jnp.abs(values)))


def at_pair(pair):
    return pl.ds(pl.multiple_of(pair * LANES, LANES), LANES)


def load_raw(got_ref, raw_ref):
    raw_ref[:, :LANES] = jnp.zeros((XB, LANES), F32)
    half_pairs = PAIRS // 2
    for first in (True, False):

        def load(pair, unused, first=first):
            place = at_pair((pair if first else pair + half_pairs) + 1)
            raw_ref[:, place] = assemble(got_ref, 0, XB, pair, first)
            return unused

        lax.fori_loop(0, half_pairs, load, 0, unroll=True)


def front_kernel(got_ref, taps_ref, heads_ref, x_ref, bc_ref, row_ref, raw_ref):
    load_raw(got_ref, raw_ref)

    def step(part, unused):
        rows = pl.ds(pl.multiple_of(part * PART, PART), PART)
        _, total = taps_of(raw_ref[rows], taps_ref[rows])
        active = (total * jax.nn.sigmoid(total)).astype(BF)

        @pl.when(part < XW // PART)
        def _():
            x_ref[rows] = active

        @pl.when(part >= XW // PART)
        def _():
            bc_ref[pl.ds(pl.multiple_of(part * PART - XW, PART), PART)] = active

        return unused

    lax.fori_loop(0, XB // PART, step, 0)
    half_pairs = PAIRS // 2
    parts = [
        assemble(got_ref, T_AT, PACK, index % half_pairs, index < half_pairs)
        for index in range(PAIRS)
    ]
    parts = jnp.concatenate(parts, axis=1)
    raw = parts[:HEADS_L] + parts[HEADS_L : 2 * HEADS_L] + heads_ref[:HEADS_L, :1]
    steps = softplus(raw)
    pad = jnp.zeros((8 - 2 * HEADS_L, LENGTH), F32)
    sums = jnp.concatenate([steps * heads_ref[HEADS_L : 2 * HEADS_L, :1], steps, pad], axis=0)
    rows = lax.broadcasted_iota(jnp.int32, sums.shape, 0)
    lane = lane_of(sums.shape) % CHUNK
    running = sums
    back = 1
    while back < CHUNK:
        running = running + jnp.where(lane >= back, pltpu.roll(running, back, 1), 0.0)
        back *= 2
    row_ref[:8] = jnp.where(rows < HEADS_L, running, sums)
    row_ref[8:] = jnp.concatenate([raw, jnp.zeros((8 - HEADS_L, LENGTH), F32)], axis=0)


def front(got, taps, heads):
    return pl.pallas_call(
        front_kernel,
        in_specs=[whole(NC, PACK, LANES), whole(XB, 8), whole(8, LANES)],
        out_specs=[whole(XW, LENGTH), whole(BC_F, LENGTH), whole(16, LENGTH)],
        out_shape=[
            shape_of((XW, LENGTH), BF),
            shape_of((BC_F, LENGTH), BF),
            shape_of((16, LENGTH), F32),
        ],
        grid=(1,),
        scratch_shapes=[pltpu.VMEM((XB, LENGTH + LANES), F32)],
        compiler_params=PARAMS,
        cost_estimate=cost(30 * XB * LENGTH, 4e6, XB * LENGTH),
        name="front",
    )(got, taps, heads)


def front_back_kernel(
    got_ref, taps_ref, heads_ref, row_ref, drow_ref, dx_ref, dbc_ref, pack_ref,
    taps_grad_ref, heads_grad_ref, raw_ref, grad_ref,
):
    half_pairs = PAIRS // 2
    load_raw(got_ref, raw_ref)

    grads = drow_ref[...]
    lane = lane_of(grads.shape) % CHUNK
    running = grads
    back = 1
    while back < CHUNK:
        running = running + jnp.where(
            lane < CHUNK - back, pltpu.roll(running, LENGTH - back, 1), 0.0
        )
        back *= 2
    rates = running[:HEADS_L]
    rate = heads_ref[HEADS_L : 2 * HEADS_L, :1]
    d_steps = grads[HEADS_L : 2 * HEADS_L] + rates * rate
    d_dt = d_steps * jax.nn.sigmoid(row_ref[8 : 8 + HEADS_L])
    steps = row_ref[HEADS_L : 2 * HEADS_L]
    heads_grad_ref[...] = jnp.concatenate(
        [
            jnp.sum(d_dt, axis=1, keepdims=True),
            jnp.sum(rates * steps, axis=1, keepdims=True) * rate,
            jnp.zeros((8 - 2 * HEADS_L, 1), F32),
        ],
        axis=0,
    )
    d_dt = jnp.concatenate([d_dt, jnp.zeros((16 - HEADS_L, LENGTH), F32)], axis=0)
    for index in range(PAIRS):
        first = index < half_pairs
        deal(
            pack_ref, T_AT, PACK, index % half_pairs, first,
            d_dt[:, index * LANES : (index + 1) * LANES],
        )

    def step(part, unused):
        rows = pl.ds(pl.multiple_of(part * PART, PART), PART)
        taps = taps_ref[rows]
        inputs, total = taps_of(raw_ref[rows], taps)
        sig = jax.nn.sigmoid(total)

        @pl.when(part < XW // PART)
        def _():
            grad_ref[:, :LENGTH] = dx_ref[rows]

        @pl.when(part >= XW // PART)
        def _():
            grad_ref[:, :LENGTH] = dbc_ref[pl.ds(pl.multiple_of(part * PART - XW, PART), PART)]

        grad = grad_ref[:, :LENGTH] * (sig + total * sig * (1.0 - sig))
        grad_ref[:, :LENGTH] = grad
        padded = grad_ref[...]
        d_raw = grad * taps[:, CONV_K - 1 : CONV_K]
        for ahead in range(1, CONV_K):
            moved = pltpu.roll(padded, LENGTH + LANES - ahead, 1)[:, :LENGTH]
            d_raw = d_raw + moved * taps[:, CONV_K - 1 - ahead : CONV_K - ahead]
        taps_grad_ref[rows] = jnp.concatenate(
            [jnp.sum(grad * moved, axis=1, keepdims=True) for moved in inputs]
            + [jnp.sum(grad, axis=1, keepdims=True)]
            + [jnp.zeros((PART, 8 - CONV_K - 1), F32)],
            axis=1,
        )
        raw_ref[rows, :LENGTH] = d_raw
        return unused

    grad_ref[:, LENGTH:] = jnp.zeros((PART, LANES), F32)
    lax.fori_loop(0, XB // PART, step, 0)
    for first in (True, False):

        def store(pair, unused, first=first):
            place = at_pair(pair if first else pair + half_pairs)
            deal(pack_ref, 0, XB, pair, first, raw_ref[:, place])
            return unused

        lax.fori_loop(0, half_pairs, store, 0, unroll=True)


def front_back(got, taps, heads, rows, drow, dx, dbc):
    return pl.pallas_call(
        front_back_kernel,
        in_specs=[
            whole(NC, PACK, LANES),
            whole(XB, 8),
            whole(8, LANES),
            whole(16, LENGTH),
            whole(8, LENGTH),
            whole(XW, LENGTH),
            whole(BC_F, LENGTH),
        ],
        out_specs=[whole(NC, PACK, LANES), whole(XB, 8), whole(8, 1)],
        out_shape=[
            shape_of((NC, PACK, LANES), BF),
            shape_of((XB, 8), F32),
            shape_of((8, 1), F32),
        ],
        grid=(1,),
        scratch_shapes=[
            pltpu.VMEM((XB, LENGTH + LANES), F32),
            pltpu.VMEM((PART, LENGTH + LANES), F32),
        ],
        compiler_params=PARAMS,
        cost_estimate=cost(60 * XB * LENGTH, 9e6, XB * LENGTH),
        name="front_back",
    )(got, taps, heads, rows, drow, dx, dbc)


def stacked(rows, width):
    return jnp.concatenate(
        [jnp.broadcast_to(row, (MDIM, width)) for row in rows], axis=0
    )


def state_sides(place_ref, bc_ref):
    quarter = STATE // BC_F
    bt = jnp.concatenate([bc_ref[place_ref[j]] for j in range(quarter)], axis=0)
    ct = jnp.concatenate([bc_ref[place_ref[quarter + j]] for j in range(quarter)], axis=0)
    return bt, ct


def chunk_terms(row_ref):
    rows = row_ref[...]
    cols = rows.T
    cum_row = [rows[h : h + 1] for h in range(HEADS_L)]
    dt_row = [rows[HEADS_L + h : HEADS_L + h + 1] for h in range(HEADS_L)]
    cum_col = [cols[:, h : h + 1] for h in range(HEADS_L)]
    dt_col = [cols[:, HEADS_L + h : HEADS_L + h + 1] for h in range(HEADS_L)]
    last = [row[:, CHUNK - 1 :] for row in cum_row]
    return cum_row, dt_row, cum_col, dt_col, last


def later_mask():
    shape = (CHUNK, CHUNK)
    return lax.broadcasted_iota(jnp.int32, shape, 1) >= lax.broadcasted_iota(jnp.int32, shape, 0)


def mamba_fwd_kernel(
    place_ref, x_ref, bc_ref, row_ref, skip_ref, pack_ref, st_out_ref, st_ref
):
    index = pl.program_id(0)

    @pl.when(index == 0)
    def _():
        st_ref[...] = jnp.zeros_like(st_ref)

    x_low = x_ref[...]
    x = x_low.astype(F32)
    bt, ct = state_sides(place_ref, bc_ref)
    st = st_ref[...]
    st_out_ref[0] = st
    cum_row, dt_row, cum_col, dt_col, last = chunk_terms(row_ref)
    inter = dot(bt, ct, 0, 0)
    carried = dot(st.astype(BF), ct, 1, 0)
    later = later_mask()
    within = []
    for h in range(HEADS_L):
        decay = jnp.exp(jnp.where(later, cum_row[h] - cum_col[h], MASKED))
        mixing = (inter * decay * dt_col[h]).astype(BF)
        within.append(dot(x_low[h * MDIM : (h + 1) * MDIM], mixing, 1, 0))
    entering = stacked([jnp.exp(row) for row in cum_row], CHUNK)
    y = jnp.concatenate(within, axis=0) + entering * carried + skip_ref[...] * x
    weights = stacked(
        [jnp.exp(end - row) * step for end, row, step in zip(last, cum_row, dt_row)], CHUNK
    )
    leaving = stacked([jnp.exp(end) for end in last], 1)
    st_ref[...] = st * leaving + dot((x * weights).astype(BF), bt, 1, 1)
    pairs = CHUNK // LANES
    early = index < CHUNKS // 2

    @pl.when(early)
    def _():
        for j in range(pairs):
            deal(pack_ref, 0, XW, pairs * index + j, True, y[:, j * LANES : (j + 1) * LANES])

    @pl.when(jnp.logical_not(early))
    def _():
        for j in range(pairs):
            deal(
                pack_ref, 0, XW, pairs * (index - CHUNKS // 2) + j, False,
                y[:, j * LANES : (j + 1) * LANES],
            )


def mamba_fwd(place, x, bc, rows, skip):
    return pl.pallas_call(
        mamba_fwd_kernel,
        grid=(CHUNKS,),
        in_specs=[
            SMEM,
            pl.BlockSpec((XW, CHUNK), lambda i: (0, i)),
            pl.BlockSpec((NF, BC_F, CHUNK), lambda i: (0, 0, i)),
            pl.BlockSpec((8, CHUNK), lambda i: (0, i)),
            whole(XW, 1),
        ],
        out_specs=[
            whole(NC, XW, LANES),
            pl.BlockSpec((1, XW, STATE), lambda i: (i, 0, 0)),
        ],
        out_shape=[
            shape_of((NC, XW, LANES), BF),
            shape_of((CHUNKS, XW, STATE), F32),
        ],
        scratch_shapes=[pltpu.VMEM((XW, STATE), F32)],
        compiler_params=PARAMS,
        cost_estimate=cost(2 * LENGTH * CHUNK * (STATE + 3 * XW), 7e6, LENGTH * CHUNK * 3),
        name="mamba_fwd",
    )(place, x, bc, rows, skip)


def mamba_bwd_kernel(
    place_ref, x_ref, got_ref, bc_ref, row_ref, st_in_ref, skip_ref,
    dx_ref, mine_ref, other_ref, drow_ref, dskip_ref, dst_ref, dy_ref,
):
    turn = pl.program_id(0)
    index = CHUNKS - 1 - turn
    pairs = CHUNK // LANES

    @pl.when(turn == 0)
    def _():
        dst_ref[...] = jnp.zeros_like(dst_ref)
        dskip_ref[...] = jnp.zeros_like(dskip_ref)

    @pl.when(index < CHUNKS // 2)
    def _():
        for j in range(pairs):
            dy_ref[:, j * LANES : (j + 1) * LANES] = assemble(
                got_ref, 0, XW, pairs * index + j, True
            )

    @pl.when(index >= CHUNKS // 2)
    def _():
        for j in range(pairs):
            dy_ref[:, j * LANES : (j + 1) * LANES] = assemble(
                got_ref, 0, XW, pairs * (index - CHUNKS // 2) + j, False
            )

    x_low = x_ref[...]
    x = x_low.astype(F32)
    dy = dy_ref[...]
    dy_low = dy.astype(BF)
    bt, ct = state_sides(place_ref, bc_ref)
    st = st_in_ref[0]
    dst = dst_ref[...]
    st_low = st.astype(BF)
    dst_low = dst.astype(BF)
    cum_row, dt_row, cum_col, dt_col, last = chunk_terms(row_ref)
    inter = dot(bt, ct, 0, 0)
    later = later_mask()
    entering = stacked([jnp.exp(row) for row in cum_row], CHUNK)
    tail = [jnp.exp(end - row) for end, row in zip(last, cum_row)]
    kept_row = [t * step for t, step in zip(tail, dt_row)]
    weights = stacked(kept_row, CHUNK)
    leaving = stacked([jnp.exp(end) for end in last], 1)
    carried = dot(st_low, ct, 1, 0) * entering
    reach = dot(dst_low, bt, 1, 0)
    dy_in = (dy * entering).astype(BF)
    x_out = (x * weights).astype(BF)
    along = dy * carried
    pulled = x * reach
    kept = jnp.sum(st * dst, axis=1, keepdims=True) * leaving
    d_inter = jnp.zeros((CHUNK, CHUNK), F32)
    dx_parts = []
    row_cum = []
    row_dt = []
    col_cum = []
    col_dt = []
    ends = lane_of((1, CHUNK)) == CHUNK - 1
    for h in range(HEADS_L):
        part = slice(h * MDIM, (h + 1) * MDIM)
        decay = jnp.exp(jnp.where(later, cum_row[h] - cum_col[h], MASKED))
        d_mix = dot(x_low[part], dy_low[part], 0, 0)
        scaled = decay * dt_col[h]
        d_inter = d_inter + d_mix * scaled
        mixing = inter * scaled
        dx_parts.append(dot(dy_low[part], mixing.astype(BF), 1, 1))
        to_dt = jnp.sum(d_mix * (inter * decay), axis=1, keepdims=True)
        q_row = jnp.sum(pulled[part], axis=0, keepdims=True)
        w_q = q_row * kept_row[h]
        d_last = jnp.sum(w_q, axis=1, keepdims=True) + jnp.sum(
            kept[part], axis=0, keepdims=True
        )
        row_cum.append(
            jnp.sum(d_mix * mixing, axis=0, keepdims=True)
            + jnp.sum(along[part], axis=0, keepdims=True)
            - w_q
            + jnp.where(ends, d_last, 0.0)
        )
        row_dt.append(q_row * tail[h])
        col_cum.append(-to_dt * dt_col[h])
        col_dt.append(to_dt)
    dx_ref[...] = jnp.concatenate(dx_parts, axis=0) + weights * reach + skip_ref[...] * dy
    d_low = d_inter.astype(BF)
    dbt = (dot(ct, d_low, 1, 1) + dot(dst_low, x_out, 0, 0)).astype(BF)
    dct = (dot(bt, d_low, 1, 0) + dot(st_low, dy_in, 0, 0)).astype(BF)
    quarter = STATE // BC_F
    parts = [
        grad[j * BC_F : (j + 1) * BC_F] for grad in (dbt, dct) for j in range(quarter)
    ]
    first = place_ref[0] < NZ
    for z in range(NZ):
        one, two = parts[2 * z], parts[2 * z + 1]
        distance = place_ref[2 * z] % NZ
        mine_ref[distance] = jnp.where(first, one, two)
        other_ref[distance] = jnp.where(first, two, one)
    dst_ref[...] = dst * leaving + dot(dy_in, ct, 1, 1)
    dskip_ref[...] += jnp.sum(dy * x, axis=1, keepdims=True)
    pad = jnp.zeros((CHUNK, 8 - 2 * HEADS_L), F32)
    columns = jnp.concatenate(col_cum + col_dt + [pad], axis=1).T
    drow_ref[...] = columns + jnp.concatenate(
        row_cum + row_dt + [jnp.zeros((8 - 2 * HEADS_L, CHUNK), F32)], axis=0
    )


def mamba_bwd(place, x, got, bc, rows, states, skip):
    end = CHUNKS - 1
    return pl.pallas_call(
        mamba_bwd_kernel,
        grid=(CHUNKS,),
        in_specs=[
            SMEM,
            pl.BlockSpec((XW, CHUNK), lambda i: (0, end - i)),
            whole(NC, BOTH, LANES),
            pl.BlockSpec((NF, BC_F, CHUNK), lambda i: (0, 0, end - i)),
            pl.BlockSpec((8, CHUNK), lambda i: (0, end - i)),
            pl.BlockSpec((1, XW, STATE), lambda i: (end - i, 0, 0)),
            whole(XW, 1),
        ],
        out_specs=[
            pl.BlockSpec((XW, CHUNK), lambda i: (0, end - i)),
            pl.BlockSpec((NZ, BC_F, CHUNK), lambda i: (0, 0, end - i)),
            pl.BlockSpec((NZ, BC_F, CHUNK), lambda i: (0, 0, end - i)),
            pl.BlockSpec((8, CHUNK), lambda i: (0, end - i)),
            whole(XW, 1),
        ],
        out_shape=[
            shape_of((XW, LENGTH), F32),
            shape_of((NZ, BC_F, LENGTH), BF),
            shape_of((NZ, BC_F, LENGTH), BF),
            shape_of((8, LENGTH), F32),
            shape_of((XW, 1), F32),
        ],
        scratch_shapes=[pltpu.VMEM((XW, STATE), F32), pltpu.VMEM((XW, CHUNK), F32)],
        compiler_params=PARAMS,
        cost_estimate=cost(
            2 * LENGTH * CHUNK * (3 * STATE + 7 * XW), 12e6, LENGTH * CHUNK * 3
        ),
        name="mamba_bwd",
    )(place, x, got, bc, rows, states, skip)


def position_of(source, odd, inside):
    block = jnp.where(source % 2 == odd, source, 2 * NC - 1 - source)
    return block * HALF + inside


def visible_mask(step, odd):
    key = lax.broadcasted_iota(jnp.int32, (1, LENGTH), 1)
    key_pos = position_of(key // ROWS, (key // HALF) % 2, key % HALF)
    query = lax.broadcasted_iota(jnp.int32, (QBLOCK, 1), 0)
    source = 2 * step + query // HALF
    query_pos = position_of(source, odd, query % HALF)
    return key_pos <= query_pos


def attn_fwd_kernel(odd_ref, q_ref, k_ref, v_ref, o_ref, lse_ref):
    q = q_ref[...].reshape(QBLOCK, HDIM)
    k = k_ref[...].reshape(LENGTH, HDIM)
    v = v_ref[...].reshape(LENGTH, HDIM)
    scores = dot(q, k, 1, 1) * SCALE
    scores = jnp.where(visible_mask(pl.program_id(0), odd_ref[0]), scores, MASKED)
    top = jnp.max(scores, axis=1, keepdims=True)
    grown = jnp.exp(scores - top)
    total = jnp.sum(grown, axis=1, keepdims=True)
    lse_ref[...] = top + jnp.log(total)
    probs = (grown * (1.0 / total)).astype(BF)
    o_ref[...] = dot(probs, v, 1, 0).astype(BF).reshape(2, HALF, HDIM)


def packed_part(at, rows, moving=False):
    block = at // rows
    if moving:
        return pl.BlockSpec((2, rows, HDIM), lambda i: (i, block, 0))
    return pl.BlockSpec((NC, rows, HDIM), lambda i: (0, block, 0))


def attn_fwd(odd, got):
    return pl.pallas_call(
        attn_fwd_kernel,
        grid=(QROWS // QBLOCK,),
        in_specs=[
            SMEM,
            packed_part(Q_AT, HALF, True),
            packed_part(K_AT, ROWS),
            packed_part(V_AT, ROWS),
        ],
        out_specs=[
            pl.BlockSpec((2, HALF, HDIM), lambda i: (i, 0, 0)),
            pl.BlockSpec((QBLOCK, 1), lambda i: (i, 0)),
        ],
        out_shape=[shape_of((NC, HALF, HDIM), BF), shape_of((QROWS, 1), F32)],
        compiler_params=PARAMS,
        cost_estimate=cost(4 * QROWS * LENGTH * HDIM, 3e6, QROWS * LENGTH),
        name="attn_fwd",
    )(odd, got, got, got)


def attn_bwd_kernel(
    odd_ref, q_ref, k_ref, v_ref, do_ref, lse_ref, pack_ref, dk_sum, dv_sum
):
    step = pl.program_id(0)

    @pl.when(step == 0)
    def _():
        dk_sum[...] = jnp.zeros_like(dk_sum)
        dv_sum[...] = jnp.zeros_like(dv_sum)

    q = q_ref[...].reshape(QBLOCK, HDIM)
    k = k_ref[...].reshape(LENGTH, HDIM)
    v = v_ref[...].reshape(LENGTH, HDIM)
    do = do_ref[...].reshape(QBLOCK, HDIM)
    scores = dot(q, k, 1, 1) * SCALE - lse_ref[...]
    probs = jnp.exp(jnp.where(visible_mask(step, odd_ref[0]), scores, MASKED))
    d_probs = dot(do, v, 1, 1)
    dv_sum[...] += dot(probs.astype(BF), do, 0, 0)
    inner = jnp.sum(probs * d_probs, axis=1, keepdims=True)
    d_scores = (probs * (d_probs - inner)).astype(BF)
    pack_ref[pl.ds(2 * step, 2), Q_AT:] = (
        (dot(d_scores, k, 1, 0) * SCALE).astype(BF).reshape(2, HALF, HDIM)
    )
    dk_sum[...] += dot(d_scores, q, 0, 0)

    @pl.when(step == pl.num_programs(0) - 1)
    def _():
        pack_ref[:, K_AT:V_AT] = (dk_sum[...] * SCALE).astype(BF).reshape(NC, ROWS, HDIM)
        pack_ref[:, V_AT:Q_AT] = dv_sum[...].astype(BF).reshape(NC, ROWS, HDIM)


def attn_bwd(odd, got, grads, lse):
    return pl.pallas_call(
        attn_bwd_kernel,
        grid=(QROWS // QBLOCK,),
        in_specs=[
            SMEM,
            packed_part(Q_AT, HALF, True),
            packed_part(K_AT, ROWS),
            packed_part(V_AT, ROWS),
            packed_part(XW, HALF, True),
            pl.BlockSpec((QBLOCK, 1), lambda i: (i, 0)),
        ],
        out_specs=whole(NC, ATTN, LANES),
        out_shape=shape_of((NC, ATTN, LANES), BF),
        scratch_shapes=[pltpu.VMEM((LENGTH, HDIM), F32), pltpu.VMEM((LENGTH, HDIM), F32)],
        compiler_params=PARAMS,
        cost_estimate=cost(10 * QROWS * LENGTH * HDIM, 4e6, QROWS * LENGTH),
        name="attn_bwd",
    )(odd, got, got, got, grads, lse)


def tiles_to_rows(refs):
    tiles = []
    for ref in refs:
        count = ref.shape[0] * SLICE
        for tile in range(ref.shape[1]):
            tiles.append(ref[:, tile].reshape(count, LANES).astype(F32))
    return jnp.concatenate(tiles, axis=1)


def unpack_kernel(*refs):
    refs[-1][...] = tiles_to_rows(refs[:-1])


def unpack_rows(tiles, at, first, rows):
    width = D // LANES
    step = NC // 2
    skip, base = first // LANES, at // width
    return pl.pallas_call(
        unpack_kernel,
        grid=(rows // LANES,),
        in_specs=[
            pl.BlockSpec(
                (step, width, SLICE, LANES),
                lambda i: ((i + skip) % 2, base + (i + skip) // 2, 0, 0),
            )
        ],
        out_specs=pl.BlockSpec((LANES, D), lambda i: (i, 0)),
        out_shape=shape_of((rows, D), F32),
        compiler_params=PARAMS,
        cost_estimate=cost(rows * D, 6 * rows * D),
        name="unpack_rows",
    )(tiles)


def unpack_gate_up(tiles):
    part = FF_F // LANES
    many = NF // 2

    def spec(j):
        return pl.BlockSpec(
            (NC, part, SLICE, LANES), lambda h, q: (0, 2 * (q * many + j) + h, 0, 0)
        )

    return pl.pallas_call(
        unpack_kernel,
        grid=(2, NF // many),
        in_specs=[spec(j) for j in range(many)],
        out_specs=pl.BlockSpec(
            (SHARD, many * FF_F), lambda h, q: (0, h * (NF // many) + q)
        ),
        out_shape=shape_of((SHARD, 2 * FF), F32),
        compiler_params=PARAMS,
        cost_estimate=cost(SHARD * 2 * FF, 6 * SHARD * 2 * FF),
        name="unpack_gate_up",
    )(*[tiles] * many)


def turned(ref, tile):
    return ref[:, tile].reshape(SHARD, LANES).astype(F32).T


def unpack_in_kernel(*refs):
    step = pl.program_id(0)
    steps = NF // 2
    wide = INNER_F // LANES
    out_ref = refs[-1]

    @pl.when(step < 2 * steps)
    def _():
        for index in range(2):
            for tile in range(wide):
                start = index * INNER_F + tile * LANES
                out_ref[start : start + LANES] = turned(refs[index], tile)

    @pl.when(step == 2 * steps)
    def _():
        for f in range(NF):
            tail = turned(refs[2 + f], 0)
            out_ref[f * BC_F : (f + 1) * BC_F] = tail[:BC_F]
            first = NF * BC_F + f * DT_F
            out_ref[first : first + DT_F] = tail[BC_F : BC_F + DT_F]


def unpack_in(tiles, z_at):
    wide = INNER_F // LANES
    half = NF // 2
    each = WM_COLS // LANES

    def spec(j):
        def index(i):
            f = 2 * (jnp.minimum(i, 2 * half - 1) % half) + j
            return (0, jnp.where(i < half, z_at + wide * f, each * f), 0, 0)

        shape = tuple(pl.Element(size) for size in (NC, wide, SLICE, LANES))
        return pl.BlockSpec(shape, index)

    def tail_spec(f):
        return pl.BlockSpec((NC, 1, SLICE, LANES), lambda i: (0, each * f + wide, 0, 0))

    specs = [spec(0), spec(1)]
    specs += [tail_spec(f) for f in range(NF)]
    return pl.pallas_call(
        unpack_in_kernel,
        grid=(2 * half + 1,),
        in_specs=specs,
        out_specs=pl.BlockSpec((2 * INNER_F, SHARD), lambda i: (i, 0)),
        out_shape=shape_of((2 * INNER + 2 * STATE + MHEADS, SHARD), F32),
        compiler_params=PARAMS,
        cost_estimate=cost(SHARD * 6704, 6 * SHARD * 6704),
        name="unpack_in",
    )(*[tiles] * len(specs))


def unpack_qkv_kernel(*refs):
    group = NF // KVHEADS

    def tile(f, index):
        return refs[3 * f + index][:, 0].reshape(SHARD, HDIM).astype(F32)

    parts = [tile(f, 0) for f in range(NF)]
    for index in (1, 2):
        for head in range(KVHEADS):
            parts.append(sum(tile(head * group + j, index) for j in range(group)))
    refs[-1][...] = jnp.concatenate(parts, axis=1)


def unpack_qkv(tiles):
    each, first = WM_COLS // LANES, MIX // LANES
    specs = [
        pl.BlockSpec((NC, 1, SLICE, LANES), lambda i, at=each * f + first + index: (0, at, 0, 0))
        for f in range(NF)
        for index in range(3)
    ]
    width = (QHEADS + 2 * KVHEADS) * HDIM
    return pl.pallas_call(
        unpack_qkv_kernel,
        grid=(1,),
        in_specs=specs,
        out_specs=whole(SHARD, width),
        out_shape=shape_of((SHARD, width), F32),
        compiler_params=PARAMS,
        cost_estimate=cost(SHARD * width, 6 * SHARD * width),
        name="unpack_qkv",
    )(*[tiles] * len(specs))


def norm_scale(values):
    return lax.rsqrt(jnp.mean(values * values, axis=-1, keepdims=True) + EPS)


def norm_back(values, scale, gain, grad):
    pulled = grad * gain
    inner = jnp.mean(pulled * values, axis=-1, keepdims=True)
    d_values = scale * pulled - values * (scale * scale * scale) * inner
    return d_values, jnp.sum(grad * values * scale, axis=0)


def columns_of(weight, start, width):
    part = weight[:, start : start + NF * width]
    return part.reshape(weight.shape[0], NF, width).transpose(1, 0, 2)


def shards(
    tokens,
    norm_gain,
    w_in,
    w_qkv,
    conv_weight,
    conv_bias,
    dt_bias,
    a_log,
    d_skip,
    mamba_gain,
    w_mout,
    w_aout,
    mlp_gain,
    w_gate_up,
    w_down,
    cotangent,
):
    ctx = lax.axis_index("ctx")
    fsdp = lax.axis_index("fsdp")
    parity = ctx % 2
    odd = parity.astype(jnp.int32).reshape(1)
    z_at, core = fsdp // 2, fsdp % 2
    pieces = jnp.arange(NF, dtype=jnp.int32)
    order = ((z_at + pieces % NZ) % NZ) * 2 + (core + pieces // NZ) % 2
    place = ((pieces % 2 + core) % 2) * NZ + (pieces // 2 - z_at) % NZ

    def even_first(rows):
        rows = rows.reshape(2, HALF, D)
        return jnp.where(parity == 1, rows[::-1], rows).reshape(ROWS, D)

    spot = jnp.concatenate([place[::2] % NZ, core.astype(jnp.int32).reshape(1)])

    hidden = even_first(tokens).astype(F32)
    scale_one = norm_scale(hidden)
    normed = ring_gather((hidden * scale_one * norm_gain).astype(BF), order)

    in_rows = lax.dynamic_slice(w_in, (ctx * SLICE, 0), (SLICE, w_in.shape[1]))
    qkv_rows = lax.dynamic_slice(w_qkv, (ctx * SLICE, 0), (SLICE, w_qkv.shape[1]))
    gu_rows = lax.dynamic_slice(w_gate_up, (ctx * SLICE, 0), (SLICE, w_gate_up.shape[1]))
    parts = [
        columns_of(in_rows, INNER, INNER_F),
        columns_of(in_rows, 2 * INNER, BC_F),
        columns_of(in_rows, 2 * INNER + 2 * STATE, DT_F),
        jnp.zeros((NF, SLICE, LANES - BC_F - DT_F), BF),
        columns_of(qkv_rows, 0, HDIM),
    ]
    for start in (QHEADS * HDIM, (QHEADS + KVHEADS) * HDIM):
        pair = qkv_rows[:, start : start + KVHEADS * HDIM].reshape(SLICE, KVHEADS, HDIM)
        parts.append(jnp.repeat(pair.transpose(1, 0, 2), NF // KVHEADS, axis=0))
    parts += [
        columns_of(in_rows, 0, INNER_F),
        columns_of(gu_rows, 0, FF_F),
        columns_of(gu_rows, FF, FF_F),
    ]
    swapped = swap_fsdp(jnp.concatenate(parts, axis=2))
    w_one = lax.all_gather(swapped[..., :W1_COLS], "ctx", axis=0)
    w_out = jnp.concatenate([w_mout, w_aout], axis=0)
    cot_low = even_first(cotangent)

    blocks = jnp.stack([ctx, 2 * NC - 1 - ctx])
    blocks = jnp.where(parity == 1, blocks[::-1], blocks)
    positions = (
        blocks[:, None] * HALF + jnp.arange(HALF, dtype=jnp.int32)[None, :]
    ).reshape(ROWS)
    half_dim = HDIM // 2
    freqs = ROPE_BASE ** (-jnp.arange(half_dim, dtype=F32) / half_dim)
    angles = positions.astype(F32)[:, None] * freqs[None, :]
    cosine, sine = jnp.cos(angles), jnp.sin(angles)
    mix_pack, attn_pack = project(normed, w_one, cosine, sine)
    gate_z = project_z(after(normed, mix_pack), w_one)
    mix_got = after(swap_ctx(mix_pack), gate_z)
    attn_got = swap_ctx(after(attn_pack, mix_got))

    x_start = fsdp * INNER_F + parity * XW
    bc_start = INNER + fsdp * BC_F
    conv_all = jnp.concatenate(
        [conv_weight, conv_bias[None], jnp.zeros((3, conv_bias.shape[0]), F32)], axis=0
    )
    taps = jnp.concatenate(
        [
            lax.dynamic_slice(conv_all, (0, x_start), (8, XW)),
            lax.dynamic_slice(conv_all, (0, bc_start), (8, BC_F)),
        ],
        axis=1,
    ).T
    head = fsdp * DT_F + parity * HEADS_L
    my_bias = lax.dynamic_slice(dt_bias, (head,), (HEADS_L,))
    my_rate = -jnp.exp(lax.dynamic_slice(a_log, (head,), (HEADS_L,)))
    heads_in = jnp.broadcast_to(
        jnp.concatenate([my_bias, my_rate, jnp.zeros((8 - 2 * HEADS_L,), F32)])[:, None],
        (8, LANES),
    )
    my_skip = jnp.repeat(lax.dynamic_slice(d_skip, (head,), (HEADS_L,)), MDIM)[:, None]
    x_act, bc_own, row_terms = front(mix_got, taps, heads_in)
    cot_all = gather_fsdp(after(cot_low, mix_pack))
    bc = jnp.concatenate(ring_pieces(bc_own), axis=0).reshape(NF, BC_F, LENGTH)
    w_gu = lax.all_gather(after(swapped[..., W1_COLS:], cot_all, x_act), "ctx", axis=0)
    bc = after(bc, attn_got)
    ssd_seq, states = mamba_fwd(place, x_act, bc, row_terms, my_skip)
    heads_seq, lse = attn_fwd(odd, after(attn_got, ssd_seq))
    ssd = after(swap_ctx(ssd_seq), heads_seq)
    heads = swap_ctx(after(heads_seq, ssd))

    my_gain = lax.dynamic_slice(mamba_gain, (fsdp * INNER_F,), (INNER_F,))[:, None]
    g, squares = gate(ssd, gate_z)
    squares = after(butterfly(squares, "fsdp", NF), w_gu)
    gated_heads, branches = branch_out(heads, g, squares, my_gain, w_out)
    mixed = hidden + scatter_fsdp(branches)

    scale_two = norm_scale(mixed)
    normed_two = gather_fsdp((mixed * scale_two * mlp_gain).astype(BF))
    d_act = act_back(after(cot_all, branches), w_down)
    act, d_gu, d_normed_two = mlp(normed_two, d_act, w_gu)
    down_mine, down_other = down_out(spot, act, w_down)

    def side_by_side(*terms):
        return jnp.concatenate([term.reshape(NC, -1, LANES) for term in terms], axis=1)

    def total_of(got):
        return jnp.sum(got.astype(F32), axis=0).astype(BF)

    def scatter_ctx(joined):
        part = lax.psum_scatter(joined, "ctx", scatter_dimension=0, tiled=False)
        return lax.optimization_barrier(part)

    def all_ctx(parts):
        joined = jnp.concatenate(parts, axis=0)
        return lax.all_gather(joined.reshape(-1, SLICE, LANES), "ctx", axis=0)

    gu_tiles = MLP_COLS // LANES
    z_tiles = INNER_F // LANES
    mix_tiles = WM_COLS // LANES
    row_tiles = OUT_ROWS // SHARD * (D // LANES)
    packed_one = side_by_side(column_grad(normed_two, d_gu), column_grad(act, cot_all))
    d_normed_two, packed_one, down_mine = lax.optimization_barrier(
        (scatter_fsdp(d_normed_two), packed_one, down_mine)
    )
    sum_one = scatter_ctx(packed_one)
    d_mixed, g_mlp_gain = norm_back(mixed, scale_two, mlp_gain, d_normed_two)
    d_mixed = d_mixed + cot_low.astype(F32)
    branch = ring_gather(d_mixed.astype(BF), order)

    dg, inner, dh = branch_back(branch, w_out, g, my_gain)
    inner = butterfly(inner, "fsdp", NF)
    d_mixers, dz, g_mamba_gain = gate_back(
        ssd, gate_z, g, dg, dh, squares, inner, my_gain
    )
    d_mixers = swap_ctx(d_mixers)
    packed_two = side_by_side(column_grad(gated_heads, branch), column_grad(normed, dz))
    d_mixers, packed_two = lax.optimization_barrier((d_mixers, packed_two))
    sum_two = scatter_ctx(packed_two)
    dx, dbc_mine, dbc_other, drow, dskip = mamba_bwd(
        place, x_act, d_mixers, bc, row_terms, states, my_skip
    )
    dbc_joined = ring_join(
        dbc_mine.reshape(NZ * BC_F, LENGTH), dbc_other.reshape(NZ * BC_F, LENGTH)
    )
    attn_pack = attn_bwd(odd, attn_got, after(d_mixers, dx), lse)
    down_at = NF * gu_tiles
    gu_part = swap_fsdp(after(sum_one, dbc_joined)[: down_at * SLICE].reshape(NF, -1, LANES))
    dbc_own, attn_pack, gu_part = lax.optimization_barrier(
        (ring_scatter(dbc_joined), attn_pack, gu_part)
    )
    all_one = all_ctx([gu_part.reshape(-1, LANES), sum_one[down_at * SLICE :]])
    attn_back = swap_ctx(attn_pack)
    mix_back, g_taps, g_heads = front_back(
        mix_got, taps, heads_in, row_terms, drow, dx, dbc_own
    )
    mix_back = swap_ctx(after(mix_back, attn_back))
    d_qkv = attn_grads(attn_back, cosine, sine)
    mix_back, d_qkv = lax.optimization_barrier((mix_back, d_qkv))
    d_mix = mix_grads(mix_back)
    packed_mix = column_grad(normed, d_mix, d_qkv).reshape(NC, -1, LANES)
    got_mix = swap_ctx(packed_mix)
    mine, other, gain_sum = back_project(
        spot, d_mix, d_qkv, after(dz, packed_mix), normed, w_one
    )
    g_norm_gain = gain_sum[0] / norm_gain

    def joined(mine, other):
        return ring_join(mine.reshape(NZ * ROWS, D), other.reshape(NZ * ROWS, D))

    d_normed = joined(mine, other)
    sum_mix = total_of(after(got_mix, d_normed))
    split = z_tiles * SLICE
    columns = swap_fsdp(
        jnp.concatenate(
            [
                sum_two[row_tiles * SLICE :].reshape(NF, -1, LANES),
                sum_mix.reshape(NF, -1, LANES),
            ],
            axis=1,
        )
    )
    mix_at = NF * mix_tiles
    out_at = mix_at + -mix_at % (D // LANES)
    z_at = out_at + row_tiles
    z_at = z_at + -z_at % z_tiles
    all_two = all_ctx(
        [
            columns[:, split:].reshape(-1, LANES),
            jnp.zeros(((out_at - mix_at) * SLICE, LANES), BF),
            sum_two[: row_tiles * SLICE],
            jnp.zeros(((z_at - out_at - row_tiles) * SLICE, LANES), BF),
            columns[:, :split].reshape(-1, LANES),
        ]
    )
    down = joined(down_mine, after(down_other, mine))
    both = ring_scatter(jnp.concatenate([d_normed, down], axis=1))
    output = even_first((mixed + both[:, D:]).astype(BF)).reshape(tokens.shape)

    g_gate_up = unpack_gate_up(all_one)
    g_down = unpack_rows(all_one, down_at, 0, OUT_ROWS)
    all_two = after(all_two, g_gate_up, g_down, output)
    g_mout = unpack_rows(all_two, out_at, 0, INNER_F)
    g_aout = unpack_rows(all_two, out_at, INNER_F, HDIM)
    g_qkv = unpack_qkv(all_two)
    g_in = unpack_in(all_two, z_at).T
    d_hidden, _ = norm_back(hidden, scale_one, norm_gain, both[:, :D])
    d_tokens = even_first((d_hidden + d_mixed).astype(BF)).reshape(tokens.shape)

    def by_half(values):
        zero = jnp.zeros_like(values)
        return jnp.where(
            parity == 1, jnp.stack([zero, values], axis=-2), jnp.stack([values, zero], axis=-2)
        )

    g_conv = g_taps.T[: CONV_K + 1]
    g_d_skip = jnp.sum(dskip.reshape(HEADS_L, MDIM), axis=1)
    per_head = jnp.stack(
        [g_heads[:HEADS_L, 0], g_heads[HEADS_L : 2 * HEADS_L, 0], g_d_skip]
    )
    own = jnp.concatenate(
        [
            by_half(g_conv[:, :XW]).reshape(-1),
            g_conv[:, XW:].reshape(-1),
            g_mamba_gain[:, 0],
            by_half(per_head).reshape(-1),
        ]
    )
    own_size = own.shape[0]
    own_pad = -(-own_size // LANES) * LANES
    own = jnp.concatenate([own, jnp.zeros((own_pad - own_size,), F32), g_mlp_gain, g_norm_gain])
    own = butterfly(own.reshape(-1, LANES), "ctx", NC).reshape(-1)
    mine = (jnp.arange(NF) == fsdp)[:, None]
    placed = jnp.where(mine, own[None, :own_pad], 0.0).reshape(-1)
    total = butterfly(
        jnp.concatenate([placed, own[own_pad:]]).reshape(-1, LANES), "fsdp", NF
    ).reshape(-1)
    each = total[: NF * own_pad].reshape(NF, own_pad)
    cut = [(CONV_K + 1) * INNER_F]
    cut.append(cut[0] + (CONV_K + 1) * BC_F)
    cut.append(cut[1] + INNER_F)
    conv_x = each[:, : cut[0]].reshape(NF, CONV_K + 1, INNER_F).transpose(1, 0, 2)
    conv_bc = each[:, cut[0] : cut[1]].reshape(NF, CONV_K + 1, BC_F).transpose(1, 0, 2)
    conv = jnp.concatenate(
        [conv_x.reshape(CONV_K + 1, INNER), conv_bc.reshape(CONV_K + 1, 2 * STATE)], axis=1
    )
    per_head = each[:, cut[2] : cut[2] + 3 * DT_F].reshape(NF, 3, DT_F).transpose(1, 0, 2)
    per_head = per_head.reshape(3, MHEADS)
    gains = total[NF * own_pad :].reshape(2, D)
    return (
        output,
        d_tokens,
        gains[1],
        g_in,
        g_qkv,
        conv[:CONV_K],
        conv[CONV_K],
        per_head[0],
        per_head[1],
        per_head[2],
        each[:, cut[1] : cut[2]].reshape(INNER),
        g_mout,
        g_aout,
        gains[0],
        g_gate_up,
        g_down,
    )


def solution(mesh):
    tokens_at = P("fsdp", "ctx", None, None)
    rows_at = P("fsdp", None)
    placed = (
        tokens_at,
        P(),
        rows_at,
        rows_at,
        P(),
        P(),
        P(),
        P(),
        P(),
        P(),
        rows_at,
        rows_at,
        P(),
        rows_at,
        rows_at,
        tokens_at,
    )
    return jax.shard_map(
        shards,
        mesh=mesh,
        in_specs=placed,
        out_specs=(
            tokens_at,
            tokens_at,
            P(),
            rows_at,
            rows_at,
            P(),
            P(),
            P(),
            P(),
            P(),
            P(),
            rows_at,
            rows_at,
            P(),
            rows_at,
            rows_at,
        ),
        check_vma=False,
    )
```

```python
import jax
import jax.numpy as jnp
from jax import lax
from jax.experimental import pallas as pl
from jax.experimental.pallas import tpu as pltpu
from jax.sharding import PartitionSpec as P

D = 2048
MHEADS = 48
MDIM = 64
STATE = 256
CONV_K = 4
QHEADS = 8
KVHEADS = 2
HDIM = 128
FF = 4096
HALF = 64
INNER = 3072
LENGTH = 2048
SEQS = 8
NC = 16
NF = 8
NZ = 4
LANES = 128
ROWS = 2 * HALF
GROUP = SEQS * ROWS
INNER_F = INNER // NF
HEADS_L = 3
XW = HEADS_L * MDIM
BC_F = 2 * STATE // NF
DT_F = MHEADS // NF
FF_F = FF // NF
CHUNK = 256
CHUNKS = LENGTH // CHUNK
PAIRS = LENGTH // LANES
QROWS = LENGTH // 2
QBLOCK = 128
SHARD = D // NF
SLICE = SHARD // NC
MIX = INNER_F + LANES
QKV = 3 * HDIM
WM_COLS = MIX + QKV
W1_COLS = WM_COLS + INNER_F
MLP_COLS = 2 * FF_F
OUT_ROWS = INNER_F + HDIM
K_AT, V_AT, Q_AT, ATTN = 0, 128, 256, 320
XB = XW + BC_F
B_AT, T_AT, PACK = XW, XB, XB + 16
BOTH = XW + HALF
GATE_SEQS = 4
PART = 16
EPS = 1e-06
ROPE_BASE = 100000000000.0
MASKED = -1e30
SCALE = HDIM ** (-0.5)
BF = jnp.bfloat16
F32 = jnp.float32
PARAMS = pltpu.CompilerParams(vmem_limit_bytes=56 * 1024 * 1024)
SMEM = pl.BlockSpec(memory_space=pltpu.SMEM)


def dot(left, right, left_dim, right_dim):
    return lax.dot_general(
        left, right, (((left_dim,), (right_dim,)), ((), ())), preferred_element_type=F32
    )


def whole(*shape):
    return pl.BlockSpec(shape, lambda *i: (0,) * len(shape))


def cost(flops, moved, transcendentals=0):
    return pl.CostEstimate(
        flops=int(flops), bytes_accessed=int(moved), transcendentals=int(transcendentals)
    )


def shape_of(shape, dtype):
    return jax.ShapeDtypeStruct(shape, dtype)


OTHER_CORE = [(i, i ^ 1) for i in range(NF)]
TO_NEXT = [(i, (i + 2) % NF) for i in range(NF)]
TO_PREV = [(i, (i - 2) % NF) for i in range(NF)]


def send(value, route):
    return lax.ppermute(value, "fsdp", route)


def gather_fsdp(value):
    return lax.all_gather(value, "fsdp", axis=0, tiled=True)


def scatter_fsdp(parts):
    return lax.psum_scatter(parts, "fsdp", scatter_dimension=0, tiled=True).astype(F32)


def ring_pieces(value):
    half = value.shape[0] // 2
    after = send(value, TO_PREV)
    before = send(value, TO_NEXT)
    near = send(value, OTHER_CORE)
    far = jnp.concatenate(
        [send(after[:half], TO_PREV), send(before[half:], TO_NEXT)], axis=0
    )
    near_after = send(after, OTHER_CORE)
    near_before = send(before, OTHER_CORE)
    near_far = send(far, OTHER_CORE)
    return [value, after, far, before, near, near_after, near_far, near_before]


def ring_gather(value, order):
    whole_value = jnp.zeros((NF * value.shape[0],) + value.shape[1:], value.dtype)
    for index, piece in enumerate(ring_pieces(value)):
        whole_value = lax.dynamic_update_slice(
            whole_value, piece, (order[index] * value.shape[0], 0)
        )
    return whole_value


def plus(*terms):
    return sum(term.astype(F32) for term in terms)


def ring_join(mine, other):
    return plus(mine, send(other, OTHER_CORE)).astype(BF)


def ring_first(joined):
    size = joined.shape[0] // NZ
    half = size // 2
    own, after, far, before = [joined[i * size : (i + 1) * size] for i in range(NZ)]
    sent = (
        send(far[:half], TO_NEXT),
        send(far[half:], TO_PREV),
        send(after[half:], TO_NEXT),
        send(before[:half], TO_PREV),
    )
    return own, after[:half], before[half:], *sent


def ring_last(own, after, before, far_next, far_prev, after_two, before_one):
    after_one = send(plus(after, far_next).astype(BF), TO_NEXT)
    before_two = send(plus(before, far_prev).astype(BF), TO_PREV)
    return plus(
        own,
        jnp.concatenate([after_one, after_two], axis=0),
        jnp.concatenate([before_one, before_two], axis=0),
    )


def ring_scatter(joined):
    return ring_last(*ring_first(joined))


def together(*values):
    return lax.optimization_barrier(values)


def swap_ctx(value):
    return lax.all_to_all(value, "ctx", 0, 0, tiled=True)


def swap_fsdp(value):
    return lax.all_to_all(value, "fsdp", 0, 0, tiled=True)


def exchange(value, axis, bit):
    size = lax.axis_size(axis)
    return value + lax.ppermute(value, axis, [(i, i ^ bit) for i in range(size)])


def butterfly(value, axis, bits):
    for bit in bits:
        value = exchange(value, axis, bit)
    return value


def rotate(values, cosine, sine):
    half = values.shape[-1] // 2
    first = values[:, :half]
    second = values[:, half:]
    return jnp.concatenate(
        [first * cosine - second * sine, second * cosine + first * sine], axis=1
    )


def proj_kernel(n_ref, w_ref, cos_ref, sin_ref, mix_ref, attn_ref):
    acc = jnp.zeros((2 * ROWS, WM_COLS), F32)
    for f in range(NF):
        acc = acc + dot(
            n_ref[:, f * SHARD : (f + 1) * SHARD],
            w_ref[:, f, :, :WM_COLS].reshape(SHARD, WM_COLS),
            1,
            0,
        )
    for j in range(2):
        rows = acc[j * ROWS : (j + 1) * ROWS]
        x_rows = rows[:, :INNER_F].T.astype(BF)
        tail = rows[:, INNER_F:MIX].T
        query = rotate(rows[:, MIX : MIX + HDIM], cos_ref[...], sin_ref[...]).astype(BF)
        key = rotate(
            rows[:, MIX + HDIM : MIX + 2 * HDIM], cos_ref[...], sin_ref[...]
        ).astype(BF)
        value = rows[:, MIX + 2 * HDIM :].astype(BF)
        for p in range(2):
            to = 2 * j + p
            attn_ref[to, K_AT:V_AT] = key
            attn_ref[to, V_AT:Q_AT] = value
            attn_ref[to, Q_AT:] = query[p * HALF : (p + 1) * HALF]
            mix_ref[to, :B_AT] = x_rows[p * XW : (p + 1) * XW]
            mix_ref[to, B_AT:T_AT] = tail[:BC_F].astype(BF)
            steps = tail[BC_F + p * HEADS_L : BC_F + (p + 1) * HEADS_L]
            high = steps.astype(BF).astype(F32)
            mix_ref[to, T_AT:] = jnp.concatenate(
                [high, steps - high, jnp.zeros((16 - 2 * HEADS_L, ROWS), F32)], axis=0
            ).astype(BF)


def packets(rows):
    return pl.BlockSpec((4, rows, LANES), lambda i: (i, 0, 0))


def token_rows(width):
    return pl.BlockSpec((2 * ROWS, width), lambda i: (i, 0))


def project(normed, w_one, cosine, sine):
    return pl.pallas_call(
        proj_kernel,
        grid=(SEQS // 2,),
        in_specs=[
            token_rows(D),
            whole(NC, NF, SLICE, W1_COLS),
            whole(ROWS, HALF),
            whole(ROWS, HALF),
        ],
        out_specs=[packets(PACK), packets(ATTN)],
        out_shape=[shape_of((NC, PACK, LANES), BF), shape_of((NC, ATTN, LANES), BF)],
        compiler_params=PARAMS,
        cost_estimate=cost(2 * GROUP * D * WM_COLS, 10e6),
        name="project",
    )(normed, w_one, cosine, sine)


def proj_z_kernel(n_ref, w_ref, z_ref):
    acc = jnp.zeros((2 * ROWS, INNER_F), F32)
    for f in range(NF):
        acc = acc + dot(
            n_ref[:, f * SHARD : (f + 1) * SHARD],
            w_ref[:, f, :, WM_COLS:].reshape(SHARD, INNER_F),
            1,
            0,
        )
    for j in range(2):
        z_ref[j] = acc[j * ROWS : (j + 1) * ROWS].T


def project_z(normed, w_z):
    return pl.pallas_call(
        proj_z_kernel,
        grid=(SEQS // 2,),
        in_specs=[token_rows(D), whole(NC, NF, SLICE, W1_COLS)],
        out_specs=pl.BlockSpec((2, INNER_F, ROWS), lambda i: (i, 0, 0)),
        out_shape=shape_of((SEQS, INNER_F, ROWS), F32),
        compiler_params=PARAMS,
        cost_estimate=cost(2 * GROUP * D * INNER_F, 8e6),
        name="project_z",
    )(normed, w_z)


def attn_grads_kernel(got_ref, cos_ref, sin_ref, out_ref):
    for j in range(2):
        one = got_ref[2 * j].astype(F32)
        two = got_ref[2 * j + 1].astype(F32)
        both = one + two
        query = jnp.concatenate([one[Q_AT:], two[Q_AT:]], axis=0)
        query = rotate(query, cos_ref[...], -sin_ref[...])
        key = rotate(both[K_AT:V_AT], cos_ref[...], -sin_ref[...])
        out_ref[j * ROWS : (j + 1) * ROWS] = jnp.concatenate(
            [query, key, both[V_AT:Q_AT]], axis=1
        ).astype(BF)


def attn_grads(got, cosine, sine):
    return pl.pallas_call(
        attn_grads_kernel,
        grid=(SEQS // 2,),
        in_specs=[packets(ATTN), whole(ROWS, HALF), whole(ROWS, HALF)],
        out_specs=token_rows(QKV),
        out_shape=shape_of((GROUP, QKV), BF),
        compiler_params=PARAMS,
        cost_estimate=cost(10 * GROUP * QKV, 2e6),
        name="attn_grads",
    )(got, cosine, sine)


def mix_grads_kernel(got_ref, out_ref):
    for j in range(2):
        one = got_ref[2 * j].astype(F32)
        two = got_ref[2 * j + 1].astype(F32)
        x_rows = jnp.concatenate([one[:B_AT], two[:B_AT]], axis=0).T
        tail = jnp.concatenate(
            [
                one[B_AT:T_AT] + two[B_AT:T_AT],
                one[T_AT : T_AT + HEADS_L],
                two[T_AT : T_AT + HEADS_L],
                jnp.zeros((LANES - BC_F - DT_F, ROWS), F32),
            ],
            axis=0,
        ).T
        out_ref[j * ROWS : (j + 1) * ROWS] = jnp.concatenate([x_rows, tail], axis=1).astype(BF)


def mix_grads(got):
    return pl.pallas_call(
        mix_grads_kernel,
        grid=(SEQS // 2,),
        in_specs=[packets(PACK)],
        out_specs=token_rows(MIX),
        out_shape=shape_of((GROUP, MIX), BF),
        compiler_params=PARAMS,
        cost_estimate=cost(4 * GROUP * MIX, 2.2e6),
        name="mix_grads",
    )(got)


def back_kernel(
    spot_ref, mix_ref, dqkv_ref, dz_ref, n_ref, w_ref, mine_ref, other_ref, gain_ref
):
    @pl.when(pl.program_id(0) == 0)
    def _():
        gain_ref[...] = jnp.zeros_like(gain_ref)

    first = spot_ref[NZ] == 0
    grad = jnp.concatenate([mix_ref[...], dqkv_ref[...], dz_ref[...]], axis=1)
    for f in range(NF):
        part = slice(f * SHARD, (f + 1) * SHARD)
        dn = dot(grad, w_ref[:, f].reshape(SHARD, W1_COLS), 1, 1)
        gain_ref[:, part] += jnp.sum(dn * n_ref[:, part].astype(F32), axis=0, keepdims=True)
        dn = dn.astype(BF)
        mine_ref[0, :, part] = jnp.where(first, dn[:ROWS], dn[ROWS:])
        other_ref[0, :, part] = jnp.where(first, dn[ROWS:], dn[:ROWS])


def back_project(spot, mix, dqkv, dz, normed, w_one):
    def rows(width):
        return pl.BlockSpec((2 * ROWS, width), lambda i, spot: (i, 0))

    specs, shapes = ring_specs(D)
    return pl.pallas_call(
        back_kernel,
        grid_spec=pltpu.PrefetchScalarGridSpec(
            num_scalar_prefetch=1,
            grid=(SEQS // 2,),
            in_specs=[
                rows(MIX),
                rows(QKV),
                rows(INNER_F),
                rows(D),
                pl.BlockSpec((NC, NF, SLICE, W1_COLS), lambda i, spot: (0, 0, 0, 0)),
            ],
            out_specs=specs + [pl.BlockSpec((1, D), lambda i, spot: (0, 0))],
        ),
        out_shape=shapes + [shape_of((1, D), F32)],
        compiler_params=PARAMS,
        cost_estimate=cost(2 * GROUP * D * W1_COLS, 18e6),
        name="back_project",
    )(spot, mix, dqkv, dz, normed, w_one)


def column_grad_kernel(left_ref, *refs):
    out_ref = refs[-1]
    first = 0
    for right_ref in refs[:-1]:
        term = dot(left_ref[...], right_ref[...], 0, 0).astype(BF)
        for block in range(out_ref.shape[1]):
            for tile in range(right_ref.shape[1] // LANES):
                out_ref[:, block, first + tile] = term[
                    block * SHARD : (block + 1) * SHARD, tile * LANES : (tile + 1) * LANES
                ].reshape(NC, SLICE, LANES)
        first += right_ref.shape[1] // LANES


def column_grad(left, *rights):
    count, width = left.shape[1] // SHARD, sum(right.shape[1] for right in rights)
    tiles = width // LANES
    many = 2
    return pl.pallas_call(
        column_grad_kernel,
        grid=(count // many,),
        in_specs=[pl.BlockSpec((GROUP, many * SHARD), lambda i: (0, i))]
        + [whole(GROUP, right.shape[1]) for right in rights],
        out_specs=pl.BlockSpec((NC, many, tiles, SLICE, LANES), lambda i: (0, i, 0, 0, 0)),
        out_shape=shape_of((NC, count, tiles, SLICE, LANES), BF),
        compiler_params=PARAMS,
        cost_estimate=cost(
            2 * GROUP * left.shape[1] * width,
            2 * GROUP * (left.shape[1] + width) + 2 * left.shape[1] * width,
        ),
        name="column_grad",
    )(left, *rights)


def channels(count):
    return pl.BlockSpec((count, INNER_F, ROWS), lambda i: (i, 0, 0))


def gate_packets(rows):
    return pl.BlockSpec((2 * GATE_SEQS, rows, LANES), lambda i: (i, 0, 0))


def gate_kernel(got_ref, z_ref, g_ref, sq_ref):
    for j in range(GATE_SEQS):
        ssd = got_ref[2 * j : 2 * j + 2, :XW].reshape(INNER_F, ROWS).astype(F32)
        z = z_ref[j]
        g = ssd * (z * jax.nn.sigmoid(z))
        g_ref[j] = g
        seq = pl.program_id(0) * GATE_SEQS + j
        sq_ref[pl.ds(seq, 1)] = jnp.sum(g * g, axis=0, keepdims=True)


def gate(got, z):
    return pl.pallas_call(
        gate_kernel,
        grid=(SEQS // GATE_SEQS,),
        in_specs=[gate_packets(XW), channels(GATE_SEQS)],
        out_specs=[channels(GATE_SEQS), whole(SEQS, ROWS)],
        out_shape=[shape_of((SEQS, INNER_F, ROWS), F32), shape_of((SEQS, ROWS), F32)],
        compiler_params=PARAMS,
        cost_estimate=cost(8 * GROUP * INNER_F, 4.2e6, GROUP * INNER_F),
        name="gate",
    )(got, z)


def branch_kernel(heads_ref, g_ref, sq_ref, gain_ref, w_ref, gh_ref, out_ref):
    step = pl.program_id(0)
    for j in range(2):
        scale = lax.rsqrt(sq_ref[pl.ds(2 * step + j, 1)] / INNER + EPS)
        gated = (g_ref[j] * scale * gain_ref[...]).T.astype(BF)
        heads = heads_ref[2 * j : 2 * j + 2].reshape(ROWS, HDIM)
        gh_ref[j * ROWS : (j + 1) * ROWS] = jnp.concatenate([gated, heads], axis=1)
    out_ref[...] = dot(gh_ref[...], w_ref[...], 1, 0).astype(BF)


def branch_out(heads, g, squares, gain, w_out):
    return pl.pallas_call(
        branch_kernel,
        grid=(SEQS // 2,),
        in_specs=[
            packets(HALF),
            channels(2),
            whole(SEQS, ROWS),
            whole(INNER_F, 1),
            whole(OUT_ROWS, D),
        ],
        out_specs=[token_rows(OUT_ROWS), token_rows(D)],
        out_shape=[shape_of((GROUP, OUT_ROWS), BF), shape_of((GROUP, D), BF)],
        compiler_params=PARAMS,
        cost_estimate=cost(2 * GROUP * OUT_ROWS * D, 10e6),
        name="branch_out",
    )(heads, g, squares, gain, w_out)


def branch_back_kernel(d_ref, w_ref, g_ref, gain_ref, dg_ref, inner_ref, dh_ref):
    step = pl.program_id(0)
    both = dot(d_ref[...], w_ref[...], 1, 1)
    for j in range(2):
        rows = both[j * ROWS : (j + 1) * ROWS]
        d_gated = rows[:, :INNER_F].T
        dg_ref[j] = d_gated
        inner_ref[pl.ds(2 * step + j, 1)] = jnp.sum(
            d_gated * gain_ref[...] * g_ref[j], axis=0, keepdims=True
        )
        heads = rows[:, INNER_F:].astype(BF)
        dh_ref[2 * j : 2 * j + 2] = heads.reshape(2, HALF, HDIM)


def branch_back(branch, w_out, g, gain):
    return pl.pallas_call(
        branch_back_kernel,
        grid=(SEQS // 2,),
        in_specs=[token_rows(D), whole(OUT_ROWS, D), channels(2), whole(INNER_F, 1)],
        out_specs=[channels(2), whole(SEQS, ROWS), packets(HALF)],
        out_shape=[
            shape_of((SEQS, INNER_F, ROWS), F32),
            shape_of((SEQS, ROWS), F32),
            shape_of((NC, HALF, HDIM), BF),
        ],
        compiler_params=PARAMS,
        cost_estimate=cost(2 * GROUP * OUT_ROWS * D, 10e6),
        name="branch_back",
    )(branch, w_out, g, gain)


def gate_back_kernel(
    got_ref, z_ref, g_ref, dg_ref, dh_ref, sq_ref, inner_ref, gain_ref,
    pack_ref, dz_ref, gain_grad_ref,
):
    index = pl.program_id(0)

    @pl.when(index == 0)
    def _():
        gain_grad_ref[...] = jnp.zeros_like(gain_grad_ref)

    pack_ref[:, XW:] = dh_ref[...]
    for j in range(GATE_SEQS):
        ssd = got_ref[2 * j : 2 * j + 2, :XW].reshape(INNER_F, ROWS).astype(F32)
        z = z_ref[j]
        g = g_ref[j]
        sig = jax.nn.sigmoid(z)
        silu = z * sig
        seq = index * GATE_SEQS + j
        scale = lax.rsqrt(sq_ref[pl.ds(seq, 1)] / INNER + EPS)
        inner = inner_ref[pl.ds(seq, 1)] / INNER
        scaled = dg_ref[j] * scale
        d_g = scaled * gain_ref[...] - g * (scale * scale * scale * inner)
        gain_grad_ref[...] += jnp.sum(scaled * g, axis=1, keepdims=True)
        pack_ref[2 * j : 2 * j + 2, :XW] = (d_g * silu).astype(BF).reshape(2, XW, LANES)
        dz_ref[j * ROWS : (j + 1) * ROWS] = (
            (d_g * ssd * (sig + silu * (1.0 - sig))).T.astype(BF)
        )


def gate_back(got, z, g, dg, dh, squares, inner, gain):
    return pl.pallas_call(
        gate_back_kernel,
        grid=(SEQS // GATE_SEQS,),
        in_specs=[
            gate_packets(XW),
            channels(GATE_SEQS),
            channels(GATE_SEQS),
            channels(GATE_SEQS),
            gate_packets(HALF),
            whole(SEQS, ROWS),
            whole(SEQS, ROWS),
            whole(INNER_F, 1),
        ],
        out_specs=[
            gate_packets(BOTH),
            pl.BlockSpec((GATE_SEQS * ROWS, INNER_F), lambda i: (i, 0)),
            whole(INNER_F, 1),
        ],
        out_shape=[
            shape_of((NC, BOTH, LANES), BF),
            shape_of((GROUP, INNER_F), BF),
            shape_of((INNER_F, 1), F32),
        ],
        compiler_params=PARAMS,
        cost_estimate=cost(20 * GROUP * INNER_F, 8e6, GROUP * INNER_F),
        name="gate_back",
    )(got, z, g, dg, dh, squares, inner, gain)


def act_back_kernel(cot_ref, down_ref, out_ref):
    out_ref[...] = dot(cot_ref[...], down_ref[...], 1, 1)


def act_back(cot, w_down):
    return pl.pallas_call(
        act_back_kernel,
        grid=(SEQS // 2,),
        in_specs=[token_rows(D), whole(FF_F, D)],
        out_specs=token_rows(FF_F),
        out_shape=shape_of((GROUP, FF_F), F32),
        compiler_params=PARAMS,
        cost_estimate=cost(2 * GROUP * D * FF_F, 9e6),
        name="act_back",
    )(cot, w_down)


def mlp_kernel(n_ref, d_act_ref, w_ref, act_ref, dgu_ref, dn_ref):
    acc = jnp.zeros((2 * ROWS, MLP_COLS), F32)
    for f in range(NF):
        acc = acc + dot(
            n_ref[:, f * SHARD : (f + 1) * SHARD], w_ref[:, f].reshape(SHARD, MLP_COLS), 1, 0
        )
    gate_part, upper = acc[:, :FF_F], acc[:, FF_F:]
    sig = jax.nn.sigmoid(gate_part)
    silu = gate_part * sig
    act_ref[...] = (silu * upper).astype(BF)
    d_act = d_act_ref[...]
    d_gu = jnp.concatenate(
        [d_act * upper * (sig + silu * (1.0 - sig)), d_act * silu], axis=1
    ).astype(BF)
    dgu_ref[...] = d_gu
    for f in range(NF):
        dn_ref[:, f * SHARD : (f + 1) * SHARD] = dot(
            d_gu, w_ref[:, f].reshape(SHARD, MLP_COLS), 1, 1
        ).astype(BF)


def mlp(normed, d_act, w_gu):
    return pl.pallas_call(
        mlp_kernel,
        grid=(SEQS // 2,),
        in_specs=[token_rows(D), token_rows(FF_F), whole(NC, NF, SLICE, MLP_COLS)],
        out_specs=[token_rows(FF_F), token_rows(MLP_COLS), token_rows(D)],
        out_shape=[
            shape_of((GROUP, FF_F), BF),
            shape_of((GROUP, MLP_COLS), BF),
            shape_of((GROUP, D), BF),
        ],
        compiler_params=PARAMS,
        cost_estimate=cost(8 * GROUP * D * FF_F, 20e6, GROUP * FF_F),
        name="mlp",
    )(normed, d_act, w_gu)


def ring_specs(width):
    def spec(*_):
        return pl.BlockSpec((1, ROWS, width), lambda i, spot: (spot[i], 0, 0))

    return [spec(), spec()], [shape_of((NZ, ROWS, width), BF)] * 2


def down_kernel(spot_ref, act_ref, down_ref, mine_ref, other_ref):
    rows = dot(act_ref[...], down_ref[...], 1, 0).astype(BF)
    first = spot_ref[NZ] == 0
    mine_ref[0] = jnp.where(first, rows[:ROWS], rows[ROWS:])
    other_ref[0] = jnp.where(first, rows[ROWS:], rows[:ROWS])


def down_out(spot, act, w_down):
    specs, shapes = ring_specs(D)
    return pl.pallas_call(
        down_kernel,
        grid_spec=pltpu.PrefetchScalarGridSpec(
            num_scalar_prefetch=1,
            grid=(SEQS // 2,),
            in_specs=[
                pl.BlockSpec((2 * ROWS, FF_F), lambda i, spot: (i, 0)),
                pl.BlockSpec((FF_F, D), lambda i, spot: (0, 0)),
            ],
            out_specs=specs,
        ),
        out_shape=shapes,
        compiler_params=PARAMS,
        cost_estimate=cost(2 * GROUP * D * FF_F, 8e6),
        name="down_out",
    )(spot, act, w_down)


def lane_of(shape):
    return lax.broadcasted_iota(jnp.int32, shape, 1)


def sources(pair, first):
    if first:
        return 2 * pair, 2 * pair + 1
    return NC - 1 - 2 * pair, NC - 2 - 2 * pair


def assemble(ref, low, high, pair, first):
    one, two = sources(pair, first)
    left = lane_of((high - low, LANES)) < HALF
    return jnp.where(left, ref[one, low:high].astype(F32), ref[two, low:high].astype(F32))


def deal(ref, low, high, pair, first, values):
    one, two = sources(pair, first)
    values = values.astype(BF)
    ref[one, low:high, :HALF] = values[:, :HALF]
    ref[two, low:high, HALF:] = values[:, HALF:]


def taps_of(padded, taps):
    current = padded[:, LANES:]
    total = current * taps[:, CONV_K - 1 : CONV_K] + taps[:, CONV_K : CONV_K + 1]
    inputs = [current]
    for back in range(1, CONV_K):
        moved = pltpu.roll(padded, back, 1)[:, LANES:]
        inputs.append(moved)
        total = total + moved * taps[:, CONV_K - 1 - back : CONV_K - back]
    return inputs[::-1], total


def softplus(values):
    return jnp.maximum(values, 0.0) + jnp.log1p(jnp.exp(-jnp.abs(values)))


def at_pair(pair):
    return pl.ds(pl.multiple_of(pair * LANES, LANES), LANES)


def load_raw(got_ref, raw_ref):
    raw_ref[:, :LANES] = jnp.zeros((XB, LANES), F32)
    half_pairs = PAIRS // 2
    for first in (True, False):

        def load(pair, unused, first=first):
            place = at_pair((pair if first else pair + half_pairs) + 1)
            raw_ref[:, place] = assemble(got_ref, 0, XB, pair, first)
            return unused

        lax.fori_loop(0, half_pairs, load, 0, unroll=True)


def front_kernel(got_ref, taps_ref, heads_ref, x_ref, bc_ref, row_ref, raw_ref):
    load_raw(got_ref, raw_ref)

    def step(part, unused):
        rows = pl.ds(pl.multiple_of(part * PART, PART), PART)
        _, total = taps_of(raw_ref[rows], taps_ref[rows])
        active = (total * jax.nn.sigmoid(total)).astype(BF)

        @pl.when(part < XW // PART)
        def _():
            x_ref[rows] = active

        @pl.when(part >= XW // PART)
        def _():
            bc_ref[pl.ds(pl.multiple_of(part * PART - XW, PART), PART)] = active

        return unused

    lax.fori_loop(0, XB // PART, step, 0)
    half_pairs = PAIRS // 2
    parts = [
        assemble(got_ref, T_AT, PACK, index % half_pairs, index < half_pairs)
        for index in range(PAIRS)
    ]
    parts = jnp.concatenate(parts, axis=1)
    raw = parts[:HEADS_L] + parts[HEADS_L : 2 * HEADS_L] + heads_ref[:HEADS_L, :1]
    steps = softplus(raw)
    pad = jnp.zeros((8 - 2 * HEADS_L, LENGTH), F32)
    sums = jnp.concatenate([steps * heads_ref[HEADS_L : 2 * HEADS_L, :1], steps, pad], axis=0)
    rows = lax.broadcasted_iota(jnp.int32, sums.shape, 0)
    lane = lane_of(sums.shape) % CHUNK
    running = sums
    back = 1
    while back < CHUNK:
        running = running + jnp.where(lane >= back, pltpu.roll(running, back, 1), 0.0)
        back *= 2
    row_ref[:8] = jnp.where(rows < HEADS_L, running, sums)
    row_ref[8:] = jnp.concatenate([raw, jnp.zeros((8 - HEADS_L, LENGTH), F32)], axis=0)


def front(got, taps, heads):
    return pl.pallas_call(
        front_kernel,
        in_specs=[whole(NC, PACK, LANES), whole(XB, 8), whole(8, LANES)],
        out_specs=[whole(XW, LENGTH), whole(BC_F, LENGTH), whole(16, LENGTH)],
        out_shape=[
            shape_of((XW, LENGTH), BF),
            shape_of((BC_F, LENGTH), BF),
            shape_of((16, LENGTH), F32),
        ],
        grid=(1,),
        scratch_shapes=[pltpu.VMEM((XB, LENGTH + LANES), F32)],
        compiler_params=PARAMS,
        cost_estimate=cost(30 * XB * LENGTH, 4e6, XB * LENGTH),
        name="front",
    )(got, taps, heads)


def front_back_kernel(
    got_ref, taps_ref, heads_ref, row_ref, drow_ref, dx_ref, dbc_ref, pack_ref,
    taps_grad_ref, heads_grad_ref, raw_ref, grad_ref,
):
    half_pairs = PAIRS // 2
    load_raw(got_ref, raw_ref)

    grads = drow_ref[...]
    lane = lane_of(grads.shape) % CHUNK
    running = grads
    back = 1
    while back < CHUNK:
        running = running + jnp.where(
            lane < CHUNK - back, pltpu.roll(running, LENGTH - back, 1), 0.0
        )
        back *= 2
    rates = running[:HEADS_L]
    rate = heads_ref[HEADS_L : 2 * HEADS_L, :1]
    d_steps = grads[HEADS_L : 2 * HEADS_L] + rates * rate
    d_dt = d_steps * jax.nn.sigmoid(row_ref[8 : 8 + HEADS_L])
    steps = row_ref[HEADS_L : 2 * HEADS_L]
    heads_grad_ref[...] = jnp.concatenate(
        [
            jnp.sum(d_dt, axis=1, keepdims=True),
            jnp.sum(rates * steps, axis=1, keepdims=True) * rate,
            jnp.zeros((8 - 2 * HEADS_L, 1), F32),
        ],
        axis=0,
    )
    d_dt = jnp.concatenate([d_dt, jnp.zeros((16 - HEADS_L, LENGTH), F32)], axis=0)
    for index in range(PAIRS):
        first = index < half_pairs
        deal(
            pack_ref, T_AT, PACK, index % half_pairs, first,
            d_dt[:, index * LANES : (index + 1) * LANES],
        )

    def step(part, unused):
        rows = pl.ds(pl.multiple_of(part * PART, PART), PART)
        taps = taps_ref[rows]
        inputs, total = taps_of(raw_ref[rows], taps)
        sig = jax.nn.sigmoid(total)

        @pl.when(part < XW // PART)
        def _():
            grad_ref[:, :LENGTH] = dx_ref[rows]

        @pl.when(part >= XW // PART)
        def _():
            grad_ref[:, :LENGTH] = dbc_ref[pl.ds(pl.multiple_of(part * PART - XW, PART), PART)]

        grad = grad_ref[:, :LENGTH] * (sig + total * sig * (1.0 - sig))
        grad_ref[:, :LENGTH] = grad
        padded = grad_ref[...]
        d_raw = grad * taps[:, CONV_K - 1 : CONV_K]
        for ahead in range(1, CONV_K):
            moved = pltpu.roll(padded, LENGTH + LANES - ahead, 1)[:, :LENGTH]
            d_raw = d_raw + moved * taps[:, CONV_K - 1 - ahead : CONV_K - ahead]
        taps_grad_ref[rows] = jnp.concatenate(
            [jnp.sum(grad * moved, axis=1, keepdims=True) for moved in inputs]
            + [jnp.sum(grad, axis=1, keepdims=True)]
            + [jnp.zeros((PART, 8 - CONV_K - 1), F32)],
            axis=1,
        )
        raw_ref[rows, :LENGTH] = d_raw
        return unused

    grad_ref[:, LENGTH:] = jnp.zeros((PART, LANES), F32)
    lax.fori_loop(0, XB // PART, step, 0)
    for first in (True, False):

        def store(pair, unused, first=first):
            place = at_pair(pair if first else pair + half_pairs)
            deal(pack_ref, 0, XB, pair, first, raw_ref[:, place])
            return unused

        lax.fori_loop(0, half_pairs, store, 0, unroll=True)


def front_back(got, taps, heads, rows, drow, dx, dbc):
    return pl.pallas_call(
        front_back_kernel,
        in_specs=[
            whole(NC, PACK, LANES),
            whole(XB, 8),
            whole(8, LANES),
            whole(16, LENGTH),
            whole(8, LENGTH),
            whole(XW, LENGTH),
            whole(BC_F, LENGTH),
        ],
        out_specs=[whole(NC, PACK, LANES), whole(XB, 8), whole(8, 1)],
        out_shape=[
            shape_of((NC, PACK, LANES), BF),
            shape_of((XB, 8), F32),
            shape_of((8, 1), F32),
        ],
        grid=(1,),
        scratch_shapes=[
            pltpu.VMEM((XB, LENGTH + LANES), F32),
            pltpu.VMEM((PART, LENGTH + LANES), F32),
        ],
        compiler_params=PARAMS,
        cost_estimate=cost(60 * XB * LENGTH, 9e6, XB * LENGTH),
        name="front_back",
    )(got, taps, heads, rows, drow, dx, dbc)


def stacked(rows, width):
    return jnp.concatenate(
        [jnp.broadcast_to(row, (MDIM, width)) for row in rows], axis=0
    )


def state_sides(place_ref, bc_ref):
    quarter = STATE // BC_F
    bt = jnp.concatenate([bc_ref[place_ref[j]] for j in range(quarter)], axis=0)
    ct = jnp.concatenate([bc_ref[place_ref[quarter + j]] for j in range(quarter)], axis=0)
    return bt, ct


def chunk_terms(row_ref):
    rows = row_ref[...]
    cols = rows.T
    cum_row = [rows[h : h + 1] for h in range(HEADS_L)]
    dt_row = [rows[HEADS_L + h : HEADS_L + h + 1] for h in range(HEADS_L)]
    cum_col = [cols[:, h : h + 1] for h in range(HEADS_L)]
    dt_col = [cols[:, HEADS_L + h : HEADS_L + h + 1] for h in range(HEADS_L)]
    last = [row[:, CHUNK - 1 :] for row in cum_row]
    return cum_row, dt_row, cum_col, dt_col, last


def later_mask():
    shape = (CHUNK, CHUNK)
    return lax.broadcasted_iota(jnp.int32, shape, 1) >= lax.broadcasted_iota(jnp.int32, shape, 0)


def mamba_fwd_kernel(
    place_ref, x_ref, bc_ref, row_ref, skip_ref, pack_ref, st_out_ref, st_ref
):
    index = pl.program_id(0)

    @pl.when(index == 0)
    def _():
        st_ref[...] = jnp.zeros_like(st_ref)

    x_low = x_ref[...]
    x = x_low.astype(F32)
    bt, ct = state_sides(place_ref, bc_ref)
    st = st_ref[...]
    st_out_ref[0] = st
    cum_row, dt_row, cum_col, dt_col, last = chunk_terms(row_ref)
    inter = dot(bt, ct, 0, 0)
    carried = dot(st.astype(BF), ct, 1, 0)
    later = later_mask()
    within = []
    for h in range(HEADS_L):
        decay = jnp.exp(jnp.where(later, cum_row[h] - cum_col[h], MASKED))
        mixing = (inter * decay * dt_col[h]).astype(BF)
        within.append(dot(x_low[h * MDIM : (h + 1) * MDIM], mixing, 1, 0))
    entering = stacked([jnp.exp(row) for row in cum_row], CHUNK)
    y = jnp.concatenate(within, axis=0) + entering * carried + skip_ref[...] * x
    weights = stacked(
        [jnp.exp(end - row) * step for end, row, step in zip(last, cum_row, dt_row)], CHUNK
    )
    leaving = stacked([jnp.exp(end) for end in last], 1)
    st_ref[...] = st * leaving + dot((x * weights).astype(BF), bt, 1, 1)
    pairs = CHUNK // LANES
    early = index < CHUNKS // 2

    @pl.when(early)
    def _():
        for j in range(pairs):
            deal(pack_ref, 0, XW, pairs * index + j, True, y[:, j * LANES : (j + 1) * LANES])

    @pl.when(jnp.logical_not(early))
    def _():
        for j in range(pairs):
            deal(
                pack_ref, 0, XW, pairs * (index - CHUNKS // 2) + j, False,
                y[:, j * LANES : (j + 1) * LANES],
            )


def mamba_fwd(place, x, bc, rows, skip):
    return pl.pallas_call(
        mamba_fwd_kernel,
        grid=(CHUNKS,),
        in_specs=[
            SMEM,
            pl.BlockSpec((XW, CHUNK), lambda i: (0, i)),
            pl.BlockSpec((NF, BC_F, CHUNK), lambda i: (0, 0, i)),
            pl.BlockSpec((8, CHUNK), lambda i: (0, i)),
            whole(XW, 1),
        ],
        out_specs=[
            whole(NC, XW, LANES),
            pl.BlockSpec((1, XW, STATE), lambda i: (i, 0, 0)),
        ],
        out_shape=[
            shape_of((NC, XW, LANES), BF),
            shape_of((CHUNKS, XW, STATE), F32),
        ],
        scratch_shapes=[pltpu.VMEM((XW, STATE), F32)],
        compiler_params=PARAMS,
        cost_estimate=cost(2 * LENGTH * CHUNK * (STATE + 3 * XW), 7e6, LENGTH * CHUNK * 3),
        name="mamba_fwd",
    )(place, x, bc, rows, skip)


def mamba_bwd_kernel(
    place_ref, x_ref, got_ref, bc_ref, row_ref, st_in_ref, skip_ref,
    dx_ref, mine_ref, other_ref, drow_ref, dskip_ref, dst_ref, dy_ref,
):
    turn = pl.program_id(0)
    index = CHUNKS - 1 - turn
    pairs = CHUNK // LANES

    @pl.when(turn == 0)
    def _():
        dst_ref[...] = jnp.zeros_like(dst_ref)
        dskip_ref[...] = jnp.zeros_like(dskip_ref)

    @pl.when(index < CHUNKS // 2)
    def _():
        for j in range(pairs):
            dy_ref[:, j * LANES : (j + 1) * LANES] = assemble(
                got_ref, 0, XW, pairs * index + j, True
            )

    @pl.when(index >= CHUNKS // 2)
    def _():
        for j in range(pairs):
            dy_ref[:, j * LANES : (j + 1) * LANES] = assemble(
                got_ref, 0, XW, pairs * (index - CHUNKS // 2) + j, False
            )

    x_low = x_ref[...]
    x = x_low.astype(F32)
    dy = dy_ref[...]
    dy_low = dy.astype(BF)
    bt, ct = state_sides(place_ref, bc_ref)
    st = st_in_ref[0]
    dst = dst_ref[...]
    st_low = st.astype(BF)
    dst_low = dst.astype(BF)
    cum_row, dt_row, cum_col, dt_col, last = chunk_terms(row_ref)
    inter = dot(bt, ct, 0, 0)
    later = later_mask()
    entering = stacked([jnp.exp(row) for row in cum_row], CHUNK)
    tail = [jnp.exp(end - row) for end, row in zip(last, cum_row)]
    kept_row = [t * step for t, step in zip(tail, dt_row)]
    weights = stacked(kept_row, CHUNK)
    leaving = stacked([jnp.exp(end) for end in last], 1)
    carried = dot(st_low, ct, 1, 0) * entering
    reach = dot(dst_low, bt, 1, 0)
    dy_in = (dy * entering).astype(BF)
    x_out = (x * weights).astype(BF)
    along = dy * carried
    pulled = x * reach
    kept = jnp.sum(st * dst, axis=1, keepdims=True) * leaving
    d_inter = jnp.zeros((CHUNK, CHUNK), F32)
    dx_parts = []
    row_cum = []
    row_dt = []
    col_cum = []
    col_dt = []
    ends = lane_of((1, CHUNK)) == CHUNK - 1
    for h in range(HEADS_L):
        part = slice(h * MDIM, (h + 1) * MDIM)
        decay = jnp.exp(jnp.where(later, cum_row[h] - cum_col[h], MASKED))
        d_mix = dot(x_low[part], dy_low[part], 0, 0)
        scaled = decay * dt_col[h]
        d_inter = d_inter + d_mix * scaled
        mixing = inter * scaled
        dx_parts.append(dot(dy_low[part], mixing.astype(BF), 1, 1))
        to_dt = jnp.sum(d_mix * (inter * decay), axis=1, keepdims=True)
        q_row = jnp.sum(pulled[part], axis=0, keepdims=True)
        w_q = q_row * kept_row[h]
        d_last = jnp.sum(w_q, axis=1, keepdims=True) + jnp.sum(
            kept[part], axis=0, keepdims=True
        )
        row_cum.append(
            jnp.sum(d_mix * mixing, axis=0, keepdims=True)
            + jnp.sum(along[part], axis=0, keepdims=True)
            - w_q
            + jnp.where(ends, d_last, 0.0)
        )
        row_dt.append(q_row * tail[h])
        col_cum.append(-to_dt * dt_col[h])
        col_dt.append(to_dt)
    dx_ref[...] = jnp.concatenate(dx_parts, axis=0) + weights * reach + skip_ref[...] * dy
    d_low = d_inter.astype(BF)
    dbt = (dot(ct, d_low, 1, 1) + dot(dst_low, x_out, 0, 0)).astype(BF)
    dct = (dot(bt, d_low, 1, 0) + dot(st_low, dy_in, 0, 0)).astype(BF)
    quarter = STATE // BC_F
    parts = [
        grad[j * BC_F : (j + 1) * BC_F] for grad in (dbt, dct) for j in range(quarter)
    ]
    first = place_ref[0] < NZ
    for z in range(NZ):
        one, two = parts[2 * z], parts[2 * z + 1]
        distance = place_ref[2 * z] % NZ
        mine_ref[distance] = jnp.where(first, one, two)
        other_ref[distance] = jnp.where(first, two, one)
    dst_ref[...] = dst * leaving + dot(dy_in, ct, 1, 1)
    dskip_ref[...] += jnp.sum(dy * x, axis=1, keepdims=True)
    pad = jnp.zeros((CHUNK, 8 - 2 * HEADS_L), F32)
    columns = jnp.concatenate(col_cum + col_dt + [pad], axis=1).T
    drow_ref[...] = columns + jnp.concatenate(
        row_cum + row_dt + [jnp.zeros((8 - 2 * HEADS_L, CHUNK), F32)], axis=0
    )


def mamba_bwd(place, x, got, bc, rows, states, skip):
    end = CHUNKS - 1
    return pl.pallas_call(
        mamba_bwd_kernel,
        grid=(CHUNKS,),
        in_specs=[
            SMEM,
            pl.BlockSpec((XW, CHUNK), lambda i: (0, end - i)),
            whole(NC, BOTH, LANES),
            pl.BlockSpec((NF, BC_F, CHUNK), lambda i: (0, 0, end - i)),
            pl.BlockSpec((8, CHUNK), lambda i: (0, end - i)),
            pl.BlockSpec((1, XW, STATE), lambda i: (end - i, 0, 0)),
            whole(XW, 1),
        ],
        out_specs=[
            pl.BlockSpec((XW, CHUNK), lambda i: (0, end - i)),
            pl.BlockSpec((NZ, BC_F, CHUNK), lambda i: (0, 0, end - i)),
            pl.BlockSpec((NZ, BC_F, CHUNK), lambda i: (0, 0, end - i)),
            pl.BlockSpec((8, CHUNK), lambda i: (0, end - i)),
            whole(XW, 1),
        ],
        out_shape=[
            shape_of((XW, LENGTH), F32),
            shape_of((NZ, BC_F, LENGTH), BF),
            shape_of((NZ, BC_F, LENGTH), BF),
            shape_of((8, LENGTH), F32),
            shape_of((XW, 1), F32),
        ],
        scratch_shapes=[pltpu.VMEM((XW, STATE), F32), pltpu.VMEM((XW, CHUNK), F32)],
        compiler_params=PARAMS,
        cost_estimate=cost(
            2 * LENGTH * CHUNK * (3 * STATE + 7 * XW), 12e6, LENGTH * CHUNK * 3
        ),
        name="mamba_bwd",
    )(place, x, got, bc, rows, states, skip)


def position_of(source, odd, inside):
    block = jnp.where(source % 2 == odd, source, 2 * NC - 1 - source)
    return block * HALF + inside


def visible_mask(step, odd):
    key = lax.broadcasted_iota(jnp.int32, (1, LENGTH), 1)
    key_pos = position_of(key // ROWS, (key // HALF) % 2, key % HALF)
    query = lax.broadcasted_iota(jnp.int32, (QBLOCK, 1), 0)
    source = 2 * step + query // HALF
    query_pos = position_of(source, odd, query % HALF)
    return key_pos <= query_pos


def attn_fwd_kernel(odd_ref, q_ref, k_ref, v_ref, o_ref, lse_ref):
    q = q_ref[...].reshape(QBLOCK, HDIM)
    k = k_ref[...].reshape(LENGTH, HDIM)
    v = v_ref[...].reshape(LENGTH, HDIM)
    scores = dot(q, k, 1, 1) * SCALE
    scores = jnp.where(visible_mask(pl.program_id(0), odd_ref[0]), scores, MASKED)
    top = jnp.max(scores, axis=1, keepdims=True)
    grown = jnp.exp(scores - top)
    total = jnp.sum(grown, axis=1, keepdims=True)
    lse_ref[...] = top + jnp.log(total)
    probs = (grown * (1.0 / total)).astype(BF)
    o_ref[...] = dot(probs, v, 1, 0).astype(BF).reshape(2, HALF, HDIM)


def packed_part(at, rows, moving=False):
    block = at // rows
    if moving:
        return pl.BlockSpec((2, rows, HDIM), lambda i: (i, block, 0))
    return pl.BlockSpec((NC, rows, HDIM), lambda i: (0, block, 0))


def attn_fwd(odd, got):
    return pl.pallas_call(
        attn_fwd_kernel,
        grid=(QROWS // QBLOCK,),
        in_specs=[
            SMEM,
            packed_part(Q_AT, HALF, True),
            packed_part(K_AT, ROWS),
            packed_part(V_AT, ROWS),
        ],
        out_specs=[
            pl.BlockSpec((2, HALF, HDIM), lambda i: (i, 0, 0)),
            pl.BlockSpec((QBLOCK, 1), lambda i: (i, 0)),
        ],
        out_shape=[shape_of((NC, HALF, HDIM), BF), shape_of((QROWS, 1), F32)],
        compiler_params=PARAMS,
        cost_estimate=cost(4 * QROWS * LENGTH * HDIM, 3e6, QROWS * LENGTH),
        name="attn_fwd",
    )(odd, got, got, got)


def attn_bwd_kernel(
    odd_ref, q_ref, k_ref, v_ref, do_ref, lse_ref, pack_ref, dk_sum, dv_sum
):
    step = pl.program_id(0)

    @pl.when(step == 0)
    def _():
        dk_sum[...] = jnp.zeros_like(dk_sum)
        dv_sum[...] = jnp.zeros_like(dv_sum)

    q = q_ref[...].reshape(QBLOCK, HDIM)
    k = k_ref[...].reshape(LENGTH, HDIM)
    v = v_ref[...].reshape(LENGTH, HDIM)
    do = do_ref[...].reshape(QBLOCK, HDIM)
    scores = dot(q, k, 1, 1) * SCALE - lse_ref[...]
    probs = jnp.exp(jnp.where(visible_mask(step, odd_ref[0]), scores, MASKED))
    d_probs = dot(do, v, 1, 1)
    dv_sum[...] += dot(probs.astype(BF), do, 0, 0)
    inner = jnp.sum(probs * d_probs, axis=1, keepdims=True)
    d_scores = (probs * (d_probs - inner)).astype(BF)
    pack_ref[pl.ds(2 * step, 2), Q_AT:] = (
        (dot(d_scores, k, 1, 0) * SCALE).astype(BF).reshape(2, HALF, HDIM)
    )
    dk_sum[...] += dot(d_scores, q, 0, 0)

    @pl.when(step == pl.num_programs(0) - 1)
    def _():
        pack_ref[:, K_AT:V_AT] = (dk_sum[...] * SCALE).astype(BF).reshape(NC, ROWS, HDIM)
        pack_ref[:, V_AT:Q_AT] = dv_sum[...].astype(BF).reshape(NC, ROWS, HDIM)


def attn_bwd(odd, got, grads, lse):
    return pl.pallas_call(
        attn_bwd_kernel,
        grid=(QROWS // QBLOCK,),
        in_specs=[
            SMEM,
            packed_part(Q_AT, HALF, True),
            packed_part(K_AT, ROWS),
            packed_part(V_AT, ROWS),
            packed_part(XW, HALF, True),
            pl.BlockSpec((QBLOCK, 1), lambda i: (i, 0)),
        ],
        out_specs=whole(NC, ATTN, LANES),
        out_shape=shape_of((NC, ATTN, LANES), BF),
        scratch_shapes=[pltpu.VMEM((LENGTH, HDIM), F32), pltpu.VMEM((LENGTH, HDIM), F32)],
        compiler_params=PARAMS,
        cost_estimate=cost(10 * QROWS * LENGTH * HDIM, 4e6, QROWS * LENGTH),
        name="attn_bwd",
    )(odd, got, got, got, grads, lse)


def tiles_to_rows(refs):
    tiles = []
    for ref in refs:
        count = ref.shape[0] * SLICE
        for tile in range(ref.shape[1]):
            tiles.append(ref[:, tile].reshape(count, LANES).astype(F32))
    return jnp.concatenate(tiles, axis=1)


def unpack_kernel(*refs):
    refs[-1][...] = tiles_to_rows(refs[:-1])


def unpack_rows(tiles, at, first, rows):
    width = D // LANES
    step = NC // 2
    skip, base = first // LANES, at // width
    return pl.pallas_call(
        unpack_kernel,
        grid=(rows // LANES,),
        in_specs=[
            pl.BlockSpec(
                (step, width, SLICE, LANES),
                lambda i: ((i + skip) % 2, base + (i + skip) // 2, 0, 0),
            )
        ],
        out_specs=pl.BlockSpec((LANES, D), lambda i: (i, 0)),
        out_shape=shape_of((rows, D), F32),
        compiler_params=PARAMS,
        cost_estimate=cost(rows * D, 6 * rows * D),
        name="unpack_rows",
    )(tiles)


def unpack_gate_up(tiles):
    part = FF_F // LANES
    many = NF // 2

    def spec(j):
        return pl.BlockSpec(
            (NC, part, SLICE, LANES), lambda h, q: (0, 2 * (q * many + j) + h, 0, 0)
        )

    return pl.pallas_call(
        unpack_kernel,
        grid=(2, NF // many),
        in_specs=[spec(j) for j in range(many)],
        out_specs=pl.BlockSpec(
            (SHARD, many * FF_F), lambda h, q: (0, h * (NF // many) + q)
        ),
        out_shape=shape_of((SHARD, 2 * FF), F32),
        compiler_params=PARAMS,
        cost_estimate=cost(SHARD * 2 * FF, 6 * SHARD * 2 * FF),
        name="unpack_gate_up",
    )(*[tiles] * many)


def turned(ref, tile):
    return ref[:, tile].reshape(SHARD, LANES).astype(F32).T


def unpack_in_kernel(*refs):
    step = pl.program_id(0)
    steps = NF // 2
    wide = INNER_F // LANES
    out_ref = refs[-1]

    @pl.when(step < 2 * steps)
    def _():
        for index in range(2):
            for tile in range(wide):
                start = index * INNER_F + tile * LANES
                out_ref[start : start + LANES] = turned(refs[index], tile)

    @pl.when(step == 2 * steps)
    def _():
        for f in range(NF):
            tail = turned(refs[2 + f], 0)
            out_ref[f * BC_F : (f + 1) * BC_F] = tail[:BC_F]
            first = NF * BC_F + f * DT_F
            out_ref[first : first + DT_F] = tail[BC_F : BC_F + DT_F]


def unpack_in(tiles):
    wide = INNER_F // LANES
    half = NF // 2
    each = W1_COLS // LANES

    def spec(j):
        def index(i):
            f = 2 * (jnp.minimum(i, 2 * half - 1) % half) + j
            return (0, each * f + jnp.where(i < half, 0, wide), 0, 0)

        shape = tuple(pl.Element(size) for size in (NC, wide, SLICE, LANES))
        return pl.BlockSpec(shape, index)

    def tail_spec(f):
        return pl.BlockSpec((NC, 1, SLICE, LANES), lambda i: (0, each * f + 2 * wide, 0, 0))

    specs = [spec(0), spec(1)]
    specs += [tail_spec(f) for f in range(NF)]
    return pl.pallas_call(
        unpack_in_kernel,
        grid=(2 * half + 1,),
        in_specs=specs,
        out_specs=pl.BlockSpec((2 * INNER_F, SHARD), lambda i: (i, 0)),
        out_shape=shape_of((2 * INNER + 2 * STATE + MHEADS, SHARD), F32),
        compiler_params=PARAMS,
        cost_estimate=cost(SHARD * 6704, 6 * SHARD * 6704),
        name="unpack_in",
    )(*[tiles] * len(specs))


def unpack_qkv_kernel(*refs):
    group = NF // KVHEADS

    def tile(f, index):
        return refs[3 * f + index][:, 0].reshape(SHARD, HDIM).astype(F32)

    parts = [tile(f, 0) for f in range(NF)]
    for index in (1, 2):
        for head in range(KVHEADS):
            parts.append(sum(tile(head * group + j, index) for j in range(group)))
    refs[-1][...] = jnp.concatenate(parts, axis=1)


def unpack_qkv(tiles):
    each, first = W1_COLS // LANES, (INNER_F + MIX) // LANES
    specs = [
        pl.BlockSpec((NC, 1, SLICE, LANES), lambda i, at=each * f + first + index: (0, at, 0, 0))
        for f in range(NF)
        for index in range(3)
    ]
    width = (QHEADS + 2 * KVHEADS) * HDIM
    return pl.pallas_call(
        unpack_qkv_kernel,
        grid=(1,),
        in_specs=specs,
        out_specs=whole(SHARD, width),
        out_shape=shape_of((SHARD, width), F32),
        compiler_params=PARAMS,
        cost_estimate=cost(SHARD * width, 6 * SHARD * width),
        name="unpack_qkv",
    )(*[tiles] * len(specs))


def norm_scale(values):
    return lax.rsqrt(jnp.mean(values * values, axis=-1, keepdims=True) + EPS)


def norm_back(values, scale, gain, grad):
    pulled = grad * gain
    inner = jnp.mean(pulled * values, axis=-1, keepdims=True)
    d_values = scale * pulled - values * (scale * scale * scale) * inner
    return d_values, jnp.sum(grad * values * scale, axis=0)


def columns_of(weight, start, width):
    part = weight[:, start : start + NF * width]
    return part.reshape(weight.shape[0], NF, width).transpose(1, 0, 2)


def shards(
    tokens,
    norm_gain,
    w_in,
    w_qkv,
    conv_weight,
    conv_bias,
    dt_bias,
    a_log,
    d_skip,
    mamba_gain,
    w_mout,
    w_aout,
    mlp_gain,
    w_gate_up,
    w_down,
    cotangent,
):
    ctx = lax.axis_index("ctx")
    fsdp = lax.axis_index("fsdp")
    parity = ctx % 2
    odd = parity.astype(jnp.int32).reshape(1)
    z_at, core = fsdp // 2, fsdp % 2
    pieces = jnp.arange(NF, dtype=jnp.int32)
    order = ((z_at + pieces % NZ) % NZ) * 2 + (core + pieces // NZ) % 2
    place = ((pieces % 2 + core) % 2) * NZ + (pieces // 2 - z_at) % NZ

    def even_first(rows):
        rows = rows.reshape(2, HALF, D)
        return jnp.where(parity == 1, rows[::-1], rows).reshape(ROWS, D)

    spot = jnp.concatenate([place[::2] % NZ, core.astype(jnp.int32).reshape(1)])

    hidden = even_first(tokens).astype(F32)
    scale_one = norm_scale(hidden)
    normed = ring_gather((hidden * scale_one * norm_gain).astype(BF), order)

    in_rows = lax.dynamic_slice(w_in, (ctx * SLICE, 0), (SLICE, w_in.shape[1]))
    qkv_rows = lax.dynamic_slice(w_qkv, (ctx * SLICE, 0), (SLICE, w_qkv.shape[1]))
    gu_rows = lax.dynamic_slice(w_gate_up, (ctx * SLICE, 0), (SLICE, w_gate_up.shape[1]))
    parts = [
        columns_of(in_rows, INNER, INNER_F),
        columns_of(in_rows, 2 * INNER, BC_F),
        columns_of(in_rows, 2 * INNER + 2 * STATE, DT_F),
        jnp.zeros((NF, SLICE, LANES - BC_F - DT_F), BF),
        columns_of(qkv_rows, 0, HDIM),
    ]
    for start in (QHEADS * HDIM, (QHEADS + KVHEADS) * HDIM):
        pair = qkv_rows[:, start : start + KVHEADS * HDIM].reshape(SLICE, KVHEADS, HDIM)
        parts.append(jnp.repeat(pair.transpose(1, 0, 2), NF // KVHEADS, axis=0))
    parts += [
        columns_of(in_rows, 0, INNER_F),
        columns_of(gu_rows, 0, FF_F),
        columns_of(gu_rows, FF, FF_F),
    ]
    swapped, gu_swapped = together(
        swap_fsdp(jnp.concatenate(parts[:-2], axis=2)), jnp.concatenate(parts[-2:], axis=2)
    )
    w_one = lax.all_gather(swapped, "ctx", axis=0)
    normed, gu_swapped = together(normed, swap_fsdp(gu_swapped))
    w_out = jnp.concatenate([w_mout, w_aout], axis=0)
    cot_low = even_first(cotangent)

    blocks = jnp.stack([ctx, 2 * NC - 1 - ctx])
    blocks = jnp.where(parity == 1, blocks[::-1], blocks)
    positions = (
        blocks[:, None] * HALF + jnp.arange(HALF, dtype=jnp.int32)[None, :]
    ).reshape(ROWS)
    half_dim = HDIM // 2
    freqs = ROPE_BASE ** (-jnp.arange(half_dim, dtype=F32) / half_dim)
    angles = positions.astype(F32)[:, None] * freqs[None, :]
    cosine, sine = jnp.cos(angles), jnp.sin(angles)
    mix_pack, attn_pack = project(normed, w_one, cosine, sine)
    mix_pack, cot_low, normed = together(mix_pack, cot_low, normed)
    cot_all = gather_fsdp(cot_low)
    mix_got, gate_z, attn_pack = together(
        swap_ctx(mix_pack), project_z(normed, w_one), attn_pack
    )
    attn_got = swap_ctx(attn_pack)

    x_start = fsdp * INNER_F + parity * XW
    bc_start = INNER + fsdp * BC_F
    conv_all = jnp.concatenate(
        [conv_weight, conv_bias[None], jnp.zeros((3, conv_bias.shape[0]), F32)], axis=0
    )
    taps = jnp.concatenate(
        [
            lax.dynamic_slice(conv_all, (0, x_start), (8, XW)),
            lax.dynamic_slice(conv_all, (0, bc_start), (8, BC_F)),
        ],
        axis=1,
    ).T
    head = fsdp * DT_F + parity * HEADS_L
    my_bias = lax.dynamic_slice(dt_bias, (head,), (HEADS_L,))
    my_rate = -jnp.exp(lax.dynamic_slice(a_log, (head,), (HEADS_L,)))
    heads_in = jnp.broadcast_to(
        jnp.concatenate([my_bias, my_rate, jnp.zeros((8 - 2 * HEADS_L,), F32)])[:, None],
        (8, LANES),
    )
    my_skip = jnp.repeat(lax.dynamic_slice(d_skip, (head,), (HEADS_L,)), MDIM)[:, None]
    x_act, bc_own, row_terms = front(mix_got, taps, heads_in)
    bc_own, gu_swapped = together(bc_own, gu_swapped)
    w_gu = lax.all_gather(gu_swapped, "ctx", axis=0)
    bc = jnp.concatenate(ring_pieces(bc_own), axis=0).reshape(NF, BC_F, LENGTH)
    ssd_seq, states = mamba_fwd(place, x_act, bc, row_terms, my_skip)
    ssd_seq, attn_got, cot_all = together(ssd_seq, attn_got, cot_all)
    heads_seq, lse = attn_fwd(odd, attn_got)
    ssd, heads_seq = together(swap_ctx(ssd_seq), heads_seq)
    heads = swap_ctx(heads_seq)

    my_gain = lax.dynamic_slice(mamba_gain, (fsdp * INNER_F,), (INNER_F,))[:, None]
    g, squares = gate(ssd, gate_z)
    squares, w_gu = together(butterfly(squares, "fsdp", (1, 2, 4)), w_gu)
    gated_heads, branches = branch_out(heads, g, squares, my_gain, w_out)
    branches, cot_all = together(branches, cot_all)
    mixed = hidden + scatter_fsdp(branches)

    scale_two = norm_scale(mixed)
    normed_two, d_act = together(
        gather_fsdp((mixed * scale_two * mlp_gain).astype(BF)), act_back(cot_all, w_down)
    )
    act, d_gu, d_normed_two = mlp(normed_two, d_act, w_gu)
    down_mine, down_other = down_out(spot, act, w_down)

    def side_by_side(*terms):
        return jnp.concatenate([term.reshape(NC, -1, LANES) for term in terms], axis=1)

    def total_of(got):
        return jnp.sum(got.astype(F32), axis=0).astype(BF)

    def scatter_ctx(joined):
        part = lax.psum_scatter(joined, "ctx", scatter_dimension=0, tiled=False)
        return lax.optimization_barrier(part)

    def all_ctx(parts):
        joined = jnp.concatenate(parts, axis=0)
        return lax.all_gather(joined.reshape(-1, SLICE, LANES), "ctx", axis=0)

    gu_tiles = MLP_COLS // LANES
    row_tiles = OUT_ROWS // SHARD * (D // LANES)
    packed_one = side_by_side(column_grad(normed_two, d_gu), column_grad(act, cot_all))
    d_normed_two, packed_one, down_mine, down_other = together(
        scatter_fsdp(d_normed_two), packed_one, down_mine, down_other
    )
    sum_one = scatter_ctx(packed_one)
    d_mixed, g_mlp_gain = norm_back(mixed, scale_two, mlp_gain, d_normed_two)
    d_mixed = d_mixed + cot_low.astype(F32)
    branch = ring_gather(d_mixed.astype(BF), order)

    dg, inner, dh = branch_back(branch, w_out, g, my_gain)
    inner = butterfly(inner, "fsdp", (1, 2, 4))
    d_mixers, dz, g_mamba_gain = gate_back(
        ssd, gate_z, g, dg, dh, squares, inner, my_gain
    )
    d_mixers = swap_ctx(d_mixers)
    packed_two = side_by_side(column_grad(gated_heads, branch), column_grad(normed, dz))
    d_mixers, packed_two = lax.optimization_barrier((d_mixers, packed_two))
    sum_two = scatter_ctx(packed_two)
    dx, dbc_mine, dbc_other, drow, dskip = mamba_bwd(
        place, x_act, d_mixers, bc, row_terms, states, my_skip
    )
    dbc_joined = ring_join(
        dbc_mine.reshape(NZ * BC_F, LENGTH), dbc_other.reshape(NZ * BC_F, LENGTH)
    )
    dx, d_mixers = together(dx, d_mixers)
    dbc_joined, sum_one = together(dbc_joined, sum_one)
    down_at = NF * gu_tiles
    out_at = down_at + row_tiles
    gu_part = swap_fsdp(sum_one[: down_at * SLICE].reshape(NF, -1, LANES))
    dbc_own, attn_pack, gu_part, down_other = together(
        ring_scatter(dbc_joined), attn_bwd(odd, attn_got, d_mixers, lse), gu_part, down_other
    )
    attn_back = swap_ctx(attn_pack)
    mix_pack, g_taps, g_heads = front_back(
        mix_got, taps, heads_in, row_terms, drow, dx, dbc_own
    )
    mix_pack, attn_back = together(mix_pack, attn_back)
    def joined(mine, other):
        return ring_join(mine.reshape(NZ * ROWS, D), other.reshape(NZ * ROWS, D))

    mix_back, d_qkv, sum_two, down = together(
        swap_ctx(mix_pack),
        attn_grads(attn_back, cosine, sine),
        sum_two,
        ring_scatter(joined(down_mine, down_other)),
    )
    output = even_first((mixed + down).astype(BF)).reshape(tokens.shape)
    all_one = all_ctx(
        [
            gu_part.reshape(-1, LANES),
            sum_one[down_at * SLICE :],
            sum_two[: row_tiles * SLICE],
        ]
    )
    d_mix = mix_grads(mix_back)
    packed_mix, dz = together(column_grad(normed, d_mix, d_qkv).reshape(NC, -1, LANES), dz)
    mine, other, gain_sum = back_project(spot, d_mix, d_qkv, dz, normed, w_one)
    g_norm_gain = gain_sum[0] / norm_gain

    got_mix, d_normed = together(swap_ctx(packed_mix), joined(mine, other))
    columns = swap_fsdp(
        jnp.concatenate(
            [
                sum_two[row_tiles * SLICE :].reshape(NF, -1, LANES),
                total_of(got_mix).reshape(NF, -1, LANES),
            ],
            axis=1,
        )
    )
    def by_half(values):
        zero = jnp.zeros_like(values)
        return jnp.where(
            parity == 1, jnp.stack([zero, values], axis=-2), jnp.stack([values, zero], axis=-2)
        )

    g_conv = g_taps.T[: CONV_K + 1]
    g_d_skip = jnp.sum(dskip.reshape(HEADS_L, MDIM), axis=1)
    per_head = jnp.stack(
        [g_heads[:HEADS_L, 0], g_heads[HEADS_L : 2 * HEADS_L, 0], g_d_skip]
    )
    own = jnp.concatenate(
        [
            by_half(g_conv[:, :XW]).reshape(-1),
            g_conv[:, XW:].reshape(-1),
            g_mamba_gain[:, 0],
            by_half(per_head).reshape(-1),
        ]
    )
    own_size = own.shape[0]
    own_pad = -(-own_size // LANES) * LANES
    own = jnp.concatenate([own, jnp.zeros((own_pad - own_size,), F32), g_mlp_gain, g_norm_gain])

    own, columns, all_one = together(own.reshape(-1, LANES), columns, all_one)
    all_two = all_ctx([columns.reshape(-1, LANES)])
    own, *d_normed = together(butterfly(own, "ctx", (1, 2, 4)), *ring_first(d_normed))
    own = butterfly(own, "ctx", (8,)).reshape(-1)
    mine = (jnp.arange(NF) == fsdp)[:, None]
    placed = jnp.where(mine, own[None, :own_pad], 0.0).reshape(-1)
    total = jnp.concatenate([placed, own[own_pad:]]).reshape(-1, LANES)
    total, d_normed = together(butterfly(total, "fsdp", (1,)), ring_last(*d_normed))

    g_gate_up = unpack_gate_up(all_one)
    g_down = unpack_rows(all_one, down_at, 0, OUT_ROWS)
    g_mout = unpack_rows(all_one, out_at, 0, INNER_F)
    g_aout = unpack_rows(all_one, out_at, INNER_F, HDIM)
    total = butterfly(total, "fsdp", (2,))
    total, g_gate_up, g_down, g_mout, g_aout = together(
        total, g_gate_up, g_down, g_mout, g_aout
    )
    g_qkv = unpack_qkv(all_two)
    g_in = unpack_in(all_two).T
    d_hidden, _ = norm_back(hidden, scale_one, norm_gain, d_normed)
    d_tokens = even_first((d_hidden + d_mixed).astype(BF)).reshape(tokens.shape)

    total = butterfly(total, "fsdp", (4,)).reshape(-1)
    each = total[: NF * own_pad].reshape(NF, own_pad)
    cut = [(CONV_K + 1) * INNER_F]
    cut.append(cut[0] + (CONV_K + 1) * BC_F)
    cut.append(cut[1] + INNER_F)
    conv_x = each[:, : cut[0]].reshape(NF, CONV_K + 1, INNER_F).transpose(1, 0, 2)
    conv_bc = each[:, cut[0] : cut[1]].reshape(NF, CONV_K + 1, BC_F).transpose(1, 0, 2)
    conv = jnp.concatenate(
        [conv_x.reshape(CONV_K + 1, INNER), conv_bc.reshape(CONV_K + 1, 2 * STATE)], axis=1
    )
    per_head = each[:, cut[2] : cut[2] + 3 * DT_F].reshape(NF, 3, DT_F).transpose(1, 0, 2)
    per_head = per_head.reshape(3, MHEADS)
    gains = total[NF * own_pad :].reshape(2, D)
    return (
        output,
        d_tokens,
        gains[1],
        g_in,
        g_qkv,
        conv[:CONV_K],
        conv[CONV_K],
        per_head[0],
        per_head[1],
        per_head[2],
        each[:, cut[1] : cut[2]].reshape(INNER),
        g_mout,
        g_aout,
        gains[0],
        g_gate_up,
        g_down,
    )


def solution(mesh):
    tokens_at = P("fsdp", "ctx", None, None)
    rows_at = P("fsdp", None)
    placed = (
        tokens_at,
        P(),
        rows_at,
        rows_at,
        P(),
        P(),
        P(),
        P(),
        P(),
        P(),
        rows_at,
        rows_at,
        P(),
        rows_at,
        rows_at,
        tokens_at,
    )
    return jax.shard_map(
        shards,
        mesh=mesh,
        in_specs=placed,
        out_specs=(
            tokens_at,
            tokens_at,
            P(),
            rows_at,
            rows_at,
            P(),
            P(),
            P(),
            P(),
            P(),
            P(),
            rows_at,
            rows_at,
            P(),
            rows_at,
            rows_at,
        ),
        check_vma=False,
    )
```

```python
import functools

import jax
import jax.numpy as jnp
from jax import lax
from jax.experimental import pallas as pl
from jax.experimental.pallas import tpu as pltpu
from jax.sharding import PartitionSpec as P

D = 2048
MHEADS = 48
MDIM = 64
STATE = 256
CONV_K = 4
QHEADS = 8
KVHEADS = 2
HDIM = 128
FF = 4096
HALF = 64
INNER = 3072
LENGTH = 2048
SEQS = 8
NC = 16
NF = 8
NZ = 4
NY = 4
LANES = 128
ROWS = 2 * HALF
GROUP = SEQS * ROWS
INNER_F = INNER // NF
HEADS_L = 3
XW = HEADS_L * MDIM
BC_F = 2 * STATE // NF
DT_F = MHEADS // NF
FF_F = FF // NF
CHUNK = 256
CHUNKS = LENGTH // CHUNK
PAIRS = LENGTH // LANES
QROWS = LENGTH // 2
QBLOCK = 128
SHARD = D // NF
SLICE = SHARD // NC
MIX = INNER_F + LANES
QKV = 3 * HDIM
WM_COLS = MIX + QKV
W1_COLS = WM_COLS + INNER_F
MLP_COLS = 2 * FF_F
OUT_ROWS = INNER_F + HDIM
K_AT, V_AT, Q_AT, ATTN = 0, 128, 256, 320
XB = XW + BC_F
B_AT, T_AT, PACK = XW, XB, XB + 16
BOTH = XW + HALF
GATE_SEQS = 4
IN_SEQS = 4
PART = 16
EPS = 1e-06
ROPE_BASE = 100000000000.0
MASKED = -1e30
SCALE = HDIM ** (-0.5)
BF = jnp.bfloat16
F32 = jnp.float32
PARAMS = pltpu.CompilerParams(vmem_limit_bytes=56 * 1024 * 1024)
SMEM = pl.BlockSpec(memory_space=pltpu.SMEM)


def dot(left, right, left_dim, right_dim):
    return lax.dot_general(
        left, right, (((left_dim,), (right_dim,)), ((), ())), preferred_element_type=F32
    )


def whole(*shape):
    return pl.BlockSpec(shape, lambda *i: (0,) * len(shape))


def cost(flops, moved, transcendentals=0):
    return pl.CostEstimate(
        flops=int(flops), bytes_accessed=int(moved), transcendentals=int(transcendentals)
    )


def shape_of(shape, dtype):
    return jax.ShapeDtypeStruct(shape, dtype)


OTHER_CORE = [(i, i ^ 1) for i in range(NF)]
TO_NEXT = [(i, (i + 2) % NF) for i in range(NF)]
TO_PREV = [(i, (i - 2) % NF) for i in range(NF)]


def send(value, route):
    return lax.ppermute(value, "fsdp", route)


def gather_fsdp(value):
    return lax.all_gather(value, "fsdp", axis=0, tiled=True)


def scatter_fsdp(parts):
    return lax.psum_scatter(parts, "fsdp", scatter_dimension=0, tiled=True).astype(F32)


def ring_pieces(value):
    half = value.shape[0] // 2
    after = send(value, TO_PREV)
    before = send(value, TO_NEXT)
    near = send(value, OTHER_CORE)
    far = jnp.concatenate(
        [send(after[:half], TO_PREV), send(before[half:], TO_NEXT)], axis=0
    )
    near_after = send(after, OTHER_CORE)
    near_before = send(before, OTHER_CORE)
    near_far = send(far, OTHER_CORE)
    return [value, after, far, before, near, near_after, near_far, near_before]


def ring_gather(value, order):
    whole_value = jnp.zeros((NF * value.shape[0],) + value.shape[1:], value.dtype)
    for index, piece in enumerate(ring_pieces(value)):
        whole_value = lax.dynamic_update_slice(
            whole_value, piece, (order[index] * value.shape[0], 0)
        )
    return whole_value


def plus(*terms):
    return sum(term.astype(F32) for term in terms)


def ring_join(mine, other):
    return plus(mine, send(other, OTHER_CORE)).astype(BF)


def ring_first(joined):
    size = joined.shape[0] // NZ
    half = size // 2
    own, after, far, before = [joined[i * size : (i + 1) * size] for i in range(NZ)]
    sent = (
        send(far[:half], TO_NEXT),
        send(far[half:], TO_PREV),
        send(after[half:], TO_NEXT),
        send(before[:half], TO_PREV),
    )
    return own, after[:half], before[half:], *sent


def ring_last(own, after, before, far_next, far_prev, after_two, before_one):
    after_one = send(plus(after, far_next).astype(BF), TO_NEXT)
    before_two = send(plus(before, far_prev).astype(BF), TO_PREV)
    return plus(
        own,
        jnp.concatenate([after_one, after_two], axis=0),
        jnp.concatenate([before_one, before_two], axis=0),
    )


def ring_scatter(joined):
    return ring_last(*ring_first(joined))


def together(*values):
    return lax.optimization_barrier(values)


def swap_ctx(value):
    return lax.all_to_all(value, "ctx", 0, 0, tiled=True)


def swap_fsdp(value):
    return lax.all_to_all(value, "fsdp", 0, 0, tiled=True)


def exchange(value, axis, bit):
    size = lax.axis_size(axis)
    return value + lax.ppermute(value, axis, [(i, i ^ bit) for i in range(size)])


def butterfly(value, axis, bits):
    for bit in bits:
        value = exchange(value, axis, bit)
    return value


def rotate(values, cosine, sine):
    half = values.shape[-1] // 2
    first = values[:, :half]
    second = values[:, half:]
    return jnp.concatenate(
        [first * cosine - second * sine, second * cosine + first * sine], axis=1
    )


def proj_kernel(n_ref, w_ref, cos_ref, sin_ref, mix_ref, attn_ref):
    acc = jnp.zeros((2 * ROWS, WM_COLS), F32)
    for f in range(NF):
        acc = acc + dot(
            n_ref[:, f * SHARD : (f + 1) * SHARD],
            w_ref[:, f, :, :WM_COLS].reshape(SHARD, WM_COLS),
            1,
            0,
        )
    for j in range(2):
        rows = acc[j * ROWS : (j + 1) * ROWS]
        x_rows = rows[:, :INNER_F].T.astype(BF)
        tail = rows[:, INNER_F:MIX].T
        query = rotate(rows[:, MIX : MIX + HDIM], cos_ref[...], sin_ref[...]).astype(BF)
        key = rotate(
            rows[:, MIX + HDIM : MIX + 2 * HDIM], cos_ref[...], sin_ref[...]
        ).astype(BF)
        value = rows[:, MIX + 2 * HDIM :].astype(BF)
        for p in range(2):
            to = 2 * j + p
            attn_ref[to, K_AT:V_AT] = key
            attn_ref[to, V_AT:Q_AT] = value
            attn_ref[to, Q_AT:] = query[p * HALF : (p + 1) * HALF]
            mix_ref[to, :B_AT] = x_rows[p * XW : (p + 1) * XW]
            mix_ref[to, B_AT:T_AT] = tail[:BC_F].astype(BF)
            steps = tail[BC_F + p * HEADS_L : BC_F + (p + 1) * HEADS_L]
            high = steps.astype(BF).astype(F32)
            mix_ref[to, T_AT:] = jnp.concatenate(
                [high, steps - high, jnp.zeros((16 - 2 * HEADS_L, ROWS), F32)], axis=0
            ).astype(BF)


def packets(rows):
    return pl.BlockSpec((4, rows, LANES), lambda i: (i, 0, 0))


def token_rows(width):
    return pl.BlockSpec((2 * ROWS, width), lambda i: (i, 0))


def project(normed, w_one, cosine, sine):
    return pl.pallas_call(
        proj_kernel,
        grid=(SEQS // 2,),
        in_specs=[
            token_rows(D),
            whole(NC, NF, SLICE, W1_COLS),
            whole(ROWS, HALF),
            whole(ROWS, HALF),
        ],
        out_specs=[packets(PACK), packets(ATTN)],
        out_shape=[shape_of((NC, PACK, LANES), BF), shape_of((NC, ATTN, LANES), BF)],
        compiler_params=PARAMS,
        cost_estimate=cost(2 * GROUP * D * WM_COLS, 10e6),
        name="project",
    )(normed, w_one, cosine, sine)


def proj_z_kernel(n_ref, w_ref, z_ref):
    acc = jnp.zeros((2 * ROWS, INNER_F), F32)
    for f in range(NF):
        acc = acc + dot(
            n_ref[:, f * SHARD : (f + 1) * SHARD],
            w_ref[:, f, :, WM_COLS:].reshape(SHARD, INNER_F),
            1,
            0,
        )
    for j in range(2):
        z_ref[j] = acc[j * ROWS : (j + 1) * ROWS].T


def project_z(normed, w_z):
    return pl.pallas_call(
        proj_z_kernel,
        grid=(SEQS // 2,),
        in_specs=[token_rows(D), whole(NC, NF, SLICE, W1_COLS)],
        out_specs=pl.BlockSpec((2, INNER_F, ROWS), lambda i: (i, 0, 0)),
        out_shape=shape_of((SEQS, INNER_F, ROWS), F32),
        compiler_params=PARAMS,
        cost_estimate=cost(2 * GROUP * D * INNER_F, 8e6),
        name="project_z",
    )(normed, w_z)


def attn_grads_kernel(got_ref, cos_ref, sin_ref, out_ref):
    for j in range(2):
        one = got_ref[2 * j].astype(F32)
        two = got_ref[2 * j + 1].astype(F32)
        both = one + two
        query = jnp.concatenate([one[Q_AT:], two[Q_AT:]], axis=0)
        query = rotate(query, cos_ref[...], -sin_ref[...])
        key = rotate(both[K_AT:V_AT], cos_ref[...], -sin_ref[...])
        out_ref[j * ROWS : (j + 1) * ROWS] = jnp.concatenate(
            [query, key, both[V_AT:Q_AT]], axis=1
        ).astype(BF)


def attn_grads(got, cosine, sine):
    return pl.pallas_call(
        attn_grads_kernel,
        grid=(SEQS // 2,),
        in_specs=[packets(ATTN), whole(ROWS, HALF), whole(ROWS, HALF)],
        out_specs=token_rows(QKV),
        out_shape=shape_of((GROUP, QKV), BF),
        compiler_params=PARAMS,
        cost_estimate=cost(10 * GROUP * QKV, 2e6),
        name="attn_grads",
    )(got, cosine, sine)


def mix_grads_kernel(got_ref, out_ref):
    for j in range(2):
        one = got_ref[2 * j].astype(F32)
        two = got_ref[2 * j + 1].astype(F32)
        x_rows = jnp.concatenate([one[:B_AT], two[:B_AT]], axis=0).T
        tail = jnp.concatenate(
            [
                one[B_AT:T_AT] + two[B_AT:T_AT],
                one[T_AT : T_AT + HEADS_L],
                two[T_AT : T_AT + HEADS_L],
                jnp.zeros((LANES - BC_F - DT_F, ROWS), F32),
            ],
            axis=0,
        ).T
        out_ref[j * ROWS : (j + 1) * ROWS] = jnp.concatenate([x_rows, tail], axis=1).astype(BF)


def mix_grads(got):
    return pl.pallas_call(
        mix_grads_kernel,
        grid=(SEQS // 2,),
        in_specs=[packets(PACK)],
        out_specs=token_rows(MIX),
        out_shape=shape_of((GROUP, MIX), BF),
        compiler_params=PARAMS,
        cost_estimate=cost(4 * GROUP * MIX, 2.2e6),
        name="mix_grads",
    )(got)


def back_kernel(
    spot_ref, mix_ref, dqkv_ref, dz_ref, n_ref, w_ref, mine_ref, other_ref, gain_ref
):
    @pl.when(pl.program_id(0) == 0)
    def _():
        gain_ref[...] = jnp.zeros_like(gain_ref)

    first = spot_ref[NZ] == 0
    grad = jnp.concatenate([mix_ref[...], dqkv_ref[...], dz_ref[...]], axis=1)
    for f in range(NF):
        part = slice(f * SHARD, (f + 1) * SHARD)
        dn = dot(grad, w_ref[:, f].reshape(SHARD, W1_COLS), 1, 1)
        gain_ref[:, part] += jnp.sum(dn * n_ref[:, part].astype(F32), axis=0, keepdims=True)
        dn = dn.astype(BF)
        mine_ref[0, :, part] = jnp.where(first, dn[:ROWS], dn[ROWS:])
        other_ref[0, :, part] = jnp.where(first, dn[ROWS:], dn[:ROWS])


def back_project(spot, mix, dqkv, dz, normed, w_one):
    def rows(width):
        return pl.BlockSpec((2 * ROWS, width), lambda i, spot: (i, 0))

    specs, shapes = ring_specs(D)
    return pl.pallas_call(
        back_kernel,
        grid_spec=pltpu.PrefetchScalarGridSpec(
            num_scalar_prefetch=1,
            grid=(SEQS // 2,),
            in_specs=[
                rows(MIX),
                rows(QKV),
                rows(INNER_F),
                rows(D),
                pl.BlockSpec((NC, NF, SLICE, W1_COLS), lambda i, spot: (0, 0, 0, 0)),
            ],
            out_specs=specs + [pl.BlockSpec((1, D), lambda i, spot: (0, 0))],
        ),
        out_shape=shapes + [shape_of((1, D), F32)],
        compiler_params=PARAMS,
        cost_estimate=cost(2 * GROUP * D * W1_COLS, 18e6),
        name="back_project",
    )(spot, mix, dqkv, dz, normed, w_one)


def column_grad_kernel(by_y, left_ref, *refs):
    out_ref = refs[-1]
    first = 0
    for right_ref in refs[:-1]:
        term = dot(left_ref[...], right_ref[...], 0, 0).astype(BF)
        for block in range(out_ref.shape[1]):
            for tile in range(right_ref.shape[1] // LANES):
                part = term[
                    block * SHARD : (block + 1) * SHARD, tile * LANES : (tile + 1) * LANES
                ]
                if by_y:
                    part = part.reshape(NC // NY, NY, SLICE, LANES)
                    for y in range(NY):
                        rows = slice(y * NC // NY, (y + 1) * NC // NY)
                        out_ref[rows, block, first + tile] = part[:, y]
                else:
                    out_ref[:, block, first + tile] = part.reshape(NC, SLICE, LANES)
        first += right_ref.shape[1] // LANES


def column_grad(left, *rights, by_y=False):
    count, width = left.shape[1] // SHARD, sum(right.shape[1] for right in rights)
    tiles = width // LANES
    many = 2
    return pl.pallas_call(
        functools.partial(column_grad_kernel, by_y),
        grid=(count // many,),
        in_specs=[pl.BlockSpec((GROUP, many * SHARD), lambda i: (0, i))]
        + [whole(GROUP, right.shape[1]) for right in rights],
        out_specs=pl.BlockSpec((NC, many, tiles, SLICE, LANES), lambda i: (0, i, 0, 0, 0)),
        out_shape=shape_of((NC, count, tiles, SLICE, LANES), BF),
        compiler_params=PARAMS,
        cost_estimate=cost(
            2 * GROUP * left.shape[1] * width,
            2 * GROUP * (left.shape[1] + width) + 2 * left.shape[1] * width,
        ),
        name="column_grad",
    )(left, *rights)


def channels(count):
    return pl.BlockSpec((count, INNER_F, ROWS), lambda i: (i, 0, 0))


def gate_packets(rows):
    return pl.BlockSpec((2 * GATE_SEQS, rows, LANES), lambda i: (i, 0, 0))


def gate_kernel(got_ref, z_ref, g_ref, sq_ref):
    for j in range(GATE_SEQS):
        ssd = got_ref[2 * j : 2 * j + 2, :XW].reshape(INNER_F, ROWS).astype(F32)
        z = z_ref[j]
        g = ssd * (z * jax.nn.sigmoid(z))
        g_ref[j] = g
        seq = pl.program_id(0) * GATE_SEQS + j
        sq_ref[pl.ds(seq, 1)] = jnp.sum(g * g, axis=0, keepdims=True)


def gate(got, z):
    return pl.pallas_call(
        gate_kernel,
        grid=(SEQS // GATE_SEQS,),
        in_specs=[gate_packets(XW), channels(GATE_SEQS)],
        out_specs=[channels(GATE_SEQS), whole(SEQS, ROWS)],
        out_shape=[shape_of((SEQS, INNER_F, ROWS), F32), shape_of((SEQS, ROWS), F32)],
        compiler_params=PARAMS,
        cost_estimate=cost(8 * GROUP * INNER_F, 4.2e6, GROUP * INNER_F),
        name="gate",
    )(got, z)


def branch_kernel(heads_ref, g_ref, sq_ref, gain_ref, w_ref, gh_ref, out_ref):
    step = pl.program_id(0)
    for j in range(2):
        scale = lax.rsqrt(sq_ref[pl.ds(2 * step + j, 1)] / INNER + EPS)
        gated = (g_ref[j] * scale * gain_ref[...]).T.astype(BF)
        heads = heads_ref[2 * j : 2 * j + 2].reshape(ROWS, HDIM)
        gh_ref[j * ROWS : (j + 1) * ROWS] = jnp.concatenate([gated, heads], axis=1)
    out_ref[...] = dot(gh_ref[...], w_ref[...], 1, 0).astype(BF)


def branch_out(heads, g, squares, gain, w_out):
    return pl.pallas_call(
        branch_kernel,
        grid=(SEQS // 2,),
        in_specs=[
            packets(HALF),
            channels(2),
            whole(SEQS, ROWS),
            whole(INNER_F, 1),
            whole(OUT_ROWS, D),
        ],
        out_specs=[token_rows(OUT_ROWS), token_rows(D)],
        out_shape=[shape_of((GROUP, OUT_ROWS), BF), shape_of((GROUP, D), BF)],
        compiler_params=PARAMS,
        cost_estimate=cost(2 * GROUP * OUT_ROWS * D, 10e6),
        name="branch_out",
    )(heads, g, squares, gain, w_out)


def branch_back_kernel(d_ref, w_ref, g_ref, gain_ref, dg_ref, inner_ref, dh_ref):
    step = pl.program_id(0)
    both = dot(d_ref[...], w_ref[...], 1, 1)
    for j in range(2):
        rows = both[j * ROWS : (j + 1) * ROWS]
        d_gated = rows[:, :INNER_F].T
        dg_ref[j] = d_gated
        inner_ref[pl.ds(2 * step + j, 1)] = jnp.sum(
            d_gated * gain_ref[...] * g_ref[j], axis=0, keepdims=True
        )
        heads = rows[:, INNER_F:].astype(BF)
        dh_ref[2 * j : 2 * j + 2] = heads.reshape(2, HALF, HDIM)


def branch_back(branch, w_out, g, gain):
    return pl.pallas_call(
        branch_back_kernel,
        grid=(SEQS // 2,),
        in_specs=[token_rows(D), whole(OUT_ROWS, D), channels(2), whole(INNER_F, 1)],
        out_specs=[channels(2), whole(SEQS, ROWS), packets(HALF)],
        out_shape=[
            shape_of((SEQS, INNER_F, ROWS), F32),
            shape_of((SEQS, ROWS), F32),
            shape_of((NC, HALF, HDIM), BF),
        ],
        compiler_params=PARAMS,
        cost_estimate=cost(2 * GROUP * OUT_ROWS * D, 10e6),
        name="branch_back",
    )(branch, w_out, g, gain)


def gate_back_kernel(
    got_ref, z_ref, g_ref, dg_ref, dh_ref, sq_ref, inner_ref, gain_ref,
    pack_ref, dz_ref, gain_grad_ref,
):
    index = pl.program_id(0)

    @pl.when(index == 0)
    def _():
        gain_grad_ref[...] = jnp.zeros_like(gain_grad_ref)

    pack_ref[:, XW:] = dh_ref[...]
    for j in range(GATE_SEQS):
        ssd = got_ref[2 * j : 2 * j + 2, :XW].reshape(INNER_F, ROWS).astype(F32)
        z = z_ref[j]
        g = g_ref[j]
        sig = jax.nn.sigmoid(z)
        silu = z * sig
        seq = index * GATE_SEQS + j
        scale = lax.rsqrt(sq_ref[pl.ds(seq, 1)] / INNER + EPS)
        inner = inner_ref[pl.ds(seq, 1)] / INNER
        scaled = dg_ref[j] * scale
        d_g = scaled * gain_ref[...] - g * (scale * scale * scale * inner)
        gain_grad_ref[...] += jnp.sum(scaled * g, axis=1, keepdims=True)
        pack_ref[2 * j : 2 * j + 2, :XW] = (d_g * silu).astype(BF).reshape(2, XW, LANES)
        dz_ref[j * ROWS : (j + 1) * ROWS] = (
            (d_g * ssd * (sig + silu * (1.0 - sig))).T.astype(BF)
        )


def gate_back(got, z, g, dg, dh, squares, inner, gain):
    return pl.pallas_call(
        gate_back_kernel,
        grid=(SEQS // GATE_SEQS,),
        in_specs=[
            gate_packets(XW),
            channels(GATE_SEQS),
            channels(GATE_SEQS),
            channels(GATE_SEQS),
            gate_packets(HALF),
            whole(SEQS, ROWS),
            whole(SEQS, ROWS),
            whole(INNER_F, 1),
        ],
        out_specs=[
            gate_packets(BOTH),
            pl.BlockSpec((GATE_SEQS * ROWS, INNER_F), lambda i: (i, 0)),
            whole(INNER_F, 1),
        ],
        out_shape=[
            shape_of((NC, BOTH, LANES), BF),
            shape_of((GROUP, INNER_F), BF),
            shape_of((INNER_F, 1), F32),
        ],
        compiler_params=PARAMS,
        cost_estimate=cost(20 * GROUP * INNER_F, 8e6, GROUP * INNER_F),
        name="gate_back",
    )(got, z, g, dg, dh, squares, inner, gain)


def act_back_kernel(cot_ref, down_ref, out_ref):
    out_ref[...] = dot(cot_ref[...], down_ref[...], 1, 1)


def act_back(cot, w_down):
    return pl.pallas_call(
        act_back_kernel,
        grid=(SEQS // 2,),
        in_specs=[token_rows(D), whole(FF_F, D)],
        out_specs=token_rows(FF_F),
        out_shape=shape_of((GROUP, FF_F), F32),
        compiler_params=PARAMS,
        cost_estimate=cost(2 * GROUP * D * FF_F, 9e6),
        name="act_back",
    )(cot, w_down)


def mlp_kernel(n_ref, d_act_ref, w_ref, act_ref, dgu_ref, dn_ref):
    acc = jnp.zeros((2 * ROWS, MLP_COLS), F32)
    for f in range(NF):
        acc = acc + dot(
            n_ref[:, f * SHARD : (f + 1) * SHARD], w_ref[:, f].reshape(SHARD, MLP_COLS), 1, 0
        )
    gate_part, upper = acc[:, :FF_F], acc[:, FF_F:]
    sig = jax.nn.sigmoid(gate_part)
    silu = gate_part * sig
    act_ref[...] = (silu * upper).astype(BF)
    d_act = d_act_ref[...]
    d_gu = jnp.concatenate(
        [d_act * upper * (sig + silu * (1.0 - sig)), d_act * silu], axis=1
    ).astype(BF)
    dgu_ref[...] = d_gu
    for f in range(NF):
        dn_ref[:, f * SHARD : (f + 1) * SHARD] = dot(
            d_gu, w_ref[:, f].reshape(SHARD, MLP_COLS), 1, 1
        ).astype(BF)


def mlp(normed, d_act, w_gu):
    return pl.pallas_call(
        mlp_kernel,
        grid=(SEQS // 2,),
        in_specs=[token_rows(D), token_rows(FF_F), whole(NC, NF, SLICE, MLP_COLS)],
        out_specs=[token_rows(FF_F), token_rows(MLP_COLS), token_rows(D)],
        out_shape=[
            shape_of((GROUP, FF_F), BF),
            shape_of((GROUP, MLP_COLS), BF),
            shape_of((GROUP, D), BF),
        ],
        compiler_params=PARAMS,
        cost_estimate=cost(8 * GROUP * D * FF_F, 20e6, GROUP * FF_F),
        name="mlp",
    )(normed, d_act, w_gu)


def ring_specs(width):
    def spec(*_):
        return pl.BlockSpec((1, ROWS, width), lambda i, spot: (spot[i], 0, 0))

    return [spec(), spec()], [shape_of((NZ, ROWS, width), BF)] * 2


def down_kernel(spot_ref, act_ref, down_ref, mine_ref, other_ref):
    rows = dot(act_ref[...], down_ref[...], 1, 0).astype(BF)
    first = spot_ref[NZ] == 0
    mine_ref[0] = jnp.where(first, rows[:ROWS], rows[ROWS:])
    other_ref[0] = jnp.where(first, rows[ROWS:], rows[:ROWS])


def down_out(spot, act, w_down):
    specs, shapes = ring_specs(D)
    return pl.pallas_call(
        down_kernel,
        grid_spec=pltpu.PrefetchScalarGridSpec(
            num_scalar_prefetch=1,
            grid=(SEQS // 2,),
            in_specs=[
                pl.BlockSpec((2 * ROWS, FF_F), lambda i, spot: (i, 0)),
                pl.BlockSpec((FF_F, D), lambda i, spot: (0, 0)),
            ],
            out_specs=specs,
        ),
        out_shape=shapes,
        compiler_params=PARAMS,
        cost_estimate=cost(2 * GROUP * D * FF_F, 8e6),
        name="down_out",
    )(spot, act, w_down)


def lane_of(shape):
    return lax.broadcasted_iota(jnp.int32, shape, 1)


def sources(pair, first):
    if first:
        return 2 * pair, 2 * pair + 1
    return NC - 1 - 2 * pair, NC - 2 - 2 * pair


def assemble(ref, low, high, pair, first):
    one, two = sources(pair, first)
    left = lane_of((high - low, LANES)) < HALF
    return jnp.where(left, ref[one, low:high].astype(F32), ref[two, low:high].astype(F32))


def deal(ref, low, high, pair, first, values):
    one, two = sources(pair, first)
    values = values.astype(BF)
    ref[one, low:high, :HALF] = values[:, :HALF]
    ref[two, low:high, HALF:] = values[:, HALF:]


def taps_of(padded, taps):
    current = padded[:, LANES:]
    total = current * taps[:, CONV_K - 1 : CONV_K] + taps[:, CONV_K : CONV_K + 1]
    inputs = [current]
    for back in range(1, CONV_K):
        moved = pltpu.roll(padded, back, 1)[:, LANES:]
        inputs.append(moved)
        total = total + moved * taps[:, CONV_K - 1 - back : CONV_K - back]
    return inputs[::-1], total


def softplus(values):
    return jnp.maximum(values, 0.0) + jnp.log1p(jnp.exp(-jnp.abs(values)))


def at_pair(pair):
    return pl.ds(pl.multiple_of(pair * LANES, LANES), LANES)


def load_raw(got_ref, raw_ref):
    raw_ref[:, :LANES] = jnp.zeros((XB, LANES), F32)
    half_pairs = PAIRS // 2
    for first in (True, False):

        def load(pair, unused, first=first):
            place = at_pair((pair if first else pair + half_pairs) + 1)
            raw_ref[:, place] = assemble(got_ref, 0, XB, pair, first)
            return unused

        lax.fori_loop(0, half_pairs, load, 0, unroll=True)


def front_kernel(got_ref, taps_ref, heads_ref, x_ref, bc_ref, row_ref, raw_ref):
    load_raw(got_ref, raw_ref)

    def step(part, unused):
        rows = pl.ds(pl.multiple_of(part * PART, PART), PART)
        _, total = taps_of(raw_ref[rows], taps_ref[rows])
        active = (total * jax.nn.sigmoid(total)).astype(BF)

        @pl.when(part < XW // PART)
        def _():
            x_ref[rows] = active

        @pl.when(part >= XW // PART)
        def _():
            bc_ref[pl.ds(pl.multiple_of(part * PART - XW, PART), PART)] = active

        return unused

    lax.fori_loop(0, XB // PART, step, 0)
    half_pairs = PAIRS // 2
    parts = [
        assemble(got_ref, T_AT, PACK, index % half_pairs, index < half_pairs)
        for index in range(PAIRS)
    ]
    parts = jnp.concatenate(parts, axis=1)
    raw = parts[:HEADS_L] + parts[HEADS_L : 2 * HEADS_L] + heads_ref[:HEADS_L, :1]
    steps = softplus(raw)
    pad = jnp.zeros((8 - 2 * HEADS_L, LENGTH), F32)
    sums = jnp.concatenate([steps * heads_ref[HEADS_L : 2 * HEADS_L, :1], steps, pad], axis=0)
    rows = lax.broadcasted_iota(jnp.int32, sums.shape, 0)
    lane = lane_of(sums.shape) % CHUNK
    running = sums
    back = 1
    while back < CHUNK:
        running = running + jnp.where(lane >= back, pltpu.roll(running, back, 1), 0.0)
        back *= 2
    row_ref[:8] = jnp.where(rows < HEADS_L, running, sums)
    row_ref[8:] = jnp.concatenate([raw, jnp.zeros((8 - HEADS_L, LENGTH), F32)], axis=0)


def front(got, taps, heads):
    return pl.pallas_call(
        front_kernel,
        in_specs=[whole(NC, PACK, LANES), whole(XB, 8), whole(8, LANES)],
        out_specs=[whole(XW, LENGTH), whole(BC_F, LENGTH), whole(16, LENGTH)],
        out_shape=[
            shape_of((XW, LENGTH), BF),
            shape_of((BC_F, LENGTH), BF),
            shape_of((16, LENGTH), F32),
        ],
        grid=(1,),
        scratch_shapes=[pltpu.VMEM((XB, LENGTH + LANES), F32)],
        compiler_params=PARAMS,
        cost_estimate=cost(30 * XB * LENGTH, 4e6, XB * LENGTH),
        name="front",
    )(got, taps, heads)


def front_back_kernel(
    got_ref, taps_ref, heads_ref, row_ref, drow_ref, dx_ref, dbc_ref, pack_ref,
    taps_grad_ref, heads_grad_ref, raw_ref, grad_ref,
):
    half_pairs = PAIRS // 2
    load_raw(got_ref, raw_ref)

    grads = drow_ref[...]
    lane = lane_of(grads.shape) % CHUNK
    running = grads
    back = 1
    while back < CHUNK:
        running = running + jnp.where(
            lane < CHUNK - back, pltpu.roll(running, LENGTH - back, 1), 0.0
        )
        back *= 2
    rates = running[:HEADS_L]
    rate = heads_ref[HEADS_L : 2 * HEADS_L, :1]
    d_steps = grads[HEADS_L : 2 * HEADS_L] + rates * rate
    d_dt = d_steps * jax.nn.sigmoid(row_ref[8 : 8 + HEADS_L])
    steps = row_ref[HEADS_L : 2 * HEADS_L]
    heads_grad_ref[...] = jnp.concatenate(
        [
            jnp.sum(d_dt, axis=1, keepdims=True),
            jnp.sum(rates * steps, axis=1, keepdims=True) * rate,
            jnp.zeros((8 - 2 * HEADS_L, 1), F32),
        ],
        axis=0,
    )
    d_dt = jnp.concatenate([d_dt, jnp.zeros((16 - HEADS_L, LENGTH), F32)], axis=0)
    for index in range(PAIRS):
        first = index < half_pairs
        deal(
            pack_ref, T_AT, PACK, index % half_pairs, first,
            d_dt[:, index * LANES : (index + 1) * LANES],
        )

    def step(part, unused):
        rows = pl.ds(pl.multiple_of(part * PART, PART), PART)
        taps = taps_ref[rows]
        inputs, total = taps_of(raw_ref[rows], taps)
        sig = jax.nn.sigmoid(total)

        @pl.when(part < XW // PART)
        def _():
            grad_ref[:, :LENGTH] = dx_ref[rows]

        @pl.when(part >= XW // PART)
        def _():
            grad_ref[:, :LENGTH] = dbc_ref[pl.ds(pl.multiple_of(part * PART - XW, PART), PART)]

        grad = grad_ref[:, :LENGTH] * (sig + total * sig * (1.0 - sig))
        grad_ref[:, :LENGTH] = grad
        padded = grad_ref[...]
        d_raw = grad * taps[:, CONV_K - 1 : CONV_K]
        for ahead in range(1, CONV_K):
            moved = pltpu.roll(padded, LENGTH + LANES - ahead, 1)[:, :LENGTH]
            d_raw = d_raw + moved * taps[:, CONV_K - 1 - ahead : CONV_K - ahead]
        taps_grad_ref[rows] = jnp.concatenate(
            [jnp.sum(grad * moved, axis=1, keepdims=True) for moved in inputs]
            + [jnp.sum(grad, axis=1, keepdims=True)]
            + [jnp.zeros((PART, 8 - CONV_K - 1), F32)],
            axis=1,
        )
        raw_ref[rows, :LENGTH] = d_raw
        return unused

    grad_ref[:, LENGTH:] = jnp.zeros((PART, LANES), F32)
    lax.fori_loop(0, XB // PART, step, 0)
    for first in (True, False):

        def store(pair, unused, first=first):
            place = at_pair(pair if first else pair + half_pairs)
            deal(pack_ref, 0, XB, pair, first, raw_ref[:, place])
            return unused

        lax.fori_loop(0, half_pairs, store, 0, unroll=True)


def front_back(got, taps, heads, rows, drow, dx, dbc):
    return pl.pallas_call(
        front_back_kernel,
        in_specs=[
            whole(NC, PACK, LANES),
            whole(XB, 8),
            whole(8, LANES),
            whole(16, LENGTH),
            whole(8, LENGTH),
            whole(XW, LENGTH),
            whole(BC_F, LENGTH),
        ],
        out_specs=[whole(NC, PACK, LANES), whole(XB, 8), whole(8, 1)],
        out_shape=[
            shape_of((NC, PACK, LANES), BF),
            shape_of((XB, 8), F32),
            shape_of((8, 1), F32),
        ],
        grid=(1,),
        scratch_shapes=[
            pltpu.VMEM((XB, LENGTH + LANES), F32),
            pltpu.VMEM((PART, LENGTH + LANES), F32),
        ],
        compiler_params=PARAMS,
        cost_estimate=cost(60 * XB * LENGTH, 9e6, XB * LENGTH),
        name="front_back",
    )(got, taps, heads, rows, drow, dx, dbc)


def stacked(rows, width):
    return jnp.concatenate(
        [jnp.broadcast_to(row, (MDIM, width)) for row in rows], axis=0
    )


def state_sides(place_ref, bc_ref):
    quarter = STATE // BC_F
    bt = jnp.concatenate([bc_ref[place_ref[j]] for j in range(quarter)], axis=0)
    ct = jnp.concatenate([bc_ref[place_ref[quarter + j]] for j in range(quarter)], axis=0)
    return bt, ct


def chunk_terms(row_ref):
    rows = row_ref[...]
    cols = rows.T
    cum_row = [rows[h : h + 1] for h in range(HEADS_L)]
    dt_row = [rows[HEADS_L + h : HEADS_L + h + 1] for h in range(HEADS_L)]
    cum_col = [cols[:, h : h + 1] for h in range(HEADS_L)]
    dt_col = [cols[:, HEADS_L + h : HEADS_L + h + 1] for h in range(HEADS_L)]
    last = [row[:, CHUNK - 1 :] for row in cum_row]
    return cum_row, dt_row, cum_col, dt_col, last


def later_mask():
    shape = (CHUNK, CHUNK)
    return lax.broadcasted_iota(jnp.int32, shape, 1) >= lax.broadcasted_iota(jnp.int32, shape, 0)


def mamba_fwd_kernel(
    place_ref, x_ref, bc_ref, row_ref, skip_ref, pack_ref, st_out_ref, st_ref
):
    index = pl.program_id(0)

    @pl.when(index == 0)
    def _():
        st_ref[...] = jnp.zeros_like(st_ref)

    x_low = x_ref[...]
    x = x_low.astype(F32)
    bt, ct = state_sides(place_ref, bc_ref)
    st = st_ref[...]
    st_out_ref[0] = st
    cum_row, dt_row, cum_col, dt_col, last = chunk_terms(row_ref)
    inter = dot(bt, ct, 0, 0)
    carried = dot(st.astype(BF), ct, 1, 0)
    later = later_mask()
    within = []
    for h in range(HEADS_L):
        decay = jnp.exp(jnp.where(later, cum_row[h] - cum_col[h], MASKED))
        mixing = (inter * decay * dt_col[h]).astype(BF)
        within.append(dot(x_low[h * MDIM : (h + 1) * MDIM], mixing, 1, 0))
    entering = stacked([jnp.exp(row) for row in cum_row], CHUNK)
    y = jnp.concatenate(within, axis=0) + entering * carried + skip_ref[...] * x
    weights = stacked(
        [jnp.exp(end - row) * step for end, row, step in zip(last, cum_row, dt_row)], CHUNK
    )
    leaving = stacked([jnp.exp(end) for end in last], 1)
    st_ref[...] = st * leaving + dot((x * weights).astype(BF), bt, 1, 1)
    pairs = CHUNK // LANES
    early = index < CHUNKS // 2

    @pl.when(early)
    def _():
        for j in range(pairs):
            deal(pack_ref, 0, XW, pairs * index + j, True, y[:, j * LANES : (j + 1) * LANES])

    @pl.when(jnp.logical_not(early))
    def _():
        for j in range(pairs):
            deal(
                pack_ref, 0, XW, pairs * (index - CHUNKS // 2) + j, False,
                y[:, j * LANES : (j + 1) * LANES],
            )


def mamba_fwd(place, x, bc, rows, skip):
    return pl.pallas_call(
        mamba_fwd_kernel,
        grid=(CHUNKS,),
        in_specs=[
            SMEM,
            pl.BlockSpec((XW, CHUNK), lambda i: (0, i)),
            pl.BlockSpec((NF, BC_F, CHUNK), lambda i: (0, 0, i)),
            pl.BlockSpec((8, CHUNK), lambda i: (0, i)),
            whole(XW, 1),
        ],
        out_specs=[
            whole(NC, XW, LANES),
            pl.BlockSpec((1, XW, STATE), lambda i: (i, 0, 0)),
        ],
        out_shape=[
            shape_of((NC, XW, LANES), BF),
            shape_of((CHUNKS, XW, STATE), F32),
        ],
        scratch_shapes=[pltpu.VMEM((XW, STATE), F32)],
        compiler_params=PARAMS,
        cost_estimate=cost(2 * LENGTH * CHUNK * (STATE + 3 * XW), 7e6, LENGTH * CHUNK * 3),
        name="mamba_fwd",
    )(place, x, bc, rows, skip)


def mamba_bwd_kernel(
    place_ref, x_ref, got_ref, bc_ref, row_ref, st_in_ref, skip_ref,
    dx_ref, mine_ref, other_ref, drow_ref, dskip_ref, dst_ref, dy_ref,
):
    turn = pl.program_id(0)
    index = CHUNKS - 1 - turn
    pairs = CHUNK // LANES

    @pl.when(turn == 0)
    def _():
        dst_ref[...] = jnp.zeros_like(dst_ref)
        dskip_ref[...] = jnp.zeros_like(dskip_ref)

    @pl.when(index < CHUNKS // 2)
    def _():
        for j in range(pairs):
            dy_ref[:, j * LANES : (j + 1) * LANES] = assemble(
                got_ref, 0, XW, pairs * index + j, True
            )

    @pl.when(index >= CHUNKS // 2)
    def _():
        for j in range(pairs):
            dy_ref[:, j * LANES : (j + 1) * LANES] = assemble(
                got_ref, 0, XW, pairs * (index - CHUNKS // 2) + j, False
            )

    x_low = x_ref[...]
    x = x_low.astype(F32)
    dy = dy_ref[...]
    dy_low = dy.astype(BF)
    bt, ct = state_sides(place_ref, bc_ref)
    st = st_in_ref[0]
    dst = dst_ref[...]
    st_low = st.astype(BF)
    dst_low = dst.astype(BF)
    cum_row, dt_row, cum_col, dt_col, last = chunk_terms(row_ref)
    inter = dot(bt, ct, 0, 0)
    later = later_mask()
    entering = stacked([jnp.exp(row) for row in cum_row], CHUNK)
    tail = [jnp.exp(end - row) for end, row in zip(last, cum_row)]
    kept_row = [t * step for t, step in zip(tail, dt_row)]
    weights = stacked(kept_row, CHUNK)
    leaving = stacked([jnp.exp(end) for end in last], 1)
    carried = dot(st_low, ct, 1, 0) * entering
    reach = dot(dst_low, bt, 1, 0)
    dy_in = (dy * entering).astype(BF)
    x_out = (x * weights).astype(BF)
    along = dy * carried
    pulled = x * reach
    kept = jnp.sum(st * dst, axis=1, keepdims=True) * leaving
    d_inter = jnp.zeros((CHUNK, CHUNK), F32)
    dx_parts = []
    row_cum = []
    row_dt = []
    col_cum = []
    col_dt = []
    ends = lane_of((1, CHUNK)) == CHUNK - 1
    for h in range(HEADS_L):
        part = slice(h * MDIM, (h + 1) * MDIM)
        decay = jnp.exp(jnp.where(later, cum_row[h] - cum_col[h], MASKED))
        d_mix = dot(x_low[part], dy_low[part], 0, 0)
        scaled = decay * dt_col[h]
        d_inter = d_inter + d_mix * scaled
        mixing = inter * scaled
        dx_parts.append(dot(dy_low[part], mixing.astype(BF), 1, 1))
        to_dt = jnp.sum(d_mix * (inter * decay), axis=1, keepdims=True)
        q_row = jnp.sum(pulled[part], axis=0, keepdims=True)
        w_q = q_row * kept_row[h]
        d_last = jnp.sum(w_q, axis=1, keepdims=True) + jnp.sum(
            kept[part], axis=0, keepdims=True
        )
        row_cum.append(
            jnp.sum(d_mix * mixing, axis=0, keepdims=True)
            + jnp.sum(along[part], axis=0, keepdims=True)
            - w_q
            + jnp.where(ends, d_last, 0.0)
        )
        row_dt.append(q_row * tail[h])
        col_cum.append(-to_dt * dt_col[h])
        col_dt.append(to_dt)
    dx_ref[...] = jnp.concatenate(dx_parts, axis=0) + weights * reach + skip_ref[...] * dy
    d_low = d_inter.astype(BF)
    dbt = (dot(ct, d_low, 1, 1) + dot(dst_low, x_out, 0, 0)).astype(BF)
    dct = (dot(bt, d_low, 1, 0) + dot(st_low, dy_in, 0, 0)).astype(BF)
    quarter = STATE // BC_F
    parts = [
        grad[j * BC_F : (j + 1) * BC_F] for grad in (dbt, dct) for j in range(quarter)
    ]
    first = place_ref[0] < NZ
    for z in range(NZ):
        one, two = parts[2 * z], parts[2 * z + 1]
        distance = place_ref[2 * z] % NZ
        mine_ref[distance] = jnp.where(first, one, two)
        other_ref[distance] = jnp.where(first, two, one)
    dst_ref[...] = dst * leaving + dot(dy_in, ct, 1, 1)
    dskip_ref[...] += jnp.sum(dy * x, axis=1, keepdims=True)
    pad = jnp.zeros((CHUNK, 8 - 2 * HEADS_L), F32)
    columns = jnp.concatenate(col_cum + col_dt + [pad], axis=1).T
    drow_ref[...] = columns + jnp.concatenate(
        row_cum + row_dt + [jnp.zeros((8 - 2 * HEADS_L, CHUNK), F32)], axis=0
    )


def mamba_bwd(place, x, got, bc, rows, states, skip):
    end = CHUNKS - 1
    return pl.pallas_call(
        mamba_bwd_kernel,
        grid=(CHUNKS,),
        in_specs=[
            SMEM,
            pl.BlockSpec((XW, CHUNK), lambda i: (0, end - i)),
            whole(NC, BOTH, LANES),
            pl.BlockSpec((NF, BC_F, CHUNK), lambda i: (0, 0, end - i)),
            pl.BlockSpec((8, CHUNK), lambda i: (0, end - i)),
            pl.BlockSpec((1, XW, STATE), lambda i: (end - i, 0, 0)),
            whole(XW, 1),
        ],
        out_specs=[
            pl.BlockSpec((XW, CHUNK), lambda i: (0, end - i)),
            pl.BlockSpec((NZ, BC_F, CHUNK), lambda i: (0, 0, end - i)),
            pl.BlockSpec((NZ, BC_F, CHUNK), lambda i: (0, 0, end - i)),
            pl.BlockSpec((8, CHUNK), lambda i: (0, end - i)),
            whole(XW, 1),
        ],
        out_shape=[
            shape_of((XW, LENGTH), F32),
            shape_of((NZ, BC_F, LENGTH), BF),
            shape_of((NZ, BC_F, LENGTH), BF),
            shape_of((8, LENGTH), F32),
            shape_of((XW, 1), F32),
        ],
        scratch_shapes=[pltpu.VMEM((XW, STATE), F32), pltpu.VMEM((XW, CHUNK), F32)],
        compiler_params=PARAMS,
        cost_estimate=cost(
            2 * LENGTH * CHUNK * (3 * STATE + 7 * XW), 12e6, LENGTH * CHUNK * 3
        ),
        name="mamba_bwd",
    )(place, x, got, bc, rows, states, skip)


def position_of(source, odd, inside):
    block = jnp.where(source % 2 == odd, source, 2 * NC - 1 - source)
    return block * HALF + inside


def visible_mask(step, odd):
    key = lax.broadcasted_iota(jnp.int32, (1, LENGTH), 1)
    key_pos = position_of(key // ROWS, (key // HALF) % 2, key % HALF)
    query = lax.broadcasted_iota(jnp.int32, (QBLOCK, 1), 0)
    source = 2 * step + query // HALF
    query_pos = position_of(source, odd, query % HALF)
    return key_pos <= query_pos


def attn_fwd_kernel(odd_ref, q_ref, k_ref, v_ref, o_ref, lse_ref):
    q = q_ref[...].reshape(QBLOCK, HDIM)
    k = k_ref[...].reshape(LENGTH, HDIM)
    v = v_ref[...].reshape(LENGTH, HDIM)
    scores = dot(q, k, 1, 1) * SCALE
    scores = jnp.where(visible_mask(pl.program_id(0), odd_ref[0]), scores, MASKED)
    top = jnp.max(scores, axis=1, keepdims=True)
    grown = jnp.exp(scores - top)
    total = jnp.sum(grown, axis=1, keepdims=True)
    lse_ref[...] = top + jnp.log(total)
    probs = (grown * (1.0 / total)).astype(BF)
    o_ref[...] = dot(probs, v, 1, 0).astype(BF).reshape(2, HALF, HDIM)


def packed_part(at, rows, moving=False):
    block = at // rows
    if moving:
        return pl.BlockSpec((2, rows, HDIM), lambda i: (i, block, 0))
    return pl.BlockSpec((NC, rows, HDIM), lambda i: (0, block, 0))


def attn_fwd(odd, got):
    return pl.pallas_call(
        attn_fwd_kernel,
        grid=(QROWS // QBLOCK,),
        in_specs=[
            SMEM,
            packed_part(Q_AT, HALF, True),
            packed_part(K_AT, ROWS),
            packed_part(V_AT, ROWS),
        ],
        out_specs=[
            pl.BlockSpec((2, HALF, HDIM), lambda i: (i, 0, 0)),
            pl.BlockSpec((QBLOCK, 1), lambda i: (i, 0)),
        ],
        out_shape=[shape_of((NC, HALF, HDIM), BF), shape_of((QROWS, 1), F32)],
        compiler_params=PARAMS,
        cost_estimate=cost(4 * QROWS * LENGTH * HDIM, 3e6, QROWS * LENGTH),
        name="attn_fwd",
    )(odd, got, got, got)


def attn_bwd_kernel(
    odd_ref, q_ref, k_ref, v_ref, do_ref, lse_ref, pack_ref, dk_sum, dv_sum
):
    step = pl.program_id(0)

    @pl.when(step == 0)
    def _():
        dk_sum[...] = jnp.zeros_like(dk_sum)
        dv_sum[...] = jnp.zeros_like(dv_sum)

    q = q_ref[...].reshape(QBLOCK, HDIM)
    k = k_ref[...].reshape(LENGTH, HDIM)
    v = v_ref[...].reshape(LENGTH, HDIM)
    do = do_ref[...].reshape(QBLOCK, HDIM)
    scores = dot(q, k, 1, 1) * SCALE - lse_ref[...]
    probs = jnp.exp(jnp.where(visible_mask(step, odd_ref[0]), scores, MASKED))
    d_probs = dot(do, v, 1, 1)
    dv_sum[...] += dot(probs.astype(BF), do, 0, 0)
    inner = jnp.sum(probs * d_probs, axis=1, keepdims=True)
    d_scores = (probs * (d_probs - inner)).astype(BF)
    pack_ref[pl.ds(2 * step, 2), Q_AT:] = (
        (dot(d_scores, k, 1, 0) * SCALE).astype(BF).reshape(2, HALF, HDIM)
    )
    dk_sum[...] += dot(d_scores, q, 0, 0)

    @pl.when(step == pl.num_programs(0) - 1)
    def _():
        pack_ref[:, K_AT:V_AT] = (dk_sum[...] * SCALE).astype(BF).reshape(NC, ROWS, HDIM)
        pack_ref[:, V_AT:Q_AT] = dv_sum[...].astype(BF).reshape(NC, ROWS, HDIM)


def attn_bwd(odd, got, grads, lse):
    return pl.pallas_call(
        attn_bwd_kernel,
        grid=(QROWS // QBLOCK,),
        in_specs=[
            SMEM,
            packed_part(Q_AT, HALF, True),
            packed_part(K_AT, ROWS),
            packed_part(V_AT, ROWS),
            packed_part(XW, HALF, True),
            pl.BlockSpec((QBLOCK, 1), lambda i: (i, 0)),
        ],
        out_specs=whole(NC, ATTN, LANES),
        out_shape=shape_of((NC, ATTN, LANES), BF),
        scratch_shapes=[pltpu.VMEM((LENGTH, HDIM), F32), pltpu.VMEM((LENGTH, HDIM), F32)],
        compiler_params=PARAMS,
        cost_estimate=cost(10 * QROWS * LENGTH * HDIM, 4e6, QROWS * LENGTH),
        name="attn_bwd",
    )(odd, got, got, got, grads, lse)


def tiles_to_rows(refs):
    tiles = []
    for ref in refs:
        count = ref.shape[0] * SLICE
        for tile in range(ref.shape[1]):
            tiles.append(ref[:, tile].reshape(count, LANES).astype(F32))
    return jnp.concatenate(tiles, axis=1)


def unpack_kernel(*refs):
    refs[-1][...] = tiles_to_rows(refs[:-1])


def unpack_rows_kernel(tiles_ref, down_ref, mout_ref, aout_ref):
    step = pl.program_id(0)
    rows = tiles_to_rows([tiles_ref])
    last = pl.num_programs(0) - 1

    @pl.when(step < FF_F // LANES)
    def _():
        down_ref[...] = rows

    @pl.when((step >= FF_F // LANES) & (step < last))
    def _():
        mout_ref[...] = rows

    @pl.when(step == last)
    def _():
        aout_ref[...] = rows


def unpack_rows(tiles, at):
    width = D // LANES
    base = at // width
    downs, outs = FF_F // LANES, INNER_F // LANES

    def rows(index):
        return pl.BlockSpec((LANES, D), index)

    return pl.pallas_call(
        unpack_rows_kernel,
        grid=((FF_F + OUT_ROWS) // LANES,),
        in_specs=[
            pl.BlockSpec(
                (NC // 2, width, SLICE, LANES), lambda i: (i % 2, base + i // 2, 0, 0)
            )
        ],
        out_specs=[
            rows(lambda i: (jnp.minimum(i, downs - 1), 0)),
            rows(lambda i: (jnp.clip(i - downs, 0, outs - 1), 0)),
            rows(lambda i: (0, 0)),
        ],
        out_shape=[shape_of((FF_F, D), F32), shape_of((INNER_F, D), F32), shape_of((HDIM, D), F32)],
        compiler_params=PARAMS,
        cost_estimate=cost((FF_F + OUT_ROWS) * D, 6 * (FF_F + OUT_ROWS) * D),
        name="unpack_rows",
    )(tiles)


def unpack_gate_up(tiles):
    part = FF_F // LANES
    many = NF // 2

    def spec(j):
        return pl.BlockSpec(
            (NC, part, SLICE, LANES), lambda h, q: (0, 2 * (q * many + j) + h, 0, 0)
        )

    return pl.pallas_call(
        unpack_kernel,
        grid=(2, NF // many),
        in_specs=[spec(j) for j in range(many)],
        out_specs=pl.BlockSpec(
            (SHARD, many * FF_F), lambda h, q: (0, h * (NF // many) + q)
        ),
        out_shape=shape_of((SHARD, 2 * FF), F32),
        compiler_params=PARAMS,
        cost_estimate=cost(SHARD * 2 * FF, 6 * SHARD * 2 * FF),
        name="unpack_gate_up",
    )(*[tiles] * many)


def turned(ref, tile):
    return ref[:, tile].reshape(SHARD, LANES).astype(F32).T


def unpack_in_kernel(*refs):
    step = pl.program_id(0)
    steps = NF // IN_SEQS
    wide = INNER_F // LANES
    out_ref = refs[-1]

    @pl.when(step < 2 * steps)
    def _():
        for index in range(IN_SEQS):
            for tile in range(wide):
                start = index * INNER_F + tile * LANES
                out_ref[start : start + LANES] = turned(refs[index], tile)

    @pl.when(step == 2 * steps)
    def _():
        for f in range(NF):
            tail = turned(refs[IN_SEQS + f], 0)
            out_ref[f * BC_F : (f + 1) * BC_F] = tail[:BC_F]
            first = NF * BC_F + f * DT_F
            out_ref[first : first + DT_F] = tail[BC_F : BC_F + DT_F]


def unpack_in(tiles):
    wide = INNER_F // LANES
    half = NF // IN_SEQS
    each = W1_COLS // LANES

    def spec(j):
        def index(i):
            f = IN_SEQS * (jnp.minimum(i, 2 * half - 1) % half) + j
            return (0, each * f + jnp.where(i < half, 0, wide), 0, 0)

        shape = tuple(pl.Element(size) for size in (NC, wide, SLICE, LANES))
        return pl.BlockSpec(shape, index)

    def tail_spec(f):
        return pl.BlockSpec((NC, 1, SLICE, LANES), lambda i: (0, each * f + 2 * wide, 0, 0))

    specs = [spec(j) for j in range(IN_SEQS)]
    specs += [tail_spec(f) for f in range(NF)]
    return pl.pallas_call(
        unpack_in_kernel,
        grid=(2 * half + 1,),
        in_specs=specs,
        out_specs=pl.BlockSpec((IN_SEQS * INNER_F, SHARD), lambda i: (i, 0)),
        out_shape=shape_of((2 * INNER + 2 * STATE + MHEADS, SHARD), F32),
        compiler_params=PARAMS,
        cost_estimate=cost(SHARD * 6704, 6 * SHARD * 6704),
        name="unpack_in",
    )(*[tiles] * len(specs))


def unpack_qkv_kernel(*refs):
    group = NF // KVHEADS

    def tile(f, index):
        return refs[3 * f + index][:, 0].reshape(SHARD, HDIM).astype(F32)

    parts = [tile(f, 0) for f in range(NF)]
    for index in (1, 2):
        for head in range(KVHEADS):
            parts.append(sum(tile(head * group + j, index) for j in range(group)))
    refs[-1][...] = jnp.concatenate(parts, axis=1)


def unpack_qkv(tiles):
    each, first = W1_COLS // LANES, (INNER_F + MIX) // LANES
    specs = [
        pl.BlockSpec((NC, 1, SLICE, LANES), lambda i, at=each * f + first + index: (0, at, 0, 0))
        for f in range(NF)
        for index in range(3)
    ]
    width = (QHEADS + 2 * KVHEADS) * HDIM
    return pl.pallas_call(
        unpack_qkv_kernel,
        grid=(1,),
        in_specs=specs,
        out_specs=whole(SHARD, width),
        out_shape=shape_of((SHARD, width), F32),
        compiler_params=PARAMS,
        cost_estimate=cost(SHARD * width, 6 * SHARD * width),
        name="unpack_qkv",
    )(*[tiles] * len(specs))


def norm_scale(values):
    return lax.rsqrt(jnp.mean(values * values, axis=-1, keepdims=True) + EPS)


def norm_back(values, scale, gain, grad):
    pulled = grad * gain
    inner = jnp.mean(pulled * values, axis=-1, keepdims=True)
    d_values = scale * pulled - values * (scale * scale * scale) * inner
    return d_values, jnp.sum(grad * values * scale, axis=0)


def columns_of(weight, start, width):
    part = weight[:, start : start + NF * width]
    return part.reshape(weight.shape[0], NF, width).transpose(1, 0, 2)


def shards(
    tokens,
    norm_gain,
    w_in,
    w_qkv,
    conv_weight,
    conv_bias,
    dt_bias,
    a_log,
    d_skip,
    mamba_gain,
    w_mout,
    w_aout,
    mlp_gain,
    w_gate_up,
    w_down,
    cotangent,
):
    ctx = lax.axis_index("ctx")
    fsdp = lax.axis_index("fsdp")
    parity = ctx % 2
    odd = parity.astype(jnp.int32).reshape(1)
    z_at, core = fsdp // 2, fsdp % 2
    pieces = jnp.arange(NF, dtype=jnp.int32)
    order = ((z_at + pieces % NZ) % NZ) * 2 + (core + pieces // NZ) % 2
    place = ((pieces % 2 + core) % 2) * NZ + (pieces // 2 - z_at) % NZ

    def even_first(rows):
        rows = rows.reshape(2, HALF, D)
        return jnp.where(parity == 1, rows[::-1], rows).reshape(ROWS, D)

    spot = jnp.concatenate([place[::2] % NZ, core.astype(jnp.int32).reshape(1)])

    hidden = even_first(tokens).astype(F32)
    scale_one = norm_scale(hidden)
    normed = ring_gather((hidden * scale_one * norm_gain).astype(BF), order)

    in_rows = lax.dynamic_slice(w_in, (ctx * SLICE, 0), (SLICE, w_in.shape[1]))
    qkv_rows = lax.dynamic_slice(w_qkv, (ctx * SLICE, 0), (SLICE, w_qkv.shape[1]))
    parts = [
        columns_of(in_rows, INNER, INNER_F),
        columns_of(in_rows, 2 * INNER, BC_F),
        columns_of(in_rows, 2 * INNER + 2 * STATE, DT_F),
        jnp.zeros((NF, SLICE, LANES - BC_F - DT_F), BF),
        columns_of(qkv_rows, 0, HDIM),
    ]
    for start in (QHEADS * HDIM, (QHEADS + KVHEADS) * HDIM):
        pair = qkv_rows[:, start : start + KVHEADS * HDIM].reshape(SLICE, KVHEADS, HDIM)
        parts.append(jnp.repeat(pair.transpose(1, 0, 2), NF // KVHEADS, axis=0))
    parts += [
        columns_of(in_rows, 0, INNER_F),
    ]
    swapped, w_gate_up = together(swap_fsdp(jnp.concatenate(parts, axis=2)), w_gate_up)
    gu_rows = lax.dynamic_slice(w_gate_up, (ctx * SLICE, 0), (SLICE, w_gate_up.shape[1]))
    gu_swapped = jnp.concatenate(
        [columns_of(gu_rows, 0, FF_F), columns_of(gu_rows, FF, FF_F)], axis=2
    )
    w_one = lax.all_gather(swapped, "ctx", axis=0)
    normed, gu_swapped = together(normed, swap_fsdp(gu_swapped))
    w_out = jnp.concatenate([w_mout, w_aout], axis=0)
    cot_low = even_first(cotangent)

    blocks = jnp.stack([ctx, 2 * NC - 1 - ctx])
    blocks = jnp.where(parity == 1, blocks[::-1], blocks)
    positions = (
        blocks[:, None] * HALF + jnp.arange(HALF, dtype=jnp.int32)[None, :]
    ).reshape(ROWS)
    half_dim = HDIM // 2
    freqs = ROPE_BASE ** (-jnp.arange(half_dim, dtype=F32) / half_dim)
    angles = positions.astype(F32)[:, None] * freqs[None, :]
    cosine, sine = jnp.cos(angles), jnp.sin(angles)
    mix_pack, attn_pack = project(normed, w_one, cosine, sine)
    mix_pack, cot_low, normed = together(mix_pack, cot_low, normed)
    cot_all = gather_fsdp(cot_low)
    mix_got, gate_z, attn_pack = together(
        swap_ctx(mix_pack), project_z(normed, w_one), attn_pack
    )
    attn_got = swap_ctx(attn_pack)

    x_start = fsdp * INNER_F + parity * XW
    bc_start = INNER + fsdp * BC_F
    conv_all = jnp.concatenate(
        [conv_weight, conv_bias[None], jnp.zeros((3, conv_bias.shape[0]), F32)], axis=0
    )
    taps = jnp.concatenate(
        [
            lax.dynamic_slice(conv_all, (0, x_start), (8, XW)),
            lax.dynamic_slice(conv_all, (0, bc_start), (8, BC_F)),
        ],
        axis=1,
    ).T
    head = fsdp * DT_F + parity * HEADS_L
    my_bias = lax.dynamic_slice(dt_bias, (head,), (HEADS_L,))
    my_rate = -jnp.exp(lax.dynamic_slice(a_log, (head,), (HEADS_L,)))
    heads_in = jnp.broadcast_to(
        jnp.concatenate([my_bias, my_rate, jnp.zeros((8 - 2 * HEADS_L,), F32)])[:, None],
        (8, LANES),
    )
    my_skip = jnp.repeat(lax.dynamic_slice(d_skip, (head,), (HEADS_L,)), MDIM)[:, None]
    x_act, bc_own, row_terms = front(mix_got, taps, heads_in)
    bc_own, gu_swapped = together(bc_own, gu_swapped)
    w_gu = lax.all_gather(gu_swapped, "ctx", axis=0)
    bc = jnp.concatenate(ring_pieces(bc_own), axis=0).reshape(NF, BC_F, LENGTH)
    ssd_seq, states = mamba_fwd(place, x_act, bc, row_terms, my_skip)
    ssd_seq, attn_got, cot_all = together(ssd_seq, attn_got, cot_all)
    heads_seq, lse = attn_fwd(odd, attn_got)
    ssd, heads_seq = together(swap_ctx(ssd_seq), heads_seq)
    heads = swap_ctx(heads_seq)

    my_gain = lax.dynamic_slice(mamba_gain, (fsdp * INNER_F,), (INNER_F,))[:, None]
    g, squares = gate(ssd, gate_z)
    squares, w_gu = together(butterfly(squares, "fsdp", (1, 2, 4)), w_gu)
    gated_heads, branches = branch_out(heads, g, squares, my_gain, w_out)
    branches, cot_all = together(branches, cot_all)
    mixed = hidden + scatter_fsdp(branches)

    scale_two = norm_scale(mixed)
    normed_two, d_act = together(
        gather_fsdp((mixed * scale_two * mlp_gain).astype(BF)), act_back(cot_all, w_down)
    )
    act, d_gu, d_normed_two = mlp(normed_two, d_act, w_gu)
    down_mine, down_other = down_out(spot, act, w_down)

    def side_by_side(*terms):
        return jnp.concatenate([term.reshape(NC, -1, LANES) for term in terms], axis=1)

    def total_of(got):
        return jnp.sum(got.astype(F32), axis=0).astype(BF)

    along_y = [[x * NY + y for y in range(NY)] for x in range(NC // NY)]
    along_x = [[x * NY + y for x in range(NC // NY)] for y in range(NY)]

    def scatter_ctx(joined, groups):
        joined = joined.reshape(len(groups[0]), -1, LANES)
        part = lax.psum_scatter(
            joined, "ctx", scatter_dimension=0, axis_index_groups=groups, tiled=False
        )
        return lax.optimization_barrier(part)

    def all_ctx(parts):
        joined = jnp.concatenate(parts, axis=0)
        return lax.all_gather(joined.reshape(-1, SLICE, LANES), "ctx", axis=0)

    gu_tiles = MLP_COLS // LANES
    row_tiles = OUT_ROWS // SHARD * (D // LANES)
    got_down = swap_ctx(column_grad(act, cot_all).reshape(NC, -1, LANES))
    packed_gu = column_grad(normed_two, d_gu, by_y=True)
    d_normed_two, packed_gu, down_mine, down_other, got_down = together(
        scatter_fsdp(d_normed_two), packed_gu, down_mine, down_other, got_down
    )
    sum_gu = scatter_ctx(packed_gu, along_y)
    sum_down = total_of(got_down)
    d_mixed, g_mlp_gain = norm_back(mixed, scale_two, mlp_gain, d_normed_two)
    d_mixed = d_mixed + cot_low.astype(F32)
    branch = ring_gather(d_mixed.astype(BF), order)

    dg, inner, dh = branch_back(branch, w_out, g, my_gain)
    inner = butterfly(inner, "fsdp", (1, 2, 4))
    d_mixers, dz, g_mamba_gain = gate_back(
        ssd, gate_z, g, dg, dh, squares, inner, my_gain
    )
    d_mixers, sum_gu = together(d_mixers, sum_gu)
    sum_gu = scatter_ctx(sum_gu, along_x)
    d_mixers = swap_ctx(d_mixers)
    packed_two = side_by_side(
        column_grad(gated_heads, branch, by_y=True), column_grad(normed, dz, by_y=True)
    )
    d_mixers, packed_two, sum_gu = together(d_mixers, packed_two, sum_gu)
    sum_two = scatter_ctx(packed_two, along_y)
    dx, dbc_mine, dbc_other, drow, dskip = mamba_bwd(
        place, x_act, d_mixers, bc, row_terms, states, my_skip
    )
    dbc_joined = ring_join(
        dbc_mine.reshape(NZ * BC_F, LENGTH), dbc_other.reshape(NZ * BC_F, LENGTH)
    )
    dx, d_mixers = together(dx, d_mixers)
    down_at = NF * gu_tiles
    out_at = down_at + row_tiles
    gu_part = swap_fsdp(sum_gu.reshape(NF, -1, LANES))
    dbc_joined, gu_part = together(dbc_joined, gu_part)
    dbc_own, attn_pack, sum_two = together(
        ring_scatter(dbc_joined), attn_bwd(odd, attn_got, d_mixers, lse), sum_two
    )
    sum_two = scatter_ctx(sum_two, along_x)
    attn_back = swap_ctx(attn_pack)
    mix_pack, g_taps, g_heads = front_back(
        mix_got, taps, heads_in, row_terms, drow, dx, dbc_own
    )
    mix_pack, attn_back, sum_two = together(mix_pack, attn_back, sum_two)
    all_one = all_ctx(
        [
            gu_part.reshape(-1, LANES),
            sum_down,
            sum_two[: row_tiles * SLICE],
        ]
    )
    mix_back, d_qkv = together(swap_ctx(mix_pack), attn_grads(attn_back, cosine, sine))
    d_mix = mix_grads(mix_back)
    packed_mix, dz = together(column_grad(normed, d_mix, d_qkv).reshape(NC, -1, LANES), dz)
    mine, other, gain_sum = back_project(spot, d_mix, d_qkv, dz, normed, w_one)
    g_norm_gain = gain_sum[0] / norm_gain

    def joined(mine, other):
        return ring_join(mine.reshape(NZ * ROWS, D), other.reshape(NZ * ROWS, D))

    mine, down_other = together(mine, down_other)
    got_mix, d_normed, down = together(
        swap_ctx(packed_mix), joined(mine, other), joined(down_mine, down_other)
    )
    columns = swap_fsdp(
        jnp.concatenate(
            [
                sum_two[row_tiles * SLICE :].reshape(NF, -1, LANES),
                total_of(got_mix).reshape(NF, -1, LANES),
            ],
            axis=1,
        )
    )
    def by_half(values):
        zero = jnp.zeros_like(values)
        return jnp.where(
            parity == 1, jnp.stack([zero, values], axis=-2), jnp.stack([values, zero], axis=-2)
        )

    g_conv = g_taps.T[: CONV_K + 1]
    g_d_skip = jnp.sum(dskip.reshape(HEADS_L, MDIM), axis=1)
    per_head = jnp.stack(
        [g_heads[:HEADS_L, 0], g_heads[HEADS_L : 2 * HEADS_L, 0], g_d_skip]
    )
    own = jnp.concatenate(
        [
            by_half(g_conv[:, :XW]).reshape(-1),
            g_conv[:, XW:].reshape(-1),
            g_mamba_gain[:, 0],
            by_half(per_head).reshape(-1),
        ]
    )
    own_size = own.shape[0]
    own_pad = -(-own_size // LANES) * LANES
    own = jnp.concatenate([own, jnp.zeros((own_pad - own_size,), F32), g_mlp_gain, g_norm_gain])

    own, columns, all_one = together(own.reshape(-1, LANES), columns, all_one)
    all_two = all_ctx([columns.reshape(-1, LANES)])
    both = jnp.concatenate([d_normed, down], axis=1)
    own, *both = together(butterfly(own, "ctx", (1, 2, 4)), *ring_first(both))
    own = butterfly(own, "ctx", (8,)).reshape(-1)
    mine = (jnp.arange(NF) == fsdp)[:, None]
    placed = jnp.where(mine, own[None, :own_pad], 0.0).reshape(-1)
    total = jnp.concatenate([placed, own[own_pad:]]).reshape(-1, LANES)
    total, both = together(butterfly(total, "fsdp", (1,)), ring_last(*both))
    d_normed, down = both[:, :D], both[:, D:]
    output = even_first((mixed + down).astype(BF)).reshape(tokens.shape)

    g_gate_up = unpack_gate_up(all_one)
    g_down, g_mout, g_aout = unpack_rows(all_one, down_at)
    total = butterfly(total, "fsdp", (2,))
    total, g_gate_up, g_down, g_mout, g_aout = together(
        total, g_gate_up, g_down, g_mout, g_aout
    )
    g_qkv = unpack_qkv(all_two)
    g_in = unpack_in(all_two).T
    d_hidden, _ = norm_back(hidden, scale_one, norm_gain, d_normed)
    d_tokens = even_first((d_hidden + d_mixed).astype(BF)).reshape(tokens.shape)

    total = butterfly(total, "fsdp", (4,)).reshape(-1)
    each = total[: NF * own_pad].reshape(NF, own_pad)
    cut = [(CONV_K + 1) * INNER_F]
    cut.append(cut[0] + (CONV_K + 1) * BC_F)
    cut.append(cut[1] + INNER_F)
    conv_x = each[:, : cut[0]].reshape(NF, CONV_K + 1, INNER_F).transpose(1, 0, 2)
    conv_bc = each[:, cut[0] : cut[1]].reshape(NF, CONV_K + 1, BC_F).transpose(1, 0, 2)
    conv = jnp.concatenate(
        [conv_x.reshape(CONV_K + 1, INNER), conv_bc.reshape(CONV_K + 1, 2 * STATE)], axis=1
    )
    per_head = each[:, cut[2] : cut[2] + 3 * DT_F].reshape(NF, 3, DT_F).transpose(1, 0, 2)
    per_head = per_head.reshape(3, MHEADS)
    gains = total[NF * own_pad :].reshape(2, D)
    return (
        output,
        d_tokens,
        gains[1],
        g_in,
        g_qkv,
        conv[:CONV_K],
        conv[CONV_K],
        per_head[0],
        per_head[1],
        per_head[2],
        each[:, cut[1] : cut[2]].reshape(INNER),
        g_mout,
        g_aout,
        gains[0],
        g_gate_up,
        g_down,
    )


def solution(mesh):
    tokens_at = P("fsdp", "ctx", None, None)
    rows_at = P("fsdp", None)
    placed = (
        tokens_at,
        P(),
        rows_at,
        rows_at,
        P(),
        P(),
        P(),
        P(),
        P(),
        P(),
        rows_at,
        rows_at,
        P(),
        rows_at,
        rows_at,
        tokens_at,
    )
    return jax.shard_map(
        shards,
        mesh=mesh,
        in_specs=placed,
        out_specs=(
            tokens_at,
            tokens_at,
            P(),
            rows_at,
            rows_at,
            P(),
            P(),
            P(),
            P(),
            P(),
            P(),
            rows_at,
            rows_at,
            P(),
            rows_at,
            rows_at,
        ),
        check_vma=False,
    )
```

```python
import functools

import jax
import jax.numpy as jnp
from jax import lax
from jax.experimental import pallas as pl
from jax.experimental.pallas import tpu as pltpu
from jax.sharding import PartitionSpec as P

D = 2048
MHEADS = 48
MDIM = 64
STATE = 256
CONV_K = 4
QHEADS = 8
KVHEADS = 2
HDIM = 128
FF = 4096
HALF = 64
INNER = 3072
LENGTH = 2048
SEQS = 8
NC = 16
NF = 8
NZ = 4
NY = 4
LANES = 128
ROWS = 2 * HALF
GROUP = SEQS * ROWS
INNER_F = INNER // NF
HEADS_L = 3
XW = HEADS_L * MDIM
BC_F = 2 * STATE // NF
DT_F = MHEADS // NF
FF_F = FF // NF
CHUNK = 256
CHUNKS = LENGTH // CHUNK
PAIRS = LENGTH // LANES
QROWS = LENGTH // 2
QBLOCK = 128
SHARD = D // NF
SLICE = SHARD // NC
MIX = INNER_F + LANES
QKV = 3 * HDIM
WM_COLS = MIX + QKV
W1_COLS = WM_COLS + INNER_F
MLP_COLS = 2 * FF_F
OUT_ROWS = INNER_F + HDIM
K_AT, V_AT, Q_AT, ATTN = 0, 128, 256, 320
XB = XW + BC_F
B_AT, T_AT, PACK = XW, XB, XB + 16
BOTH = XW + HALF
GATE_SEQS = 4
IN_SEQS = 4
PART = 16
EPS = 1e-06
ROPE_BASE = 100000000000.0
MASKED = -1e30
SCALE = HDIM ** (-0.5)
BF = jnp.bfloat16
F32 = jnp.float32
PARAMS = pltpu.CompilerParams(vmem_limit_bytes=56 * 1024 * 1024)
SMEM = pl.BlockSpec(memory_space=pltpu.SMEM)


def dot(left, right, left_dim, right_dim):
    return lax.dot_general(
        left, right, (((left_dim,), (right_dim,)), ((), ())), preferred_element_type=F32
    )


def whole(*shape):
    return pl.BlockSpec(shape, lambda *i: (0,) * len(shape))


def cost(flops, moved, transcendentals=0):
    return pl.CostEstimate(
        flops=int(flops), bytes_accessed=int(moved), transcendentals=int(transcendentals)
    )


def shape_of(shape, dtype):
    return jax.ShapeDtypeStruct(shape, dtype)


OTHER_CORE = [(i, i ^ 1) for i in range(NF)]
TO_NEXT = [(i, (i + 2) % NF) for i in range(NF)]
TO_PREV = [(i, (i - 2) % NF) for i in range(NF)]


def send(value, route):
    return lax.ppermute(value, "fsdp", route)


def gather_fsdp(value):
    return lax.all_gather(value, "fsdp", axis=0, tiled=True)


def scatter_fsdp(parts):
    return lax.psum_scatter(parts, "fsdp", scatter_dimension=0, tiled=True).astype(F32)


def ring_pieces(value):
    half = value.shape[0] // 2
    after = send(value, TO_PREV)
    before = send(value, TO_NEXT)
    near = send(value, OTHER_CORE)
    far = jnp.concatenate(
        [send(after[:half], TO_PREV), send(before[half:], TO_NEXT)], axis=0
    )
    near_after = send(after, OTHER_CORE)
    near_before = send(before, OTHER_CORE)
    near_far = send(far, OTHER_CORE)
    return [value, after, far, before, near, near_after, near_far, near_before]


def ring_gather(value, order):
    whole_value = jnp.zeros((NF * value.shape[0],) + value.shape[1:], value.dtype)
    for index, piece in enumerate(ring_pieces(value)):
        whole_value = lax.dynamic_update_slice(
            whole_value, piece, (order[index] * value.shape[0], 0)
        )
    return whole_value


def plus(*terms):
    return sum(term.astype(F32) for term in terms)


def ring_join(mine, other):
    return plus(mine, send(other, OTHER_CORE)).astype(BF)


def ring_first(joined):
    size = joined.shape[0] // NZ
    half = size // 2
    own, after, far, before = [joined[i * size : (i + 1) * size] for i in range(NZ)]
    sent = (
        send(far[:half], TO_NEXT),
        send(far[half:], TO_PREV),
        send(after[half:], TO_NEXT),
        send(before[:half], TO_PREV),
    )
    return own, after[:half], before[half:], *sent


def ring_last(own, after, before, far_next, far_prev, after_two, before_one):
    after_one = send(plus(after, far_next).astype(BF), TO_NEXT)
    before_two = send(plus(before, far_prev).astype(BF), TO_PREV)
    return plus(
        own,
        jnp.concatenate([after_one, after_two], axis=0),
        jnp.concatenate([before_one, before_two], axis=0),
    )


def ring_scatter(joined):
    return ring_last(*ring_first(joined))


def together(*values):
    return lax.optimization_barrier(values)


def swap_ctx(value):
    return lax.all_to_all(value, "ctx", 0, 0, tiled=True)


def swap_fsdp(value):
    return lax.all_to_all(value, "fsdp", 0, 0, tiled=True)


def exchange(value, axis, bit):
    size = lax.axis_size(axis)
    return value + lax.ppermute(value, axis, [(i, i ^ bit) for i in range(size)])


def butterfly(value, axis, bits):
    for bit in bits:
        value = exchange(value, axis, bit)
    return value


def rotate(values, cosine, sine):
    half = values.shape[-1] // 2
    first = values[:, :half]
    second = values[:, half:]
    return jnp.concatenate(
        [first * cosine - second * sine, second * cosine + first * sine], axis=1
    )


def proj_kernel(n_ref, w_ref, cos_ref, sin_ref, mix_ref, attn_ref):
    acc = jnp.zeros((2 * ROWS, WM_COLS), F32)
    for f in range(NF):
        acc = acc + dot(
            n_ref[:, f * SHARD : (f + 1) * SHARD],
            w_ref[:, f, :, :WM_COLS].reshape(SHARD, WM_COLS),
            1,
            0,
        )
    for j in range(2):
        rows = acc[j * ROWS : (j + 1) * ROWS]
        x_rows = rows[:, :INNER_F].T.astype(BF)
        tail = rows[:, INNER_F:MIX].T
        query = rotate(rows[:, MIX : MIX + HDIM], cos_ref[...], sin_ref[...]).astype(BF)
        key = rotate(
            rows[:, MIX + HDIM : MIX + 2 * HDIM], cos_ref[...], sin_ref[...]
        ).astype(BF)
        value = rows[:, MIX + 2 * HDIM :].astype(BF)
        for p in range(2):
            to = 2 * j + p
            attn_ref[to, K_AT:V_AT] = key
            attn_ref[to, V_AT:Q_AT] = value
            attn_ref[to, Q_AT:] = query[p * HALF : (p + 1) * HALF]
            mix_ref[to, :B_AT] = x_rows[p * XW : (p + 1) * XW]
            mix_ref[to, B_AT:T_AT] = tail[:BC_F].astype(BF)
            steps = tail[BC_F + p * HEADS_L : BC_F + (p + 1) * HEADS_L]
            high = steps.astype(BF).astype(F32)
            mix_ref[to, T_AT:] = jnp.concatenate(
                [high, steps - high, jnp.zeros((16 - 2 * HEADS_L, ROWS), F32)], axis=0
            ).astype(BF)


def packets(rows):
    return pl.BlockSpec((4, rows, LANES), lambda i: (i, 0, 0))


def token_rows(width):
    return pl.BlockSpec((2 * ROWS, width), lambda i: (i, 0))


def project(normed, w_one, cosine, sine):
    return pl.pallas_call(
        proj_kernel,
        grid=(SEQS // 2,),
        in_specs=[
            token_rows(D),
            whole(NC, NF, SLICE, W1_COLS),
            whole(ROWS, HALF),
            whole(ROWS, HALF),
        ],
        out_specs=[packets(PACK), packets(ATTN)],
        out_shape=[shape_of((NC, PACK, LANES), BF), shape_of((NC, ATTN, LANES), BF)],
        compiler_params=PARAMS,
        cost_estimate=cost(2 * GROUP * D * WM_COLS, 10e6),
        name="project",
    )(normed, w_one, cosine, sine)


def proj_z_kernel(n_ref, w_ref, z_ref):
    acc = jnp.zeros((2 * ROWS, INNER_F), F32)
    for f in range(NF):
        acc = acc + dot(
            n_ref[:, f * SHARD : (f + 1) * SHARD],
            w_ref[:, f, :, WM_COLS:].reshape(SHARD, INNER_F),
            1,
            0,
        )
    for j in range(2):
        z_ref[j] = acc[j * ROWS : (j + 1) * ROWS].T


def project_z(normed, w_z):
    return pl.pallas_call(
        proj_z_kernel,
        grid=(SEQS // 2,),
        in_specs=[token_rows(D), whole(NC, NF, SLICE, W1_COLS)],
        out_specs=pl.BlockSpec((2, INNER_F, ROWS), lambda i: (i, 0, 0)),
        out_shape=shape_of((SEQS, INNER_F, ROWS), F32),
        compiler_params=PARAMS,
        cost_estimate=cost(2 * GROUP * D * INNER_F, 8e6),
        name="project_z",
    )(normed, w_z)


def attn_grads_kernel(got_ref, cos_ref, sin_ref, out_ref):
    for j in range(2):
        one = got_ref[2 * j].astype(F32)
        two = got_ref[2 * j + 1].astype(F32)
        both = one + two
        query = jnp.concatenate([one[Q_AT:], two[Q_AT:]], axis=0)
        query = rotate(query, cos_ref[...], -sin_ref[...])
        key = rotate(both[K_AT:V_AT], cos_ref[...], -sin_ref[...])
        out_ref[j * ROWS : (j + 1) * ROWS] = jnp.concatenate(
            [query, key, both[V_AT:Q_AT]], axis=1
        ).astype(BF)


def attn_grads(got, cosine, sine):
    return pl.pallas_call(
        attn_grads_kernel,
        grid=(SEQS // 2,),
        in_specs=[packets(ATTN), whole(ROWS, HALF), whole(ROWS, HALF)],
        out_specs=token_rows(QKV),
        out_shape=shape_of((GROUP, QKV), BF),
        compiler_params=PARAMS,
        cost_estimate=cost(10 * GROUP * QKV, 2e6),
        name="attn_grads",
    )(got, cosine, sine)


def mix_grads_kernel(got_ref, out_ref):
    for j in range(2):
        one = got_ref[2 * j].astype(F32)
        two = got_ref[2 * j + 1].astype(F32)
        x_rows = jnp.concatenate([one[:B_AT], two[:B_AT]], axis=0).T
        tail = jnp.concatenate(
            [
                one[B_AT:T_AT] + two[B_AT:T_AT],
                one[T_AT : T_AT + HEADS_L],
                two[T_AT : T_AT + HEADS_L],
                jnp.zeros((LANES - BC_F - DT_F, ROWS), F32),
            ],
            axis=0,
        ).T
        out_ref[j * ROWS : (j + 1) * ROWS] = jnp.concatenate([x_rows, tail], axis=1).astype(BF)


def mix_grads(got):
    return pl.pallas_call(
        mix_grads_kernel,
        grid=(SEQS // 2,),
        in_specs=[packets(PACK)],
        out_specs=token_rows(MIX),
        out_shape=shape_of((GROUP, MIX), BF),
        compiler_params=PARAMS,
        cost_estimate=cost(4 * GROUP * MIX, 2.2e6),
        name="mix_grads",
    )(got)


def back_kernel(
    spot_ref, mix_ref, dqkv_ref, dz_ref, n_ref, w_ref, mine_ref, other_ref, gain_ref
):
    @pl.when(pl.program_id(0) == 0)
    def _():
        gain_ref[...] = jnp.zeros_like(gain_ref)

    first = spot_ref[NZ] == 0
    grad = jnp.concatenate([mix_ref[...], dqkv_ref[...], dz_ref[...]], axis=1)
    for f in range(NF):
        part = slice(f * SHARD, (f + 1) * SHARD)
        dn = dot(grad, w_ref[:, f].reshape(SHARD, W1_COLS), 1, 1)
        gain_ref[:, part] += jnp.sum(dn * n_ref[:, part].astype(F32), axis=0, keepdims=True)
        dn = dn.astype(BF)
        mine_ref[0, :, part] = jnp.where(first, dn[:ROWS], dn[ROWS:])
        other_ref[0, :, part] = jnp.where(first, dn[ROWS:], dn[:ROWS])


def back_project(spot, mix, dqkv, dz, normed, w_one):
    def rows(width):
        return pl.BlockSpec((2 * ROWS, width), lambda i, spot: (i, 0))

    specs, shapes = ring_specs(D)
    return pl.pallas_call(
        back_kernel,
        grid_spec=pltpu.PrefetchScalarGridSpec(
            num_scalar_prefetch=1,
            grid=(SEQS // 2,),
            in_specs=[
                rows(MIX),
                rows(QKV),
                rows(INNER_F),
                rows(D),
                pl.BlockSpec((NC, NF, SLICE, W1_COLS), lambda i, spot: (0, 0, 0, 0)),
            ],
            out_specs=specs + [pl.BlockSpec((1, D), lambda i, spot: (0, 0))],
        ),
        out_shape=shapes + [shape_of((1, D), F32)],
        compiler_params=PARAMS,
        cost_estimate=cost(2 * GROUP * D * W1_COLS, 18e6),
        name="back_project",
    )(spot, mix, dqkv, dz, normed, w_one)


def column_grad_kernel(by_y, left_ref, *refs):
    out_ref = refs[-1]
    first = 0
    for right_ref in refs[:-1]:
        term = dot(left_ref[...], right_ref[...], 0, 0).astype(BF)
        for block in range(out_ref.shape[1]):
            for tile in range(right_ref.shape[1] // LANES):
                part = term[
                    block * SHARD : (block + 1) * SHARD, tile * LANES : (tile + 1) * LANES
                ]
                if by_y:
                    part = part.reshape(NC // NY, NY, SLICE, LANES)
                    for y in range(NY):
                        rows = slice(y * NC // NY, (y + 1) * NC // NY)
                        out_ref[rows, block, first + tile] = part[:, y]
                else:
                    out_ref[:, block, first + tile] = part.reshape(NC, SLICE, LANES)
        first += right_ref.shape[1] // LANES


def column_grad(left, *rights, by_y=False):
    count, width = left.shape[1] // SHARD, sum(right.shape[1] for right in rights)
    tiles = width // LANES
    many = 2
    return pl.pallas_call(
        functools.partial(column_grad_kernel, by_y),
        grid=(count // many,),
        in_specs=[pl.BlockSpec((GROUP, many * SHARD), lambda i: (0, i))]
        + [whole(GROUP, right.shape[1]) for right in rights],
        out_specs=pl.BlockSpec((NC, many, tiles, SLICE, LANES), lambda i: (0, i, 0, 0, 0)),
        out_shape=shape_of((NC, count, tiles, SLICE, LANES), BF),
        compiler_params=PARAMS,
        cost_estimate=cost(
            2 * GROUP * left.shape[1] * width,
            2 * GROUP * (left.shape[1] + width) + 2 * left.shape[1] * width,
        ),
        name="column_grad",
    )(left, *rights)


def channels(count):
    return pl.BlockSpec((count, INNER_F, ROWS), lambda i: (i, 0, 0))


def gate_packets(rows):
    return pl.BlockSpec((2 * GATE_SEQS, rows, LANES), lambda i: (i, 0, 0))


def gate_kernel(got_ref, z_ref, g_ref, sq_ref):
    for j in range(GATE_SEQS):
        ssd = got_ref[2 * j : 2 * j + 2, :XW].reshape(INNER_F, ROWS).astype(F32)
        z = z_ref[j]
        g = ssd * (z * jax.nn.sigmoid(z))
        g_ref[j] = g
        seq = pl.program_id(0) * GATE_SEQS + j
        sq_ref[pl.ds(seq, 1)] = jnp.sum(g * g, axis=0, keepdims=True)


def gate(got, z):
    return pl.pallas_call(
        gate_kernel,
        grid=(SEQS // GATE_SEQS,),
        in_specs=[gate_packets(XW), channels(GATE_SEQS)],
        out_specs=[channels(GATE_SEQS), whole(SEQS, ROWS)],
        out_shape=[shape_of((SEQS, INNER_F, ROWS), F32), shape_of((SEQS, ROWS), F32)],
        compiler_params=PARAMS,
        cost_estimate=cost(8 * GROUP * INNER_F, 4.2e6, GROUP * INNER_F),
        name="gate",
    )(got, z)


def branch_kernel(heads_ref, g_ref, sq_ref, gain_ref, w_ref, gh_ref, out_ref):
    step = pl.program_id(0)
    for j in range(2):
        scale = lax.rsqrt(sq_ref[pl.ds(2 * step + j, 1)] / INNER + EPS)
        gated = (g_ref[j] * scale * gain_ref[...]).T.astype(BF)
        heads = heads_ref[2 * j : 2 * j + 2].reshape(ROWS, HDIM)
        gh_ref[j * ROWS : (j + 1) * ROWS] = jnp.concatenate([gated, heads], axis=1)
    out_ref[...] = dot(gh_ref[...], w_ref[...], 1, 0).astype(BF)


def branch_out(heads, g, squares, gain, w_out):
    return pl.pallas_call(
        branch_kernel,
        grid=(SEQS // 2,),
        in_specs=[
            packets(HALF),
            channels(2),
            whole(SEQS, ROWS),
            whole(INNER_F, 1),
            whole(OUT_ROWS, D),
        ],
        out_specs=[token_rows(OUT_ROWS), token_rows(D)],
        out_shape=[shape_of((GROUP, OUT_ROWS), BF), shape_of((GROUP, D), BF)],
        compiler_params=PARAMS,
        cost_estimate=cost(2 * GROUP * OUT_ROWS * D, 10e6),
        name="branch_out",
    )(heads, g, squares, gain, w_out)


def branch_back_kernel(d_ref, w_ref, g_ref, gain_ref, dg_ref, inner_ref, dh_ref):
    step = pl.program_id(0)
    both = dot(d_ref[...], w_ref[...], 1, 1)
    for j in range(2):
        rows = both[j * ROWS : (j + 1) * ROWS]
        d_gated = rows[:, :INNER_F].T
        dg_ref[j] = d_gated
        inner_ref[pl.ds(2 * step + j, 1)] = jnp.sum(
            d_gated * gain_ref[...] * g_ref[j], axis=0, keepdims=True
        )
        heads = rows[:, INNER_F:].astype(BF)
        dh_ref[2 * j : 2 * j + 2] = heads.reshape(2, HALF, HDIM)


def branch_back(branch, w_out, g, gain):
    return pl.pallas_call(
        branch_back_kernel,
        grid=(SEQS // 2,),
        in_specs=[token_rows(D), whole(OUT_ROWS, D), channels(2), whole(INNER_F, 1)],
        out_specs=[channels(2), whole(SEQS, ROWS), packets(HALF)],
        out_shape=[
            shape_of((SEQS, INNER_F, ROWS), F32),
            shape_of((SEQS, ROWS), F32),
            shape_of((NC, HALF, HDIM), BF),
        ],
        compiler_params=PARAMS,
        cost_estimate=cost(2 * GROUP * OUT_ROWS * D, 10e6),
        name="branch_back",
    )(branch, w_out, g, gain)


def gate_back_kernel(
    got_ref, z_ref, g_ref, dg_ref, dh_ref, sq_ref, inner_ref, gain_ref,
    pack_ref, dz_ref, gain_grad_ref,
):
    index = pl.program_id(0)

    @pl.when(index == 0)
    def _():
        gain_grad_ref[...] = jnp.zeros_like(gain_grad_ref)

    pack_ref[:, XW:] = dh_ref[...]
    for j in range(GATE_SEQS):
        ssd = got_ref[2 * j : 2 * j + 2, :XW].reshape(INNER_F, ROWS).astype(F32)
        z = z_ref[j]
        g = g_ref[j]
        sig = jax.nn.sigmoid(z)
        silu = z * sig
        seq = index * GATE_SEQS + j
        scale = lax.rsqrt(sq_ref[pl.ds(seq, 1)] / INNER + EPS)
        inner = inner_ref[pl.ds(seq, 1)] / INNER
        scaled = dg_ref[j] * scale
        d_g = scaled * gain_ref[...] - g * (scale * scale * scale * inner)
        gain_grad_ref[...] += jnp.sum(scaled * g, axis=1, keepdims=True)
        pack_ref[2 * j : 2 * j + 2, :XW] = (d_g * silu).astype(BF).reshape(2, XW, LANES)
        dz_ref[j * ROWS : (j + 1) * ROWS] = (
            (d_g * ssd * (sig + silu * (1.0 - sig))).T.astype(BF)
        )


def gate_back(got, z, g, dg, dh, squares, inner, gain):
    return pl.pallas_call(
        gate_back_kernel,
        grid=(SEQS // GATE_SEQS,),
        in_specs=[
            gate_packets(XW),
            channels(GATE_SEQS),
            channels(GATE_SEQS),
            channels(GATE_SEQS),
            gate_packets(HALF),
            whole(SEQS, ROWS),
            whole(SEQS, ROWS),
            whole(INNER_F, 1),
        ],
        out_specs=[
            gate_packets(BOTH),
            pl.BlockSpec((GATE_SEQS * ROWS, INNER_F), lambda i: (i, 0)),
            whole(INNER_F, 1),
        ],
        out_shape=[
            shape_of((NC, BOTH, LANES), BF),
            shape_of((GROUP, INNER_F), BF),
            shape_of((INNER_F, 1), F32),
        ],
        compiler_params=PARAMS,
        cost_estimate=cost(20 * GROUP * INNER_F, 8e6, GROUP * INNER_F),
        name="gate_back",
    )(got, z, g, dg, dh, squares, inner, gain)


def act_back_kernel(cot_ref, down_ref, out_ref):
    out_ref[...] = dot(cot_ref[...], down_ref[...], 1, 1)


def act_back(cot, w_down):
    return pl.pallas_call(
        act_back_kernel,
        grid=(SEQS // 2,),
        in_specs=[token_rows(D), whole(FF_F, D)],
        out_specs=token_rows(FF_F),
        out_shape=shape_of((GROUP, FF_F), F32),
        compiler_params=PARAMS,
        cost_estimate=cost(2 * GROUP * D * FF_F, 9e6),
        name="act_back",
    )(cot, w_down)


def mlp_kernel(n_ref, d_act_ref, w_ref, act_ref, dgu_ref, dn_ref):
    acc = jnp.zeros((2 * ROWS, MLP_COLS), F32)
    for f in range(NF):
        acc = acc + dot(
            n_ref[:, f * SHARD : (f + 1) * SHARD], w_ref[:, f].reshape(SHARD, MLP_COLS), 1, 0
        )
    gate_part, upper = acc[:, :FF_F], acc[:, FF_F:]
    sig = jax.nn.sigmoid(gate_part)
    silu = gate_part * sig
    act_ref[...] = (silu * upper).astype(BF)
    d_act = d_act_ref[...]
    d_gu = jnp.concatenate(
        [d_act * upper * (sig + silu * (1.0 - sig)), d_act * silu], axis=1
    ).astype(BF)
    dgu_ref[...] = d_gu
    for f in range(NF):
        dn_ref[:, f * SHARD : (f + 1) * SHARD] = dot(
            d_gu, w_ref[:, f].reshape(SHARD, MLP_COLS), 1, 1
        ).astype(BF)


def mlp(normed, d_act, w_gu):
    return pl.pallas_call(
        mlp_kernel,
        grid=(SEQS // 2,),
        in_specs=[token_rows(D), token_rows(FF_F), whole(NC, NF, SLICE, MLP_COLS)],
        out_specs=[token_rows(FF_F), token_rows(MLP_COLS), token_rows(D)],
        out_shape=[
            shape_of((GROUP, FF_F), BF),
            shape_of((GROUP, MLP_COLS), BF),
            shape_of((GROUP, D), BF),
        ],
        compiler_params=PARAMS,
        cost_estimate=cost(8 * GROUP * D * FF_F, 20e6, GROUP * FF_F),
        name="mlp",
    )(normed, d_act, w_gu)


def ring_specs(width):
    def spec(*_):
        return pl.BlockSpec((1, ROWS, width), lambda i, spot: (spot[i], 0, 0))

    return [spec(), spec()], [shape_of((NZ, ROWS, width), BF)] * 2


def down_kernel(spot_ref, act_ref, down_ref, mine_ref, other_ref):
    rows = dot(act_ref[...], down_ref[...], 1, 0).astype(BF)
    first = spot_ref[NZ] == 0
    mine_ref[0] = jnp.where(first, rows[:ROWS], rows[ROWS:])
    other_ref[0] = jnp.where(first, rows[ROWS:], rows[:ROWS])


def down_out(spot, act, w_down):
    specs, shapes = ring_specs(D)
    return pl.pallas_call(
        down_kernel,
        grid_spec=pltpu.PrefetchScalarGridSpec(
            num_scalar_prefetch=1,
            grid=(SEQS // 2,),
            in_specs=[
                pl.BlockSpec((2 * ROWS, FF_F), lambda i, spot: (i, 0)),
                pl.BlockSpec((FF_F, D), lambda i, spot: (0, 0)),
            ],
            out_specs=specs,
        ),
        out_shape=shapes,
        compiler_params=PARAMS,
        cost_estimate=cost(2 * GROUP * D * FF_F, 8e6),
        name="down_out",
    )(spot, act, w_down)


def lane_of(shape):
    return lax.broadcasted_iota(jnp.int32, shape, 1)


def sources(pair, first):
    if first:
        return 2 * pair, 2 * pair + 1
    return NC - 1 - 2 * pair, NC - 2 - 2 * pair


def assemble(ref, low, high, pair, first):
    one, two = sources(pair, first)
    left = lane_of((high - low, LANES)) < HALF
    return jnp.where(left, ref[one, low:high].astype(F32), ref[two, low:high].astype(F32))


def deal(ref, low, high, pair, first, values):
    one, two = sources(pair, first)
    values = values.astype(BF)
    ref[one, low:high, :HALF] = values[:, :HALF]
    ref[two, low:high, HALF:] = values[:, HALF:]


def taps_of(padded, taps):
    current = padded[:, LANES:]
    total = current * taps[:, CONV_K - 1 : CONV_K] + taps[:, CONV_K : CONV_K + 1]
    inputs = [current]
    for back in range(1, CONV_K):
        moved = pltpu.roll(padded, back, 1)[:, LANES:]
        inputs.append(moved)
        total = total + moved * taps[:, CONV_K - 1 - back : CONV_K - back]
    return inputs[::-1], total


def softplus(values):
    return jnp.maximum(values, 0.0) + jnp.log1p(jnp.exp(-jnp.abs(values)))


def at_pair(pair):
    return pl.ds(pl.multiple_of(pair * LANES, LANES), LANES)


def load_raw(got_ref, raw_ref):
    raw_ref[:, :LANES] = jnp.zeros((XB, LANES), F32)
    half_pairs = PAIRS // 2
    for first in (True, False):

        def load(pair, unused, first=first):
            place = at_pair((pair if first else pair + half_pairs) + 1)
            raw_ref[:, place] = assemble(got_ref, 0, XB, pair, first)
            return unused

        lax.fori_loop(0, half_pairs, load, 0, unroll=True)


def front_kernel(got_ref, taps_ref, heads_ref, x_ref, bc_ref, row_ref, raw_ref):
    load_raw(got_ref, raw_ref)

    def step(part, unused):
        rows = pl.ds(pl.multiple_of(part * PART, PART), PART)
        _, total = taps_of(raw_ref[rows], taps_ref[rows])
        active = (total * jax.nn.sigmoid(total)).astype(BF)

        @pl.when(part < XW // PART)
        def _():
            x_ref[rows] = active

        @pl.when(part >= XW // PART)
        def _():
            bc_ref[pl.ds(pl.multiple_of(part * PART - XW, PART), PART)] = active

        return unused

    lax.fori_loop(0, XB // PART, step, 0)
    half_pairs = PAIRS // 2
    parts = [
        assemble(got_ref, T_AT, PACK, index % half_pairs, index < half_pairs)
        for index in range(PAIRS)
    ]
    parts = jnp.concatenate(parts, axis=1)
    raw = parts[:HEADS_L] + parts[HEADS_L : 2 * HEADS_L] + heads_ref[:HEADS_L, :1]
    steps = softplus(raw)
    pad = jnp.zeros((8 - 2 * HEADS_L, LENGTH), F32)
    sums = jnp.concatenate([steps * heads_ref[HEADS_L : 2 * HEADS_L, :1], steps, pad], axis=0)
    rows = lax.broadcasted_iota(jnp.int32, sums.shape, 0)
    lane = lane_of(sums.shape) % CHUNK
    running = sums
    back = 1
    while back < CHUNK:
        running = running + jnp.where(lane >= back, pltpu.roll(running, back, 1), 0.0)
        back *= 2
    row_ref[:8] = jnp.where(rows < HEADS_L, running, sums)
    row_ref[8:] = jnp.concatenate([raw, jnp.zeros((8 - HEADS_L, LENGTH), F32)], axis=0)


def front(got, taps, heads):
    return pl.pallas_call(
        front_kernel,
        in_specs=[whole(NC, PACK, LANES), whole(XB, 8), whole(8, LANES)],
        out_specs=[whole(XW, LENGTH), whole(BC_F, LENGTH), whole(16, LENGTH)],
        out_shape=[
            shape_of((XW, LENGTH), BF),
            shape_of((BC_F, LENGTH), BF),
            shape_of((16, LENGTH), F32),
        ],
        grid=(1,),
        scratch_shapes=[pltpu.VMEM((XB, LENGTH + LANES), F32)],
        compiler_params=PARAMS,
        cost_estimate=cost(30 * XB * LENGTH, 4e6, XB * LENGTH),
        name="front",
    )(got, taps, heads)


def front_back_kernel(
    got_ref, taps_ref, heads_ref, row_ref, drow_ref, dx_ref, dbc_ref, pack_ref,
    taps_grad_ref, heads_grad_ref, raw_ref, grad_ref,
):
    half_pairs = PAIRS // 2
    load_raw(got_ref, raw_ref)

    grads = drow_ref[...]
    lane = lane_of(grads.shape) % CHUNK
    running = grads
    back = 1
    while back < CHUNK:
        running = running + jnp.where(
            lane < CHUNK - back, pltpu.roll(running, LENGTH - back, 1), 0.0
        )
        back *= 2
    rates = running[:HEADS_L]
    rate = heads_ref[HEADS_L : 2 * HEADS_L, :1]
    d_steps = grads[HEADS_L : 2 * HEADS_L] + rates * rate
    d_dt = d_steps * jax.nn.sigmoid(row_ref[8 : 8 + HEADS_L])
    steps = row_ref[HEADS_L : 2 * HEADS_L]
    heads_grad_ref[...] = jnp.concatenate(
        [
            jnp.sum(d_dt, axis=1, keepdims=True),
            jnp.sum(rates * steps, axis=1, keepdims=True) * rate,
            jnp.zeros((8 - 2 * HEADS_L, 1), F32),
        ],
        axis=0,
    )
    d_dt = jnp.concatenate([d_dt, jnp.zeros((16 - HEADS_L, LENGTH), F32)], axis=0)
    for index in range(PAIRS):
        first = index < half_pairs
        deal(
            pack_ref, T_AT, PACK, index % half_pairs, first,
            d_dt[:, index * LANES : (index + 1) * LANES],
        )

    def step(part, unused):
        rows = pl.ds(pl.multiple_of(part * PART, PART), PART)
        taps = taps_ref[rows]
        inputs, total = taps_of(raw_ref[rows], taps)
        sig = jax.nn.sigmoid(total)

        @pl.when(part < XW // PART)
        def _():
            grad_ref[:, :LENGTH] = dx_ref[rows]

        @pl.when(part >= XW // PART)
        def _():
            grad_ref[:, :LENGTH] = dbc_ref[pl.ds(pl.multiple_of(part * PART - XW, PART), PART)]

        grad = grad_ref[:, :LENGTH] * (sig + total * sig * (1.0 - sig))
        grad_ref[:, :LENGTH] = grad
        padded = grad_ref[...]
        d_raw = grad * taps[:, CONV_K - 1 : CONV_K]
        for ahead in range(1, CONV_K):
            moved = pltpu.roll(padded, LENGTH + LANES - ahead, 1)[:, :LENGTH]
            d_raw = d_raw + moved * taps[:, CONV_K - 1 - ahead : CONV_K - ahead]
        taps_grad_ref[rows] = jnp.concatenate(
            [jnp.sum(grad * moved, axis=1, keepdims=True) for moved in inputs]
            + [jnp.sum(grad, axis=1, keepdims=True)]
            + [jnp.zeros((PART, 8 - CONV_K - 1), F32)],
            axis=1,
        )
        raw_ref[rows, :LENGTH] = d_raw
        return unused

    grad_ref[:, LENGTH:] = jnp.zeros((PART, LANES), F32)
    lax.fori_loop(0, XB // PART, step, 0)
    for first in (True, False):

        def store(pair, unused, first=first):
            place = at_pair(pair if first else pair + half_pairs)
            deal(pack_ref, 0, XB, pair, first, raw_ref[:, place])
            return unused

        lax.fori_loop(0, half_pairs, store, 0, unroll=True)


def front_back(got, taps, heads, rows, drow, dx, dbc):
    return pl.pallas_call(
        front_back_kernel,
        in_specs=[
            whole(NC, PACK, LANES),
            whole(XB, 8),
            whole(8, LANES),
            whole(16, LENGTH),
            whole(8, LENGTH),
            whole(XW, LENGTH),
            whole(BC_F, LENGTH),
        ],
        out_specs=[whole(NC, PACK, LANES), whole(XB, 8), whole(8, 1)],
        out_shape=[
            shape_of((NC, PACK, LANES), BF),
            shape_of((XB, 8), F32),
            shape_of((8, 1), F32),
        ],
        grid=(1,),
        scratch_shapes=[
            pltpu.VMEM((XB, LENGTH + LANES), F32),
            pltpu.VMEM((PART, LENGTH + LANES), F32),
        ],
        compiler_params=PARAMS,
        cost_estimate=cost(60 * XB * LENGTH, 9e6, XB * LENGTH),
        name="front_back",
    )(got, taps, heads, rows, drow, dx, dbc)


def stacked(rows, width):
    return jnp.concatenate(
        [jnp.broadcast_to(row, (MDIM, width)) for row in rows], axis=0
    )


def state_sides(place_ref, bc_ref):
    quarter = STATE // BC_F
    bt = jnp.concatenate([bc_ref[place_ref[j]] for j in range(quarter)], axis=0)
    ct = jnp.concatenate([bc_ref[place_ref[quarter + j]] for j in range(quarter)], axis=0)
    return bt, ct


def chunk_terms(row_ref):
    rows = row_ref[...]
    cols = rows.T
    cum_row = [rows[h : h + 1] for h in range(HEADS_L)]
    dt_row = [rows[HEADS_L + h : HEADS_L + h + 1] for h in range(HEADS_L)]
    cum_col = [cols[:, h : h + 1] for h in range(HEADS_L)]
    dt_col = [cols[:, HEADS_L + h : HEADS_L + h + 1] for h in range(HEADS_L)]
    last = [row[:, CHUNK - 1 :] for row in cum_row]
    return cum_row, dt_row, cum_col, dt_col, last


def later_mask():
    shape = (CHUNK, CHUNK)
    return lax.broadcasted_iota(jnp.int32, shape, 1) >= lax.broadcasted_iota(jnp.int32, shape, 0)


def mamba_fwd_kernel(
    place_ref, x_ref, bc_ref, row_ref, skip_ref, pack_ref, st_out_ref, st_ref
):
    index = pl.program_id(0)

    @pl.when(index == 0)
    def _():
        st_ref[...] = jnp.zeros_like(st_ref)

    x_low = x_ref[...]
    x = x_low.astype(F32)
    bt, ct = state_sides(place_ref, bc_ref)
    st = st_ref[...]
    st_out_ref[0] = st
    cum_row, dt_row, cum_col, dt_col, last = chunk_terms(row_ref)
    inter = dot(bt, ct, 0, 0)
    carried = dot(st.astype(BF), ct, 1, 0)
    later = later_mask()
    within = []
    for h in range(HEADS_L):
        decay = jnp.exp(jnp.where(later, cum_row[h] - cum_col[h], MASKED))
        mixing = (inter * decay * dt_col[h]).astype(BF)
        within.append(dot(x_low[h * MDIM : (h + 1) * MDIM], mixing, 1, 0))
    entering = stacked([jnp.exp(row) for row in cum_row], CHUNK)
    y = jnp.concatenate(within, axis=0) + entering * carried + skip_ref[...] * x
    weights = stacked(
        [jnp.exp(end - row) * step for end, row, step in zip(last, cum_row, dt_row)], CHUNK
    )
    leaving = stacked([jnp.exp(end) for end in last], 1)
    st_ref[...] = st * leaving + dot((x * weights).astype(BF), bt, 1, 1)
    pairs = CHUNK // LANES
    early = index < CHUNKS // 2

    @pl.when(early)
    def _():
        for j in range(pairs):
            deal(pack_ref, 0, XW, pairs * index + j, True, y[:, j * LANES : (j + 1) * LANES])

    @pl.when(jnp.logical_not(early))
    def _():
        for j in range(pairs):
            deal(
                pack_ref, 0, XW, pairs * (index - CHUNKS // 2) + j, False,
                y[:, j * LANES : (j + 1) * LANES],
            )


def mamba_fwd(place, x, bc, rows, skip):
    return pl.pallas_call(
        mamba_fwd_kernel,
        grid=(CHUNKS,),
        in_specs=[
            SMEM,
            pl.BlockSpec((XW, CHUNK), lambda i: (0, i)),
            pl.BlockSpec((NF, BC_F, CHUNK), lambda i: (0, 0, i)),
            pl.BlockSpec((8, CHUNK), lambda i: (0, i)),
            whole(XW, 1),
        ],
        out_specs=[
            whole(NC, XW, LANES),
            pl.BlockSpec((1, XW, STATE), lambda i: (i, 0, 0)),
        ],
        out_shape=[
            shape_of((NC, XW, LANES), BF),
            shape_of((CHUNKS, XW, STATE), F32),
        ],
        scratch_shapes=[pltpu.VMEM((XW, STATE), F32)],
        compiler_params=PARAMS,
        cost_estimate=cost(2 * LENGTH * CHUNK * (STATE + 3 * XW), 7e6, LENGTH * CHUNK * 3),
        name="mamba_fwd",
    )(place, x, bc, rows, skip)


def mamba_bwd_kernel(
    place_ref, x_ref, got_ref, bc_ref, row_ref, st_in_ref, skip_ref,
    dx_ref, mine_ref, other_ref, drow_ref, dskip_ref, dst_ref, dy_ref,
):
    turn = pl.program_id(0)
    index = CHUNKS - 1 - turn
    pairs = CHUNK // LANES

    @pl.when(turn == 0)
    def _():
        dst_ref[...] = jnp.zeros_like(dst_ref)
        dskip_ref[...] = jnp.zeros_like(dskip_ref)

    @pl.when(index < CHUNKS // 2)
    def _():
        for j in range(pairs):
            dy_ref[:, j * LANES : (j + 1) * LANES] = assemble(
                got_ref, 0, XW, pairs * index + j, True
            )

    @pl.when(index >= CHUNKS // 2)
    def _():
        for j in range(pairs):
            dy_ref[:, j * LANES : (j + 1) * LANES] = assemble(
                got_ref, 0, XW, pairs * (index - CHUNKS // 2) + j, False
            )

    x_low = x_ref[...]
    x = x_low.astype(F32)
    dy = dy_ref[...]
    dy_low = dy.astype(BF)
    bt, ct = state_sides(place_ref, bc_ref)
    st = st_in_ref[0]
    dst = dst_ref[...]
    st_low = st.astype(BF)
    dst_low = dst.astype(BF)
    cum_row, dt_row, cum_col, dt_col, last = chunk_terms(row_ref)
    inter = dot(bt, ct, 0, 0)
    later = later_mask()
    entering = stacked([jnp.exp(row) for row in cum_row], CHUNK)
    tail = [jnp.exp(end - row) for end, row in zip(last, cum_row)]
    kept_row = [t * step for t, step in zip(tail, dt_row)]
    weights = stacked(kept_row, CHUNK)
    leaving = stacked([jnp.exp(end) for end in last], 1)
    carried = dot(st_low, ct, 1, 0) * entering
    reach = dot(dst_low, bt, 1, 0)
    dy_in = (dy * entering).astype(BF)
    x_out = (x * weights).astype(BF)
    along = dy * carried
    pulled = x * reach
    kept = jnp.sum(st * dst, axis=1, keepdims=True) * leaving
    d_inter = jnp.zeros((CHUNK, CHUNK), F32)
    dx_parts = []
    row_cum = []
    row_dt = []
    col_cum = []
    col_dt = []
    ends = lane_of((1, CHUNK)) == CHUNK - 1
    for h in range(HEADS_L):
        part = slice(h * MDIM, (h + 1) * MDIM)
        decay = jnp.exp(jnp.where(later, cum_row[h] - cum_col[h], MASKED))
        d_mix = dot(x_low[part], dy_low[part], 0, 0)
        scaled = decay * dt_col[h]
        d_inter = d_inter + d_mix * scaled
        mixing = inter * scaled
        dx_parts.append(dot(dy_low[part], mixing.astype(BF), 1, 1))
        to_dt = jnp.sum(d_mix * (inter * decay), axis=1, keepdims=True)
        q_row = jnp.sum(pulled[part], axis=0, keepdims=True)
        w_q = q_row * kept_row[h]
        d_last = jnp.sum(w_q, axis=1, keepdims=True) + jnp.sum(
            kept[part], axis=0, keepdims=True
        )
        row_cum.append(
            jnp.sum(d_mix * mixing, axis=0, keepdims=True)
            + jnp.sum(along[part], axis=0, keepdims=True)
            - w_q
            + jnp.where(ends, d_last, 0.0)
        )
        row_dt.append(q_row * tail[h])
        col_cum.append(-to_dt * dt_col[h])
        col_dt.append(to_dt)
    dx_ref[...] = jnp.concatenate(dx_parts, axis=0) + weights * reach + skip_ref[...] * dy
    d_low = d_inter.astype(BF)
    dbt = (dot(ct, d_low, 1, 1) + dot(dst_low, x_out, 0, 0)).astype(BF)
    dct = (dot(bt, d_low, 1, 0) + dot(st_low, dy_in, 0, 0)).astype(BF)
    quarter = STATE // BC_F
    parts = [
        grad[j * BC_F : (j + 1) * BC_F] for grad in (dbt, dct) for j in range(quarter)
    ]
    first = place_ref[0] < NZ
    for z in range(NZ):
        one, two = parts[2 * z], parts[2 * z + 1]
        distance = place_ref[2 * z] % NZ
        mine_ref[distance] = jnp.where(first, one, two)
        other_ref[distance] = jnp.where(first, two, one)
    dst_ref[...] = dst * leaving + dot(dy_in, ct, 1, 1)
    dskip_ref[...] += jnp.sum(dy * x, axis=1, keepdims=True)
    pad = jnp.zeros((CHUNK, 8 - 2 * HEADS_L), F32)
    columns = jnp.concatenate(col_cum + col_dt + [pad], axis=1).T
    drow_ref[...] = columns + jnp.concatenate(
        row_cum + row_dt + [jnp.zeros((8 - 2 * HEADS_L, CHUNK), F32)], axis=0
    )


def mamba_bwd(place, x, got, bc, rows, states, skip):
    end = CHUNKS - 1
    return pl.pallas_call(
        mamba_bwd_kernel,
        grid=(CHUNKS,),
        in_specs=[
            SMEM,
            pl.BlockSpec((XW, CHUNK), lambda i: (0, end - i)),
            whole(NC, BOTH, LANES),
            pl.BlockSpec((NF, BC_F, CHUNK), lambda i: (0, 0, end - i)),
            pl.BlockSpec((8, CHUNK), lambda i: (0, end - i)),
            pl.BlockSpec((1, XW, STATE), lambda i: (end - i, 0, 0)),
            whole(XW, 1),
        ],
        out_specs=[
            pl.BlockSpec((XW, CHUNK), lambda i: (0, end - i)),
            pl.BlockSpec((NZ, BC_F, CHUNK), lambda i: (0, 0, end - i)),
            pl.BlockSpec((NZ, BC_F, CHUNK), lambda i: (0, 0, end - i)),
            pl.BlockSpec((8, CHUNK), lambda i: (0, end - i)),
            whole(XW, 1),
        ],
        out_shape=[
            shape_of((XW, LENGTH), F32),
            shape_of((NZ, BC_F, LENGTH), BF),
            shape_of((NZ, BC_F, LENGTH), BF),
            shape_of((8, LENGTH), F32),
            shape_of((XW, 1), F32),
        ],
        scratch_shapes=[pltpu.VMEM((XW, STATE), F32), pltpu.VMEM((XW, CHUNK), F32)],
        compiler_params=PARAMS,
        cost_estimate=cost(
            2 * LENGTH * CHUNK * (3 * STATE + 7 * XW), 12e6, LENGTH * CHUNK * 3
        ),
        name="mamba_bwd",
    )(place, x, got, bc, rows, states, skip)


def position_of(source, odd, inside):
    block = jnp.where(source % 2 == odd, source, 2 * NC - 1 - source)
    return block * HALF + inside


def visible_mask(step, odd):
    key = lax.broadcasted_iota(jnp.int32, (1, LENGTH), 1)
    key_pos = position_of(key // ROWS, (key // HALF) % 2, key % HALF)
    query = lax.broadcasted_iota(jnp.int32, (QBLOCK, 1), 0)
    source = 2 * step + query // HALF
    query_pos = position_of(source, odd, query % HALF)
    return key_pos <= query_pos


def attn_fwd_kernel(odd_ref, q_ref, k_ref, v_ref, o_ref, lse_ref):
    q = q_ref[...].reshape(QBLOCK, HDIM)
    k = k_ref[...].reshape(LENGTH, HDIM)
    v = v_ref[...].reshape(LENGTH, HDIM)
    scores = dot(q, k, 1, 1) * SCALE
    scores = jnp.where(visible_mask(pl.program_id(0), odd_ref[0]), scores, MASKED)
    top = jnp.max(scores, axis=1, keepdims=True)
    grown = jnp.exp(scores - top)
    total = jnp.sum(grown, axis=1, keepdims=True)
    lse_ref[...] = top + jnp.log(total)
    probs = (grown * (1.0 / total)).astype(BF)
    o_ref[...] = dot(probs, v, 1, 0).astype(BF).reshape(2, HALF, HDIM)


def packed_part(at, rows, moving=False):
    block = at // rows
    if moving:
        return pl.BlockSpec((2, rows, HDIM), lambda i: (i, block, 0))
    return pl.BlockSpec((NC, rows, HDIM), lambda i: (0, block, 0))


def attn_fwd(odd, got):
    return pl.pallas_call(
        attn_fwd_kernel,
        grid=(QROWS // QBLOCK,),
        in_specs=[
            SMEM,
            packed_part(Q_AT, HALF, True),
            packed_part(K_AT, ROWS),
            packed_part(V_AT, ROWS),
        ],
        out_specs=[
            pl.BlockSpec((2, HALF, HDIM), lambda i: (i, 0, 0)),
            pl.BlockSpec((QBLOCK, 1), lambda i: (i, 0)),
        ],
        out_shape=[shape_of((NC, HALF, HDIM), BF), shape_of((QROWS, 1), F32)],
        compiler_params=PARAMS,
        cost_estimate=cost(4 * QROWS * LENGTH * HDIM, 3e6, QROWS * LENGTH),
        name="attn_fwd",
    )(odd, got, got, got)


def attn_bwd_kernel(
    odd_ref, q_ref, k_ref, v_ref, do_ref, lse_ref, pack_ref, dk_sum, dv_sum
):
    step = pl.program_id(0)

    @pl.when(step == 0)
    def _():
        dk_sum[...] = jnp.zeros_like(dk_sum)
        dv_sum[...] = jnp.zeros_like(dv_sum)

    q = q_ref[...].reshape(QBLOCK, HDIM)
    k = k_ref[...].reshape(LENGTH, HDIM)
    v = v_ref[...].reshape(LENGTH, HDIM)
    do = do_ref[...].reshape(QBLOCK, HDIM)
    scores = dot(q, k, 1, 1) * SCALE - lse_ref[...]
    probs = jnp.exp(jnp.where(visible_mask(step, odd_ref[0]), scores, MASKED))
    d_probs = dot(do, v, 1, 1)
    dv_sum[...] += dot(probs.astype(BF), do, 0, 0)
    inner = jnp.sum(probs * d_probs, axis=1, keepdims=True)
    d_scores = (probs * (d_probs - inner)).astype(BF)
    pack_ref[pl.ds(2 * step, 2), Q_AT:] = (
        (dot(d_scores, k, 1, 0) * SCALE).astype(BF).reshape(2, HALF, HDIM)
    )
    dk_sum[...] += dot(d_scores, q, 0, 0)

    @pl.when(step == pl.num_programs(0) - 1)
    def _():
        pack_ref[:, K_AT:V_AT] = (dk_sum[...] * SCALE).astype(BF).reshape(NC, ROWS, HDIM)
        pack_ref[:, V_AT:Q_AT] = dv_sum[...].astype(BF).reshape(NC, ROWS, HDIM)


def attn_bwd(odd, got, grads, lse):
    return pl.pallas_call(
        attn_bwd_kernel,
        grid=(QROWS // QBLOCK,),
        in_specs=[
            SMEM,
            packed_part(Q_AT, HALF, True),
            packed_part(K_AT, ROWS),
            packed_part(V_AT, ROWS),
            packed_part(XW, HALF, True),
            pl.BlockSpec((QBLOCK, 1), lambda i: (i, 0)),
        ],
        out_specs=whole(NC, ATTN, LANES),
        out_shape=shape_of((NC, ATTN, LANES), BF),
        scratch_shapes=[pltpu.VMEM((LENGTH, HDIM), F32), pltpu.VMEM((LENGTH, HDIM), F32)],
        compiler_params=PARAMS,
        cost_estimate=cost(10 * QROWS * LENGTH * HDIM, 4e6, QROWS * LENGTH),
        name="attn_bwd",
    )(odd, got, got, got, grads, lse)


def tiles_to_rows(refs):
    tiles = []
    for ref in refs:
        count = ref.shape[0] * SLICE
        for tile in range(ref.shape[1]):
            tiles.append(ref[:, tile].reshape(count, LANES).astype(F32))
    return jnp.concatenate(tiles, axis=1)


def unpack_kernel(*refs):
    refs[-1][...] = tiles_to_rows(refs[:-1])


def unpack_down(tiles, at):
    width = D // LANES
    base = at // width
    return pl.pallas_call(
        unpack_kernel,
        grid=(FF_F // SHARD,),
        in_specs=[pl.BlockSpec((NC, width, SLICE, LANES), lambda i: (0, base + i, 0, 0))],
        out_specs=pl.BlockSpec((SHARD, D), lambda i: (i, 0)),
        out_shape=shape_of((FF_F, D), F32),
        compiler_params=PARAMS,
        cost_estimate=cost(FF_F * D, 6 * FF_F * D),
        name="unpack_down",
    )(tiles)


def unpack_out_kernel(tiles_ref, mout_ref, aout_ref):
    step = pl.program_id(0)
    last = pl.num_programs(0) - 1
    rows = tiles_to_rows([tiles_ref])

    @pl.when(step < last)
    def _():
        mout_ref[...] = rows

    @pl.when(step == last)
    def _():
        aout_ref[...] = rows


def unpack_out(tiles, at):
    width = D // LANES
    base = at // width
    outs = INNER_F // LANES
    return pl.pallas_call(
        unpack_out_kernel,
        grid=(OUT_ROWS // LANES,),
        in_specs=[
            pl.BlockSpec(
                (NC // 2, width, SLICE, LANES), lambda i: (i % 2, base + i // 2, 0, 0)
            )
        ],
        out_specs=[
            pl.BlockSpec((LANES, D), lambda i: (jnp.minimum(i, outs - 1), 0)),
            pl.BlockSpec((LANES, D), lambda i: (0, 0)),
        ],
        out_shape=[shape_of((INNER_F, D), F32), shape_of((HDIM, D), F32)],
        compiler_params=PARAMS,
        cost_estimate=cost(OUT_ROWS * D, 6 * OUT_ROWS * D),
        name="unpack_out",
    )(tiles)


def unpack_gate_up(tiles):
    part = FF_F // LANES
    many = NF // 2

    def spec(j):
        return pl.BlockSpec(
            (NC, part, SLICE, LANES), lambda h, q: (0, 2 * (q * many + j) + h, 0, 0)
        )

    return pl.pallas_call(
        unpack_kernel,
        grid=(2, NF // many),
        in_specs=[spec(j) for j in range(many)],
        out_specs=pl.BlockSpec(
            (SHARD, many * FF_F), lambda h, q: (0, h * (NF // many) + q)
        ),
        out_shape=shape_of((SHARD, 2 * FF), F32),
        compiler_params=PARAMS,
        cost_estimate=cost(SHARD * 2 * FF, 6 * SHARD * 2 * FF),
        name="unpack_gate_up",
    )(*[tiles] * many)


def turned(ref, tile):
    return ref[:, tile].reshape(SHARD, LANES).astype(F32).T


def unpack_in_kernel(*refs):
    step = pl.program_id(0)
    steps = NF // IN_SEQS
    wide = INNER_F // LANES
    out_ref = refs[-1]

    @pl.when(step < 2 * steps)
    def _():
        for index in range(IN_SEQS):
            for tile in range(wide):
                start = index * INNER_F + tile * LANES
                out_ref[start : start + LANES] = turned(refs[index], tile)

    @pl.when(step == 2 * steps)
    def _():
        for f in range(NF):
            tail = turned(refs[IN_SEQS + f], 0)
            out_ref[f * BC_F : (f + 1) * BC_F] = tail[:BC_F]
            first = NF * BC_F + f * DT_F
            out_ref[first : first + DT_F] = tail[BC_F : BC_F + DT_F]


def unpack_in(tiles):
    wide = INNER_F // LANES
    half = NF // IN_SEQS
    each = W1_COLS // LANES

    def spec(j):
        def index(i):
            f = IN_SEQS * (jnp.minimum(i, 2 * half - 1) % half) + j
            return (0, each * f + jnp.where(i < half, 0, wide), 0, 0)

        shape = tuple(pl.Element(size) for size in (NC, wide, SLICE, LANES))
        return pl.BlockSpec(shape, index)

    def tail_spec(f):
        return pl.BlockSpec((NC, 1, SLICE, LANES), lambda i: (0, each * f + 2 * wide, 0, 0))

    specs = [spec(j) for j in range(IN_SEQS)]
    specs += [tail_spec(f) for f in range(NF)]
    return pl.pallas_call(
        unpack_in_kernel,
        grid=(2 * half + 1,),
        in_specs=specs,
        out_specs=pl.BlockSpec((IN_SEQS * INNER_F, SHARD), lambda i: (i, 0)),
        out_shape=shape_of((2 * INNER + 2 * STATE + MHEADS, SHARD), F32),
        compiler_params=PARAMS,
        cost_estimate=cost(SHARD * 6704, 6 * SHARD * 6704),
        name="unpack_in",
    )(*[tiles] * len(specs))


def unpack_qkv_kernel(*refs):
    group = NF // KVHEADS

    def tile(f, index):
        return refs[3 * f + index][:, 0].reshape(SHARD, HDIM).astype(F32)

    parts = [tile(f, 0) for f in range(NF)]
    for index in (1, 2):
        for head in range(KVHEADS):
            parts.append(sum(tile(head * group + j, index) for j in range(group)))
    refs[-1][...] = jnp.concatenate(parts, axis=1)


def unpack_qkv(tiles):
    each, first = W1_COLS // LANES, (INNER_F + MIX) // LANES
    specs = [
        pl.BlockSpec((NC, 1, SLICE, LANES), lambda i, at=each * f + first + index: (0, at, 0, 0))
        for f in range(NF)
        for index in range(3)
    ]
    width = (QHEADS + 2 * KVHEADS) * HDIM
    return pl.pallas_call(
        unpack_qkv_kernel,
        grid=(1,),
        in_specs=specs,
        out_specs=whole(SHARD, width),
        out_shape=shape_of((SHARD, width), F32),
        compiler_params=PARAMS,
        cost_estimate=cost(SHARD * width, 6 * SHARD * width),
        name="unpack_qkv",
    )(*[tiles] * len(specs))


def norm_scale(values):
    return lax.rsqrt(jnp.mean(values * values, axis=-1, keepdims=True) + EPS)


def norm_back(values, scale, gain, grad):
    pulled = grad * gain
    inner = jnp.mean(pulled * values, axis=-1, keepdims=True)
    d_values = scale * pulled - values * (scale * scale * scale) * inner
    return d_values, jnp.sum(grad * values * scale, axis=0)


def columns_of(weight, start, width):
    part = weight[:, start : start + NF * width]
    return part.reshape(weight.shape[0], NF, width).transpose(1, 0, 2)


def shards(
    tokens,
    norm_gain,
    w_in,
    w_qkv,
    conv_weight,
    conv_bias,
    dt_bias,
    a_log,
    d_skip,
    mamba_gain,
    w_mout,
    w_aout,
    mlp_gain,
    w_gate_up,
    w_down,
    cotangent,
):
    ctx = lax.axis_index("ctx")
    fsdp = lax.axis_index("fsdp")
    parity = ctx % 2
    odd = parity.astype(jnp.int32).reshape(1)
    z_at, core = fsdp // 2, fsdp % 2
    pieces = jnp.arange(NF, dtype=jnp.int32)
    order = ((z_at + pieces % NZ) % NZ) * 2 + (core + pieces // NZ) % 2
    place = ((pieces % 2 + core) % 2) * NZ + (pieces // 2 - z_at) % NZ

    def even_first(rows):
        rows = rows.reshape(2, HALF, D)
        return jnp.where(parity == 1, rows[::-1], rows).reshape(ROWS, D)

    spot = jnp.concatenate([place[::2] % NZ, core.astype(jnp.int32).reshape(1)])

    hidden = even_first(tokens).astype(F32)
    scale_one = norm_scale(hidden)
    normed = ring_gather((hidden * scale_one * norm_gain).astype(BF), order)

    in_rows = lax.dynamic_slice(w_in, (ctx * SLICE, 0), (SLICE, w_in.shape[1]))
    qkv_rows = lax.dynamic_slice(w_qkv, (ctx * SLICE, 0), (SLICE, w_qkv.shape[1]))
    parts = [
        columns_of(in_rows, INNER, INNER_F),
        columns_of(in_rows, 2 * INNER, BC_F),
        columns_of(in_rows, 2 * INNER + 2 * STATE, DT_F),
        jnp.zeros((NF, SLICE, LANES - BC_F - DT_F), BF),
        columns_of(qkv_rows, 0, HDIM),
    ]
    for start in (QHEADS * HDIM, (QHEADS + KVHEADS) * HDIM):
        pair = qkv_rows[:, start : start + KVHEADS * HDIM].reshape(SLICE, KVHEADS, HDIM)
        parts.append(jnp.repeat(pair.transpose(1, 0, 2), NF // KVHEADS, axis=0))
    parts += [
        columns_of(in_rows, 0, INNER_F),
    ]
    swapped, w_gate_up = together(swap_fsdp(jnp.concatenate(parts, axis=2)), w_gate_up)
    gu_rows = lax.dynamic_slice(w_gate_up, (ctx * SLICE, 0), (SLICE, w_gate_up.shape[1]))
    gu_swapped = jnp.concatenate(
        [columns_of(gu_rows, 0, FF_F), columns_of(gu_rows, FF, FF_F)], axis=2
    )
    w_one = lax.all_gather(swapped, "ctx", axis=0)
    normed, gu_swapped = together(normed, swap_fsdp(gu_swapped))
    w_out = jnp.concatenate([w_mout, w_aout], axis=0)
    cot_low = even_first(cotangent)

    blocks = jnp.stack([ctx, 2 * NC - 1 - ctx])
    blocks = jnp.where(parity == 1, blocks[::-1], blocks)
    positions = (
        blocks[:, None] * HALF + jnp.arange(HALF, dtype=jnp.int32)[None, :]
    ).reshape(ROWS)
    half_dim = HDIM // 2
    freqs = ROPE_BASE ** (-jnp.arange(half_dim, dtype=F32) / half_dim)
    angles = positions.astype(F32)[:, None] * freqs[None, :]
    cosine, sine = jnp.cos(angles), jnp.sin(angles)
    mix_pack, attn_pack = project(normed, w_one, cosine, sine)
    mix_pack, cot_low, normed = together(mix_pack, cot_low, normed)
    cot_all = gather_fsdp(cot_low)
    mix_got, gate_z, attn_pack = together(
        swap_ctx(mix_pack), project_z(normed, w_one), attn_pack
    )
    attn_got = swap_ctx(attn_pack)

    x_start = fsdp * INNER_F + parity * XW
    bc_start = INNER + fsdp * BC_F
    conv_all = jnp.concatenate(
        [conv_weight, conv_bias[None], jnp.zeros((3, conv_bias.shape[0]), F32)], axis=0
    )
    taps = jnp.concatenate(
        [
            lax.dynamic_slice(conv_all, (0, x_start), (8, XW)),
            lax.dynamic_slice(conv_all, (0, bc_start), (8, BC_F)),
        ],
        axis=1,
    ).T
    head = fsdp * DT_F + parity * HEADS_L
    my_bias = lax.dynamic_slice(dt_bias, (head,), (HEADS_L,))
    my_rate = -jnp.exp(lax.dynamic_slice(a_log, (head,), (HEADS_L,)))
    heads_in = jnp.broadcast_to(
        jnp.concatenate([my_bias, my_rate, jnp.zeros((8 - 2 * HEADS_L,), F32)])[:, None],
        (8, LANES),
    )
    my_skip = jnp.repeat(lax.dynamic_slice(d_skip, (head,), (HEADS_L,)), MDIM)[:, None]
    x_act, bc_own, row_terms = front(mix_got, taps, heads_in)
    bc_own, gu_swapped = together(bc_own, gu_swapped)
    w_gu = lax.all_gather(gu_swapped, "ctx", axis=0)
    bc = jnp.concatenate(ring_pieces(bc_own), axis=0).reshape(NF, BC_F, LENGTH)
    ssd_seq, states = mamba_fwd(place, x_act, bc, row_terms, my_skip)
    ssd_seq, attn_got, cot_all = together(ssd_seq, attn_got, cot_all)
    heads_seq, lse = attn_fwd(odd, attn_got)
    ssd, heads_seq = together(swap_ctx(ssd_seq), heads_seq)
    heads = swap_ctx(heads_seq)

    my_gain = lax.dynamic_slice(mamba_gain, (fsdp * INNER_F,), (INNER_F,))[:, None]
    g, squares = gate(ssd, gate_z)
    squares, w_gu = together(butterfly(squares, "fsdp", (1, 2, 4)), w_gu)
    gated_heads, branches = branch_out(heads, g, squares, my_gain, w_out)
    branches, cot_all = together(branches, cot_all)
    mixed = hidden + scatter_fsdp(branches)

    scale_two = norm_scale(mixed)
    normed_two, d_act = together(
        gather_fsdp((mixed * scale_two * mlp_gain).astype(BF)), act_back(cot_all, w_down)
    )
    act, d_gu, d_normed_two = mlp(normed_two, d_act, w_gu)
    down_mine, down_other = down_out(spot, act, w_down)

    def side_by_side(*terms):
        return jnp.concatenate([term.reshape(NC, -1, LANES) for term in terms], axis=1)

    def total_of(got):
        return jnp.sum(got.astype(F32), axis=0).astype(BF)

    along_y = [[x * NY + y for y in range(NY)] for x in range(NC // NY)]
    along_x = [[x * NY + y for x in range(NC // NY)] for y in range(NY)]

    def scatter_ctx(joined, groups):
        joined = joined.reshape(len(groups[0]), -1, LANES)
        part = lax.psum_scatter(
            joined, "ctx", scatter_dimension=0, axis_index_groups=groups, tiled=False
        )
        return lax.optimization_barrier(part)

    def all_ctx(parts):
        joined = jnp.concatenate(parts, axis=0)
        return lax.all_gather(joined.reshape(-1, SLICE, LANES), "ctx", axis=0)

    gu_tiles = MLP_COLS // LANES
    row_tiles = OUT_ROWS // SHARD * (D // LANES)
    got_down = swap_ctx(column_grad(act, cot_all).reshape(NC, -1, LANES))
    packed_gu = column_grad(normed_two, d_gu, by_y=True)
    d_normed_two, packed_gu, down_mine, down_other, got_down = together(
        scatter_fsdp(d_normed_two), packed_gu, down_mine, down_other, got_down
    )
    sum_gu = scatter_ctx(packed_gu, along_y)
    sum_down = total_of(got_down)
    d_mixed, g_mlp_gain = norm_back(mixed, scale_two, mlp_gain, d_normed_two)
    d_mixed = d_mixed + cot_low.astype(F32)
    branch = ring_gather(d_mixed.astype(BF), order)

    dg, inner, dh = branch_back(branch, w_out, g, my_gain)
    inner = butterfly(inner, "fsdp", (1, 2, 4))
    d_mixers, dz, g_mamba_gain = gate_back(
        ssd, gate_z, g, dg, dh, squares, inner, my_gain
    )
    d_mixers, sum_gu = together(d_mixers, sum_gu)
    sum_gu = scatter_ctx(sum_gu, along_x)
    d_mixers = swap_ctx(d_mixers)
    packed_two = side_by_side(
        column_grad(gated_heads, branch, by_y=True), column_grad(normed, dz, by_y=True)
    )
    d_mixers, packed_two, sum_gu = together(d_mixers, packed_two, sum_gu)
    sum_two = scatter_ctx(packed_two, along_y)
    dx, dbc_mine, dbc_other, drow, dskip = mamba_bwd(
        place, x_act, d_mixers, bc, row_terms, states, my_skip
    )
    dbc_joined = ring_join(
        dbc_mine.reshape(NZ * BC_F, LENGTH), dbc_other.reshape(NZ * BC_F, LENGTH)
    )
    dx, d_mixers = together(dx, d_mixers)
    down_at = NF * gu_tiles
    gu_part = swap_fsdp(sum_gu.reshape(NF, -1, LANES))
    dbc_joined, gu_part = together(dbc_joined, gu_part)
    all_one = all_ctx([gu_part.reshape(-1, LANES), sum_down])
    dbc_own, attn_pack, sum_two = together(
        ring_scatter(dbc_joined), attn_bwd(odd, attn_got, d_mixers, lse), sum_two
    )
    attn_back = swap_ctx(attn_pack)
    mix_pack, g_taps, g_heads = front_back(
        mix_got, taps, heads_in, row_terms, drow, dx, dbc_own
    )
    mix_pack, attn_back = together(mix_pack, attn_back)
    mix_back, d_qkv, sum_two = together(
        swap_ctx(mix_pack), attn_grads(attn_back, cosine, sine), sum_two
    )
    sum_two = scatter_ctx(sum_two, along_x)
    d_mix = mix_grads(mix_back)
    packed_mix, dz = together(column_grad(normed, d_mix, d_qkv).reshape(NC, -1, LANES), dz)
    mine, other, gain_sum = back_project(spot, d_mix, d_qkv, dz, normed, w_one)
    g_norm_gain = gain_sum[0] / norm_gain

    def joined(mine, other):
        return ring_join(mine.reshape(NZ * ROWS, D), other.reshape(NZ * ROWS, D))

    mine, down_other, all_one = together(mine, down_other, all_one)
    got_mix, d_normed, down, g_gate_up, g_down = together(
        swap_ctx(packed_mix),
        joined(mine, other),
        joined(down_mine, down_other),
        unpack_gate_up(all_one),
        unpack_down(all_one, down_at),
    )
    columns = swap_fsdp(
        jnp.concatenate(
            [
                sum_two[row_tiles * SLICE :].reshape(NF, -1, LANES),
                total_of(got_mix).reshape(NF, -1, LANES),
            ],
            axis=1,
        )
    )
    def by_half(values):
        zero = jnp.zeros_like(values)
        return jnp.where(
            parity == 1, jnp.stack([zero, values], axis=-2), jnp.stack([values, zero], axis=-2)
        )

    g_conv = g_taps.T[: CONV_K + 1]
    g_d_skip = jnp.sum(dskip.reshape(HEADS_L, MDIM), axis=1)
    per_head = jnp.stack(
        [g_heads[:HEADS_L, 0], g_heads[HEADS_L : 2 * HEADS_L, 0], g_d_skip]
    )
    own = jnp.concatenate(
        [
            by_half(g_conv[:, :XW]).reshape(-1),
            g_conv[:, XW:].reshape(-1),
            g_mamba_gain[:, 0],
            by_half(per_head).reshape(-1),
        ]
    )
    own_size = own.shape[0]
    own_pad = -(-own_size // LANES) * LANES
    own = jnp.concatenate([own, jnp.zeros((own_pad - own_size,), F32), g_mlp_gain, g_norm_gain])

    own, columns = together(own.reshape(-1, LANES), columns)
    out_at = NF * W1_COLS // LANES
    all_two = all_ctx([columns.reshape(-1, LANES), sum_two[: row_tiles * SLICE]])
    both = jnp.concatenate([d_normed, down], axis=1)
    own, *both = together(butterfly(own, "ctx", (1, 2, 4)), *ring_first(both))
    own = butterfly(own, "ctx", (8,)).reshape(-1)
    mine = (jnp.arange(NF) == fsdp)[:, None]
    placed = jnp.where(mine, own[None, :own_pad], 0.0).reshape(-1)
    total = jnp.concatenate([placed, own[own_pad:]]).reshape(-1, LANES)
    total, both = together(butterfly(total, "fsdp", (1,)), ring_last(*both))
    d_normed, down = both[:, :D], both[:, D:]
    output = even_first((mixed + down).astype(BF)).reshape(tokens.shape)

    g_mout, g_aout = unpack_out(all_two, out_at)
    g_qkv = unpack_qkv(all_two)
    g_in = unpack_in(all_two).T
    d_hidden, _ = norm_back(hidden, scale_one, norm_gain, d_normed)
    d_tokens = even_first((d_hidden + d_mixed).astype(BF)).reshape(tokens.shape)

    total = butterfly(total, "fsdp", (2, 4)).reshape(-1)
    each = total[: NF * own_pad].reshape(NF, own_pad)
    cut = [(CONV_K + 1) * INNER_F]
    cut.append(cut[0] + (CONV_K + 1) * BC_F)
    cut.append(cut[1] + INNER_F)
    conv_x = each[:, : cut[0]].reshape(NF, CONV_K + 1, INNER_F).transpose(1, 0, 2)
    conv_bc = each[:, cut[0] : cut[1]].reshape(NF, CONV_K + 1, BC_F).transpose(1, 0, 2)
    conv = jnp.concatenate(
        [conv_x.reshape(CONV_K + 1, INNER), conv_bc.reshape(CONV_K + 1, 2 * STATE)], axis=1
    )
    per_head = each[:, cut[2] : cut[2] + 3 * DT_F].reshape(NF, 3, DT_F).transpose(1, 0, 2)
    per_head = per_head.reshape(3, MHEADS)
    gains = total[NF * own_pad :].reshape(2, D)
    return (
        output,
        d_tokens,
        gains[1],
        g_in,
        g_qkv,
        conv[:CONV_K],
        conv[CONV_K],
        per_head[0],
        per_head[1],
        per_head[2],
        each[:, cut[1] : cut[2]].reshape(INNER),
        g_mout,
        g_aout,
        gains[0],
        g_gate_up,
        g_down,
    )


def solution(mesh):
    tokens_at = P("fsdp", "ctx", None, None)
    rows_at = P("fsdp", None)
    placed = (
        tokens_at,
        P(),
        rows_at,
        rows_at,
        P(),
        P(),
        P(),
        P(),
        P(),
        P(),
        rows_at,
        rows_at,
        P(),
        rows_at,
        rows_at,
        tokens_at,
    )
    return jax.shard_map(
        shards,
        mesh=mesh,
        in_specs=placed,
        out_specs=(
            tokens_at,
            tokens_at,
            P(),
            rows_at,
            rows_at,
            P(),
            P(),
            P(),
            P(),
            P(),
            P(),
            rows_at,
            rows_at,
            P(),
            rows_at,
            rows_at,
        ),
        check_vma=False,
    )
```

```python
import functools

import jax
import jax.numpy as jnp
from jax import lax
from jax.experimental import pallas as pl
from jax.experimental.pallas import tpu as pltpu
from jax.sharding import PartitionSpec as P

D = 2048
MHEADS = 48
MDIM = 64
STATE = 256
CONV_K = 4
QHEADS = 8
KVHEADS = 2
HDIM = 128
FF = 4096
HALF = 64
INNER = 3072
LENGTH = 2048
SEQS = 8
NC = 16
NF = 8
NZ = 4
NY = 4
LANES = 128
ROWS = 2 * HALF
GROUP = SEQS * ROWS
INNER_F = INNER // NF
HEADS_L = 3
XW = HEADS_L * MDIM
BC_F = 2 * STATE // NF
DT_F = MHEADS // NF
FF_F = FF // NF
CHUNK = 256
CHUNKS = LENGTH // CHUNK
PAIRS = LENGTH // LANES
QROWS = LENGTH // 2
QBLOCK = 128
SHARD = D // NF
SLICE = SHARD // NC
MIX = INNER_F + LANES
QKV = 3 * HDIM
WM_COLS = MIX + QKV
W1_COLS = WM_COLS + INNER_F
MLP_COLS = 2 * FF_F
OUT_ROWS = INNER_F + HDIM
K_AT, V_AT, Q_AT, ATTN = 0, 128, 256, 320
XB = XW + BC_F
B_AT, T_AT, PACK = XW, XB, XB + 16
BOTH = XW + HALF
GATE_SEQS = 4
IN_SEQS = 4
PART = 16
EPS = 1e-06
ROPE_BASE = 100000000000.0
MASKED = -1e30
SCALE = HDIM ** (-0.5)
BF = jnp.bfloat16
F32 = jnp.float32
PARAMS = pltpu.CompilerParams(vmem_limit_bytes=56 * 1024 * 1024)
SMEM = pl.BlockSpec(memory_space=pltpu.SMEM)


def dot(left, right, left_dim, right_dim):
    return lax.dot_general(
        left, right, (((left_dim,), (right_dim,)), ((), ())), preferred_element_type=F32
    )


def whole(*shape):
    return pl.BlockSpec(shape, lambda *i: (0,) * len(shape))


def cost(flops, moved, transcendentals=0):
    return pl.CostEstimate(
        flops=int(flops), bytes_accessed=int(moved), transcendentals=int(transcendentals)
    )


def shape_of(shape, dtype):
    return jax.ShapeDtypeStruct(shape, dtype)


OTHER_CORE = [(i, i ^ 1) for i in range(NF)]
TO_NEXT = [(i, (i + 2) % NF) for i in range(NF)]
TO_PREV = [(i, (i - 2) % NF) for i in range(NF)]


def send(value, route):
    return lax.ppermute(value, "fsdp", route)


def gather_fsdp(value):
    return lax.all_gather(value, "fsdp", axis=0, tiled=True)


def scatter_fsdp(parts):
    return lax.psum_scatter(parts, "fsdp", scatter_dimension=0, tiled=True).astype(F32)


def ring_pieces(value):
    half = value.shape[0] // 2
    after = send(value, TO_PREV)
    before = send(value, TO_NEXT)
    near = send(value, OTHER_CORE)
    far = jnp.concatenate(
        [send(after[:half], TO_PREV), send(before[half:], TO_NEXT)], axis=0
    )
    near_after = send(after, OTHER_CORE)
    near_before = send(before, OTHER_CORE)
    near_far = send(far, OTHER_CORE)
    return [value, after, far, before, near, near_after, near_far, near_before]


def ring_gather(value, order):
    whole_value = jnp.zeros((NF * value.shape[0],) + value.shape[1:], value.dtype)
    for index, piece in enumerate(ring_pieces(value)):
        whole_value = lax.dynamic_update_slice(
            whole_value, piece, (order[index] * value.shape[0], 0)
        )
    return whole_value


def plus(*terms):
    return sum(term.astype(F32) for term in terms)


def ring_join(mine, other):
    return plus(mine, send(other, OTHER_CORE)).astype(BF)


def ring_first(joined):
    size = joined.shape[0] // NZ
    half = size // 2
    own, after, far, before = [joined[i * size : (i + 1) * size] for i in range(NZ)]
    sent = (
        send(far[:half], TO_NEXT),
        send(far[half:], TO_PREV),
        send(after[half:], TO_NEXT),
        send(before[:half], TO_PREV),
    )
    return own, after[:half], before[half:], *sent


def ring_second(own, after, before, far_next, far_prev, after_two, before_one):
    after_one = send(plus(after, far_next).astype(BF), TO_NEXT)
    before_two = send(plus(before, far_prev).astype(BF), TO_PREV)
    return own, after_one, after_two, before_one, before_two


def ring_last(own, after_one, after_two, before_one, before_two):
    return plus(
        own,
        jnp.concatenate([after_one, after_two], axis=0),
        jnp.concatenate([before_one, before_two], axis=0),
    )


def ring_scatter(joined):
    return ring_last(*ring_second(*ring_first(joined)))


def together(*values):
    return lax.optimization_barrier(values)


def swap_ctx(value):
    return lax.all_to_all(value, "ctx", 0, 0, tiled=True)


def swap_fsdp(value):
    return lax.all_to_all(value, "fsdp", 0, 0, tiled=True)


def exchange(value, axis, bit):
    size = lax.axis_size(axis)
    return value + lax.ppermute(value, axis, [(i, i ^ bit) for i in range(size)])


def butterfly(value, axis, bits):
    for bit in bits:
        value = exchange(value, axis, bit)
    return value


def rotate(values, cosine, sine):
    half = values.shape[-1] // 2
    first = values[:, :half]
    second = values[:, half:]
    return jnp.concatenate(
        [first * cosine - second * sine, second * cosine + first * sine], axis=1
    )


def proj_kernel(n_ref, w_ref, cos_ref, sin_ref, mix_ref, attn_ref):
    acc = jnp.zeros((2 * ROWS, WM_COLS), F32)
    for f in range(NF):
        acc = acc + dot(
            n_ref[:, f * SHARD : (f + 1) * SHARD],
            w_ref[:, f, :, :WM_COLS].reshape(SHARD, WM_COLS),
            1,
            0,
        )
    for j in range(2):
        rows = acc[j * ROWS : (j + 1) * ROWS]
        x_rows = rows[:, :INNER_F].T.astype(BF)
        tail = rows[:, INNER_F:MIX].T
        query = rotate(rows[:, MIX : MIX + HDIM], cos_ref[...], sin_ref[...]).astype(BF)
        key = rotate(
            rows[:, MIX + HDIM : MIX + 2 * HDIM], cos_ref[...], sin_ref[...]
        ).astype(BF)
        value = rows[:, MIX + 2 * HDIM :].astype(BF)
        for p in range(2):
            to = 2 * j + p
            attn_ref[to, K_AT:V_AT] = key
            attn_ref[to, V_AT:Q_AT] = value
            attn_ref[to, Q_AT:] = query[p * HALF : (p + 1) * HALF]
            mix_ref[to, :B_AT] = x_rows[p * XW : (p + 1) * XW]
            mix_ref[to, B_AT:T_AT] = tail[:BC_F].astype(BF)
            steps = tail[BC_F + p * HEADS_L : BC_F + (p + 1) * HEADS_L]
            high = steps.astype(BF).astype(F32)
            mix_ref[to, T_AT:] = jnp.concatenate(
                [high, steps - high, jnp.zeros((16 - 2 * HEADS_L, ROWS), F32)], axis=0
            ).astype(BF)


def packets(rows):
    return pl.BlockSpec((4, rows, LANES), lambda i: (i, 0, 0))


def token_rows(width):
    return pl.BlockSpec((2 * ROWS, width), lambda i: (i, 0))


def project(normed, w_one, cosine, sine):
    return pl.pallas_call(
        proj_kernel,
        grid=(SEQS // 2,),
        in_specs=[
            token_rows(D),
            whole(NC, NF, SLICE, W1_COLS),
            whole(ROWS, HALF),
            whole(ROWS, HALF),
        ],
        out_specs=[packets(PACK), packets(ATTN)],
        out_shape=[shape_of((NC, PACK, LANES), BF), shape_of((NC, ATTN, LANES), BF)],
        compiler_params=PARAMS,
        cost_estimate=cost(2 * GROUP * D * WM_COLS, 10e6),
        name="project",
    )(normed, w_one, cosine, sine)


def proj_z_kernel(n_ref, w_ref, z_ref):
    acc = jnp.zeros((2 * ROWS, INNER_F), F32)
    for f in range(NF):
        acc = acc + dot(
            n_ref[:, f * SHARD : (f + 1) * SHARD],
            w_ref[:, f, :, WM_COLS:].reshape(SHARD, INNER_F),
            1,
            0,
        )
    for j in range(2):
        z_ref[j] = acc[j * ROWS : (j + 1) * ROWS].T


def project_z(normed, w_z):
    return pl.pallas_call(
        proj_z_kernel,
        grid=(SEQS // 2,),
        in_specs=[token_rows(D), whole(NC, NF, SLICE, W1_COLS)],
        out_specs=pl.BlockSpec((2, INNER_F, ROWS), lambda i: (i, 0, 0)),
        out_shape=shape_of((SEQS, INNER_F, ROWS), F32),
        compiler_params=PARAMS,
        cost_estimate=cost(2 * GROUP * D * INNER_F, 8e6),
        name="project_z",
    )(normed, w_z)


def attn_grads_kernel(got_ref, cos_ref, sin_ref, out_ref):
    for j in range(2):
        one = got_ref[2 * j].astype(F32)
        two = got_ref[2 * j + 1].astype(F32)
        both = one + two
        query = jnp.concatenate([one[Q_AT:], two[Q_AT:]], axis=0)
        query = rotate(query, cos_ref[...], -sin_ref[...])
        key = rotate(both[K_AT:V_AT], cos_ref[...], -sin_ref[...])
        out_ref[j * ROWS : (j + 1) * ROWS] = jnp.concatenate(
            [query, key, both[V_AT:Q_AT]], axis=1
        ).astype(BF)


def attn_grads(got, cosine, sine):
    return pl.pallas_call(
        attn_grads_kernel,
        grid=(SEQS // 2,),
        in_specs=[packets(ATTN), whole(ROWS, HALF), whole(ROWS, HALF)],
        out_specs=token_rows(QKV),
        out_shape=shape_of((GROUP, QKV), BF),
        compiler_params=PARAMS,
        cost_estimate=cost(10 * GROUP * QKV, 2e6),
        name="attn_grads",
    )(got, cosine, sine)


def mix_grads_kernel(got_ref, out_ref):
    for j in range(2):
        one = got_ref[2 * j].astype(F32)
        two = got_ref[2 * j + 1].astype(F32)
        x_rows = jnp.concatenate([one[:B_AT], two[:B_AT]], axis=0).T
        tail = jnp.concatenate(
            [
                one[B_AT:T_AT] + two[B_AT:T_AT],
                one[T_AT : T_AT + HEADS_L],
                two[T_AT : T_AT + HEADS_L],
                jnp.zeros((LANES - BC_F - DT_F, ROWS), F32),
            ],
            axis=0,
        ).T
        out_ref[j * ROWS : (j + 1) * ROWS] = jnp.concatenate([x_rows, tail], axis=1).astype(BF)


def mix_grads(got):
    return pl.pallas_call(
        mix_grads_kernel,
        grid=(SEQS // 2,),
        in_specs=[packets(PACK)],
        out_specs=token_rows(MIX),
        out_shape=shape_of((GROUP, MIX), BF),
        compiler_params=PARAMS,
        cost_estimate=cost(4 * GROUP * MIX, 2.2e6),
        name="mix_grads",
    )(got)


def back_kernel(
    spot_ref, mix_ref, dqkv_ref, dz_ref, n_ref, w_ref, mine_ref, other_ref, gain_ref
):
    @pl.when(pl.program_id(0) == 0)
    def _():
        gain_ref[...] = jnp.zeros_like(gain_ref)

    first = spot_ref[NZ] == 0
    grad = jnp.concatenate([mix_ref[...], dqkv_ref[...], dz_ref[...]], axis=1)
    for f in range(NF):
        part = slice(f * SHARD, (f + 1) * SHARD)
        dn = dot(grad, w_ref[:, f].reshape(SHARD, W1_COLS), 1, 1)
        gain_ref[:, part] += jnp.sum(dn * n_ref[:, part].astype(F32), axis=0, keepdims=True)
        dn = dn.astype(BF)
        mine_ref[0, :, part] = jnp.where(first, dn[:ROWS], dn[ROWS:])
        other_ref[0, :, part] = jnp.where(first, dn[ROWS:], dn[:ROWS])


def back_project(spot, mix, dqkv, dz, normed, w_one):
    def rows(width):
        return pl.BlockSpec((2 * ROWS, width), lambda i, spot: (i, 0))

    specs, shapes = ring_specs(D)
    return pl.pallas_call(
        back_kernel,
        grid_spec=pltpu.PrefetchScalarGridSpec(
            num_scalar_prefetch=1,
            grid=(SEQS // 2,),
            in_specs=[
                rows(MIX),
                rows(QKV),
                rows(INNER_F),
                rows(D),
                pl.BlockSpec((NC, NF, SLICE, W1_COLS), lambda i, spot: (0, 0, 0, 0)),
            ],
            out_specs=specs + [pl.BlockSpec((1, D), lambda i, spot: (0, 0))],
        ),
        out_shape=shapes + [shape_of((1, D), F32)],
        compiler_params=PARAMS,
        cost_estimate=cost(2 * GROUP * D * W1_COLS, 18e6),
        name="back_project",
    )(spot, mix, dqkv, dz, normed, w_one)


def column_grad_kernel(by_y, left_ref, *refs):
    out_ref = refs[-1]
    first = 0
    for right_ref in refs[:-1]:
        term = dot(left_ref[...], right_ref[...], 0, 0).astype(BF)
        for block in range(out_ref.shape[1]):
            for tile in range(right_ref.shape[1] // LANES):
                part = term[
                    block * SHARD : (block + 1) * SHARD, tile * LANES : (tile + 1) * LANES
                ]
                if by_y:
                    part = part.reshape(NC // NY, NY, SLICE, LANES)
                    for y in range(NY):
                        rows = slice(y * NC // NY, (y + 1) * NC // NY)
                        out_ref[rows, block, first + tile] = part[:, y]
                else:
                    out_ref[:, block, first + tile] = part.reshape(NC, SLICE, LANES)
        first += right_ref.shape[1] // LANES


def column_grad(left, *rights, by_y=False):
    count, width = left.shape[1] // SHARD, sum(right.shape[1] for right in rights)
    tiles = width // LANES
    many = 2
    return pl.pallas_call(
        functools.partial(column_grad_kernel, by_y),
        grid=(count // many,),
        in_specs=[pl.BlockSpec((GROUP, many * SHARD), lambda i: (0, i))]
        + [whole(GROUP, right.shape[1]) for right in rights],
        out_specs=pl.BlockSpec((NC, many, tiles, SLICE, LANES), lambda i: (0, i, 0, 0, 0)),
        out_shape=shape_of((NC, count, tiles, SLICE, LANES), BF),
        compiler_params=PARAMS,
        cost_estimate=cost(
            2 * GROUP * left.shape[1] * width,
            2 * GROUP * (left.shape[1] + width) + 2 * left.shape[1] * width,
        ),
        name="column_grad",
    )(left, *rights)


def channels(count):
    return pl.BlockSpec((count, INNER_F, ROWS), lambda i: (i, 0, 0))


def gate_packets(rows):
    return pl.BlockSpec((2 * GATE_SEQS, rows, LANES), lambda i: (i, 0, 0))


def gate_kernel(got_ref, z_ref, g_ref, sq_ref):
    for j in range(GATE_SEQS):
        ssd = got_ref[2 * j : 2 * j + 2, :XW].reshape(INNER_F, ROWS).astype(F32)
        z = z_ref[j]
        g = ssd * (z * jax.nn.sigmoid(z))
        g_ref[j] = g
        seq = pl.program_id(0) * GATE_SEQS + j
        sq_ref[pl.ds(seq, 1)] = jnp.sum(g * g, axis=0, keepdims=True)


def gate(got, z):
    return pl.pallas_call(
        gate_kernel,
        grid=(SEQS // GATE_SEQS,),
        in_specs=[gate_packets(XW), channels(GATE_SEQS)],
        out_specs=[channels(GATE_SEQS), whole(SEQS, ROWS)],
        out_shape=[shape_of((SEQS, INNER_F, ROWS), F32), shape_of((SEQS, ROWS), F32)],
        compiler_params=PARAMS,
        cost_estimate=cost(8 * GROUP * INNER_F, 4.2e6, GROUP * INNER_F),
        name="gate",
    )(got, z)


def branch_kernel(heads_ref, g_ref, sq_ref, gain_ref, w_ref, gh_ref, out_ref):
    step = pl.program_id(0)
    for j in range(2):
        scale = lax.rsqrt(sq_ref[pl.ds(2 * step + j, 1)] / INNER + EPS)
        gated = (g_ref[j] * scale * gain_ref[...]).T.astype(BF)
        heads = heads_ref[2 * j : 2 * j + 2].reshape(ROWS, HDIM)
        gh_ref[j * ROWS : (j + 1) * ROWS] = jnp.concatenate([gated, heads], axis=1)
    out_ref[...] = dot(gh_ref[...], w_ref[...], 1, 0).astype(BF)


def branch_out(heads, g, squares, gain, w_out):
    return pl.pallas_call(
        branch_kernel,
        grid=(SEQS // 2,),
        in_specs=[
            packets(HALF),
            channels(2),
            whole(SEQS, ROWS),
            whole(INNER_F, 1),
            whole(OUT_ROWS, D),
        ],
        out_specs=[token_rows(OUT_ROWS), token_rows(D)],
        out_shape=[shape_of((GROUP, OUT_ROWS), BF), shape_of((GROUP, D), BF)],
        compiler_params=PARAMS,
        cost_estimate=cost(2 * GROUP * OUT_ROWS * D, 10e6),
        name="branch_out",
    )(heads, g, squares, gain, w_out)


def branch_back_kernel(d_ref, w_ref, g_ref, gain_ref, dg_ref, inner_ref, dh_ref):
    step = pl.program_id(0)
    both = dot(d_ref[...], w_ref[...], 1, 1)
    for j in range(2):
        rows = both[j * ROWS : (j + 1) * ROWS]
        d_gated = rows[:, :INNER_F].T
        dg_ref[j] = d_gated
        inner_ref[pl.ds(2 * step + j, 1)] = jnp.sum(
            d_gated * gain_ref[...] * g_ref[j], axis=0, keepdims=True
        )
        heads = rows[:, INNER_F:].astype(BF)
        dh_ref[2 * j : 2 * j + 2] = heads.reshape(2, HALF, HDIM)


def branch_back(branch, w_out, g, gain):
    return pl.pallas_call(
        branch_back_kernel,
        grid=(SEQS // 2,),
        in_specs=[token_rows(D), whole(OUT_ROWS, D), channels(2), whole(INNER_F, 1)],
        out_specs=[channels(2), whole(SEQS, ROWS), packets(HALF)],
        out_shape=[
            shape_of((SEQS, INNER_F, ROWS), F32),
            shape_of((SEQS, ROWS), F32),
            shape_of((NC, HALF, HDIM), BF),
        ],
        compiler_params=PARAMS,
        cost_estimate=cost(2 * GROUP * OUT_ROWS * D, 10e6),
        name="branch_back",
    )(branch, w_out, g, gain)


def gate_back_kernel(
    got_ref, z_ref, g_ref, dg_ref, dh_ref, sq_ref, inner_ref, gain_ref,
    pack_ref, dz_ref, gain_grad_ref,
):
    index = pl.program_id(0)

    @pl.when(index == 0)
    def _():
        gain_grad_ref[...] = jnp.zeros_like(gain_grad_ref)

    pack_ref[:, XW:] = dh_ref[...]
    for j in range(GATE_SEQS):
        ssd = got_ref[2 * j : 2 * j + 2, :XW].reshape(INNER_F, ROWS).astype(F32)
        z = z_ref[j]
        g = g_ref[j]
        sig = jax.nn.sigmoid(z)
        silu = z * sig
        seq = index * GATE_SEQS + j
        scale = lax.rsqrt(sq_ref[pl.ds(seq, 1)] / INNER + EPS)
        inner = inner_ref[pl.ds(seq, 1)] / INNER
        scaled = dg_ref[j] * scale
        d_g = scaled * gain_ref[...] - g * (scale * scale * scale * inner)
        gain_grad_ref[...] += jnp.sum(scaled * g, axis=1, keepdims=True)
        pack_ref[2 * j : 2 * j + 2, :XW] = (d_g * silu).astype(BF).reshape(2, XW, LANES)
        dz_ref[j * ROWS : (j + 1) * ROWS] = (
            (d_g * ssd * (sig + silu * (1.0 - sig))).T.astype(BF)
        )


def gate_back(got, z, g, dg, dh, squares, inner, gain):
    return pl.pallas_call(
        gate_back_kernel,
        grid=(SEQS // GATE_SEQS,),
        in_specs=[
            gate_packets(XW),
            channels(GATE_SEQS),
            channels(GATE_SEQS),
            channels(GATE_SEQS),
            gate_packets(HALF),
            whole(SEQS, ROWS),
            whole(SEQS, ROWS),
            whole(INNER_F, 1),
        ],
        out_specs=[
            gate_packets(BOTH),
            pl.BlockSpec((GATE_SEQS * ROWS, INNER_F), lambda i: (i, 0)),
            whole(INNER_F, 1),
        ],
        out_shape=[
            shape_of((NC, BOTH, LANES), BF),
            shape_of((GROUP, INNER_F), BF),
            shape_of((INNER_F, 1), F32),
        ],
        compiler_params=PARAMS,
        cost_estimate=cost(20 * GROUP * INNER_F, 8e6, GROUP * INNER_F),
        name="gate_back",
    )(got, z, g, dg, dh, squares, inner, gain)


def act_back_kernel(cot_ref, down_ref, out_ref):
    out_ref[...] = dot(cot_ref[...], down_ref[...], 1, 1)


def act_back(cot, w_down):
    return pl.pallas_call(
        act_back_kernel,
        grid=(SEQS // 2,),
        in_specs=[token_rows(D), whole(FF_F, D)],
        out_specs=token_rows(FF_F),
        out_shape=shape_of((GROUP, FF_F), F32),
        compiler_params=PARAMS,
        cost_estimate=cost(2 * GROUP * D * FF_F, 9e6),
        name="act_back",
    )(cot, w_down)


def mlp_kernel(n_ref, d_act_ref, w_ref, act_ref, dgu_ref, dn_ref):
    acc = jnp.zeros((2 * ROWS, MLP_COLS), F32)
    for f in range(NF):
        acc = acc + dot(
            n_ref[:, f * SHARD : (f + 1) * SHARD], w_ref[:, f].reshape(SHARD, MLP_COLS), 1, 0
        )
    gate_part, upper = acc[:, :FF_F], acc[:, FF_F:]
    sig = jax.nn.sigmoid(gate_part)
    silu = gate_part * sig
    act_ref[...] = (silu * upper).astype(BF)
    d_act = d_act_ref[...]
    d_gu = jnp.concatenate(
        [d_act * upper * (sig + silu * (1.0 - sig)), d_act * silu], axis=1
    ).astype(BF)
    dgu_ref[...] = d_gu
    for f in range(NF):
        dn_ref[:, f * SHARD : (f + 1) * SHARD] = dot(
            d_gu, w_ref[:, f].reshape(SHARD, MLP_COLS), 1, 1
        ).astype(BF)


def mlp(normed, d_act, w_gu):
    return pl.pallas_call(
        mlp_kernel,
        grid=(SEQS // 2,),
        in_specs=[token_rows(D), token_rows(FF_F), whole(NC, NF, SLICE, MLP_COLS)],
        out_specs=[token_rows(FF_F), token_rows(MLP_COLS), token_rows(D)],
        out_shape=[
            shape_of((GROUP, FF_F), BF),
            shape_of((GROUP, MLP_COLS), BF),
            shape_of((GROUP, D), BF),
        ],
        compiler_params=PARAMS,
        cost_estimate=cost(8 * GROUP * D * FF_F, 20e6, GROUP * FF_F),
        name="mlp",
    )(normed, d_act, w_gu)


def ring_specs(width):
    def spec(*_):
        return pl.BlockSpec((1, ROWS, width), lambda i, spot: (spot[i], 0, 0))

    return [spec(), spec()], [shape_of((NZ, ROWS, width), BF)] * 2


def down_kernel(spot_ref, act_ref, down_ref, mine_ref, other_ref):
    rows = dot(act_ref[...], down_ref[...], 1, 0).astype(BF)
    first = spot_ref[NZ] == 0
    mine_ref[0] = jnp.where(first, rows[:ROWS], rows[ROWS:])
    other_ref[0] = jnp.where(first, rows[ROWS:], rows[:ROWS])


def down_out(spot, act, w_down):
    specs, shapes = ring_specs(D)
    return pl.pallas_call(
        down_kernel,
        grid_spec=pltpu.PrefetchScalarGridSpec(
            num_scalar_prefetch=1,
            grid=(SEQS // 2,),
            in_specs=[
                pl.BlockSpec((2 * ROWS, FF_F), lambda i, spot: (i, 0)),
                pl.BlockSpec((FF_F, D), lambda i, spot: (0, 0)),
            ],
            out_specs=specs,
        ),
        out_shape=shapes,
        compiler_params=PARAMS,
        cost_estimate=cost(2 * GROUP * D * FF_F, 8e6),
        name="down_out",
    )(spot, act, w_down)


def lane_of(shape):
    return lax.broadcasted_iota(jnp.int32, shape, 1)


def sources(pair, first):
    if first:
        return 2 * pair, 2 * pair + 1
    return NC - 1 - 2 * pair, NC - 2 - 2 * pair


def assemble(ref, low, high, pair, first):
    one, two = sources(pair, first)
    left = lane_of((high - low, LANES)) < HALF
    return jnp.where(left, ref[one, low:high].astype(F32), ref[two, low:high].astype(F32))


def deal(ref, low, high, pair, first, values):
    one, two = sources(pair, first)
    values = values.astype(BF)
    ref[one, low:high, :HALF] = values[:, :HALF]
    ref[two, low:high, HALF:] = values[:, HALF:]


def taps_of(padded, taps):
    current = padded[:, LANES:]
    total = current * taps[:, CONV_K - 1 : CONV_K] + taps[:, CONV_K : CONV_K + 1]
    inputs = [current]
    for back in range(1, CONV_K):
        moved = pltpu.roll(padded, back, 1)[:, LANES:]
        inputs.append(moved)
        total = total + moved * taps[:, CONV_K - 1 - back : CONV_K - back]
    return inputs[::-1], total


def softplus(values):
    return jnp.maximum(values, 0.0) + jnp.log1p(jnp.exp(-jnp.abs(values)))


def at_pair(pair):
    return pl.ds(pl.multiple_of(pair * LANES, LANES), LANES)


def load_raw(got_ref, raw_ref):
    raw_ref[:, :LANES] = jnp.zeros((XB, LANES), F32)
    half_pairs = PAIRS // 2
    for first in (True, False):

        def load(pair, unused, first=first):
            place = at_pair((pair if first else pair + half_pairs) + 1)
            raw_ref[:, place] = assemble(got_ref, 0, XB, pair, first)
            return unused

        lax.fori_loop(0, half_pairs, load, 0, unroll=True)


def front_kernel(got_ref, taps_ref, heads_ref, x_ref, bc_ref, row_ref, raw_ref):
    load_raw(got_ref, raw_ref)

    def step(part, unused):
        rows = pl.ds(pl.multiple_of(part * PART, PART), PART)
        _, total = taps_of(raw_ref[rows], taps_ref[rows])
        active = (total * jax.nn.sigmoid(total)).astype(BF)

        @pl.when(part < XW // PART)
        def _():
            x_ref[rows] = active

        @pl.when(part >= XW // PART)
        def _():
            bc_ref[pl.ds(pl.multiple_of(part * PART - XW, PART), PART)] = active

        return unused

    lax.fori_loop(0, XB // PART, step, 0)
    half_pairs = PAIRS // 2
    parts = [
        assemble(got_ref, T_AT, PACK, index % half_pairs, index < half_pairs)
        for index in range(PAIRS)
    ]
    parts = jnp.concatenate(parts, axis=1)
    raw = parts[:HEADS_L] + parts[HEADS_L : 2 * HEADS_L] + heads_ref[:HEADS_L, :1]
    steps = softplus(raw)
    pad = jnp.zeros((8 - 2 * HEADS_L, LENGTH), F32)
    sums = jnp.concatenate([steps * heads_ref[HEADS_L : 2 * HEADS_L, :1], steps, pad], axis=0)
    rows = lax.broadcasted_iota(jnp.int32, sums.shape, 0)
    lane = lane_of(sums.shape) % CHUNK
    running = sums
    back = 1
    while back < CHUNK:
        running = running + jnp.where(lane >= back, pltpu.roll(running, back, 1), 0.0)
        back *= 2
    row_ref[:8] = jnp.where(rows < HEADS_L, running, sums)
    row_ref[8:] = jnp.concatenate([raw, jnp.zeros((8 - HEADS_L, LENGTH), F32)], axis=0)


def front(got, taps, heads):
    return pl.pallas_call(
        front_kernel,
        in_specs=[whole(NC, PACK, LANES), whole(XB, 8), whole(8, LANES)],
        out_specs=[whole(XW, LENGTH), whole(BC_F, LENGTH), whole(16, LENGTH)],
        out_shape=[
            shape_of((XW, LENGTH), BF),
            shape_of((BC_F, LENGTH), BF),
            shape_of((16, LENGTH), F32),
        ],
        grid=(1,),
        scratch_shapes=[pltpu.VMEM((XB, LENGTH + LANES), F32)],
        compiler_params=PARAMS,
        cost_estimate=cost(30 * XB * LENGTH, 4e6, XB * LENGTH),
        name="front",
    )(got, taps, heads)


def front_back_kernel(
    got_ref, taps_ref, heads_ref, row_ref, drow_ref, dx_ref, dbc_ref, pack_ref,
    taps_grad_ref, heads_grad_ref, raw_ref, grad_ref,
):
    half_pairs = PAIRS // 2
    load_raw(got_ref, raw_ref)

    grads = drow_ref[...]
    lane = lane_of(grads.shape) % CHUNK
    running = grads
    back = 1
    while back < CHUNK:
        running = running + jnp.where(
            lane < CHUNK - back, pltpu.roll(running, LENGTH - back, 1), 0.0
        )
        back *= 2
    rates = running[:HEADS_L]
    rate = heads_ref[HEADS_L : 2 * HEADS_L, :1]
    d_steps = grads[HEADS_L : 2 * HEADS_L] + rates * rate
    d_dt = d_steps * jax.nn.sigmoid(row_ref[8 : 8 + HEADS_L])
    steps = row_ref[HEADS_L : 2 * HEADS_L]
    heads_grad_ref[...] = jnp.concatenate(
        [
            jnp.sum(d_dt, axis=1, keepdims=True),
            jnp.sum(rates * steps, axis=1, keepdims=True) * rate,
            jnp.zeros((8 - 2 * HEADS_L, 1), F32),
        ],
        axis=0,
    )
    d_dt = jnp.concatenate([d_dt, jnp.zeros((16 - HEADS_L, LENGTH), F32)], axis=0)
    for index in range(PAIRS):
        first = index < half_pairs
        deal(
            pack_ref, T_AT, PACK, index % half_pairs, first,
            d_dt[:, index * LANES : (index + 1) * LANES],
        )

    def step(part, unused):
        rows = pl.ds(pl.multiple_of(part * PART, PART), PART)
        taps = taps_ref[rows]
        inputs, total = taps_of(raw_ref[rows], taps)
        sig = jax.nn.sigmoid(total)

        @pl.when(part < XW // PART)
        def _():
            grad_ref[:, :LENGTH] = dx_ref[rows]

        @pl.when(part >= XW // PART)
        def _():
            grad_ref[:, :LENGTH] = dbc_ref[pl.ds(pl.multiple_of(part * PART - XW, PART), PART)]

        grad = grad_ref[:, :LENGTH] * (sig + total * sig * (1.0 - sig))
        grad_ref[:, :LENGTH] = grad
        padded = grad_ref[...]
        d_raw = grad * taps[:, CONV_K - 1 : CONV_K]
        for ahead in range(1, CONV_K):
            moved = pltpu.roll(padded, LENGTH + LANES - ahead, 1)[:, :LENGTH]
            d_raw = d_raw + moved * taps[:, CONV_K - 1 - ahead : CONV_K - ahead]
        taps_grad_ref[rows] = jnp.concatenate(
            [jnp.sum(grad * moved, axis=1, keepdims=True) for moved in inputs]
            + [jnp.sum(grad, axis=1, keepdims=True)]
            + [jnp.zeros((PART, 8 - CONV_K - 1), F32)],
            axis=1,
        )
        raw_ref[rows, :LENGTH] = d_raw
        return unused

    grad_ref[:, LENGTH:] = jnp.zeros((PART, LANES), F32)
    lax.fori_loop(0, XB // PART, step, 0)
    for first in (True, False):

        def store(pair, unused, first=first):
            place = at_pair(pair if first else pair + half_pairs)
            deal(pack_ref, 0, XB, pair, first, raw_ref[:, place])
            return unused

        lax.fori_loop(0, half_pairs, store, 0, unroll=True)


def front_back(got, taps, heads, rows, drow, dx, dbc):
    return pl.pallas_call(
        front_back_kernel,
        in_specs=[
            whole(NC, PACK, LANES),
            whole(XB, 8),
            whole(8, LANES),
            whole(16, LENGTH),
            whole(8, LENGTH),
            whole(XW, LENGTH),
            whole(BC_F, LENGTH),
        ],
        out_specs=[whole(NC, PACK, LANES), whole(XB, 8), whole(8, 1)],
        out_shape=[
            shape_of((NC, PACK, LANES), BF),
            shape_of((XB, 8), F32),
            shape_of((8, 1), F32),
        ],
        grid=(1,),
        scratch_shapes=[
            pltpu.VMEM((XB, LENGTH + LANES), F32),
            pltpu.VMEM((PART, LENGTH + LANES), F32),
        ],
        compiler_params=PARAMS,
        cost_estimate=cost(60 * XB * LENGTH, 9e6, XB * LENGTH),
        name="front_back",
    )(got, taps, heads, rows, drow, dx, dbc)


def stacked(rows, width):
    return jnp.concatenate(
        [jnp.broadcast_to(row, (MDIM, width)) for row in rows], axis=0
    )


def state_sides(place_ref, bc_ref):
    quarter = STATE // BC_F
    bt = jnp.concatenate([bc_ref[place_ref[j]] for j in range(quarter)], axis=0)
    ct = jnp.concatenate([bc_ref[place_ref[quarter + j]] for j in range(quarter)], axis=0)
    return bt, ct


def chunk_terms(row_ref):
    rows = row_ref[...]
    cols = rows.T
    cum_row = [rows[h : h + 1] for h in range(HEADS_L)]
    dt_row = [rows[HEADS_L + h : HEADS_L + h + 1] for h in range(HEADS_L)]
    cum_col = [cols[:, h : h + 1] for h in range(HEADS_L)]
    dt_col = [cols[:, HEADS_L + h : HEADS_L + h + 1] for h in range(HEADS_L)]
    last = [row[:, CHUNK - 1 :] for row in cum_row]
    return cum_row, dt_row, cum_col, dt_col, last


def later_mask():
    shape = (CHUNK, CHUNK)
    return lax.broadcasted_iota(jnp.int32, shape, 1) >= lax.broadcasted_iota(jnp.int32, shape, 0)


def mamba_fwd_kernel(
    place_ref, x_ref, bc_ref, row_ref, skip_ref, pack_ref, st_out_ref, st_ref
):
    index = pl.program_id(0)

    @pl.when(index == 0)
    def _():
        st_ref[...] = jnp.zeros_like(st_ref)

    x_low = x_ref[...]
    x = x_low.astype(F32)
    bt, ct = state_sides(place_ref, bc_ref)
    st = st_ref[...]
    st_out_ref[0] = st
    cum_row, dt_row, cum_col, dt_col, last = chunk_terms(row_ref)
    inter = dot(bt, ct, 0, 0)
    carried = dot(st.astype(BF), ct, 1, 0)
    later = later_mask()
    within = []
    for h in range(HEADS_L):
        decay = jnp.exp(jnp.where(later, cum_row[h] - cum_col[h], MASKED))
        mixing = (inter * decay * dt_col[h]).astype(BF)
        within.append(dot(x_low[h * MDIM : (h + 1) * MDIM], mixing, 1, 0))
    entering = stacked([jnp.exp(row) for row in cum_row], CHUNK)
    y = jnp.concatenate(within, axis=0) + entering * carried + skip_ref[...] * x
    weights = stacked(
        [jnp.exp(end - row) * step for end, row, step in zip(last, cum_row, dt_row)], CHUNK
    )
    leaving = stacked([jnp.exp(end) for end in last], 1)
    st_ref[...] = st * leaving + dot((x * weights).astype(BF), bt, 1, 1)
    pairs = CHUNK // LANES
    early = index < CHUNKS // 2

    @pl.when(early)
    def _():
        for j in range(pairs):
            deal(pack_ref, 0, XW, pairs * index + j, True, y[:, j * LANES : (j + 1) * LANES])

    @pl.when(jnp.logical_not(early))
    def _():
        for j in range(pairs):
            deal(
                pack_ref, 0, XW, pairs * (index - CHUNKS // 2) + j, False,
                y[:, j * LANES : (j + 1) * LANES],
            )


def mamba_fwd(place, x, bc, rows, skip):
    return pl.pallas_call(
        mamba_fwd_kernel,
        grid=(CHUNKS,),
        in_specs=[
            SMEM,
            pl.BlockSpec((XW, CHUNK), lambda i: (0, i)),
            pl.BlockSpec((NF, BC_F, CHUNK), lambda i: (0, 0, i)),
            pl.BlockSpec((8, CHUNK), lambda i: (0, i)),
            whole(XW, 1),
        ],
        out_specs=[
            whole(NC, XW, LANES),
            pl.BlockSpec((1, XW, STATE), lambda i: (i, 0, 0)),
        ],
        out_shape=[
            shape_of((NC, XW, LANES), BF),
            shape_of((CHUNKS, XW, STATE), F32),
        ],
        scratch_shapes=[pltpu.VMEM((XW, STATE), F32)],
        compiler_params=PARAMS,
        cost_estimate=cost(2 * LENGTH * CHUNK * (STATE + 3 * XW), 7e6, LENGTH * CHUNK * 3),
        name="mamba_fwd",
    )(place, x, bc, rows, skip)


def mamba_bwd_kernel(
    place_ref, x_ref, got_ref, bc_ref, row_ref, st_in_ref, skip_ref,
    dx_ref, mine_ref, other_ref, drow_ref, dskip_ref, dst_ref, dy_ref,
):
    turn = pl.program_id(0)
    index = CHUNKS - 1 - turn
    pairs = CHUNK // LANES

    @pl.when(turn == 0)
    def _():
        dst_ref[...] = jnp.zeros_like(dst_ref)
        dskip_ref[...] = jnp.zeros_like(dskip_ref)

    @pl.when(index < CHUNKS // 2)
    def _():
        for j in range(pairs):
            dy_ref[:, j * LANES : (j + 1) * LANES] = assemble(
                got_ref, 0, XW, pairs * index + j, True
            )

    @pl.when(index >= CHUNKS // 2)
    def _():
        for j in range(pairs):
            dy_ref[:, j * LANES : (j + 1) * LANES] = assemble(
                got_ref, 0, XW, pairs * (index - CHUNKS // 2) + j, False
            )

    x_low = x_ref[...]
    x = x_low.astype(F32)
    dy = dy_ref[...]
    dy_low = dy.astype(BF)
    bt, ct = state_sides(place_ref, bc_ref)
    st = st_in_ref[0]
    dst = dst_ref[...]
    st_low = st.astype(BF)
    dst_low = dst.astype(BF)
    cum_row, dt_row, cum_col, dt_col, last = chunk_terms(row_ref)
    inter = dot(bt, ct, 0, 0)
    later = later_mask()
    entering = stacked([jnp.exp(row) for row in cum_row], CHUNK)
    tail = [jnp.exp(end - row) for end, row in zip(last, cum_row)]
    kept_row = [t * step for t, step in zip(tail, dt_row)]
    weights = stacked(kept_row, CHUNK)
    leaving = stacked([jnp.exp(end) for end in last], 1)
    carried = dot(st_low, ct, 1, 0) * entering
    reach = dot(dst_low, bt, 1, 0)
    dy_in = (dy * entering).astype(BF)
    x_out = (x * weights).astype(BF)
    along = dy * carried
    pulled = x * reach
    kept = jnp.sum(st * dst, axis=1, keepdims=True) * leaving
    d_inter = jnp.zeros((CHUNK, CHUNK), F32)
    dx_parts = []
    row_cum = []
    row_dt = []
    col_cum = []
    col_dt = []
    ends = lane_of((1, CHUNK)) == CHUNK - 1
    for h in range(HEADS_L):
        part = slice(h * MDIM, (h + 1) * MDIM)
        decay = jnp.exp(jnp.where(later, cum_row[h] - cum_col[h], MASKED))
        d_mix = dot(x_low[part], dy_low[part], 0, 0)
        scaled = decay * dt_col[h]
        d_inter = d_inter + d_mix * scaled
        mixing = inter * scaled
        dx_parts.append(dot(dy_low[part], mixing.astype(BF), 1, 1))
        to_dt = jnp.sum(d_mix * (inter * decay), axis=1, keepdims=True)
        q_row = jnp.sum(pulled[part], axis=0, keepdims=True)
        w_q = q_row * kept_row[h]
        d_last = jnp.sum(w_q, axis=1, keepdims=True) + jnp.sum(
            kept[part], axis=0, keepdims=True
        )
        row_cum.append(
            jnp.sum(d_mix * mixing, axis=0, keepdims=True)
            + jnp.sum(along[part], axis=0, keepdims=True)
            - w_q
            + jnp.where(ends, d_last, 0.0)
        )
        row_dt.append(q_row * tail[h])
        col_cum.append(-to_dt * dt_col[h])
        col_dt.append(to_dt)
    dx_ref[...] = jnp.concatenate(dx_parts, axis=0) + weights * reach + skip_ref[...] * dy
    d_low = d_inter.astype(BF)
    dbt = (dot(ct, d_low, 1, 1) + dot(dst_low, x_out, 0, 0)).astype(BF)
    dct = (dot(bt, d_low, 1, 0) + dot(st_low, dy_in, 0, 0)).astype(BF)
    quarter = STATE // BC_F
    parts = [
        grad[j * BC_F : (j + 1) * BC_F] for grad in (dbt, dct) for j in range(quarter)
    ]
    first = place_ref[0] < NZ
    for z in range(NZ):
        one, two = parts[2 * z], parts[2 * z + 1]
        distance = place_ref[2 * z] % NZ
        mine_ref[distance] = jnp.where(first, one, two)
        other_ref[distance] = jnp.where(first, two, one)
    dst_ref[...] = dst * leaving + dot(dy_in, ct, 1, 1)
    dskip_ref[...] += jnp.sum(dy * x, axis=1, keepdims=True)
    pad = jnp.zeros((CHUNK, 8 - 2 * HEADS_L), F32)
    columns = jnp.concatenate(col_cum + col_dt + [pad], axis=1).T
    drow_ref[...] = columns + jnp.concatenate(
        row_cum + row_dt + [jnp.zeros((8 - 2 * HEADS_L, CHUNK), F32)], axis=0
    )


def mamba_bwd(place, x, got, bc, rows, states, skip):
    end = CHUNKS - 1
    return pl.pallas_call(
        mamba_bwd_kernel,
        grid=(CHUNKS,),
        in_specs=[
            SMEM,
            pl.BlockSpec((XW, CHUNK), lambda i: (0, end - i)),
            whole(NC, BOTH, LANES),
            pl.BlockSpec((NF, BC_F, CHUNK), lambda i: (0, 0, end - i)),
            pl.BlockSpec((8, CHUNK), lambda i: (0, end - i)),
            pl.BlockSpec((1, XW, STATE), lambda i: (end - i, 0, 0)),
            whole(XW, 1),
        ],
        out_specs=[
            pl.BlockSpec((XW, CHUNK), lambda i: (0, end - i)),
            pl.BlockSpec((NZ, BC_F, CHUNK), lambda i: (0, 0, end - i)),
            pl.BlockSpec((NZ, BC_F, CHUNK), lambda i: (0, 0, end - i)),
            pl.BlockSpec((8, CHUNK), lambda i: (0, end - i)),
            whole(XW, 1),
        ],
        out_shape=[
            shape_of((XW, LENGTH), F32),
            shape_of((NZ, BC_F, LENGTH), BF),
            shape_of((NZ, BC_F, LENGTH), BF),
            shape_of((8, LENGTH), F32),
            shape_of((XW, 1), F32),
        ],
        scratch_shapes=[pltpu.VMEM((XW, STATE), F32), pltpu.VMEM((XW, CHUNK), F32)],
        compiler_params=PARAMS,
        cost_estimate=cost(
            2 * LENGTH * CHUNK * (3 * STATE + 7 * XW), 12e6, LENGTH * CHUNK * 3
        ),
        name="mamba_bwd",
    )(place, x, got, bc, rows, states, skip)


def position_of(source, odd, inside):
    block = jnp.where(source % 2 == odd, source, 2 * NC - 1 - source)
    return block * HALF + inside


def visible_mask(step, odd):
    key = lax.broadcasted_iota(jnp.int32, (1, LENGTH), 1)
    key_pos = position_of(key // ROWS, (key // HALF) % 2, key % HALF)
    query = lax.broadcasted_iota(jnp.int32, (QBLOCK, 1), 0)
    source = 2 * step + query // HALF
    query_pos = position_of(source, odd, query % HALF)
    return key_pos <= query_pos


def attn_fwd_kernel(odd_ref, q_ref, k_ref, v_ref, o_ref, lse_ref):
    q = q_ref[...].reshape(QBLOCK, HDIM)
    k = k_ref[...].reshape(LENGTH, HDIM)
    v = v_ref[...].reshape(LENGTH, HDIM)
    scores = dot(q, k, 1, 1) * SCALE
    scores = jnp.where(visible_mask(pl.program_id(0), odd_ref[0]), scores, MASKED)
    top = jnp.max(scores, axis=1, keepdims=True)
    grown = jnp.exp(scores - top)
    total = jnp.sum(grown, axis=1, keepdims=True)
    lse_ref[...] = top + jnp.log(total)
    probs = (grown * (1.0 / total)).astype(BF)
    o_ref[...] = dot(probs, v, 1, 0).astype(BF).reshape(2, HALF, HDIM)


def packed_part(at, rows, moving=False):
    block = at // rows
    if moving:
        return pl.BlockSpec((2, rows, HDIM), lambda i: (i, block, 0))
    return pl.BlockSpec((NC, rows, HDIM), lambda i: (0, block, 0))


def attn_fwd(odd, got):
    return pl.pallas_call(
        attn_fwd_kernel,
        grid=(QROWS // QBLOCK,),
        in_specs=[
            SMEM,
            packed_part(Q_AT, HALF, True),
            packed_part(K_AT, ROWS),
            packed_part(V_AT, ROWS),
        ],
        out_specs=[
            pl.BlockSpec((2, HALF, HDIM), lambda i: (i, 0, 0)),
            pl.BlockSpec((QBLOCK, 1), lambda i: (i, 0)),
        ],
        out_shape=[shape_of((NC, HALF, HDIM), BF), shape_of((QROWS, 1), F32)],
        compiler_params=PARAMS,
        cost_estimate=cost(4 * QROWS * LENGTH * HDIM, 3e6, QROWS * LENGTH),
        name="attn_fwd",
    )(odd, got, got, got)


def attn_bwd_kernel(
    odd_ref, q_ref, k_ref, v_ref, do_ref, lse_ref, pack_ref, dk_sum, dv_sum
):
    step = pl.program_id(0)

    @pl.when(step == 0)
    def _():
        dk_sum[...] = jnp.zeros_like(dk_sum)
        dv_sum[...] = jnp.zeros_like(dv_sum)

    q = q_ref[...].reshape(QBLOCK, HDIM)
    k = k_ref[...].reshape(LENGTH, HDIM)
    v = v_ref[...].reshape(LENGTH, HDIM)
    do = do_ref[...].reshape(QBLOCK, HDIM)
    scores = dot(q, k, 1, 1) * SCALE - lse_ref[...]
    probs = jnp.exp(jnp.where(visible_mask(step, odd_ref[0]), scores, MASKED))
    d_probs = dot(do, v, 1, 1)
    dv_sum[...] += dot(probs.astype(BF), do, 0, 0)
    inner = jnp.sum(probs * d_probs, axis=1, keepdims=True)
    d_scores = (probs * (d_probs - inner)).astype(BF)
    pack_ref[pl.ds(2 * step, 2), Q_AT:] = (
        (dot(d_scores, k, 1, 0) * SCALE).astype(BF).reshape(2, HALF, HDIM)
    )
    dk_sum[...] += dot(d_scores, q, 0, 0)

    @pl.when(step == pl.num_programs(0) - 1)
    def _():
        pack_ref[:, K_AT:V_AT] = (dk_sum[...] * SCALE).astype(BF).reshape(NC, ROWS, HDIM)
        pack_ref[:, V_AT:Q_AT] = dv_sum[...].astype(BF).reshape(NC, ROWS, HDIM)


def attn_bwd(odd, got, grads, lse):
    return pl.pallas_call(
        attn_bwd_kernel,
        grid=(QROWS // QBLOCK,),
        in_specs=[
            SMEM,
            packed_part(Q_AT, HALF, True),
            packed_part(K_AT, ROWS),
            packed_part(V_AT, ROWS),
            packed_part(XW, HALF, True),
            pl.BlockSpec((QBLOCK, 1), lambda i: (i, 0)),
        ],
        out_specs=whole(NC, ATTN, LANES),
        out_shape=shape_of((NC, ATTN, LANES), BF),
        scratch_shapes=[pltpu.VMEM((LENGTH, HDIM), F32), pltpu.VMEM((LENGTH, HDIM), F32)],
        compiler_params=PARAMS,
        cost_estimate=cost(10 * QROWS * LENGTH * HDIM, 4e6, QROWS * LENGTH),
        name="attn_bwd",
    )(odd, got, got, got, grads, lse)


def tiles_to_rows(refs):
    tiles = []
    for ref in refs:
        count = ref.shape[0] * SLICE
        for tile in range(ref.shape[1]):
            tiles.append(ref[:, tile].reshape(count, LANES).astype(F32))
    return jnp.concatenate(tiles, axis=1)


def unpack_kernel(*refs):
    refs[-1][...] = tiles_to_rows(refs[:-1])


def unpack_rows_kernel(tiles_ref, down_ref, mout_ref, aout_ref):
    step = pl.program_id(0)
    rows = tiles_to_rows([tiles_ref])
    last = pl.num_programs(0) - 1

    @pl.when(step < FF_F // LANES)
    def _():
        down_ref[...] = rows

    @pl.when((step >= FF_F // LANES) & (step < last))
    def _():
        mout_ref[...] = rows

    @pl.when(step == last)
    def _():
        aout_ref[...] = rows


def unpack_rows(tiles, at):
    width = D // LANES
    base = at // width
    downs, outs = FF_F // LANES, INNER_F // LANES

    def rows(index):
        return pl.BlockSpec((LANES, D), index)

    return pl.pallas_call(
        unpack_rows_kernel,
        grid=((FF_F + OUT_ROWS) // LANES,),
        in_specs=[
            pl.BlockSpec(
                (NC // 2, width, SLICE, LANES), lambda i: (i % 2, base + i // 2, 0, 0)
            )
        ],
        out_specs=[
            rows(lambda i: (jnp.minimum(i, downs - 1), 0)),
            rows(lambda i: (jnp.clip(i - downs, 0, outs - 1), 0)),
            rows(lambda i: (0, 0)),
        ],
        out_shape=[shape_of((FF_F, D), F32), shape_of((INNER_F, D), F32), shape_of((HDIM, D), F32)],
        compiler_params=PARAMS,
        cost_estimate=cost((FF_F + OUT_ROWS) * D, 6 * (FF_F + OUT_ROWS) * D),
        name="unpack_rows",
    )(tiles)


def unpack_gate_up(tiles):
    part = FF_F // LANES
    many = NF // 2

    def spec(j):
        return pl.BlockSpec(
            (NC, part, SLICE, LANES), lambda h, q: (0, 2 * (q * many + j) + h, 0, 0)
        )

    return pl.pallas_call(
        unpack_kernel,
        grid=(2, NF // many),
        in_specs=[spec(j) for j in range(many)],
        out_specs=pl.BlockSpec(
            (SHARD, many * FF_F), lambda h, q: (0, h * (NF // many) + q)
        ),
        out_shape=shape_of((SHARD, 2 * FF), F32),
        compiler_params=PARAMS,
        cost_estimate=cost(SHARD * 2 * FF, 6 * SHARD * 2 * FF),
        name="unpack_gate_up",
    )(*[tiles] * many)


def turned(ref, tile):
    return ref[:, tile].reshape(SHARD, LANES).astype(F32).T


def unpack_in_kernel(*refs):
    step = pl.program_id(0)
    steps = NF // IN_SEQS
    wide = INNER_F // LANES
    out_ref = refs[-1]

    @pl.when(step < 2 * steps)
    def _():
        for index in range(IN_SEQS):
            for tile in range(wide):
                start = index * INNER_F + tile * LANES
                out_ref[start : start + LANES] = turned(refs[index], tile)

    @pl.when(step == 2 * steps)
    def _():
        for f in range(NF):
            tail = turned(refs[IN_SEQS + f], 0)
            out_ref[f * BC_F : (f + 1) * BC_F] = tail[:BC_F]
            first = NF * BC_F + f * DT_F
            out_ref[first : first + DT_F] = tail[BC_F : BC_F + DT_F]


def unpack_in(tiles):
    wide = INNER_F // LANES
    half = NF // IN_SEQS
    each = W1_COLS // LANES

    def spec(j):
        def index(i):
            f = IN_SEQS * (jnp.minimum(i, 2 * half - 1) % half) + j
            return (0, each * f + jnp.where(i < half, 0, wide), 0, 0)

        shape = tuple(pl.Element(size) for size in (NC, wide, SLICE, LANES))
        return pl.BlockSpec(shape, index)

    def tail_spec(f):
        return pl.BlockSpec((NC, 1, SLICE, LANES), lambda i: (0, each * f + 2 * wide, 0, 0))

    specs = [spec(j) for j in range(IN_SEQS)]
    specs += [tail_spec(f) for f in range(NF)]
    return pl.pallas_call(
        unpack_in_kernel,
        grid=(2 * half + 1,),
        in_specs=specs,
        out_specs=pl.BlockSpec((IN_SEQS * INNER_F, SHARD), lambda i: (i, 0)),
        out_shape=shape_of((2 * INNER + 2 * STATE + MHEADS, SHARD), F32),
        compiler_params=PARAMS,
        cost_estimate=cost(SHARD * 6704, 6 * SHARD * 6704),
        name="unpack_in",
    )(*[tiles] * len(specs))


def unpack_qkv_kernel(*refs):
    group = NF // KVHEADS

    def tile(f, index):
        return refs[3 * f + index][:, 0].reshape(SHARD, HDIM).astype(F32)

    parts = [tile(f, 0) for f in range(NF)]
    for index in (1, 2):
        for head in range(KVHEADS):
            parts.append(sum(tile(head * group + j, index) for j in range(group)))
    refs[-1][...] = jnp.concatenate(parts, axis=1)


def unpack_qkv(tiles):
    each, first = W1_COLS // LANES, (INNER_F + MIX) // LANES
    specs = [
        pl.BlockSpec((NC, 1, SLICE, LANES), lambda i, at=each * f + first + index: (0, at, 0, 0))
        for f in range(NF)
        for index in range(3)
    ]
    width = (QHEADS + 2 * KVHEADS) * HDIM
    return pl.pallas_call(
        unpack_qkv_kernel,
        grid=(1,),
        in_specs=specs,
        out_specs=whole(SHARD, width),
        out_shape=shape_of((SHARD, width), F32),
        compiler_params=PARAMS,
        cost_estimate=cost(SHARD * width, 6 * SHARD * width),
        name="unpack_qkv",
    )(*[tiles] * len(specs))


def norm_scale(values):
    return lax.rsqrt(jnp.mean(values * values, axis=-1, keepdims=True) + EPS)


def norm_back(values, scale, gain, grad):
    pulled = grad * gain
    inner = jnp.mean(pulled * values, axis=-1, keepdims=True)
    d_values = scale * pulled - values * (scale * scale * scale) * inner
    return d_values, jnp.sum(grad * values * scale, axis=0)


def columns_of(weight, start, width):
    part = weight[:, start : start + NF * width]
    return part.reshape(weight.shape[0], NF, width).transpose(1, 0, 2)


def shards(
    tokens,
    norm_gain,
    w_in,
    w_qkv,
    conv_weight,
    conv_bias,
    dt_bias,
    a_log,
    d_skip,
    mamba_gain,
    w_mout,
    w_aout,
    mlp_gain,
    w_gate_up,
    w_down,
    cotangent,
):
    ctx = lax.axis_index("ctx")
    fsdp = lax.axis_index("fsdp")
    parity = ctx % 2
    odd = parity.astype(jnp.int32).reshape(1)
    z_at, core = fsdp // 2, fsdp % 2
    pieces = jnp.arange(NF, dtype=jnp.int32)
    order = ((z_at + pieces % NZ) % NZ) * 2 + (core + pieces // NZ) % 2
    place = ((pieces % 2 + core) % 2) * NZ + (pieces // 2 - z_at) % NZ

    def even_first(rows):
        rows = rows.reshape(2, HALF, D)
        return jnp.where(parity == 1, rows[::-1], rows).reshape(ROWS, D)

    spot = jnp.concatenate([place[::2] % NZ, core.astype(jnp.int32).reshape(1)])

    hidden = even_first(tokens).astype(F32)
    scale_one = norm_scale(hidden)
    normed = ring_gather((hidden * scale_one * norm_gain).astype(BF), order)

    in_rows = lax.dynamic_slice(w_in, (ctx * SLICE, 0), (SLICE, w_in.shape[1]))
    qkv_rows = lax.dynamic_slice(w_qkv, (ctx * SLICE, 0), (SLICE, w_qkv.shape[1]))
    parts = [
        columns_of(in_rows, INNER, INNER_F),
        columns_of(in_rows, 2 * INNER, BC_F),
        columns_of(in_rows, 2 * INNER + 2 * STATE, DT_F),
        jnp.zeros((NF, SLICE, LANES - BC_F - DT_F), BF),
        columns_of(qkv_rows, 0, HDIM),
    ]
    for start in (QHEADS * HDIM, (QHEADS + KVHEADS) * HDIM):
        pair = qkv_rows[:, start : start + KVHEADS * HDIM].reshape(SLICE, KVHEADS, HDIM)
        parts.append(jnp.repeat(pair.transpose(1, 0, 2), NF // KVHEADS, axis=0))
    parts += [
        columns_of(in_rows, 0, INNER_F),
    ]
    swapped, w_gate_up = together(swap_fsdp(jnp.concatenate(parts, axis=2)), w_gate_up)
    gu_rows = lax.dynamic_slice(w_gate_up, (ctx * SLICE, 0), (SLICE, w_gate_up.shape[1]))
    gu_swapped = jnp.concatenate(
        [columns_of(gu_rows, 0, FF_F), columns_of(gu_rows, FF, FF_F)], axis=2
    )
    w_one = lax.all_gather(swapped, "ctx", axis=0)
    normed, gu_swapped = together(normed, swap_fsdp(gu_swapped))
    w_out = jnp.concatenate([w_mout, w_aout], axis=0)
    cot_low = even_first(cotangent)

    blocks = jnp.stack([ctx, 2 * NC - 1 - ctx])
    blocks = jnp.where(parity == 1, blocks[::-1], blocks)
    positions = (
        blocks[:, None] * HALF + jnp.arange(HALF, dtype=jnp.int32)[None, :]
    ).reshape(ROWS)
    half_dim = HDIM // 2
    freqs = ROPE_BASE ** (-jnp.arange(half_dim, dtype=F32) / half_dim)
    angles = positions.astype(F32)[:, None] * freqs[None, :]
    cosine, sine = jnp.cos(angles), jnp.sin(angles)
    mix_pack, attn_pack = project(normed, w_one, cosine, sine)
    mix_pack, cot_low, normed = together(mix_pack, cot_low, normed)
    cot_all = gather_fsdp(cot_low)
    mix_got, gate_z, attn_pack = together(
        swap_ctx(mix_pack), project_z(normed, w_one), attn_pack
    )
    attn_got = swap_ctx(attn_pack)

    x_start = fsdp * INNER_F + parity * XW
    bc_start = INNER + fsdp * BC_F
    conv_all = jnp.concatenate(
        [conv_weight, conv_bias[None], jnp.zeros((3, conv_bias.shape[0]), F32)], axis=0
    )
    taps = jnp.concatenate(
        [
            lax.dynamic_slice(conv_all, (0, x_start), (8, XW)),
            lax.dynamic_slice(conv_all, (0, bc_start), (8, BC_F)),
        ],
        axis=1,
    ).T
    head = fsdp * DT_F + parity * HEADS_L
    my_bias = lax.dynamic_slice(dt_bias, (head,), (HEADS_L,))
    my_rate = -jnp.exp(lax.dynamic_slice(a_log, (head,), (HEADS_L,)))
    heads_in = jnp.broadcast_to(
        jnp.concatenate([my_bias, my_rate, jnp.zeros((8 - 2 * HEADS_L,), F32)])[:, None],
        (8, LANES),
    )
    my_skip = jnp.repeat(lax.dynamic_slice(d_skip, (head,), (HEADS_L,)), MDIM)[:, None]
    x_act, bc_own, row_terms = front(mix_got, taps, heads_in)
    bc_own, gu_swapped = together(bc_own, gu_swapped)
    w_gu = lax.all_gather(gu_swapped, "ctx", axis=0)
    bc = jnp.concatenate(ring_pieces(bc_own), axis=0).reshape(NF, BC_F, LENGTH)
    ssd_seq, states = mamba_fwd(place, x_act, bc, row_terms, my_skip)
    ssd_seq, attn_got, cot_all = together(ssd_seq, attn_got, cot_all)
    heads_seq, lse = attn_fwd(odd, attn_got)
    ssd, heads_seq = together(swap_ctx(ssd_seq), heads_seq)
    heads = swap_ctx(heads_seq)

    my_gain = lax.dynamic_slice(mamba_gain, (fsdp * INNER_F,), (INNER_F,))[:, None]
    g, squares = gate(ssd, gate_z)
    squares, w_gu = together(butterfly(squares, "fsdp", (1, 2, 4)), w_gu)
    gated_heads, branches = branch_out(heads, g, squares, my_gain, w_out)
    branches, cot_all = together(branches, cot_all)
    mixed = hidden + scatter_fsdp(branches)

    scale_two = norm_scale(mixed)
    normed_two, d_act = together(
        gather_fsdp((mixed * scale_two * mlp_gain).astype(BF)), act_back(cot_all, w_down)
    )
    act, d_gu, d_normed_two = mlp(normed_two, d_act, w_gu)
    down_mine, down_other = down_out(spot, act, w_down)

    def side_by_side(*terms):
        return jnp.concatenate([term.reshape(NC, -1, LANES) for term in terms], axis=1)

    def total_of(got):
        return jnp.sum(got.astype(F32), axis=0).astype(BF)

    along_y = [[x * NY + y for y in range(NY)] for x in range(NC // NY)]
    along_x = [[x * NY + y for x in range(NC // NY)] for y in range(NY)]

    def scatter_ctx(joined, groups):
        joined = joined.reshape(len(groups[0]), -1, LANES)
        part = lax.psum_scatter(
            joined, "ctx", scatter_dimension=0, axis_index_groups=groups, tiled=False
        )
        return lax.optimization_barrier(part)

    def all_ctx(parts):
        joined = jnp.concatenate(parts, axis=0)
        return lax.all_gather(joined.reshape(-1, SLICE, LANES), "ctx", axis=0)

    gu_tiles = MLP_COLS // LANES
    row_tiles = OUT_ROWS // SHARD * (D // LANES)
    got_down = swap_ctx(column_grad(act, cot_all).reshape(NC, -1, LANES))
    packed_gu = column_grad(normed_two, d_gu, by_y=True)
    d_normed_two, packed_gu, down_mine, down_other, got_down = together(
        scatter_fsdp(d_normed_two), packed_gu, down_mine, down_other, got_down
    )
    sum_gu = scatter_ctx(packed_gu, along_y)
    sum_down = total_of(got_down)
    d_mixed, g_mlp_gain = norm_back(mixed, scale_two, mlp_gain, d_normed_two)
    d_mixed = d_mixed + cot_low.astype(F32)
    branch = ring_gather(d_mixed.astype(BF), order)

    dg, inner, dh = branch_back(branch, w_out, g, my_gain)
    inner = butterfly(inner, "fsdp", (1, 2, 4))
    d_mixers, dz, g_mamba_gain = gate_back(
        ssd, gate_z, g, dg, dh, squares, inner, my_gain
    )
    d_mixers, sum_gu = together(d_mixers, sum_gu)
    sum_gu = scatter_ctx(sum_gu, along_x)
    d_mixers = swap_ctx(d_mixers)
    packed_two = side_by_side(
        column_grad(gated_heads, branch, by_y=True), column_grad(normed, dz, by_y=True)
    )
    d_mixers, packed_two, sum_gu = together(d_mixers, packed_two, sum_gu)
    sum_two = scatter_ctx(packed_two, along_y)
    dx, dbc_mine, dbc_other, drow, dskip = mamba_bwd(
        place, x_act, d_mixers, bc, row_terms, states, my_skip
    )
    dbc_joined = ring_join(
        dbc_mine.reshape(NZ * BC_F, LENGTH), dbc_other.reshape(NZ * BC_F, LENGTH)
    )
    dx, d_mixers = together(dx, d_mixers)
    down_at = NF * gu_tiles
    out_at = down_at + row_tiles
    gu_part = swap_fsdp(sum_gu.reshape(NF, -1, LANES))
    dbc_joined, gu_part = together(dbc_joined, gu_part)
    dbc_own, attn_pack, sum_two = together(
        ring_scatter(dbc_joined), attn_bwd(odd, attn_got, d_mixers, lse), sum_two
    )
    sum_two = scatter_ctx(sum_two, along_x)
    attn_back = swap_ctx(attn_pack)
    mix_pack, g_taps, g_heads = front_back(
        mix_got, taps, heads_in, row_terms, drow, dx, dbc_own
    )
    mix_pack, attn_back, sum_two = together(mix_pack, attn_back, sum_two)
    all_one = all_ctx(
        [
            gu_part.reshape(-1, LANES),
            sum_down,
            sum_two[: row_tiles * SLICE],
        ]
    )
    mix_back, d_qkv = together(swap_ctx(mix_pack), attn_grads(attn_back, cosine, sine))
    d_mix = mix_grads(mix_back)
    packed_mix, dz = together(column_grad(normed, d_mix, d_qkv).reshape(NC, -1, LANES), dz)
    mine, other, gain_sum = back_project(spot, d_mix, d_qkv, dz, normed, w_one)
    g_norm_gain = gain_sum[0] / norm_gain

    def joined(mine, other):
        return ring_join(mine.reshape(NZ * ROWS, D), other.reshape(NZ * ROWS, D))

    mine, down_other = together(mine, down_other)
    got_mix, d_normed, down = together(
        swap_ctx(packed_mix), joined(mine, other), joined(down_mine, down_other)
    )
    def by_half(values):
        zero = jnp.zeros_like(values)
        return jnp.where(
            parity == 1, jnp.stack([zero, values], axis=-2), jnp.stack([values, zero], axis=-2)
        )

    g_conv = g_taps.T[: CONV_K + 1]
    g_d_skip = jnp.sum(dskip.reshape(HEADS_L, MDIM), axis=1)
    per_head = jnp.stack(
        [g_heads[:HEADS_L, 0], g_heads[HEADS_L : 2 * HEADS_L, 0], g_d_skip]
    )
    own = jnp.concatenate(
        [
            by_half(g_conv[:, :XW]).reshape(-1),
            g_conv[:, XW:].reshape(-1),
            g_mamba_gain[:, 0],
            by_half(per_head).reshape(-1),
        ]
    )
    own_size = own.shape[0]
    own_pad = -(-own_size // LANES) * LANES
    own = jnp.concatenate([own, jnp.zeros((own_pad - own_size,), F32), g_mlp_gain, g_norm_gain])

    own, got_mix = together(own.reshape(-1, LANES), got_mix)
    own = butterfly(own, "ctx", (1, 2))
    columns = swap_fsdp(
        jnp.concatenate(
            [
                sum_two[row_tiles * SLICE :].reshape(NF, -1, LANES),
                total_of(got_mix).reshape(NF, -1, LANES),
            ],
            axis=1,
        )
    )
    columns, all_one = together(columns, all_one)
    all_two = all_ctx([columns.reshape(-1, LANES)])
    both = jnp.concatenate([d_normed, down], axis=1)
    own, *both = together(butterfly(own, "ctx", (4,)), *ring_first(both))
    own = butterfly(own, "ctx", (8,)).reshape(-1)
    mine = (jnp.arange(NF) == fsdp)[:, None]
    placed = jnp.where(mine, own[None, :own_pad], 0.0).reshape(-1)
    total = jnp.concatenate([placed, own[own_pad:]]).reshape(-1, LANES)
    total, g_gate_up, g_down, g_mout, g_aout, *both = together(
        butterfly(total, "fsdp", (1,)),
        unpack_gate_up(all_one),
        *unpack_rows(all_one, down_at),
        *ring_second(*both),
    )
    both = ring_last(*both)
    d_normed, down = both[:, :D], both[:, D:]
    output = even_first((mixed + down).astype(BF)).reshape(tokens.shape)

    g_qkv = unpack_qkv(all_two)
    g_in = unpack_in(all_two).T
    d_hidden, _ = norm_back(hidden, scale_one, norm_gain, d_normed)
    d_tokens = even_first((d_hidden + d_mixed).astype(BF)).reshape(tokens.shape)

    total = butterfly(total, "fsdp", (2, 4)).reshape(-1)
    each = total[: NF * own_pad].reshape(NF, own_pad)
    cut = [(CONV_K + 1) * INNER_F]
    cut.append(cut[0] + (CONV_K + 1) * BC_F)
    cut.append(cut[1] + INNER_F)
    conv_x = each[:, : cut[0]].reshape(NF, CONV_K + 1, INNER_F).transpose(1, 0, 2)
    conv_bc = each[:, cut[0] : cut[1]].reshape(NF, CONV_K + 1, BC_F).transpose(1, 0, 2)
    conv = jnp.concatenate(
        [conv_x.reshape(CONV_K + 1, INNER), conv_bc.reshape(CONV_K + 1, 2 * STATE)], axis=1
    )
    per_head = each[:, cut[2] : cut[2] + 3 * DT_F].reshape(NF, 3, DT_F).transpose(1, 0, 2)
    per_head = per_head.reshape(3, MHEADS)
    gains = total[NF * own_pad :].reshape(2, D)
    return (
        output,
        d_tokens,
        gains[1],
        g_in,
        g_qkv,
        conv[:CONV_K],
        conv[CONV_K],
        per_head[0],
        per_head[1],
        per_head[2],
        each[:, cut[1] : cut[2]].reshape(INNER),
        g_mout,
        g_aout,
        gains[0],
        g_gate_up,
        g_down,
    )


def solution(mesh):
    tokens_at = P("fsdp", "ctx", None, None)
    rows_at = P("fsdp", None)
    placed = (
        tokens_at,
        P(),
        rows_at,
        rows_at,
        P(),
        P(),
        P(),
        P(),
        P(),
        P(),
        rows_at,
        rows_at,
        P(),
        rows_at,
        rows_at,
        tokens_at,
    )
    return jax.shard_map(
        shards,
        mesh=mesh,
        in_specs=placed,
        out_specs=(
            tokens_at,
            tokens_at,
            P(),
            rows_at,
            rows_at,
            P(),
            P(),
            P(),
            P(),
            P(),
            P(),
            rows_at,
            rows_at,
            P(),
            rows_at,
            rows_at,
        ),
        check_vma=False,
    )
```

```python
import functools

import jax
import jax.numpy as jnp
from jax import lax
from jax.experimental import pallas as pl
from jax.experimental.pallas import tpu as pltpu
from jax.sharding import PartitionSpec as P

D = 2048
MHEADS = 48
MDIM = 64
STATE = 256
CONV_K = 4
QHEADS = 8
KVHEADS = 2
HDIM = 128
FF = 4096
HALF = 64
INNER = 3072
LENGTH = 2048
SEQS = 8
NC = 16
NF = 8
NZ = 4
NY = 4
LANES = 128
ROWS = 2 * HALF
GROUP = SEQS * ROWS
INNER_F = INNER // NF
HEADS_L = 3
XW = HEADS_L * MDIM
BC_F = 2 * STATE // NF
DT_F = MHEADS // NF
FF_F = FF // NF
CHUNK = 256
CHUNKS = LENGTH // CHUNK
PAIRS = LENGTH // LANES
QROWS = LENGTH // 2
QBLOCK = 128
SHARD = D // NF
SLICE = SHARD // NC
MIX = INNER_F + LANES
QKV = 3 * HDIM
WM_COLS = MIX + QKV
W1_COLS = WM_COLS + INNER_F
MLP_COLS = 2 * FF_F
OUT_ROWS = INNER_F + HDIM
K_AT, V_AT, Q_AT, ATTN = 0, 128, 256, 320
XB = XW + BC_F
B_AT, T_AT, PACK = XW, XB, XB + 16
BOTH = XW + HALF
GATE_SEQS = 4
IN_SEQS = 4
PART = 16
EPS = 1e-06
ROPE_BASE = 100000000000.0
MASKED = -1e30
SCALE = HDIM ** (-0.5)
BF = jnp.bfloat16
F32 = jnp.float32
PARAMS = pltpu.CompilerParams(vmem_limit_bytes=56 * 1024 * 1024)
SMEM = pl.BlockSpec(memory_space=pltpu.SMEM)


def dot(left, right, left_dim, right_dim):
    return lax.dot_general(
        left, right, (((left_dim,), (right_dim,)), ((), ())), preferred_element_type=F32
    )


def whole(*shape):
    return pl.BlockSpec(shape, lambda *i: (0,) * len(shape))


def cost(flops, moved, transcendentals=0):
    return pl.CostEstimate(
        flops=int(flops), bytes_accessed=int(moved), transcendentals=int(transcendentals)
    )


def shape_of(shape, dtype):
    return jax.ShapeDtypeStruct(shape, dtype)


OTHER_CORE = [(i, i ^ 1) for i in range(NF)]
TO_NEXT = [(i, (i + 2) % NF) for i in range(NF)]
TO_PREV = [(i, (i - 2) % NF) for i in range(NF)]


def send(value, route):
    return lax.ppermute(value, "fsdp", route)


def gather_fsdp(value):
    return lax.all_gather(value, "fsdp", axis=0, tiled=True)


def scatter_fsdp(parts):
    return lax.psum_scatter(parts, "fsdp", scatter_dimension=0, tiled=True).astype(F32)


def ring_pieces(value):
    half = value.shape[0] // 2
    after = send(value, TO_PREV)
    before = send(value, TO_NEXT)
    near = send(value, OTHER_CORE)
    far = jnp.concatenate(
        [send(after[:half], TO_PREV), send(before[half:], TO_NEXT)], axis=0
    )
    near_after = send(after, OTHER_CORE)
    near_before = send(before, OTHER_CORE)
    near_far = send(far, OTHER_CORE)
    return [value, after, far, before, near, near_after, near_far, near_before]


def ring_gather(value, order):
    whole_value = jnp.zeros((NF * value.shape[0],) + value.shape[1:], value.dtype)
    for index, piece in enumerate(ring_pieces(value)):
        whole_value = lax.dynamic_update_slice(
            whole_value, piece, (order[index] * value.shape[0], 0)
        )
    return whole_value


def plus(*terms):
    return sum(term.astype(F32) for term in terms)


def ring_join(mine, other):
    return plus(mine, send(other, OTHER_CORE)).astype(BF)


def ring_first(joined):
    size = joined.shape[0] // NZ
    half = size // 2
    own, after, far, before = [joined[i * size : (i + 1) * size] for i in range(NZ)]
    sent = (
        send(far[:half], TO_NEXT),
        send(far[half:], TO_PREV),
        send(after[half:], TO_NEXT),
        send(before[:half], TO_PREV),
    )
    return own, after[:half], before[half:], *sent


def ring_second(own, after, before, far_next, far_prev, after_two, before_one):
    after_one = send(plus(after, far_next).astype(BF), TO_NEXT)
    before_two = send(plus(before, far_prev).astype(BF), TO_PREV)
    return own, after_one, after_two, before_one, before_two


def ring_last(own, after_one, after_two, before_one, before_two):
    return plus(
        own,
        jnp.concatenate([after_one, after_two], axis=0),
        jnp.concatenate([before_one, before_two], axis=0),
    )


def ring_scatter(joined):
    return ring_last(*ring_second(*ring_first(joined)))


def together(*values):
    return lax.optimization_barrier(values)


def swap_ctx(value):
    return lax.all_to_all(value, "ctx", 0, 0, tiled=True)


def swap_fsdp(value):
    return lax.all_to_all(value, "fsdp", 0, 0, tiled=True)


def exchange(value, axis, bit):
    size = lax.axis_size(axis)
    return value + lax.ppermute(value, axis, [(i, i ^ bit) for i in range(size)])


def butterfly(value, axis, bits):
    for bit in bits:
        value = exchange(value, axis, bit)
    return value


def rotate(values, cosine, sine):
    half = values.shape[-1] // 2
    first = values[:, :half]
    second = values[:, half:]
    return jnp.concatenate(
        [first * cosine - second * sine, second * cosine + first * sine], axis=1
    )


def proj_kernel(n_ref, w_ref, cos_ref, sin_ref, mix_ref, attn_ref):
    acc = jnp.zeros((2 * ROWS, WM_COLS), F32)
    for f in range(NF):
        acc = acc + dot(
            n_ref[:, f * SHARD : (f + 1) * SHARD],
            w_ref[:, f, :, :WM_COLS].reshape(SHARD, WM_COLS),
            1,
            0,
        )
    for j in range(2):
        rows = acc[j * ROWS : (j + 1) * ROWS]
        x_rows = rows[:, :INNER_F].T.astype(BF)
        tail = rows[:, INNER_F:MIX].T
        query = rotate(rows[:, MIX : MIX + HDIM], cos_ref[...], sin_ref[...]).astype(BF)
        key = rotate(
            rows[:, MIX + HDIM : MIX + 2 * HDIM], cos_ref[...], sin_ref[...]
        ).astype(BF)
        value = rows[:, MIX + 2 * HDIM :].astype(BF)
        for p in range(2):
            to = 2 * j + p
            attn_ref[to, K_AT:V_AT] = key
            attn_ref[to, V_AT:Q_AT] = value
            attn_ref[to, Q_AT:] = query[p * HALF : (p + 1) * HALF]
            mix_ref[to, :B_AT] = x_rows[p * XW : (p + 1) * XW]
            mix_ref[to, B_AT:T_AT] = tail[:BC_F].astype(BF)
            steps = tail[BC_F + p * HEADS_L : BC_F + (p + 1) * HEADS_L]
            high = steps.astype(BF).astype(F32)
            mix_ref[to, T_AT:] = jnp.concatenate(
                [high, steps - high, jnp.zeros((16 - 2 * HEADS_L, ROWS), F32)], axis=0
            ).astype(BF)


def packets(rows):
    return pl.BlockSpec((4, rows, LANES), lambda i: (i, 0, 0))


def token_rows(width):
    return pl.BlockSpec((2 * ROWS, width), lambda i: (i, 0))


def project(normed, w_one, cosine, sine):
    return pl.pallas_call(
        proj_kernel,
        grid=(SEQS // 2,),
        in_specs=[
            token_rows(D),
            whole(NC, NF, SLICE, W1_COLS),
            whole(ROWS, HALF),
            whole(ROWS, HALF),
        ],
        out_specs=[packets(PACK), packets(ATTN)],
        out_shape=[shape_of((NC, PACK, LANES), BF), shape_of((NC, ATTN, LANES), BF)],
        compiler_params=PARAMS,
        cost_estimate=cost(2 * GROUP * D * WM_COLS, 10e6),
        name="project",
    )(normed, w_one, cosine, sine)


def proj_z_kernel(n_ref, w_ref, z_ref):
    acc = jnp.zeros((2 * ROWS, INNER_F), F32)
    for f in range(NF):
        acc = acc + dot(
            n_ref[:, f * SHARD : (f + 1) * SHARD],
            w_ref[:, f, :, WM_COLS:].reshape(SHARD, INNER_F),
            1,
            0,
        )
    for j in range(2):
        z_ref[j] = acc[j * ROWS : (j + 1) * ROWS].T


def project_z(normed, w_z):
    return pl.pallas_call(
        proj_z_kernel,
        grid=(SEQS // 2,),
        in_specs=[token_rows(D), whole(NC, NF, SLICE, W1_COLS)],
        out_specs=pl.BlockSpec((2, INNER_F, ROWS), lambda i: (i, 0, 0)),
        out_shape=shape_of((SEQS, INNER_F, ROWS), F32),
        compiler_params=PARAMS,
        cost_estimate=cost(2 * GROUP * D * INNER_F, 8e6),
        name="project_z",
    )(normed, w_z)


def attn_grads_kernel(got_ref, cos_ref, sin_ref, out_ref):
    for j in range(2):
        one = got_ref[2 * j].astype(F32)
        two = got_ref[2 * j + 1].astype(F32)
        both = one + two
        query = jnp.concatenate([one[Q_AT:], two[Q_AT:]], axis=0)
        query = rotate(query, cos_ref[...], -sin_ref[...])
        key = rotate(both[K_AT:V_AT], cos_ref[...], -sin_ref[...])
        out_ref[j * ROWS : (j + 1) * ROWS] = jnp.concatenate(
            [query, key, both[V_AT:Q_AT]], axis=1
        ).astype(BF)


def attn_grads(got, cosine, sine):
    return pl.pallas_call(
        attn_grads_kernel,
        grid=(SEQS // 2,),
        in_specs=[packets(ATTN), whole(ROWS, HALF), whole(ROWS, HALF)],
        out_specs=token_rows(QKV),
        out_shape=shape_of((GROUP, QKV), BF),
        compiler_params=PARAMS,
        cost_estimate=cost(10 * GROUP * QKV, 2e6),
        name="attn_grads",
    )(got, cosine, sine)


def mix_grads_kernel(got_ref, out_ref):
    for j in range(2):
        one = got_ref[2 * j].astype(F32)
        two = got_ref[2 * j + 1].astype(F32)
        x_rows = jnp.concatenate([one[:B_AT], two[:B_AT]], axis=0).T
        tail = jnp.concatenate(
            [
                one[B_AT:T_AT] + two[B_AT:T_AT],
                one[T_AT : T_AT + HEADS_L],
                two[T_AT : T_AT + HEADS_L],
                jnp.zeros((LANES - BC_F - DT_F, ROWS), F32),
            ],
            axis=0,
        ).T
        out_ref[j * ROWS : (j + 1) * ROWS] = jnp.concatenate([x_rows, tail], axis=1).astype(BF)


def mix_grads(got):
    return pl.pallas_call(
        mix_grads_kernel,
        grid=(SEQS // 2,),
        in_specs=[packets(PACK)],
        out_specs=token_rows(MIX),
        out_shape=shape_of((GROUP, MIX), BF),
        compiler_params=PARAMS,
        cost_estimate=cost(4 * GROUP * MIX, 2.2e6),
        name="mix_grads",
    )(got)


def back_kernel(
    spot_ref, mix_ref, dqkv_ref, dz_ref, n_ref, w_ref, mine_ref, other_ref, gain_ref
):
    @pl.when(pl.program_id(0) == 0)
    def _():
        gain_ref[...] = jnp.zeros_like(gain_ref)

    first = spot_ref[NZ] == 0
    grad = jnp.concatenate([mix_ref[...], dqkv_ref[...], dz_ref[...]], axis=1)
    for f in range(NF):
        part = slice(f * SHARD, (f + 1) * SHARD)
        dn = dot(grad, w_ref[:, f].reshape(SHARD, W1_COLS), 1, 1)
        gain_ref[:, part] += jnp.sum(dn * n_ref[:, part].astype(F32), axis=0, keepdims=True)
        dn = dn.astype(BF)
        mine_ref[0, :, part] = jnp.where(first, dn[:ROWS], dn[ROWS:])
        other_ref[0, :, part] = jnp.where(first, dn[ROWS:], dn[:ROWS])


def back_project(spot, mix, dqkv, dz, normed, w_one):
    def rows(width):
        return pl.BlockSpec((2 * ROWS, width), lambda i, spot: (i, 0))

    specs, shapes = ring_specs(D)
    return pl.pallas_call(
        back_kernel,
        grid_spec=pltpu.PrefetchScalarGridSpec(
            num_scalar_prefetch=1,
            grid=(SEQS // 2,),
            in_specs=[
                rows(MIX),
                rows(QKV),
                rows(INNER_F),
                rows(D),
                pl.BlockSpec((NC, NF, SLICE, W1_COLS), lambda i, spot: (0, 0, 0, 0)),
            ],
            out_specs=specs + [pl.BlockSpec((1, D), lambda i, spot: (0, 0))],
        ),
        out_shape=shapes + [shape_of((1, D), F32)],
        compiler_params=PARAMS,
        cost_estimate=cost(2 * GROUP * D * W1_COLS, 18e6),
        name="back_project",
    )(spot, mix, dqkv, dz, normed, w_one)


def column_grad_kernel(by_y, left_ref, *refs):
    out_ref = refs[-1]
    first = 0
    for right_ref in refs[:-1]:
        term = dot(left_ref[...], right_ref[...], 0, 0).astype(BF)
        for block in range(out_ref.shape[1]):
            for tile in range(right_ref.shape[1] // LANES):
                part = term[
                    block * SHARD : (block + 1) * SHARD, tile * LANES : (tile + 1) * LANES
                ]
                if by_y:
                    part = part.reshape(NC // NY, NY, SLICE, LANES)
                    for y in range(NY):
                        rows = slice(y * NC // NY, (y + 1) * NC // NY)
                        out_ref[rows, block, first + tile] = part[:, y]
                else:
                    out_ref[:, block, first + tile] = part.reshape(NC, SLICE, LANES)
        first += right_ref.shape[1] // LANES


def column_grad(left, *rights, by_y=False):
    count, width = left.shape[1] // SHARD, sum(right.shape[1] for right in rights)
    tiles = width // LANES
    many = 2
    return pl.pallas_call(
        functools.partial(column_grad_kernel, by_y),
        grid=(count // many,),
        in_specs=[pl.BlockSpec((GROUP, many * SHARD), lambda i: (0, i))]
        + [whole(GROUP, right.shape[1]) for right in rights],
        out_specs=pl.BlockSpec((NC, many, tiles, SLICE, LANES), lambda i: (0, i, 0, 0, 0)),
        out_shape=shape_of((NC, count, tiles, SLICE, LANES), BF),
        compiler_params=PARAMS,
        cost_estimate=cost(
            2 * GROUP * left.shape[1] * width,
            2 * GROUP * (left.shape[1] + width) + 2 * left.shape[1] * width,
        ),
        name="column_grad",
    )(left, *rights)


def channels(count):
    return pl.BlockSpec((count, INNER_F, ROWS), lambda i: (i, 0, 0))


def gate_packets(rows):
    return pl.BlockSpec((2 * GATE_SEQS, rows, LANES), lambda i: (i, 0, 0))


def gate_kernel(got_ref, z_ref, g_ref, sq_ref):
    for j in range(GATE_SEQS):
        ssd = got_ref[2 * j : 2 * j + 2, :XW].reshape(INNER_F, ROWS).astype(F32)
        z = z_ref[j]
        g = ssd * (z * jax.nn.sigmoid(z))
        g_ref[j] = g
        seq = pl.program_id(0) * GATE_SEQS + j
        sq_ref[pl.ds(seq, 1)] = jnp.sum(g * g, axis=0, keepdims=True)


def gate(got, z):
    return pl.pallas_call(
        gate_kernel,
        grid=(SEQS // GATE_SEQS,),
        in_specs=[gate_packets(XW), channels(GATE_SEQS)],
        out_specs=[channels(GATE_SEQS), whole(SEQS, ROWS)],
        out_shape=[shape_of((SEQS, INNER_F, ROWS), F32), shape_of((SEQS, ROWS), F32)],
        compiler_params=PARAMS,
        cost_estimate=cost(8 * GROUP * INNER_F, 4.2e6, GROUP * INNER_F),
        name="gate",
    )(got, z)


def branch_kernel(heads_ref, g_ref, sq_ref, gain_ref, w_ref, gh_ref, out_ref):
    step = pl.program_id(0)
    for j in range(2):
        scale = lax.rsqrt(sq_ref[pl.ds(2 * step + j, 1)] / INNER + EPS)
        gated = (g_ref[j] * scale * gain_ref[...]).T.astype(BF)
        heads = heads_ref[2 * j : 2 * j + 2].reshape(ROWS, HDIM)
        gh_ref[j * ROWS : (j + 1) * ROWS] = jnp.concatenate([gated, heads], axis=1)
    out_ref[...] = dot(gh_ref[...], w_ref[...], 1, 0).astype(BF)


def branch_out(heads, g, squares, gain, w_out):
    return pl.pallas_call(
        branch_kernel,
        grid=(SEQS // 2,),
        in_specs=[
            packets(HALF),
            channels(2),
            whole(SEQS, ROWS),
            whole(INNER_F, 1),
            whole(OUT_ROWS, D),
        ],
        out_specs=[token_rows(OUT_ROWS), token_rows(D)],
        out_shape=[shape_of((GROUP, OUT_ROWS), BF), shape_of((GROUP, D), BF)],
        compiler_params=PARAMS,
        cost_estimate=cost(2 * GROUP * OUT_ROWS * D, 10e6),
        name="branch_out",
    )(heads, g, squares, gain, w_out)


def branch_back_kernel(d_ref, w_ref, g_ref, gain_ref, dg_ref, inner_ref, dh_ref):
    step = pl.program_id(0)
    both = dot(d_ref[...], w_ref[...], 1, 1)
    for j in range(2):
        rows = both[j * ROWS : (j + 1) * ROWS]
        d_gated = rows[:, :INNER_F].T
        dg_ref[j] = d_gated
        inner_ref[pl.ds(2 * step + j, 1)] = jnp.sum(
            d_gated * gain_ref[...] * g_ref[j], axis=0, keepdims=True
        )
        heads = rows[:, INNER_F:].astype(BF)
        dh_ref[2 * j : 2 * j + 2] = heads.reshape(2, HALF, HDIM)


def branch_back(branch, w_out, g, gain):
    return pl.pallas_call(
        branch_back_kernel,
        grid=(SEQS // 2,),
        in_specs=[token_rows(D), whole(OUT_ROWS, D), channels(2), whole(INNER_F, 1)],
        out_specs=[channels(2), whole(SEQS, ROWS), packets(HALF)],
        out_shape=[
            shape_of((SEQS, INNER_F, ROWS), F32),
            shape_of((SEQS, ROWS), F32),
            shape_of((NC, HALF, HDIM), BF),
        ],
        compiler_params=PARAMS,
        cost_estimate=cost(2 * GROUP * OUT_ROWS * D, 10e6),
        name="branch_back",
    )(branch, w_out, g, gain)


def gate_back_kernel(
    got_ref, z_ref, g_ref, dg_ref, dh_ref, sq_ref, inner_ref, gain_ref,
    pack_ref, dz_ref, gain_grad_ref,
):
    index = pl.program_id(0)

    @pl.when(index == 0)
    def _():
        gain_grad_ref[...] = jnp.zeros_like(gain_grad_ref)

    pack_ref[:, XW:] = dh_ref[...]
    for j in range(GATE_SEQS):
        ssd = got_ref[2 * j : 2 * j + 2, :XW].reshape(INNER_F, ROWS).astype(F32)
        z = z_ref[j]
        g = g_ref[j]
        sig = jax.nn.sigmoid(z)
        silu = z * sig
        seq = index * GATE_SEQS + j
        scale = lax.rsqrt(sq_ref[pl.ds(seq, 1)] / INNER + EPS)
        inner = inner_ref[pl.ds(seq, 1)] / INNER
        scaled = dg_ref[j] * scale
        d_g = scaled * gain_ref[...] - g * (scale * scale * scale * inner)
        gain_grad_ref[...] += jnp.sum(scaled * g, axis=1, keepdims=True)
        pack_ref[2 * j : 2 * j + 2, :XW] = (d_g * silu).astype(BF).reshape(2, XW, LANES)
        dz_ref[j * ROWS : (j + 1) * ROWS] = (
            (d_g * ssd * (sig + silu * (1.0 - sig))).T.astype(BF)
        )


def gate_back(got, z, g, dg, dh, squares, inner, gain):
    return pl.pallas_call(
        gate_back_kernel,
        grid=(SEQS // GATE_SEQS,),
        in_specs=[
            gate_packets(XW),
            channels(GATE_SEQS),
            channels(GATE_SEQS),
            channels(GATE_SEQS),
            gate_packets(HALF),
            whole(SEQS, ROWS),
            whole(SEQS, ROWS),
            whole(INNER_F, 1),
        ],
        out_specs=[
            gate_packets(BOTH),
            pl.BlockSpec((GATE_SEQS * ROWS, INNER_F), lambda i: (i, 0)),
            whole(INNER_F, 1),
        ],
        out_shape=[
            shape_of((NC, BOTH, LANES), BF),
            shape_of((GROUP, INNER_F), BF),
            shape_of((INNER_F, 1), F32),
        ],
        compiler_params=PARAMS,
        cost_estimate=cost(20 * GROUP * INNER_F, 8e6, GROUP * INNER_F),
        name="gate_back",
    )(got, z, g, dg, dh, squares, inner, gain)


def act_back_kernel(cot_ref, down_ref, out_ref):
    out_ref[...] = dot(cot_ref[...], down_ref[...], 1, 1)


def act_back(cot, w_down):
    return pl.pallas_call(
        act_back_kernel,
        grid=(SEQS // 2,),
        in_specs=[token_rows(D), whole(FF_F, D)],
        out_specs=token_rows(FF_F),
        out_shape=shape_of((GROUP, FF_F), F32),
        compiler_params=PARAMS,
        cost_estimate=cost(2 * GROUP * D * FF_F, 9e6),
        name="act_back",
    )(cot, w_down)


def mlp_kernel(n_ref, d_act_ref, w_ref, act_ref, dgu_ref, dn_ref):
    acc = jnp.zeros((2 * ROWS, MLP_COLS), F32)
    for f in range(NF):
        acc = acc + dot(
            n_ref[:, f * SHARD : (f + 1) * SHARD], w_ref[:, f].reshape(SHARD, MLP_COLS), 1, 0
        )
    gate_part, upper = acc[:, :FF_F], acc[:, FF_F:]
    sig = jax.nn.sigmoid(gate_part)
    silu = gate_part * sig
    act_ref[...] = (silu * upper).astype(BF)
    d_act = d_act_ref[...]
    d_gu = jnp.concatenate(
        [d_act * upper * (sig + silu * (1.0 - sig)), d_act * silu], axis=1
    ).astype(BF)
    dgu_ref[...] = d_gu
    for f in range(NF):
        dn_ref[:, f * SHARD : (f + 1) * SHARD] = dot(
            d_gu, w_ref[:, f].reshape(SHARD, MLP_COLS), 1, 1
        ).astype(BF)


def mlp(normed, d_act, w_gu):
    return pl.pallas_call(
        mlp_kernel,
        grid=(SEQS // 2,),
        in_specs=[token_rows(D), token_rows(FF_F), whole(NC, NF, SLICE, MLP_COLS)],
        out_specs=[token_rows(FF_F), token_rows(MLP_COLS), token_rows(D)],
        out_shape=[
            shape_of((GROUP, FF_F), BF),
            shape_of((GROUP, MLP_COLS), BF),
            shape_of((GROUP, D), BF),
        ],
        compiler_params=PARAMS,
        cost_estimate=cost(8 * GROUP * D * FF_F, 20e6, GROUP * FF_F),
        name="mlp",
    )(normed, d_act, w_gu)


def ring_specs(width):
    def spec(*_):
        return pl.BlockSpec((1, ROWS, width), lambda i, spot: (spot[i], 0, 0))

    return [spec(), spec()], [shape_of((NZ, ROWS, width), BF)] * 2


def down_kernel(spot_ref, act_ref, down_ref, mine_ref, other_ref):
    rows = dot(act_ref[...], down_ref[...], 1, 0).astype(BF)
    first = spot_ref[NZ] == 0
    mine_ref[0] = jnp.where(first, rows[:ROWS], rows[ROWS:])
    other_ref[0] = jnp.where(first, rows[ROWS:], rows[:ROWS])


def down_out(spot, act, w_down):
    specs, shapes = ring_specs(D)
    return pl.pallas_call(
        down_kernel,
        grid_spec=pltpu.PrefetchScalarGridSpec(
            num_scalar_prefetch=1,
            grid=(SEQS // 2,),
            in_specs=[
                pl.BlockSpec((2 * ROWS, FF_F), lambda i, spot: (i, 0)),
                pl.BlockSpec((FF_F, D), lambda i, spot: (0, 0)),
            ],
            out_specs=specs,
        ),
        out_shape=shapes,
        compiler_params=PARAMS,
        cost_estimate=cost(2 * GROUP * D * FF_F, 8e6),
        name="down_out",
    )(spot, act, w_down)


def lane_of(shape):
    return lax.broadcasted_iota(jnp.int32, shape, 1)


def sources(pair, first):
    if first:
        return 2 * pair, 2 * pair + 1
    return NC - 1 - 2 * pair, NC - 2 - 2 * pair


def assemble(ref, low, high, pair, first):
    one, two = sources(pair, first)
    left = lane_of((high - low, LANES)) < HALF
    return jnp.where(left, ref[one, low:high].astype(F32), ref[two, low:high].astype(F32))


def deal(ref, low, high, pair, first, values):
    one, two = sources(pair, first)
    values = values.astype(BF)
    ref[one, low:high, :HALF] = values[:, :HALF]
    ref[two, low:high, HALF:] = values[:, HALF:]


def taps_of(padded, taps):
    current = padded[:, LANES:]
    total = current * taps[:, CONV_K - 1 : CONV_K] + taps[:, CONV_K : CONV_K + 1]
    inputs = [current]
    for back in range(1, CONV_K):
        moved = pltpu.roll(padded, back, 1)[:, LANES:]
        inputs.append(moved)
        total = total + moved * taps[:, CONV_K - 1 - back : CONV_K - back]
    return inputs[::-1], total


def softplus(values):
    return jnp.maximum(values, 0.0) + jnp.log1p(jnp.exp(-jnp.abs(values)))


def at_pair(pair):
    return pl.ds(pl.multiple_of(pair * LANES, LANES), LANES)


def load_raw(got_ref, raw_ref):
    raw_ref[:, :LANES] = jnp.zeros((XB, LANES), F32)
    half_pairs = PAIRS // 2
    for first in (True, False):

        def load(pair, unused, first=first):
            place = at_pair((pair if first else pair + half_pairs) + 1)
            raw_ref[:, place] = assemble(got_ref, 0, XB, pair, first)
            return unused

        lax.fori_loop(0, half_pairs, load, 0, unroll=True)


def front_kernel(got_ref, taps_ref, heads_ref, x_ref, bc_ref, row_ref, raw_ref):
    load_raw(got_ref, raw_ref)

    def step(part, unused):
        rows = pl.ds(pl.multiple_of(part * PART, PART), PART)
        _, total = taps_of(raw_ref[rows], taps_ref[rows])
        active = (total * jax.nn.sigmoid(total)).astype(BF)

        @pl.when(part < XW // PART)
        def _():
            x_ref[rows] = active

        @pl.when(part >= XW // PART)
        def _():
            bc_ref[pl.ds(pl.multiple_of(part * PART - XW, PART), PART)] = active

        return unused

    lax.fori_loop(0, XB // PART, step, 0)
    half_pairs = PAIRS // 2
    parts = [
        assemble(got_ref, T_AT, PACK, index % half_pairs, index < half_pairs)
        for index in range(PAIRS)
    ]
    parts = jnp.concatenate(parts, axis=1)
    raw = parts[:HEADS_L] + parts[HEADS_L : 2 * HEADS_L] + heads_ref[:HEADS_L, :1]
    steps = softplus(raw)
    pad = jnp.zeros((8 - 2 * HEADS_L, LENGTH), F32)
    sums = jnp.concatenate([steps * heads_ref[HEADS_L : 2 * HEADS_L, :1], steps, pad], axis=0)
    rows = lax.broadcasted_iota(jnp.int32, sums.shape, 0)
    lane = lane_of(sums.shape) % CHUNK
    running = sums
    back = 1
    while back < CHUNK:
        running = running + jnp.where(lane >= back, pltpu.roll(running, back, 1), 0.0)
        back *= 2
    row_ref[:8] = jnp.where(rows < HEADS_L, running, sums)
    row_ref[8:] = jnp.concatenate([raw, jnp.zeros((8 - HEADS_L, LENGTH), F32)], axis=0)


def front(got, taps, heads):
    return pl.pallas_call(
        front_kernel,
        in_specs=[whole(NC, PACK, LANES), whole(XB, 8), whole(8, LANES)],
        out_specs=[whole(XW, LENGTH), whole(BC_F, LENGTH), whole(16, LENGTH)],
        out_shape=[
            shape_of((XW, LENGTH), BF),
            shape_of((BC_F, LENGTH), BF),
            shape_of((16, LENGTH), F32),
        ],
        grid=(1,),
        scratch_shapes=[pltpu.VMEM((XB, LENGTH + LANES), F32)],
        compiler_params=PARAMS,
        cost_estimate=cost(30 * XB * LENGTH, 4e6, XB * LENGTH),
        name="front",
    )(got, taps, heads)


def front_back_kernel(
    got_ref, taps_ref, heads_ref, row_ref, drow_ref, dx_ref, dbc_ref, pack_ref,
    taps_grad_ref, heads_grad_ref, raw_ref, grad_ref,
):
    half_pairs = PAIRS // 2
    load_raw(got_ref, raw_ref)

    grads = drow_ref[...]
    lane = lane_of(grads.shape) % CHUNK
    running = grads
    back = 1
    while back < CHUNK:
        running = running + jnp.where(
            lane < CHUNK - back, pltpu.roll(running, LENGTH - back, 1), 0.0
        )
        back *= 2
    rates = running[:HEADS_L]
    rate = heads_ref[HEADS_L : 2 * HEADS_L, :1]
    d_steps = grads[HEADS_L : 2 * HEADS_L] + rates * rate
    d_dt = d_steps * jax.nn.sigmoid(row_ref[8 : 8 + HEADS_L])
    steps = row_ref[HEADS_L : 2 * HEADS_L]
    heads_grad_ref[...] = jnp.concatenate(
        [
            jnp.sum(d_dt, axis=1, keepdims=True),
            jnp.sum(rates * steps, axis=1, keepdims=True) * rate,
            jnp.zeros((8 - 2 * HEADS_L, 1), F32),
        ],
        axis=0,
    )
    d_dt = jnp.concatenate([d_dt, jnp.zeros((16 - HEADS_L, LENGTH), F32)], axis=0)
    for index in range(PAIRS):
        first = index < half_pairs
        deal(
            pack_ref, T_AT, PACK, index % half_pairs, first,
            d_dt[:, index * LANES : (index + 1) * LANES],
        )

    def step(part, unused):
        rows = pl.ds(pl.multiple_of(part * PART, PART), PART)
        taps = taps_ref[rows]
        inputs, total = taps_of(raw_ref[rows], taps)
        sig = jax.nn.sigmoid(total)

        @pl.when(part < XW // PART)
        def _():
            grad_ref[:, :LENGTH] = dx_ref[rows]

        @pl.when(part >= XW // PART)
        def _():
            grad_ref[:, :LENGTH] = dbc_ref[pl.ds(pl.multiple_of(part * PART - XW, PART), PART)]

        grad = grad_ref[:, :LENGTH] * (sig + total * sig * (1.0 - sig))
        grad_ref[:, :LENGTH] = grad
        padded = grad_ref[...]
        d_raw = grad * taps[:, CONV_K - 1 : CONV_K]
        for ahead in range(1, CONV_K):
            moved = pltpu.roll(padded, LENGTH + LANES - ahead, 1)[:, :LENGTH]
            d_raw = d_raw + moved * taps[:, CONV_K - 1 - ahead : CONV_K - ahead]
        taps_grad_ref[rows] = jnp.concatenate(
            [jnp.sum(grad * moved, axis=1, keepdims=True) for moved in inputs]
            + [jnp.sum(grad, axis=1, keepdims=True)]
            + [jnp.zeros((PART, 8 - CONV_K - 1), F32)],
            axis=1,
        )
        raw_ref[rows, :LENGTH] = d_raw
        return unused

    grad_ref[:, LENGTH:] = jnp.zeros((PART, LANES), F32)
    lax.fori_loop(0, XB // PART, step, 0)
    for first in (True, False):

        def store(pair, unused, first=first):
            place = at_pair(pair if first else pair + half_pairs)
            deal(pack_ref, 0, XB, pair, first, raw_ref[:, place])
            return unused

        lax.fori_loop(0, half_pairs, store, 0, unroll=True)


def front_back(got, taps, heads, rows, drow, dx, dbc):
    return pl.pallas_call(
        front_back_kernel,
        in_specs=[
            whole(NC, PACK, LANES),
            whole(XB, 8),
            whole(8, LANES),
            whole(16, LENGTH),
            whole(8, LENGTH),
            whole(XW, LENGTH),
            whole(BC_F, LENGTH),
        ],
        out_specs=[whole(NC, PACK, LANES), whole(XB, 8), whole(8, 1)],
        out_shape=[
            shape_of((NC, PACK, LANES), BF),
            shape_of((XB, 8), F32),
            shape_of((8, 1), F32),
        ],
        grid=(1,),
        scratch_shapes=[
            pltpu.VMEM((XB, LENGTH + LANES), F32),
            pltpu.VMEM((PART, LENGTH + LANES), F32),
        ],
        compiler_params=PARAMS,
        cost_estimate=cost(60 * XB * LENGTH, 9e6, XB * LENGTH),
        name="front_back",
    )(got, taps, heads, rows, drow, dx, dbc)


def stacked(rows, width):
    return jnp.concatenate(
        [jnp.broadcast_to(row, (MDIM, width)) for row in rows], axis=0
    )


def state_sides(place_ref, bc_ref):
    quarter = STATE // BC_F
    bt = jnp.concatenate([bc_ref[place_ref[j]] for j in range(quarter)], axis=0)
    ct = jnp.concatenate([bc_ref[place_ref[quarter + j]] for j in range(quarter)], axis=0)
    return bt, ct


def chunk_terms(row_ref):
    rows = row_ref[...]
    cols = rows.T
    cum_row = [rows[h : h + 1] for h in range(HEADS_L)]
    dt_row = [rows[HEADS_L + h : HEADS_L + h + 1] for h in range(HEADS_L)]
    cum_col = [cols[:, h : h + 1] for h in range(HEADS_L)]
    dt_col = [cols[:, HEADS_L + h : HEADS_L + h + 1] for h in range(HEADS_L)]
    last = [row[:, CHUNK - 1 :] for row in cum_row]
    return cum_row, dt_row, cum_col, dt_col, last


def later_mask():
    shape = (CHUNK, CHUNK)
    return lax.broadcasted_iota(jnp.int32, shape, 1) >= lax.broadcasted_iota(jnp.int32, shape, 0)


def mamba_fwd_kernel(
    place_ref, x_ref, bc_ref, row_ref, skip_ref, pack_ref, st_out_ref, st_ref
):
    index = pl.program_id(0)

    @pl.when(index == 0)
    def _():
        st_ref[...] = jnp.zeros_like(st_ref)

    x_low = x_ref[...]
    x = x_low.astype(F32)
    bt, ct = state_sides(place_ref, bc_ref)
    st = st_ref[...]
    st_out_ref[0] = st
    cum_row, dt_row, cum_col, dt_col, last = chunk_terms(row_ref)
    inter = dot(bt, ct, 0, 0)
    carried = dot(st.astype(BF), ct, 1, 0)
    later = later_mask()
    within = []
    for h in range(HEADS_L):
        decay = jnp.exp(jnp.where(later, cum_row[h] - cum_col[h], MASKED))
        mixing = (inter * decay * dt_col[h]).astype(BF)
        within.append(dot(x_low[h * MDIM : (h + 1) * MDIM], mixing, 1, 0))
    entering = stacked([jnp.exp(row) for row in cum_row], CHUNK)
    y = jnp.concatenate(within, axis=0) + entering * carried + skip_ref[...] * x
    weights = stacked(
        [jnp.exp(end - row) * step for end, row, step in zip(last, cum_row, dt_row)], CHUNK
    )
    leaving = stacked([jnp.exp(end) for end in last], 1)
    st_ref[...] = st * leaving + dot((x * weights).astype(BF), bt, 1, 1)
    pairs = CHUNK // LANES
    early = index < CHUNKS // 2

    @pl.when(early)
    def _():
        for j in range(pairs):
            deal(pack_ref, 0, XW, pairs * index + j, True, y[:, j * LANES : (j + 1) * LANES])

    @pl.when(jnp.logical_not(early))
    def _():
        for j in range(pairs):
            deal(
                pack_ref, 0, XW, pairs * (index - CHUNKS // 2) + j, False,
                y[:, j * LANES : (j + 1) * LANES],
            )


def mamba_fwd(place, x, bc, rows, skip):
    return pl.pallas_call(
        mamba_fwd_kernel,
        grid=(CHUNKS,),
        in_specs=[
            SMEM,
            pl.BlockSpec((XW, CHUNK), lambda i: (0, i)),
            pl.BlockSpec((NF, BC_F, CHUNK), lambda i: (0, 0, i)),
            pl.BlockSpec((8, CHUNK), lambda i: (0, i)),
            whole(XW, 1),
        ],
        out_specs=[
            whole(NC, XW, LANES),
            pl.BlockSpec((1, XW, STATE), lambda i: (i, 0, 0)),
        ],
        out_shape=[
            shape_of((NC, XW, LANES), BF),
            shape_of((CHUNKS, XW, STATE), F32),
        ],
        scratch_shapes=[pltpu.VMEM((XW, STATE), F32)],
        compiler_params=PARAMS,
        cost_estimate=cost(2 * LENGTH * CHUNK * (STATE + 3 * XW), 7e6, LENGTH * CHUNK * 3),
        name="mamba_fwd",
    )(place, x, bc, rows, skip)


def mamba_bwd_kernel(
    place_ref, x_ref, got_ref, bc_ref, row_ref, st_in_ref, skip_ref,
    dx_ref, mine_ref, other_ref, drow_ref, dskip_ref, dst_ref, dy_ref,
):
    turn = pl.program_id(0)
    index = CHUNKS - 1 - turn
    pairs = CHUNK // LANES

    @pl.when(turn == 0)
    def _():
        dst_ref[...] = jnp.zeros_like(dst_ref)
        dskip_ref[...] = jnp.zeros_like(dskip_ref)

    @pl.when(index < CHUNKS // 2)
    def _():
        for j in range(pairs):
            dy_ref[:, j * LANES : (j + 1) * LANES] = assemble(
                got_ref, 0, XW, pairs * index + j, True
            )

    @pl.when(index >= CHUNKS // 2)
    def _():
        for j in range(pairs):
            dy_ref[:, j * LANES : (j + 1) * LANES] = assemble(
                got_ref, 0, XW, pairs * (index - CHUNKS // 2) + j, False
            )

    x_low = x_ref[...]
    x = x_low.astype(F32)
    dy = dy_ref[...]
    dy_low = dy.astype(BF)
    bt, ct = state_sides(place_ref, bc_ref)
    st = st_in_ref[0]
    dst = dst_ref[...]
    st_low = st.astype(BF)
    dst_low = dst.astype(BF)
    cum_row, dt_row, cum_col, dt_col, last = chunk_terms(row_ref)
    inter = dot(bt, ct, 0, 0)
    later = later_mask()
    entering = stacked([jnp.exp(row) for row in cum_row], CHUNK)
    tail = [jnp.exp(end - row) for end, row in zip(last, cum_row)]
    kept_row = [t * step for t, step in zip(tail, dt_row)]
    weights = stacked(kept_row, CHUNK)
    leaving = stacked([jnp.exp(end) for end in last], 1)
    carried = dot(st_low, ct, 1, 0) * entering
    reach = dot(dst_low, bt, 1, 0)
    dy_in = (dy * entering).astype(BF)
    x_out = (x * weights).astype(BF)
    along = dy * carried
    pulled = x * reach
    kept = jnp.sum(st * dst, axis=1, keepdims=True) * leaving
    d_inter = jnp.zeros((CHUNK, CHUNK), F32)
    dx_parts = []
    row_cum = []
    row_dt = []
    col_cum = []
    col_dt = []
    ends = lane_of((1, CHUNK)) == CHUNK - 1
    for h in range(HEADS_L):
        part = slice(h * MDIM, (h + 1) * MDIM)
        decay = jnp.exp(jnp.where(later, cum_row[h] - cum_col[h], MASKED))
        d_mix = dot(x_low[part], dy_low[part], 0, 0)
        scaled = decay * dt_col[h]
        d_inter = d_inter + d_mix * scaled
        mixing = inter * scaled
        dx_parts.append(dot(dy_low[part], mixing.astype(BF), 1, 1))
        to_dt = jnp.sum(d_mix * (inter * decay), axis=1, keepdims=True)
        q_row = jnp.sum(pulled[part], axis=0, keepdims=True)
        w_q = q_row * kept_row[h]
        d_last = jnp.sum(w_q, axis=1, keepdims=True) + jnp.sum(
            kept[part], axis=0, keepdims=True
        )
        row_cum.append(
            jnp.sum(d_mix * mixing, axis=0, keepdims=True)
            + jnp.sum(along[part], axis=0, keepdims=True)
            - w_q
            + jnp.where(ends, d_last, 0.0)
        )
        row_dt.append(q_row * tail[h])
        col_cum.append(-to_dt * dt_col[h])
        col_dt.append(to_dt)
    dx_ref[...] = jnp.concatenate(dx_parts, axis=0) + weights * reach + skip_ref[...] * dy
    d_low = d_inter.astype(BF)
    dbt = (dot(ct, d_low, 1, 1) + dot(dst_low, x_out, 0, 0)).astype(BF)
    dct = (dot(bt, d_low, 1, 0) + dot(st_low, dy_in, 0, 0)).astype(BF)
    quarter = STATE // BC_F
    parts = [
        grad[j * BC_F : (j + 1) * BC_F] for grad in (dbt, dct) for j in range(quarter)
    ]
    first = place_ref[0] < NZ
    for z in range(NZ):
        one, two = parts[2 * z], parts[2 * z + 1]
        distance = place_ref[2 * z] % NZ
        mine_ref[distance] = jnp.where(first, one, two)
        other_ref[distance] = jnp.where(first, two, one)
    dst_ref[...] = dst * leaving + dot(dy_in, ct, 1, 1)
    dskip_ref[...] += jnp.sum(dy * x, axis=1, keepdims=True)
    pad = jnp.zeros((CHUNK, 8 - 2 * HEADS_L), F32)
    columns = jnp.concatenate(col_cum + col_dt + [pad], axis=1).T
    drow_ref[...] = columns + jnp.concatenate(
        row_cum + row_dt + [jnp.zeros((8 - 2 * HEADS_L, CHUNK), F32)], axis=0
    )


def mamba_bwd(place, x, got, bc, rows, states, skip):
    end = CHUNKS - 1
    return pl.pallas_call(
        mamba_bwd_kernel,
        grid=(CHUNKS,),
        in_specs=[
            SMEM,
            pl.BlockSpec((XW, CHUNK), lambda i: (0, end - i)),
            whole(NC, BOTH, LANES),
            pl.BlockSpec((NF, BC_F, CHUNK), lambda i: (0, 0, end - i)),
            pl.BlockSpec((8, CHUNK), lambda i: (0, end - i)),
            pl.BlockSpec((1, XW, STATE), lambda i: (end - i, 0, 0)),
            whole(XW, 1),
        ],
        out_specs=[
            pl.BlockSpec((XW, CHUNK), lambda i: (0, end - i)),
            pl.BlockSpec((NZ, BC_F, CHUNK), lambda i: (0, 0, end - i)),
            pl.BlockSpec((NZ, BC_F, CHUNK), lambda i: (0, 0, end - i)),
            pl.BlockSpec((8, CHUNK), lambda i: (0, end - i)),
            whole(XW, 1),
        ],
        out_shape=[
            shape_of((XW, LENGTH), F32),
            shape_of((NZ, BC_F, LENGTH), BF),
            shape_of((NZ, BC_F, LENGTH), BF),
            shape_of((8, LENGTH), F32),
            shape_of((XW, 1), F32),
        ],
        scratch_shapes=[pltpu.VMEM((XW, STATE), F32), pltpu.VMEM((XW, CHUNK), F32)],
        compiler_params=PARAMS,
        cost_estimate=cost(
            2 * LENGTH * CHUNK * (3 * STATE + 7 * XW), 12e6, LENGTH * CHUNK * 3
        ),
        name="mamba_bwd",
    )(place, x, got, bc, rows, states, skip)


def position_of(source, odd, inside):
    block = jnp.where(source % 2 == odd, source, 2 * NC - 1 - source)
    return block * HALF + inside


def visible_mask(step, odd):
    key = lax.broadcasted_iota(jnp.int32, (1, LENGTH), 1)
    key_pos = position_of(key // ROWS, (key // HALF) % 2, key % HALF)
    query = lax.broadcasted_iota(jnp.int32, (QBLOCK, 1), 0)
    source = 2 * step + query // HALF
    query_pos = position_of(source, odd, query % HALF)
    return key_pos <= query_pos


def attn_fwd_kernel(odd_ref, q_ref, k_ref, v_ref, o_ref, lse_ref):
    q = q_ref[...].reshape(QBLOCK, HDIM)
    k = k_ref[...].reshape(LENGTH, HDIM)
    v = v_ref[...].reshape(LENGTH, HDIM)
    scores = dot(q, k, 1, 1) * SCALE
    scores = jnp.where(visible_mask(pl.program_id(0), odd_ref[0]), scores, MASKED)
    top = jnp.max(scores, axis=1, keepdims=True)
    grown = jnp.exp(scores - top)
    total = jnp.sum(grown, axis=1, keepdims=True)
    lse_ref[...] = top + jnp.log(total)
    probs = (grown * (1.0 / total)).astype(BF)
    o_ref[...] = dot(probs, v, 1, 0).astype(BF).reshape(2, HALF, HDIM)


def packed_part(at, rows, moving=False):
    block = at // rows
    if moving:
        return pl.BlockSpec((2, rows, HDIM), lambda i: (i, block, 0))
    return pl.BlockSpec((NC, rows, HDIM), lambda i: (0, block, 0))


def attn_fwd(odd, got):
    return pl.pallas_call(
        attn_fwd_kernel,
        grid=(QROWS // QBLOCK,),
        in_specs=[
            SMEM,
            packed_part(Q_AT, HALF, True),
            packed_part(K_AT, ROWS),
            packed_part(V_AT, ROWS),
        ],
        out_specs=[
            pl.BlockSpec((2, HALF, HDIM), lambda i: (i, 0, 0)),
            pl.BlockSpec((QBLOCK, 1), lambda i: (i, 0)),
        ],
        out_shape=[shape_of((NC, HALF, HDIM), BF), shape_of((QROWS, 1), F32)],
        compiler_params=PARAMS,
        cost_estimate=cost(4 * QROWS * LENGTH * HDIM, 3e6, QROWS * LENGTH),
        name="attn_fwd",
    )(odd, got, got, got)


def attn_bwd_kernel(
    odd_ref, q_ref, k_ref, v_ref, do_ref, lse_ref, pack_ref, dk_sum, dv_sum
):
    step = pl.program_id(0)

    @pl.when(step == 0)
    def _():
        dk_sum[...] = jnp.zeros_like(dk_sum)
        dv_sum[...] = jnp.zeros_like(dv_sum)

    q = q_ref[...].reshape(QBLOCK, HDIM)
    k = k_ref[...].reshape(LENGTH, HDIM)
    v = v_ref[...].reshape(LENGTH, HDIM)
    do = do_ref[...].reshape(QBLOCK, HDIM)
    scores = dot(q, k, 1, 1) * SCALE - lse_ref[...]
    probs = jnp.exp(jnp.where(visible_mask(step, odd_ref[0]), scores, MASKED))
    d_probs = dot(do, v, 1, 1)
    dv_sum[...] += dot(probs.astype(BF), do, 0, 0)
    inner = jnp.sum(probs * d_probs, axis=1, keepdims=True)
    d_scores = (probs * (d_probs - inner)).astype(BF)
    pack_ref[pl.ds(2 * step, 2), Q_AT:] = (
        (dot(d_scores, k, 1, 0) * SCALE).astype(BF).reshape(2, HALF, HDIM)
    )
    dk_sum[...] += dot(d_scores, q, 0, 0)

    @pl.when(step == pl.num_programs(0) - 1)
    def _():
        pack_ref[:, K_AT:V_AT] = (dk_sum[...] * SCALE).astype(BF).reshape(NC, ROWS, HDIM)
        pack_ref[:, V_AT:Q_AT] = dv_sum[...].astype(BF).reshape(NC, ROWS, HDIM)


def attn_bwd(odd, got, grads, lse):
    return pl.pallas_call(
        attn_bwd_kernel,
        grid=(QROWS // QBLOCK,),
        in_specs=[
            SMEM,
            packed_part(Q_AT, HALF, True),
            packed_part(K_AT, ROWS),
            packed_part(V_AT, ROWS),
            packed_part(XW, HALF, True),
            pl.BlockSpec((QBLOCK, 1), lambda i: (i, 0)),
        ],
        out_specs=whole(NC, ATTN, LANES),
        out_shape=shape_of((NC, ATTN, LANES), BF),
        scratch_shapes=[pltpu.VMEM((LENGTH, HDIM), F32), pltpu.VMEM((LENGTH, HDIM), F32)],
        compiler_params=PARAMS,
        cost_estimate=cost(10 * QROWS * LENGTH * HDIM, 4e6, QROWS * LENGTH),
        name="attn_bwd",
    )(odd, got, got, got, grads, lse)


def tiles_to_rows(refs):
    tiles = []
    for ref in refs:
        count = ref.shape[0] * SLICE
        for tile in range(ref.shape[1]):
            tiles.append(ref[:, tile].reshape(count, LANES).astype(F32))
    return jnp.concatenate(tiles, axis=1)


def unpack_kernel(*refs):
    refs[-1][...] = tiles_to_rows(refs[:-1])


def unpack_rows_kernel(tiles_ref, down_ref, mout_ref, aout_ref):
    step = pl.program_id(0)
    rows = tiles_to_rows([tiles_ref])
    last = pl.num_programs(0) - 1

    @pl.when(step < FF_F // LANES)
    def _():
        down_ref[...] = rows

    @pl.when((step >= FF_F // LANES) & (step < last))
    def _():
        mout_ref[...] = rows

    @pl.when(step == last)
    def _():
        aout_ref[...] = rows


def unpack_rows(tiles, at):
    width = D // LANES
    base = at // width
    downs, outs = FF_F // LANES, INNER_F // LANES

    def rows(index):
        return pl.BlockSpec((LANES, D), index)

    return pl.pallas_call(
        unpack_rows_kernel,
        grid=((FF_F + OUT_ROWS) // LANES,),
        in_specs=[
            pl.BlockSpec(
                (NC // 2, width, SLICE, LANES), lambda i: (i % 2, base + i // 2, 0, 0)
            )
        ],
        out_specs=[
            rows(lambda i: (jnp.minimum(i, downs - 1), 0)),
            rows(lambda i: (jnp.clip(i - downs, 0, outs - 1), 0)),
            rows(lambda i: (0, 0)),
        ],
        out_shape=[shape_of((FF_F, D), F32), shape_of((INNER_F, D), F32), shape_of((HDIM, D), F32)],
        compiler_params=PARAMS,
        cost_estimate=cost((FF_F + OUT_ROWS) * D, 6 * (FF_F + OUT_ROWS) * D),
        name="unpack_rows",
    )(tiles)


def unpack_gate_up(tiles):
    part = FF_F // LANES
    many = NF // 2

    def spec(j):
        return pl.BlockSpec(
            (NC, part, SLICE, LANES), lambda h, q: (0, 2 * (q * many + j) + h, 0, 0)
        )

    return pl.pallas_call(
        unpack_kernel,
        grid=(2, NF // many),
        in_specs=[spec(j) for j in range(many)],
        out_specs=pl.BlockSpec(
            (SHARD, many * FF_F), lambda h, q: (0, h * (NF // many) + q)
        ),
        out_shape=shape_of((SHARD, 2 * FF), F32),
        compiler_params=PARAMS,
        cost_estimate=cost(SHARD * 2 * FF, 6 * SHARD * 2 * FF),
        name="unpack_gate_up",
    )(*[tiles] * many)


def turned(ref, tile):
    return ref[:, tile].reshape(SHARD, LANES).astype(F32).T


def unpack_in_kernel(*refs):
    step = pl.program_id(0)
    steps = NF // IN_SEQS
    wide = INNER_F // LANES
    out_ref = refs[-1]

    @pl.when(step < 2 * steps)
    def _():
        for index in range(IN_SEQS):
            for tile in range(wide):
                start = index * INNER_F + tile * LANES
                out_ref[start : start + LANES] = turned(refs[index], tile)

    @pl.when(step == 2 * steps)
    def _():
        for f in range(NF):
            tail = turned(refs[IN_SEQS + f], 0)
            out_ref[f * BC_F : (f + 1) * BC_F] = tail[:BC_F]
            first = NF * BC_F + f * DT_F
            out_ref[first : first + DT_F] = tail[BC_F : BC_F + DT_F]


def unpack_in(tiles):
    wide = INNER_F // LANES
    half = NF // IN_SEQS
    each = W1_COLS // LANES

    def spec(j):
        def index(i):
            f = IN_SEQS * (jnp.minimum(i, 2 * half - 1) % half) + j
            return (0, each * f + jnp.where(i < half, 0, wide), 0, 0)

        shape = tuple(pl.Element(size) for size in (NC, wide, SLICE, LANES))
        return pl.BlockSpec(shape, index)

    def tail_spec(f):
        return pl.BlockSpec((NC, 1, SLICE, LANES), lambda i: (0, each * f + 2 * wide, 0, 0))

    specs = [spec(j) for j in range(IN_SEQS)]
    specs += [tail_spec(f) for f in range(NF)]
    return pl.pallas_call(
        unpack_in_kernel,
        grid=(2 * half + 1,),
        in_specs=specs,
        out_specs=pl.BlockSpec((IN_SEQS * INNER_F, SHARD), lambda i: (i, 0)),
        out_shape=shape_of((2 * INNER + 2 * STATE + MHEADS, SHARD), F32),
        compiler_params=PARAMS,
        cost_estimate=cost(SHARD * 6704, 6 * SHARD * 6704),
        name="unpack_in",
    )(*[tiles] * len(specs))


def unpack_qkv_kernel(*refs):
    group = NF // KVHEADS

    def tile(f, index):
        return refs[3 * f + index][:, 0].reshape(SHARD, HDIM).astype(F32)

    parts = [tile(f, 0) for f in range(NF)]
    for index in (1, 2):
        for head in range(KVHEADS):
            parts.append(sum(tile(head * group + j, index) for j in range(group)))
    refs[-1][...] = jnp.concatenate(parts, axis=1)


def unpack_qkv(tiles):
    each, first = W1_COLS // LANES, (INNER_F + MIX) // LANES
    specs = [
        pl.BlockSpec((NC, 1, SLICE, LANES), lambda i, at=each * f + first + index: (0, at, 0, 0))
        for f in range(NF)
        for index in range(3)
    ]
    width = (QHEADS + 2 * KVHEADS) * HDIM
    return pl.pallas_call(
        unpack_qkv_kernel,
        grid=(1,),
        in_specs=specs,
        out_specs=whole(SHARD, width),
        out_shape=shape_of((SHARD, width), F32),
        compiler_params=PARAMS,
        cost_estimate=cost(SHARD * width, 6 * SHARD * width),
        name="unpack_qkv",
    )(*[tiles] * len(specs))


def norm_scale(values):
    return lax.rsqrt(jnp.mean(values * values, axis=-1, keepdims=True) + EPS)


def norm_back(values, scale, gain, grad):
    pulled = grad * gain
    inner = jnp.mean(pulled * values, axis=-1, keepdims=True)
    d_values = scale * pulled - values * (scale * scale * scale) * inner
    return d_values, jnp.sum(grad * values * scale, axis=0)


def columns_of(weight, start, width):
    part = weight[:, start : start + NF * width]
    return part.reshape(weight.shape[0], NF, width).transpose(1, 0, 2)


def shards(
    tokens,
    norm_gain,
    w_in,
    w_qkv,
    conv_weight,
    conv_bias,
    dt_bias,
    a_log,
    d_skip,
    mamba_gain,
    w_mout,
    w_aout,
    mlp_gain,
    w_gate_up,
    w_down,
    cotangent,
):
    ctx = lax.axis_index("ctx")
    fsdp = lax.axis_index("fsdp")
    parity = ctx % 2
    odd = parity.astype(jnp.int32).reshape(1)
    z_at, core = fsdp // 2, fsdp % 2
    pieces = jnp.arange(NF, dtype=jnp.int32)
    order = ((z_at + pieces % NZ) % NZ) * 2 + (core + pieces // NZ) % 2
    place = ((pieces % 2 + core) % 2) * NZ + (pieces // 2 - z_at) % NZ

    def even_first(rows):
        rows = rows.reshape(2, HALF, D)
        return jnp.where(parity == 1, rows[::-1], rows).reshape(ROWS, D)

    spot = jnp.concatenate([place[::2] % NZ, core.astype(jnp.int32).reshape(1)])

    hidden = even_first(tokens).astype(F32)
    scale_one = norm_scale(hidden)
    normed = ring_gather((hidden * scale_one * norm_gain).astype(BF), order)

    in_rows = lax.dynamic_slice(w_in, (ctx * SLICE, 0), (SLICE, w_in.shape[1]))
    qkv_rows = lax.dynamic_slice(w_qkv, (ctx * SLICE, 0), (SLICE, w_qkv.shape[1]))
    parts = [
        columns_of(in_rows, INNER, INNER_F),
        columns_of(in_rows, 2 * INNER, BC_F),
        columns_of(in_rows, 2 * INNER + 2 * STATE, DT_F),
        jnp.zeros((NF, SLICE, LANES - BC_F - DT_F), BF),
        columns_of(qkv_rows, 0, HDIM),
    ]
    for start in (QHEADS * HDIM, (QHEADS + KVHEADS) * HDIM):
        pair = qkv_rows[:, start : start + KVHEADS * HDIM].reshape(SLICE, KVHEADS, HDIM)
        parts.append(jnp.repeat(pair.transpose(1, 0, 2), NF // KVHEADS, axis=0))
    parts += [
        columns_of(in_rows, 0, INNER_F),
    ]
    swapped, w_gate_up = together(swap_fsdp(jnp.concatenate(parts, axis=2)), w_gate_up)
    gu_rows = lax.dynamic_slice(w_gate_up, (ctx * SLICE, 0), (SLICE, w_gate_up.shape[1]))
    gu_swapped = jnp.concatenate(
        [columns_of(gu_rows, 0, FF_F), columns_of(gu_rows, FF, FF_F)], axis=2
    )
    w_one = lax.all_gather(swapped, "ctx", axis=0)
    normed, gu_swapped = together(normed, swap_fsdp(gu_swapped))
    w_out = jnp.concatenate([w_mout, w_aout], axis=0)
    cot_low = even_first(cotangent)

    blocks = jnp.stack([ctx, 2 * NC - 1 - ctx])
    blocks = jnp.where(parity == 1, blocks[::-1], blocks)
    positions = (
        blocks[:, None] * HALF + jnp.arange(HALF, dtype=jnp.int32)[None, :]
    ).reshape(ROWS)
    half_dim = HDIM // 2
    freqs = ROPE_BASE ** (-jnp.arange(half_dim, dtype=F32) / half_dim)
    angles = positions.astype(F32)[:, None] * freqs[None, :]
    cosine, sine = jnp.cos(angles), jnp.sin(angles)
    mix_pack, attn_pack = project(normed, w_one, cosine, sine)
    mix_pack, cot_low, normed = together(mix_pack, cot_low, normed)
    cot_all = gather_fsdp(cot_low)
    mix_got, gate_z, attn_pack = together(
        swap_ctx(mix_pack), project_z(normed, w_one), attn_pack
    )
    attn_got = swap_ctx(attn_pack)

    x_start = fsdp * INNER_F + parity * XW
    bc_start = INNER + fsdp * BC_F
    conv_all = jnp.concatenate(
        [conv_weight, conv_bias[None], jnp.zeros((3, conv_bias.shape[0]), F32)], axis=0
    )
    taps = jnp.concatenate(
        [
            lax.dynamic_slice(conv_all, (0, x_start), (8, XW)),
            lax.dynamic_slice(conv_all, (0, bc_start), (8, BC_F)),
        ],
        axis=1,
    ).T
    head = fsdp * DT_F + parity * HEADS_L
    my_bias = lax.dynamic_slice(dt_bias, (head,), (HEADS_L,))
    my_rate = -jnp.exp(lax.dynamic_slice(a_log, (head,), (HEADS_L,)))
    heads_in = jnp.broadcast_to(
        jnp.concatenate([my_bias, my_rate, jnp.zeros((8 - 2 * HEADS_L,), F32)])[:, None],
        (8, LANES),
    )
    my_skip = jnp.repeat(lax.dynamic_slice(d_skip, (head,), (HEADS_L,)), MDIM)[:, None]
    x_act, bc_own, row_terms = front(mix_got, taps, heads_in)
    bc_own, gu_swapped = together(bc_own, gu_swapped)
    w_gu = lax.all_gather(gu_swapped, "ctx", axis=0)
    bc = jnp.concatenate(ring_pieces(bc_own), axis=0).reshape(NF, BC_F, LENGTH)
    ssd_seq, states = mamba_fwd(place, x_act, bc, row_terms, my_skip)
    ssd_seq, attn_got, cot_all = together(ssd_seq, attn_got, cot_all)
    heads_seq, lse = attn_fwd(odd, attn_got)
    ssd, heads_seq = together(swap_ctx(ssd_seq), heads_seq)
    heads = swap_ctx(heads_seq)

    my_gain = lax.dynamic_slice(mamba_gain, (fsdp * INNER_F,), (INNER_F,))[:, None]
    g, squares = gate(ssd, gate_z)
    squares, w_gu = together(butterfly(squares, "fsdp", (1, 2, 4)), w_gu)
    gated_heads, branches = branch_out(heads, g, squares, my_gain, w_out)
    branches, cot_all = together(branches, cot_all)
    mixed = hidden + scatter_fsdp(branches)

    scale_two = norm_scale(mixed)
    normed_two, d_act = together(
        gather_fsdp((mixed * scale_two * mlp_gain).astype(BF)), act_back(cot_all, w_down)
    )
    act, d_gu, d_normed_two = mlp(normed_two, d_act, w_gu)
    down_mine, down_other = down_out(spot, act, w_down)

    def side_by_side(*terms):
        return jnp.concatenate([term.reshape(NC, -1, LANES) for term in terms], axis=1)

    def total_of(got):
        return jnp.sum(got.astype(F32), axis=0).astype(BF)

    along_y = [[x * NY + y for y in range(NY)] for x in range(NC // NY)]
    along_x = [[x * NY + y for x in range(NC // NY)] for y in range(NY)]

    def scatter_ctx(joined, groups):
        joined = joined.reshape(len(groups[0]), -1, LANES)
        part = lax.psum_scatter(
            joined, "ctx", scatter_dimension=0, axis_index_groups=groups, tiled=False
        )
        return lax.optimization_barrier(part)

    def all_ctx(parts):
        joined = jnp.concatenate(parts, axis=0)
        return lax.all_gather(joined.reshape(-1, SLICE, LANES), "ctx", axis=0)

    gu_tiles = MLP_COLS // LANES
    row_tiles = OUT_ROWS // SHARD * (D // LANES)
    got_down = swap_ctx(column_grad(act, cot_all).reshape(NC, -1, LANES))
    packed_gu = column_grad(normed_two, d_gu, by_y=True)
    d_normed_two, packed_gu, down_mine, down_other, got_down = together(
        scatter_fsdp(d_normed_two), packed_gu, down_mine, down_other, got_down
    )
    sum_gu = scatter_ctx(packed_gu, along_y)
    sum_down = total_of(got_down)
    d_mixed, g_mlp_gain = norm_back(mixed, scale_two, mlp_gain, d_normed_two)
    d_mixed = d_mixed + cot_low.astype(F32)
    branch = ring_gather(d_mixed.astype(BF), order)

    dg, inner, dh = branch_back(branch, w_out, g, my_gain)
    inner = butterfly(inner, "fsdp", (1, 2, 4))
    d_mixers, dz, g_mamba_gain = gate_back(
        ssd, gate_z, g, dg, dh, squares, inner, my_gain
    )
    d_mixers, sum_gu = together(d_mixers, sum_gu)
    sum_gu = scatter_ctx(sum_gu, along_x)
    d_mixers = swap_ctx(d_mixers)
    packed_two = side_by_side(
        column_grad(gated_heads, branch, by_y=True), column_grad(normed, dz, by_y=True)
    )
    d_mixers, packed_two = together(d_mixers, packed_two)
    sum_two = scatter_ctx(packed_two, along_y)
    dx, dbc_mine, dbc_other, drow, dskip = mamba_bwd(
        place, x_act, d_mixers, bc, row_terms, states, my_skip
    )
    dbc_joined = ring_join(
        dbc_mine.reshape(NZ * BC_F, LENGTH), dbc_other.reshape(NZ * BC_F, LENGTH)
    )
    dx, d_mixers, sum_gu = together(dx, d_mixers, sum_gu)
    down_at = NF * gu_tiles
    out_at = down_at + row_tiles
    gu_part = swap_fsdp(sum_gu.reshape(NF, -1, LANES))
    dbc_joined, gu_part = together(dbc_joined, gu_part)
    dbc_own, attn_pack, sum_two = together(
        ring_scatter(dbc_joined), attn_bwd(odd, attn_got, d_mixers, lse), sum_two
    )
    sum_two = scatter_ctx(sum_two, along_x)
    attn_back = swap_ctx(attn_pack)
    mix_pack, g_taps, g_heads = front_back(
        mix_got, taps, heads_in, row_terms, drow, dx, dbc_own
    )
    mix_pack, attn_back, sum_two = together(mix_pack, attn_back, sum_two)
    all_one = all_ctx(
        [
            gu_part.reshape(-1, LANES),
            sum_down,
            sum_two[: row_tiles * SLICE],
        ]
    )
    mix_back, d_qkv = together(swap_ctx(mix_pack), attn_grads(attn_back, cosine, sine))
    d_mix = mix_grads(mix_back)
    packed_mix, dz = together(column_grad(normed, d_mix, d_qkv).reshape(NC, -1, LANES), dz)
    mine, other, gain_sum = back_project(spot, d_mix, d_qkv, dz, normed, w_one)
    g_norm_gain = gain_sum[0] / norm_gain

    def joined(mine, other):
        return ring_join(mine.reshape(NZ * ROWS, D), other.reshape(NZ * ROWS, D))

    mine, down_other = together(mine, down_other)
    got_mix, d_normed, down = together(
        swap_ctx(packed_mix), joined(mine, other), joined(down_mine, down_other)
    )
    def by_half(values):
        zero = jnp.zeros_like(values)
        return jnp.where(
            parity == 1, jnp.stack([zero, values], axis=-2), jnp.stack([values, zero], axis=-2)
        )

    g_conv = g_taps.T[: CONV_K + 1]
    g_d_skip = jnp.sum(dskip.reshape(HEADS_L, MDIM), axis=1)
    per_head = jnp.stack(
        [g_heads[:HEADS_L, 0], g_heads[HEADS_L : 2 * HEADS_L, 0], g_d_skip]
    )
    own = jnp.concatenate(
        [
            by_half(g_conv[:, :XW]).reshape(-1),
            g_conv[:, XW:].reshape(-1),
            g_mamba_gain[:, 0],
            by_half(per_head).reshape(-1),
        ]
    )
    own_size = own.shape[0]
    own_pad = -(-own_size // LANES) * LANES
    own = jnp.concatenate([own, jnp.zeros((own_pad - own_size,), F32), g_mlp_gain, g_norm_gain])

    own, got_mix = together(own.reshape(-1, LANES), got_mix)
    own = butterfly(own, "ctx", (1, 2))
    columns = swap_fsdp(
        jnp.concatenate(
            [
                sum_two[row_tiles * SLICE :].reshape(NF, -1, LANES),
                total_of(got_mix).reshape(NF, -1, LANES),
            ],
            axis=1,
        )
    )
    columns, all_one = together(columns, all_one)
    all_two = all_ctx([columns.reshape(-1, LANES)])
    both = jnp.concatenate([d_normed, down], axis=1)
    own, *both = together(butterfly(own, "ctx", (4,)), *ring_first(both))
    own = butterfly(own, "ctx", (8,)).reshape(-1)
    mine = (jnp.arange(NF) == fsdp)[:, None]
    placed = jnp.where(mine, own[None, :own_pad], 0.0).reshape(-1)
    total = jnp.concatenate([placed, own[own_pad:]]).reshape(-1, LANES)
    total, g_gate_up, g_down, g_mout, g_aout, *both = together(
        butterfly(total, "fsdp", (1, 2, 4)),
        unpack_gate_up(all_one),
        *unpack_rows(all_one, down_at),
        *ring_second(*both),
    )
    both = ring_last(*both)
    d_normed, down = both[:, :D], both[:, D:]
    output = even_first((mixed + down).astype(BF)).reshape(tokens.shape)

    g_qkv = unpack_qkv(all_two)
    g_in = unpack_in(all_two).T
    d_hidden, _ = norm_back(hidden, scale_one, norm_gain, d_normed)
    d_tokens = even_first((d_hidden + d_mixed).astype(BF)).reshape(tokens.shape)

    total = total.reshape(-1)
    each = total[: NF * own_pad].reshape(NF, own_pad)
    cut = [(CONV_K + 1) * INNER_F]
    cut.append(cut[0] + (CONV_K + 1) * BC_F)
    cut.append(cut[1] + INNER_F)
    conv_x = each[:, : cut[0]].reshape(NF, CONV_K + 1, INNER_F).transpose(1, 0, 2)
    conv_bc = each[:, cut[0] : cut[1]].reshape(NF, CONV_K + 1, BC_F).transpose(1, 0, 2)
    conv = jnp.concatenate(
        [conv_x.reshape(CONV_K + 1, INNER), conv_bc.reshape(CONV_K + 1, 2 * STATE)], axis=1
    )
    per_head = each[:, cut[2] : cut[2] + 3 * DT_F].reshape(NF, 3, DT_F).transpose(1, 0, 2)
    per_head = per_head.reshape(3, MHEADS)
    gains = total[NF * own_pad :].reshape(2, D)
    return (
        output,
        d_tokens,
        gains[1],
        g_in,
        g_qkv,
        conv[:CONV_K],
        conv[CONV_K],
        per_head[0],
        per_head[1],
        per_head[2],
        each[:, cut[1] : cut[2]].reshape(INNER),
        g_mout,
        g_aout,
        gains[0],
        g_gate_up,
        g_down,
    )


def solution(mesh):
    tokens_at = P("fsdp", "ctx", None, None)
    rows_at = P("fsdp", None)
    placed = (
        tokens_at,
        P(),
        rows_at,
        rows_at,
        P(),
        P(),
        P(),
        P(),
        P(),
        P(),
        rows_at,
        rows_at,
        P(),
        rows_at,
        rows_at,
        tokens_at,
    )
    return jax.shard_map(
        shards,
        mesh=mesh,
        in_specs=placed,
        out_specs=(
            tokens_at,
            tokens_at,
            P(),
            rows_at,
            rows_at,
            P(),
            P(),
            P(),
            P(),
            P(),
            P(),
            rows_at,
            rows_at,
            P(),
            rows_at,
            rows_at,
        ),
        check_vma=False,
    )
```
